32 devices in a mesh: dp: 8 (over y, x, core), chan: 4 (over z).
Axes of the slice: x: 2, y: 2, z: 4, core: 2. Of those that a mesh axis runs over, the one named last changes fastest.
Arguments:
- mel_input: bfloat16 [80, 32, 1536], P('chan', 'dp'), may hold values from -6 to 6
- w_conv1: bfloat16 [3, 80, 768], replicated, may hold values from -0.375 to 0.375
- b_conv1: bfloat16 [768], replicated, may hold values from -4 to 4
- w_conv2: bfloat16 [3, 768, 768], replicated, may hold values from -0.125 to 0.125
- b_conv2: bfloat16 [768], replicated, may hold values from -4 to 4
- gain_attn: bfloat16 [768], replicated, may hold values from 0.5 to 1.5
- bias_attn: bfloat16 [768], replicated, may hold values from -3 to 3
- w_qkv: bfloat16 [768, 2304], replicated, may hold values from -0.375 to 0.375
- b_query: bfloat16 [768], replicated, may hold values from -4 to 4
- b_value: bfloat16 [768], replicated, may hold values from -0.75 to 0.75
- w_out: bfloat16 [768, 768], replicated, may hold values from -0.21875 to 0.21875
- b_out: bfloat16 [768], replicated, may hold values from -4 to 4
- gain_mlp: bfloat16 [768], replicated, may hold values from 0.5 to 1.5
- bias_mlp: bfloat16 [768], replicated, may hold values from -3 to 3
- w_up: bfloat16 [768, 3072], replicated, may hold values from -0.21875 to 0.21875
- b_up: bfloat16 [3072], replicated, may hold values from -4 to 4
- w_down: bfloat16 [3072, 768], replicated, may hold values from -0.109375 to 0.109375
- b_down: bfloat16 [768], replicated, may hold values from -4 to 4
- target: bfloat16 [32, 768, 768], P(('dp', 'chan')), may hold values from -12 to 12
- lengths: int32 [32], replicated, may hold values from 256 to 768, as said below
- row_clip: int32 [32], replicated, may hold values from 0 to 31, each once
- language: int32 [32], replicated, may hold values from 0 to 98
Outputs:
- block_out: bfloat16 [32, 768, 768], P(('dp', 'chan'))
- group_loss: float32 [99], replicated
- grad_mel: bfloat16 [80, 32, 1536], P('chan', 'dp')
- grad_w_conv1: float32 [3, 80, 768], P(None, 'chan', 'dp')
- grad_b_conv1: float32 [768], replicated
- grad_w_conv2: float32 [3, 768, 768], P(None, 'chan', 'dp')
- grad_b_conv2: float32 [768], replicated
- grad_gain_attn: float32 [768], replicated
- grad_bias_attn: float32 [768], replicated
- grad_w_qkv: float32 [768, 2304], P('dp', 'chan')
- grad_b_query: float32 [768], replicated
- grad_b_value: float32 [768], replicated
- grad_w_out: float32 [768, 768], P('dp', 'chan')
- grad_b_out: float32 [768], replicated
- grad_gain_mlp: float32 [768], replicated
- grad_bias_mlp: float32 [768], replicated
- grad_w_up: float32 [768, 3072], P('dp', 'chan')
- grad_b_up: float32 [3072], replicated
- grad_w_down: float32 [3072, 768], P('dp', 'chan')
- grad_b_down: float32 [768], replicated
The draws below stay inside these ranges and needn't reach their ends.
Inputs may be any that keep to these rules, and one draw needn't show every extreme that they name: `lengths`: valid downsampled frames of each clip; some clip has all 768. `row_clip`: each clip number appears once.
All inputs are finite; a program needn't handle non-finite values.
Results may differ from the reference program's by a relative error of at most 0.017.
Values may be sent and summed in bfloat16 or wider, within the bound.
A program may use at most 256 MiB of HBM per device.

```python
import math
import jax
import jax.numpy as jnp
import numpy as np
from jax import lax

D = 768
HEADS = 12
HEAD_DIM = 64
FF = 3072
N_MEL = 80
GROUPS = 99
FRAMES = 768
MEL_FRAMES = 1536
CLIPS = 32


def draw_lengths(key, part):
    key = jax.random.fold_in(key, 7)
    first_key, second_key = jax.random.split(key)
    counts = jax.random.randint(first_key, (CLIPS,), FRAMES // 3, FRAMES + 1)
    chosen = jax.random.randint(second_key, (), 0, CLIPS)
    return jnp.where(jnp.arange(CLIPS) == chosen, FRAMES, counts).astype(jnp.int32)


def place_ends(result, own_key, low, top_value):
    longest = result.shape.index(max(result.shape))
    spots = []
    for shift in (0, 1):
        where = [jax.random.randint(jax.random.fold_in(own_key, axis), (), 0, length) for axis, length in enumerate(result.shape)]
        where[longest] = (where[longest] + shift) % result.shape[longest]
        spots.append(tuple(where))
    return result.at[spots[0]].set(low).at[spots[1]].set(top_value)


def levels(stream_key, dims, shards, smallest, largest):
    gain, own = 1.0, jax.random.fold_in(stream_key, 6)
    for axis_at, blocks in shards:
        steps = jnp.exp(jax.random.uniform(jax.random.fold_in(own, axis_at), (blocks,), jnp.float32, smallest / len(shards), largest / len(shards)))
        gain = gain * jnp.repeat(steps, dims[axis_at] // blocks).reshape([-1 if axis == axis_at else 1 for axis in range(len(dims))])
    return gain


def rank_bounds(amount, skew):
    portions = [(1 << 20) // math.isqrt(standing ** skew) + 1 for standing in range(1, amount + 1)]
    deviation = 1 + sum(portions) // (1 << 30)
    return np.cumsum(np.array([max(1, weight // deviation) for weight in portions]))


def skewed_ids(key, shape, number_of, slope):
    listing = rank_bounds(number_of, slope)
    pick = jax.random.randint(jax.random.fold_in(key, 1), shape, 0, int(listing[number_of - 1]))
    rank = jnp.searchsorted(jnp.asarray(listing, jnp.int32), pick, side="right")
    return jax.random.permutation(jax.random.fold_in(key, 2), number_of)[rank].astype(jnp.int32)


def noise(key, extent, spread, bound, cuts=(), kind=jnp.bfloat16):
    factor_of = levels(key, extent, cuts, -0.22, 0.18) if cuts else 1.0
    values = jax.random.normal(key, extent, jnp.float32) * spread * factor_of
    return jnp.minimum(jnp.maximum(values, -bound), bound).astype(kind)


def setup_inputs(seed: int = 0) -> dict:
    arg_keys = jax.random.split(jax.random.key(seed), 23)
    return {
        "mel_input": noise(arg_keys[0], (N_MEL, CLIPS, MEL_FRAMES), 1.0, 6.0, ((0, 4), (1, 8))),
        "w_conv1": noise(arg_keys[1], (3, N_MEL, D), (3 * N_MEL) ** -0.5, 0.375),
        "b_conv1": noise(arg_keys[2], (D,), 0.3, 4.0),
        "w_conv2": noise(arg_keys[3], (3, D, D), (3 * D) ** -0.5, 0.125),
        "b_conv2": noise(arg_keys[4], (D,), 0.3, 4.0),
        "gain_attn": jnp.clip(1.0 + 0.1 * jax.random.normal(arg_keys[5], (D,), jnp.float32), 0.5, 1.5).astype(jnp.bfloat16),
        "bias_attn": noise(arg_keys[6], (D,), 0.2, 3.0),
        "w_qkv": noise(arg_keys[7], (D, 3 * D), (max(D // 3, 1)) ** -0.5, 0.375),
        "b_query": noise(arg_keys[8], (D,), 0.3, 4.0),
        "b_value": noise(arg_keys[9], (D,), 0.05, 0.75),
        "w_out": noise(arg_keys[10], (D, D), D ** -0.5, 0.21875),
        "b_out": noise(arg_keys[11], (D,), 0.3, 4.0),
        "gain_mlp": jnp.clip(1.0 + 0.1 * jax.random.normal(arg_keys[12], (D,), jnp.float32), 0.5, 1.5).astype(jnp.bfloat16),
        "bias_mlp": noise(arg_keys[13], (D,), 0.2, 3.0),
        "w_up": noise(arg_keys[14], (D, FF), D ** -0.5, 0.21875),
        "b_up": noise(arg_keys[15], (FF,), 0.3, 4.0),
        "w_down": noise(arg_keys[16], (FF, D), FF ** -0.5, 0.109375),
        "b_down": noise(arg_keys[17], (D,), 0.3, 4.0),
        "target": noise(arg_keys[18], (CLIPS, FRAMES, D), 2.0, 12.0, ((0, 32),)),
        "lengths": draw_lengths(jax.random.fold_in(arg_keys[22], 71), 0),
        "row_clip": jax.random.permutation(arg_keys[20], CLIPS).astype(jnp.int32),
        "language": place_ends(skewed_ids(arg_keys[21], (CLIPS,), GROUPS, 2), jax.random.fold_in(arg_keys[21], 3), 0, GROUPS - 1).astype(jnp.int32),
    }


precise = lax.Precision.HIGHEST

@jax.custom_vjp
def low(v):
    return lax.optimization_barrier(v.astype(jnp.bfloat16)).astype(jnp.float32)

@jax.custom_vjp
def low_back(v):
    return v

def low_keep(v):
    return (low(v), None)

def low_pass(kept, grad):
    return (grad,)

def back_keep(v):
    return (v, None)

def back_low(kept, grad):
    return (low(grad),)
low.defvjp(low_keep, low_pass)
low_back.defvjp(back_keep, back_low)

def gelu_exact(values):
    return jax.nn.gelu(values, approximate=False)

def normalize(values, ln_gain, ln_bias):
    average = lax.optimization_barrier(jnp.mean(values, axis=-1, keepdims=True))
    centred = values - average
    variance = lax.optimization_barrier(jnp.mean(centred * centred, axis=-1, keepdims=True))
    return centred * lax.rsqrt(variance + 1e-05) * ln_gain + ln_bias

def sinusoids(length, channels):
    half_width = channels // 2
    increment = math.log(10000.0) / (half_width - 1)
    inverse = jnp.exp(-increment * jnp.arange(half_width, dtype=jnp.float32))
    angles = jnp.arange(length, dtype=jnp.float32)[:, None] * inverse[None, :]
    return jnp.concatenate([jnp.sin(angles), jnp.cos(angles)], axis=1)

def clip_forward(weights, mel_clip, valid_len):
    w_conv1, b_conv1, w_conv2, b_conv2, gain_attn, bias_attn, w_qkv, b_query, b_value, w_out, b_out, gain_mlp, bias_mlp, w_up, b_up, w_down, b_down = weights
    padded = jnp.pad(mel_clip, ((0, 0), (1, 1)))
    conv_one = b_conv1[:, None]
    for offset in range(3):
        conv_one = conv_one + jnp.dot(w_conv1[offset].T, padded[:, offset:offset + MEL_FRAMES], precision=precise)
    conv_one = low_back(conv_one)
    act_one = low(gelu_exact(conv_one))
    padded = jnp.pad(act_one, ((0, 0), (1, 1)))
    second = b_conv2[None, :]
    for offset in range(3):
        second = second + jnp.dot(padded[:, offset:offset + 2 * FRAMES:2].T, w_conv2[offset], precision=precise)
    second = low_back(second)
    stem_out = low_back(low(gelu_exact(second) + sinusoids(FRAMES, D)))
    normed = low(normalize(stem_out, gain_attn, bias_attn))
    joined = jnp.dot(normed, w_qkv, precision=precise) + jnp.concatenate([b_query, jnp.zeros_like(b_query), b_value])
    joined = low_back(low(joined))
    query_heads = joined[:, :D].reshape(FRAMES, HEADS, HEAD_DIM)
    key_heads = joined[:, D:2 * D].reshape(FRAMES, HEADS, HEAD_DIM)
    value_heads = joined[:, 2 * D:].reshape(FRAMES, HEADS, HEAD_DIM)
    scores = jnp.einsum('qhd,khd->hqk', query_heads, key_heads, precision=precise) * HEAD_DIM ** (-0.5)
    scores = low_back(scores)
    key_ok = jnp.arange(FRAMES, dtype=jnp.int32) < valid_len
    scores = jnp.where(key_ok[None, None, :], scores, -1e+30)
    attention = jax.nn.softmax(scores, axis=-1)
    context = jnp.einsum('hqk,khd->qhd', low(attention), value_heads, precision=precise).reshape(FRAMES, D)
    context = low_back(low(context))
    attended = low_back(jnp.dot(context, w_out, precision=precise) + b_out)
    middle = stem_out + attended
    normed_two = low(normalize(middle, gain_mlp, bias_mlp))
    upward = low_back(jnp.dot(normed_two, w_up, precision=precise) + b_up)
    hidden = low(gelu_exact(upward))
    branch = low_back(jnp.dot(hidden, w_down, precision=precise) + b_down)
    return middle + branch

def reference(mel_input, w_conv1, b_conv1, w_conv2, b_conv2, gain_attn, bias_attn, w_qkv, b_query, b_value, w_out, b_out, gain_mlp, bias_mlp, w_up, b_up, w_down, b_down, target, lengths, row_clip, language):
    params = tuple((weight_arg.astype(jnp.float32) for weight_arg in (w_conv1, b_conv1, w_conv2, b_conv2, gain_attn, bias_attn, w_qkv, b_query, b_value, w_out, b_out, gain_mlp, bias_mlp, w_up, b_up, w_down, b_down)))
    row_length = lengths[row_clip].astype(jnp.int32)
    mel_clips = jnp.transpose(mel_input.astype(jnp.float32), (1, 0, 2))

    def forward(weights, clips_in):

        def one_clip(pieces):
            return jax.checkpoint(clip_forward)(weights, pieces[0], pieces[1])
        return lax.map(one_clip, (clips_in, row_length))
    outputs, pullback = jax.vjp(forward, params, mel_clips)
    frame_ok = (jnp.arange(FRAMES, dtype=jnp.int32)[None, :] < row_length[:, None]).astype(jnp.float32)
    mismatch = (outputs - target.astype(jnp.float32)) * frame_ok[:, :, None]
    gradients, mel_grad = pullback(mismatch)
    clip_loss = 0.5 * lax.optimization_barrier(jnp.sum(mismatch * mismatch, axis=(1, 2)))
    group_ids = jnp.arange(GROUPS, dtype=jnp.int32)
    member = language[row_clip][:, None] == group_ids[None, :]
    totals = lax.optimization_barrier(jnp.sum(jnp.where(member, clip_loss[:, None], 0.0), axis=0))
    member_all = language[:, None] == group_ids[None, :]
    frames_group = lax.optimization_barrier(jnp.sum(jnp.where(member_all, lengths[:, None], 0), axis=0))
    group_loss = totals / (D * jnp.maximum(frames_group, 1).astype(jnp.float32))
    grad_mel = jnp.transpose(mel_grad, (1, 0, 2)).astype(jnp.bfloat16)
    return (outputs.astype(jnp.bfloat16), group_loss, grad_mel, gradients[0], gradients[1], gradients[2], gradients[3], gradients[4], gradients[5], gradients[6], gradients[7], gradients[8], gradients[9], gradients[10], gradients[11], gradients[12], gradients[13], gradients[14], gradients[15], gradients[16])
```

```python
import math

import jax
import jax.numpy as jnp
import numpy as np
from jax import lax
from jax.sharding import PartitionSpec as P

HEAD_DIM = 64
GROUPS = 99

bf16 = jnp.bfloat16
f32 = jnp.float32
epsilon = 1e-05
masked_score = -1e30


def gelu_exact(values):
    return jax.nn.gelu(values, approximate=False)


def normalize(values, ln_gain, ln_bias):
    average = jnp.mean(values, axis=-1, keepdims=True)
    centred = values - average
    variance = jnp.mean(centred * centred, axis=-1, keepdims=True)
    return centred * lax.rsqrt(variance + epsilon) * ln_gain + ln_bias


def sinusoids(length, channels):
    half_width = channels // 2
    increment = math.log(10000.0) / (half_width - 1)
    inverse = np.exp(-increment * np.arange(half_width, dtype=np.float64))
    angles = np.arange(length, dtype=np.float64)[:, None] * inverse[None, :]
    return np.concatenate([np.sin(angles), np.cos(angles)], axis=1).astype(np.float32)


def lookup(row_id, table):
    matches = row_id == jnp.arange(table.shape[0], dtype=jnp.int32)
    return jnp.sum(jnp.where(matches, table, 0))


def mm(a, b):
    return jnp.dot(a, b, preferred_element_type=f32)


def mm_nt(a, b):
    return lax.dot_general(a, b, (((1,), (1,)), ((), ())), preferred_element_type=f32)


def mm_tn(a, b):
    return lax.dot_general(a, b, (((0,), (0,)), ((), ())), preferred_element_type=f32)


def ahead(values):
    return jnp.pad(values[1:], ((0, 1), (0, 0)))


def behind(values):
    return jnp.pad(values[:-1], ((1, 0), (0, 0)))


def pick_frames(mel_count, offset):
    frame = lax.broadcasted_iota(jnp.int32, (mel_count, mel_count // 2), 0)
    slot = lax.broadcasted_iota(jnp.int32, (mel_count, mel_count // 2), 1)
    return (frame == 2 * slot + offset).astype(bf16)


def heads_of(block):
    return block.reshape(block.shape[0], -1, HEAD_DIM).transpose(1, 0, 2)


def from_heads(items):
    return items.transpose(1, 0, 2).reshape(items.shape[1], -1)


def attend(pieces):
    query, key, value, key_ok = pieces
    scores = mm_nt(query, key) * HEAD_DIM ** (-0.5)
    scores = jnp.where(key_ok[None, :], scores, masked_score)
    exponent = jnp.exp(scores - jnp.max(scores, axis=-1, keepdims=True))
    attention = (exponent / jnp.sum(exponent, axis=-1, keepdims=True)).astype(bf16)
    return mm(attention, value).astype(bf16), attention


def attend_back(pieces):
    query, key, value, attention, grad = pieces
    weight = attention.astype(f32)
    grad_attention = mm_nt(grad, value)
    inner = jnp.sum(weight * grad_attention, axis=-1, keepdims=True)
    grad_scores = (weight * (grad_attention - inner)).astype(bf16)
    score_scale = HEAD_DIM ** (-0.5)
    return (
        (mm(grad_scores, key) * score_scale).astype(bf16),
        (mm_tn(grad_scores, query) * score_scale).astype(bf16),
        mm_tn(attention, grad).astype(bf16),
    )


def column_sum(values):
    return jnp.sum(values.astype(f32), axis=0)


def on_device(
    mel_input,
    w_conv1,
    b_conv1,
    w_conv2,
    b_conv2,
    gain_attn,
    bias_attn,
    w_qkv,
    b_query,
    b_value,
    w_out,
    b_out,
    gain_mlp,
    bias_mlp,
    w_up,
    b_up,
    w_down,
    b_down,
    target,
    lengths,
    row_clip,
    language,
):
    clip_count, frame_count, model_width = target.shape
    mel_count = mel_input.shape[2]
    row_at = lax.axis_index("dp") * lax.axis_size("chan") + lax.axis_index("chan")
    own_id = lax.dynamic_index_in_dim(row_clip, row_at * clip_count, keepdims=False)
    valid_len = lookup(own_id, lengths)
    own_lang = lookup(own_id, language)
    frame_ok = jnp.arange(frame_count, dtype=jnp.int32) < valid_len
    wide = lambda v: v.astype(f32)

    mel = lax.all_to_all(mel_input, "chan", split_axis=1, concat_axis=0, tiled=True)[:, 0]
    pick_even, pick_odd = pick_frames(mel_count, 0), pick_frames(mel_count, 1)
    mel_even = mm_tn(pick_even, mel.T).astype(bf16)
    mel_odd = mm_tn(pick_odd, mel.T).astype(bf16)
    taps_even = (behind(mel_odd), mel_even, mel_odd)
    taps_odd = (mel_even, mel_odd, ahead(mel_even))
    one_even = sum(mm(taps_even[j], w_conv1[j]) for j in range(3)) + wide(b_conv1)
    one_odd = sum(mm(taps_odd[j], w_conv1[j]) for j in range(3)) + wide(b_conv1)
    act_even, pull_even = jax.vjp(gelu_exact, one_even)
    act_odd, pull_odd = jax.vjp(gelu_exact, one_odd)
    act_even, act_odd = act_even.astype(bf16), act_odd.astype(bf16)
    taps_two = (behind(act_odd), act_even, act_odd)
    conv_two = sum(mm(taps_two[j], w_conv2[j]) for j in range(3)) + wide(b_conv2)
    act_two, pull_two = jax.vjp(gelu_exact, conv_two)
    stem = (act_two + sinusoids(frame_count, model_width)).astype(bf16)
    stem_float = stem.astype(f32)
    normed_a, norm_a_pull = jax.vjp(normalize, stem_float, wide(gain_attn), wide(bias_attn))
    normed_a = normed_a.astype(bf16)
    flat_zero = jnp.zeros((model_width,), f32)
    qkv_bias = jnp.concatenate([wide(b_query), flat_zero, wide(b_value)])
    joined = (mm(normed_a, w_qkv) + qkv_bias).astype(bf16)
    query, key, value = (
        heads_of(joined[:, i * model_width : (i + 1) * model_width]) for i in range(3)
    )
    head_count = query.shape[0]
    context, attention = lax.map(
        attend, (query, key, value, jnp.broadcast_to(frame_ok, (head_count, frame_count)))
    )
    context = from_heads(context)
    middle = stem_float + mm(context, w_out) + wide(b_out)
    normed_b, norm_b_pull = jax.vjp(normalize, middle, wide(gain_mlp), wide(bias_mlp))
    normed_b = normed_b.astype(bf16)
    upward = mm(normed_b, w_up) + wide(b_up)
    hidden, pull_up = jax.vjp(gelu_exact, upward)
    hidden = hidden.astype(bf16)
    final_rows = middle + mm(hidden, w_down) + wide(b_down)
    mismatch = jnp.where(frame_ok[:, None], final_rows - target[0].astype(f32), 0.0)
    clip_loss = 0.5 * jnp.sum(mismatch * mismatch)
    group_ids = jnp.arange(GROUPS, dtype=jnp.int32)
    group_part = jnp.where(own_lang == group_ids, clip_loss, 0.0)

    grad_branch = mismatch.astype(bf16)
    grad_b_down = column_sum(grad_branch)
    grad_w_down = mm_tn(hidden, grad_branch).astype(bf16)
    grad_up = pull_up(mm_nt(grad_branch, w_down))[0].astype(bf16)
    grad_b_up = column_sum(grad_up)
    grad_w_up = mm_tn(normed_b, grad_up).astype(bf16)
    grad_mid_norm, grad_gain_mlp, grad_bias_mlp = norm_b_pull(mm_nt(grad_up, w_up))
    grad_middle = mismatch + grad_mid_norm
    grad_attended = grad_middle.astype(bf16)
    grad_b_out = column_sum(grad_attended)
    grad_w_out = mm_tn(context, grad_attended).astype(bf16)
    grad_context = heads_of(mm_nt(grad_attended, w_out).astype(bf16))
    grads = lax.map(attend_back, (query, key, value, attention, grad_context))
    grad_joined = jnp.concatenate([from_heads(g) for g in grads], axis=1)
    grad_b_query = column_sum(grad_joined[:, :model_width])
    grad_b_value = column_sum(grad_joined[:, 2 * model_width :])
    grad_w_qkv = mm_tn(normed_a, grad_joined).astype(bf16)
    grad_stem_norm, grad_gain_attn, grad_bias_attn = norm_a_pull(mm_nt(grad_joined, w_qkv))
    grad_stem = (grad_middle + grad_stem_norm).astype(bf16)
    grad_two = pull_two(grad_stem.astype(f32))[0].astype(bf16)
    grad_b_two = column_sum(grad_two)
    grad_w_two = jnp.stack([mm_tn(taps_two[j], grad_two).astype(bf16) for j in range(3)])
    grad_act_even = mm_nt(grad_two, w_conv2[1])
    grad_act_odd = mm_nt(grad_two, w_conv2[2]) + mm_nt(ahead(grad_two), w_conv2[0])
    grad_even = pull_even(grad_act_even)[0].astype(bf16)
    grad_odd = pull_odd(grad_act_odd)[0].astype(bf16)
    grad_b_one = column_sum(grad_even) + column_sum(grad_odd)
    grad_w_one = jnp.stack(
        [
            (mm_tn(taps_even[j], grad_even) + mm_tn(taps_odd[j], grad_odd)).astype(bf16)
            for j in range(3)
        ]
    )
    grad_mel_even = (
        mm_nt(grad_odd, w_conv1[0]) + mm_nt(grad_even, w_conv1[1]) + mm_nt(behind(grad_odd), w_conv1[2])
    )
    grad_mel_odd = (
        mm_nt(ahead(grad_even), w_conv1[0]) + mm_nt(grad_odd, w_conv1[1]) + mm_nt(grad_even, w_conv1[2])
    )
    back_mel = (
        lax.dot_general(grad_mel_even.astype(bf16), pick_even, (((0,), (1,)), ((), ())), preferred_element_type=f32)
        + lax.dot_general(grad_mel_odd.astype(bf16), pick_odd, (((0,), (1,)), ((), ())), preferred_element_type=f32)
    ).astype(bf16)
    grad_mel = lax.all_to_all(back_mel[:, None], "chan", split_axis=0, concat_axis=1, tiled=True)

    def scatter(values, dp_at, chan_at):
        part = lax.psum_scatter(values, "dp", scatter_dimension=dp_at, tiled=True)
        return lax.psum_scatter(part, "chan", scatter_dimension=chan_at, tiled=True).astype(f32)

    final_down = scatter(grad_w_down, 0, 1)
    final_up = scatter(grad_w_up, 0, 1)
    final_out = scatter(grad_w_out, 0, 1)
    final_qkv = scatter(grad_w_qkv, 0, 1)
    part_two = scatter(grad_w_two, 2, 1)
    part_one = scatter(grad_w_one, 2, 1)
    totals_all = lax.psum(
        (
            group_part,
            grad_b_one,
            grad_b_two,
            grad_gain_attn,
            grad_bias_attn,
            grad_b_query,
            grad_b_value,
            grad_b_out,
            grad_gain_mlp,
            grad_bias_mlp,
            grad_b_up,
            grad_b_down,
        ),
        ("dp", "chan"),
    )
    member_all = language[:, None] == group_ids[None, :]
    frames_group = jnp.sum(jnp.where(member_all, lengths[:, None], 0), axis=0)
    group_loss = totals_all[0] / (model_width * jnp.maximum(frames_group, 1).astype(f32))
    block_out = final_rows.astype(bf16).reshape(clip_count, frame_count, model_width)
    return (
        block_out,
        group_loss,
        grad_mel,
        part_one,
        totals_all[1],
        part_two,
        totals_all[2],
        totals_all[3],
        totals_all[4],
        final_qkv,
        totals_all[5],
        totals_all[6],
        final_out,
        totals_all[7],
        totals_all[8],
        totals_all[9],
        final_up,
        totals_all[10],
        final_down,
        totals_all[11],
    )


def solution(mesh):
    whole = P()
    by_row = P(("dp", "chan"), None, None)
    return jax.shard_map(
        on_device,
        mesh=mesh,
        in_specs=(P("chan", "dp", None),) + (whole,) * 17 + (by_row,) + (whole,) * 3,
        out_specs=(
            by_row,
            whole,
            P("chan", "dp", None),
            P(None, "chan", "dp"),
            whole,
            P(None, "chan", "dp"),
            whole,
            whole,
            whole,
            P("dp", "chan"),
            whole,
            whole,
            P("dp", "chan"),
            whole,
            whole,
            whole,
            P("dp", "chan"),
            whole,
            P("dp", "chan"),
            whole,
        ),
        check_vma=False,
    )
```

```python
import math

import jax
import jax.numpy as jnp
import numpy as np
from jax import lax
from jax.experimental import pallas as pl
from jax.experimental.pallas import tpu as pltpu
from jax.sharding import PartitionSpec as P

HEAD_DIM = 64
GROUPS = 99

bf16 = jnp.bfloat16
f32 = jnp.float32
epsilon = 1e-05
masked_score = -1e30


def sinusoids(length, channels):
    half_width = channels // 2
    increment = math.log(10000.0) / (half_width - 1)
    inverse = np.exp(-increment * np.arange(half_width, dtype=np.float64))
    angles = np.arange(length, dtype=np.float64)[:, None] * inverse[None, :]
    return np.concatenate([np.sin(angles), np.cos(angles)], axis=1).astype(np.float32)


def lookup(row_id, table):
    matches = row_id == jnp.arange(table.shape[0], dtype=jnp.int32)
    return jnp.sum(jnp.where(matches, table, 0))


def mm(a, b):
    return jnp.dot(a, b, preferred_element_type=f32)


def mm_nt(a, b):
    return lax.dot_general(a, b, (((1,), (1,)), ((), ())), preferred_element_type=f32)


def mm_tn(a, b):
    return lax.dot_general(a, b, (((0,), (0,)), ((), ())), preferred_element_type=f32)


BLOCK = 256
VMEM_LIMIT = 60 * 1024 * 1024
TAIL_RATE = 0.31
TAIL = (
    0.12366556625478936,
    0.12390820374862553,
    0.10876305868035366,
    0.10683424297390944,
    -0.008837395578103507,
    0.14867850286492648,
    -0.13802626195746664,
    0.0350141511339579,
)


def gelu_pair(v):
    size = jnp.abs(v)
    base = 1.0 + TAIL_RATE * size
    rough = pl.reciprocal(base, approx=True)
    t = rough * (2.0 - base * rough)
    total = jnp.full_like(t, TAIL[-1])
    for coefficient in TAIL[-2::-1]:
        total = total * t + coefficient
    bell = jnp.exp(-0.5 * (v * v))
    tail = total * t * bell
    phi = jnp.where(v < 0.0, tail, 1.0 - tail)
    return v * phi, phi + v * (bell * (1.0 / math.sqrt(2.0 * math.pi)))


def turned(values):
    return values.astype(f32).T.astype(bf16)


def chunks(length, size):
    return [slice(at, min(at + size, length)) for at in range(0, length, size)]


def attend_kernel(len_ref, q_ref, k_ref, v_ref, ctx_ref, et_ref, inv_ref):
    length, width = q_ref.shape
    lane = lax.broadcasted_iota(jnp.int32, (length, width), 1)
    frame = lax.broadcasted_iota(jnp.int32, (length, width), 0)
    bias = jnp.where(frame < len_ref[0], 0.0, masked_score)
    q = q_ref[...].astype(f32) * HEAD_DIM ** (-0.5)
    k = k_ref[...].astype(f32)
    v_t = turned(v_ref[...])
    found = [[] for _ in chunks(length, BLOCK)]
    for h in range(2):
        mine = lane // HEAD_DIM == h
        spare = lane == HEAD_DIM * (1 - h)
        own_q = jnp.where(mine, q, jnp.where(spare, 1.0, 0.0)).astype(bf16)
        own_k = jnp.where(mine, k, jnp.where(spare, bias, 0.0)).astype(bf16)
        for at, cols in enumerate(chunks(length, BLOCK)):
            scores = mm_nt(own_k, own_q[cols])
            weight = jnp.exp(scores - jnp.max(scores, axis=0, keepdims=True))
            inverse = 1.0 / jnp.sum(weight, axis=0, keepdims=True)
            weight = weight.astype(bf16)
            et_ref[h, :, cols] = weight
            inv_ref[h, :, cols] = inverse
            found[at].append(mm(v_t[h * HEAD_DIM : (h + 1) * HEAD_DIM], weight) * inverse)
    for at, cols in enumerate(chunks(length, BLOCK)):
        ctx_ref[cols, :] = jnp.concatenate(found[at], axis=0).T.astype(bf16)


def attend_back_kernel(
    q_ref, k_ref, v_ref, et_ref, inv_ref, gctx_ref, ctx_ref, dq_ref, dk_ref, dv_ref, sums_ref, ds_ref
):
    length, width = q_ref.shape
    lane = lax.broadcasted_iota(jnp.int32, (length, width), 1)
    row = lax.broadcasted_iota(jnp.int32, (width, length), 0)
    scale = HEAD_DIM ** (-0.5)
    grad_t = gctx_ref[...].astype(f32).T * jnp.where(row < HEAD_DIM, inv_ref[0], inv_ref[1])
    grad_t = grad_t.astype(bf16).astype(f32)
    grad = grad_t.T
    inner_all = grad_t * ctx_ref[...].astype(f32).T
    k_t = turned(k_ref[...])
    q = q_ref[...].astype(f32) * scale
    v = v_ref[...].astype(f32)
    dq_t = []
    dk = jnp.zeros((length, width), f32)
    dv = jnp.zeros((length, width), f32)
    for h in range(2):
        at = HEAD_DIM * (1 - h)
        mine = lane // HEAD_DIM == h
        inner = jnp.sum(inner_all[h * HEAD_DIM : (h + 1) * HEAD_DIM], axis=0, keepdims=True)
        high = inner.astype(bf16).astype(f32)
        own_grad_t = jnp.where(row // HEAD_DIM == h, grad_t, 0.0)
        own_grad_t = jnp.where(row == at, -high, jnp.where(row == at + 1, high - inner, own_grad_t))
        own_grad_t = own_grad_t.astype(bf16)
        own_v = jnp.where(mine, v, jnp.where((lane == at) | (lane == at + 1), 1.0, 0.0)).astype(bf16)
        own_q = jnp.where(mine, q, 0.0).astype(bf16)
        own_grad = jnp.where(mine, grad, 0.0).astype(bf16)
        for cols in chunks(length, BLOCK):
            shifted = mm(own_v, own_grad_t[:, cols])
            ds_ref[:, cols] = (et_ref[h, :, cols].astype(f32) * shifted).astype(bf16)
        dk += mm(ds_ref[...], own_q)
        dv += mm(et_ref[h], own_grad)
        dq_t.append(mm(k_t[h * HEAD_DIM : (h + 1) * HEAD_DIM], ds_ref[...]))
    dq = (jnp.concatenate(dq_t, axis=0).T * scale).astype(bf16)
    dv = dv.astype(bf16)
    dq_ref[...] = dq
    dk_ref[...] = dk.astype(bf16)
    dv_ref[...] = dv
    sums_ref[0:1] = jnp.sum(dq.astype(f32), axis=0, keepdims=True)
    sums_ref[1:2] = jnp.sum(dv.astype(f32), axis=0, keepdims=True)


def attend(joined, valid_len):
    length, width = joined.shape[0], 2 * HEAD_DIM
    pairs = joined.shape[1] // (3 * width)
    block = lambda part: pl.BlockSpec((length, width), lambda p, n: (0, part * pairs + p))
    return pl.pallas_call(
        attend_kernel,
        grid_spec=pltpu.PrefetchScalarGridSpec(
            num_scalar_prefetch=1,
            grid=(pairs,),
            in_specs=[block(0), block(1), block(2)],
            out_specs=[
                block(0),
                pl.BlockSpec((2, length, length), lambda p, n: (p, 0, 0)),
                pl.BlockSpec((2, 1, length), lambda p, n: (p, 0, 0)),
            ],
        ),
        out_shape=[
            jax.ShapeDtypeStruct((length, pairs * width), bf16),
            jax.ShapeDtypeStruct((2 * pairs, length, length), bf16),
            jax.ShapeDtypeStruct((2 * pairs, 1, length), f32),
        ],
        compiler_params=pltpu.CompilerParams(vmem_limit_bytes=VMEM_LIMIT),
        name="attend",
    )(valid_len, joined, joined, joined)


def attend_back(joined, et, inverse, grad_context, context):
    length, width = joined.shape[0], 2 * HEAD_DIM
    pairs = joined.shape[1] // (3 * width)
    block = lambda part: pl.BlockSpec((length, width), lambda p: (0, part * pairs + p))
    one = jax.ShapeDtypeStruct((length, pairs * width), bf16)
    return pl.pallas_call(
        attend_back_kernel,
        grid=(pairs,),
        in_specs=[
            block(0),
            block(1),
            block(2),
            pl.BlockSpec((2, length, length), lambda p: (p, 0, 0)),
            pl.BlockSpec((2, 1, length), lambda p: (p, 0, 0)),
            block(0),
            block(0),
        ],
        out_specs=[block(0), block(0), block(0), pl.BlockSpec((8, width), lambda p: (0, p))],
        out_shape=[one, one, one, jax.ShapeDtypeStruct((8, pairs * width), f32)],
        scratch_shapes=[pltpu.VMEM((length, length), bf16)],
        compiler_params=pltpu.CompilerParams(vmem_limit_bytes=VMEM_LIMIT),
        name="attend_back",
    )(joined, joined, joined, et, inverse, grad_context, context)


def mean_of(values):
    return jnp.mean(values, axis=-1, keepdims=True)


def mlp_kernel(
    len_ref,
    ctx_ref,
    stem_ref,
    w_out_ref,
    b_out_ref,
    gain_ref,
    bias_ref,
    w_up_ref,
    b_up_ref,
    w_down_ref,
    b_down_ref,
    target_ref,
    out_ref,
    gctx_ref,
    gmid_ref,
    gw_up_ref,
    gw_down_ref,
    gw_out_ref,
    sums_ref,
    gb_up_ref,
    mid_ref,
    normed_ref,
    normed_t_ref,
    hidden_ref,
    slope_ref,
    branch_ref,
    branch_t_ref,
):
    length, width = ctx_ref.shape
    inner = w_up_ref.shape[1]
    row_steps, tile_steps = length // BLOCK, inner // BLOCK
    ones = lambda v: jnp.sum(v, axis=0, keepdims=True)
    sums_ref[...] = jnp.zeros_like(sums_ref)

    @pl.loop(0, row_steps)
    def _(i):
        rows = pl.ds(pl.multiple_of(i * BLOCK, BLOCK), BLOCK)
        middle = stem_ref[rows].astype(f32) + mm(ctx_ref[rows], w_out_ref[...]) + b_out_ref[...]
        mid_ref[rows] = middle
        centred = middle - mean_of(middle)
        scale = lax.rsqrt(mean_of(centred * centred) + epsilon)
        normed_ref[rows] = (centred * scale * gain_ref[...] + bias_ref[...]).astype(bf16)

    @pl.loop(0, tile_steps)
    def _(j):
        cols = pl.ds(pl.multiple_of(j * BLOCK, BLOCK), BLOCK)
        upward = mm(normed_ref[...], w_up_ref[:, cols]) + b_up_ref[:, cols]
        hidden, slope = gelu_pair(upward)
        hidden_ref[:, cols] = hidden.astype(bf16)
        slope_ref[:, cols] = slope.astype(bf16)

    @pl.loop(0, row_steps)
    def _(i):
        rows = pl.ds(pl.multiple_of(i * BLOCK, BLOCK), BLOCK)
        final = mid_ref[rows] + mm(hidden_ref[rows], w_down_ref[...]) + b_down_ref[...]
        out_ref[rows] = final.astype(bf16)
        frame = i * BLOCK + lax.broadcasted_iota(jnp.int32, final.shape, 0)
        mismatch = jnp.where(frame < len_ref[0], final - target_ref[rows].astype(f32), 0.0)
        gmid_ref[rows] = mismatch
        branch = mismatch.astype(bf16)
        branch_ref[rows] = branch
        branch_t_ref[:, rows] = turned(branch)
        normed_t_ref[:, rows] = turned(normed_ref[rows])
        sums_ref[0:1] += ones(mismatch * mismatch)
        sums_ref[1:2] += ones(branch.astype(f32))

    @pl.loop(0, tile_steps)
    def _(j):
        cols = pl.ds(pl.multiple_of(j * BLOCK, BLOCK), BLOCK)
        grad = mm_nt(branch_ref[...], w_down_ref[cols]) * slope_ref[:, cols].astype(f32)
        grad = grad.astype(bf16)
        gb_up_ref[:, cols] = ones(grad.astype(f32))
        gw_down_ref[:, cols] = mm(branch_t_ref[...], hidden_ref[:, cols]).astype(bf16)
        gw_up_ref[:, cols] = mm(normed_t_ref[...], grad).astype(bf16)
        slope_ref[:, cols] = grad

    @pl.loop(0, row_steps)
    def _(i):
        rows = pl.ds(pl.multiple_of(i * BLOCK, BLOCK), BLOCK)
        grad = mm_nt(slope_ref[rows], w_up_ref[...])
        middle = mid_ref[rows]
        centred = middle - mean_of(middle)
        scale = lax.rsqrt(mean_of(centred * centred) + epsilon)
        unit = centred * scale
        gained = grad * gain_ref[...]
        back = scale * (gained - mean_of(gained) - unit * mean_of(gained * unit))
        grad_middle = gmid_ref[rows] + back
        gmid_ref[rows] = grad_middle
        attended = grad_middle.astype(bf16)
        branch_ref[rows] = attended
        gctx_ref[rows] = mm_nt(attended, w_out_ref[...]).astype(bf16)
        normed_t_ref[:, rows] = turned(ctx_ref[rows])
        sums_ref[2:3] += ones(grad * unit)
        sums_ref[3:4] += ones(grad)
        sums_ref[4:5] += ones(attended.astype(f32))

    @pl.loop(0, width // BLOCK)
    def _(j):
        cols = pl.ds(pl.multiple_of(j * BLOCK, BLOCK), BLOCK)
        gw_out_ref[:, cols] = mm(normed_t_ref[...], branch_ref[:, cols]).astype(bf16)


def shifted(values, step, axis):
    length = values.shape[axis]
    moved = pltpu.roll(values, step % length, axis)
    place = lax.broadcasted_iota(jnp.int32, values.shape, axis)
    return jnp.where(place == (0 if step > 0 else length - 1), 0.0, moved)


def pick_frames(slots, frames, offset):
    slot = lax.broadcasted_iota(jnp.int32, (slots, frames), 0)
    frame = lax.broadcasted_iota(jnp.int32, (slots, frames), 1)
    return jnp.where(frame == 2 * slot + offset, 1.0, 0.0).astype(bf16)


def flat_taps(ref):
    return ref[...].reshape(-1, ref.shape[-1])


def stem_kernel(
    mel_ref,
    w_one_ref,
    b_one_ref,
    w_two_ref,
    b_two_ref,
    pos_ref,
    gain_ref,
    bias_ref,
    w_qkv_ref,
    b_query_ref,
    b_value_ref,
    taps_ref,
    act_even_ref,
    act_odd_ref,
    slope_even_ref,
    slope_odd_ref,
    slope_two_ref,
    stem_ref,
    normed_ref,
    joined_ref,
    behind_ref,
):
    length, width = stem_ref.shape
    steps = length // BLOCK
    mel = mel_ref[...].astype(f32)
    taps = jnp.concatenate([shifted(mel, 1, 1), mel, shifted(mel, -1, 1)], axis=0).astype(bf16)
    taps_ref[...] = taps
    w_one = flat_taps(w_one_ref)
    for offset, act_ref, slope_ref in (
        (0, act_even_ref, slope_even_ref),
        (1, act_odd_ref, slope_odd_ref),
    ):
        for i in range(steps):
            rows = slice(i * BLOCK, (i + 1) * BLOCK)
            frames = slice(2 * i * BLOCK, 2 * (i + 1) * BLOCK)
            picked = mm_nt(pick_frames(BLOCK, 2 * BLOCK, offset), taps[:, frames]).astype(bf16)
            act, slope = gelu_pair(mm(picked, w_one) + b_one_ref[...])
            act_ref[rows] = act.astype(bf16)
            slope_ref[rows] = slope.astype(bf16)
    for cols in chunks(width, BLOCK):
        behind_ref[:, cols] = shifted(act_odd_ref[:, cols].astype(f32), 1, 0).astype(bf16)

    @pl.loop(0, steps)
    def _(i):
        rows = pl.ds(pl.multiple_of(i * BLOCK, BLOCK), BLOCK)
        two = (
            mm(behind_ref[rows], w_two_ref[0])
            + mm(act_even_ref[rows], w_two_ref[1])
            + mm(act_odd_ref[rows], w_two_ref[2])
            + b_two_ref[...]
        )
        act, slope = gelu_pair(two)
        slope_two_ref[rows] = slope.astype(bf16)
        stem = (act + pos_ref[rows]).astype(bf16)
        stem_ref[rows] = stem
        stem = stem.astype(f32)
        centred = stem - mean_of(stem)
        scale = lax.rsqrt(mean_of(centred * centred) + epsilon)
        normed = (centred * scale * gain_ref[...] + bias_ref[...]).astype(bf16)
        normed_ref[rows] = normed
        query, key, value = (slice(part * width, (part + 1) * width) for part in range(3))
        joined_ref[rows, query] = (mm(normed, w_qkv_ref[:, query]) + b_query_ref[...]).astype(bf16)
        joined_ref[rows, key] = mm(normed, w_qkv_ref[:, key]).astype(bf16)
        joined_ref[rows, value] = (mm(normed, w_qkv_ref[:, value]) + b_value_ref[...]).astype(bf16)


def stem_back_kernel(
    gq_ref,
    gk_ref,
    gv_ref,
    w_qkv_ref,
    gmid_ref,
    stem_ref,
    normed_ref,
    gain_ref,
    slope_two_ref,
    w_two_ref,
    act_even_ref,
    act_odd_ref,
    slope_even_ref,
    slope_odd_ref,
    w_one_ref,
    taps_ref,
    gw_qkv_ref,
    gw_two_ref,
    gw_one_ref,
    gmel_ref,
    sums_ref,
    normed_t_ref,
    two_ref,
    two_ahead_ref,
    two_t_ref,
    two_ahead_t_ref,
    even_ref,
    odd_ref,
):
    length, width = stem_ref.shape
    steps = length // BLOCK
    ones = lambda v: jnp.sum(v, axis=0, keepdims=True)
    sums_ref[...] = jnp.zeros_like(sums_ref)

    @pl.loop(0, steps)
    def _(i):
        rows = pl.ds(pl.multiple_of(i * BLOCK, BLOCK), BLOCK)
        normed_t_ref[:, rows] = turned(normed_ref[rows])
        grad = (
            mm_nt(gq_ref[rows], w_qkv_ref[:, 0:width])
            + mm_nt(gk_ref[rows], w_qkv_ref[:, width : 2 * width])
            + mm_nt(gv_ref[rows], w_qkv_ref[:, 2 * width : 3 * width])
        )
        stem = stem_ref[rows].astype(f32)
        centred = stem - mean_of(stem)
        scale = lax.rsqrt(mean_of(centred * centred) + epsilon)
        unit = centred * scale
        gained = grad * gain_ref[...]
        back = scale * (gained - mean_of(gained) - unit * mean_of(gained * unit))
        grad_stem = (gmid_ref[rows] + back).astype(bf16).astype(f32)
        two = (grad_stem * slope_two_ref[rows].astype(f32)).astype(bf16)
        two_ref[rows] = two
        two_t_ref[:, rows] = turned(two)
        sums_ref[0:1] += ones(grad * unit)
        sums_ref[1:2] += ones(grad)
        sums_ref[2:3] += ones(two.astype(f32))

    for cols in chunks(width, BLOCK):
        two_ahead_ref[:, cols] = shifted(two_ref[:, cols].astype(f32), -1, 0).astype(bf16)

    @pl.loop(0, steps)
    def _(i):
        rows = pl.ds(pl.multiple_of(i * BLOCK, BLOCK), BLOCK)
        two_ahead_t_ref[:, rows] = turned(two_ahead_ref[rows])
        even = mm_nt(two_ref[rows], w_two_ref[1]) * slope_even_ref[rows].astype(f32)
        odd = mm_nt(two_ref[rows], w_two_ref[2]) + mm_nt(two_ahead_ref[rows], w_two_ref[0])
        odd = odd * slope_odd_ref[rows].astype(f32)
        even_ref[rows] = even.astype(bf16)
        odd_ref[rows] = odd.astype(bf16)
        sums_ref[3:4] += ones(even.astype(bf16).astype(f32)) + ones(odd.astype(bf16).astype(f32))

    @pl.loop(0, width // BLOCK)
    def _(j):
        cols = pl.ds(pl.multiple_of(j * BLOCK, BLOCK), BLOCK)
        for part, grad_ref in enumerate((gq_ref, gk_ref, gv_ref)):
            out = pl.ds(pl.multiple_of(part * width + j * BLOCK, BLOCK), BLOCK)
            gw_qkv_ref[:, out] = mm(normed_t_ref[...], grad_ref[:, cols]).astype(bf16)
        gw_two_ref[0, :, cols] = mm(two_ahead_t_ref[...], act_odd_ref[:, cols]).astype(bf16)
        gw_two_ref[1, :, cols] = mm(two_t_ref[...], act_even_ref[:, cols]).astype(bf16)
        gw_two_ref[2, :, cols] = mm(two_t_ref[...], act_odd_ref[:, cols]).astype(bf16)

    bins = w_one_ref.shape[1]
    gw_one = jnp.zeros((3 * bins, width), f32)
    for offset, grad_ref in ((0, even_ref), (1, odd_ref)):
        picked = [
            mm_nt(taps_ref[:, 2 * i * BLOCK : 2 * (i + 1) * BLOCK], pick_frames(BLOCK, 2 * BLOCK, offset))
            for i in range(steps)
        ]
        gw_one += mm(jnp.concatenate(picked, axis=1).astype(bf16), grad_ref[...])
    gw_one_ref[...] = gw_one.astype(bf16).reshape(gw_one_ref.shape)
    even, odd = even_ref[...], odd_ref[...]
    mel_even = (
        mm_nt(odd, w_one_ref[0])
        + mm_nt(even, w_one_ref[1])
        + shifted(mm_nt(odd, w_one_ref[2]), 1, 0)
    )
    mel_odd = (
        shifted(mm_nt(even, w_one_ref[0]), -1, 0)
        + mm_nt(odd, w_one_ref[1])
        + mm_nt(even, w_one_ref[2])
    )
    mel_even, mel_odd = turned(mel_even), turned(mel_odd)
    for i in range(steps):
        cols = slice(i * BLOCK, (i + 1) * BLOCK)
        frames = slice(2 * i * BLOCK, 2 * (i + 1) * BLOCK)
        gmel_ref[:, frames] = (
            mm(mel_even[:, cols], pick_frames(BLOCK, 2 * BLOCK, 0))
            + mm(mel_odd[:, cols], pick_frames(BLOCK, 2 * BLOCK, 1))
        ).astype(bf16)


def run_whole(kernel, name, operands, results, scratch):
    held = pl.BlockSpec(memory_space=pltpu.VMEM)
    scalar = pl.BlockSpec(memory_space=pltpu.SMEM)
    return pl.pallas_call(
        kernel,
        in_specs=[scalar if o.dtype == jnp.int32 else held for o in operands],
        out_specs=[held] * len(results),
        out_shape=[jax.ShapeDtypeStruct(*r) for r in results],
        scratch_shapes=[pltpu.VMEM(*s) for s in scratch],
        compiler_params=pltpu.CompilerParams(vmem_limit_bytes=VMEM_LIMIT),
        name=name,
    )(*operands)


def on_device(
    mel_input,
    w_conv1,
    b_conv1,
    w_conv2,
    b_conv2,
    gain_attn,
    bias_attn,
    w_qkv,
    b_query,
    b_value,
    w_out,
    b_out,
    gain_mlp,
    bias_mlp,
    w_up,
    b_up,
    w_down,
    b_down,
    target,
    lengths,
    row_clip,
    language,
):
    clip_count, frame_count, model_width = target.shape
    mel_count = mel_input.shape[2]
    row_at = lax.axis_index("dp") * lax.axis_size("chan") + lax.axis_index("chan")
    own_id = lax.dynamic_index_in_dim(row_clip, row_at * clip_count, keepdims=False)
    valid_len = lookup(own_id, lengths)
    own_lang = lookup(own_id, language)

    mel = lax.all_to_all(mel_input, "chan", split_axis=1, concat_axis=0, tiled=True)[:, 0]
    bins = w_conv1.shape[1]
    line = lambda v: v.astype(f32).reshape(1, -1)
    square = (frame_count, model_width)
    (
        taps,
        act_even,
        act_odd,
        slope_even,
        slope_odd,
        slope_two,
        stem,
        normed_a,
        joined,
    ) = run_whole(
        stem_kernel,
        "stem",
        (
            mel,
            w_conv1,
            line(b_conv1),
            w_conv2,
            line(b_conv2),
            sinusoids(frame_count, model_width),
            line(gain_attn),
            line(bias_attn),
            w_qkv,
            line(b_query),
            line(b_value),
        ),
        [((3 * bins, mel_count), bf16)] + [(square, bf16)] * 7 + [((frame_count, 3 * model_width), bf16)],
        [(square, bf16)],
    )
    valid = valid_len.reshape(1)
    context, weights_t, inverse = attend(joined, valid)
    inner = w_up.shape[1]
    deep = (model_width, inner)
    (
        block_rows,
        grad_context,
        grad_middle,
        grad_w_up,
        grad_w_down_t,
        grad_w_out,
        sums_b,
        grad_b_up,
    ) = run_whole(
        mlp_kernel,
        "mlp",
        (
            valid,
            context,
            stem,
            w_out,
            line(b_out),
            line(gain_mlp),
            line(bias_mlp),
            w_up,
            line(b_up),
            w_down,
            line(b_down),
            target[0],
        ),
        [
            (square, bf16),
            (square, bf16),
            (square, f32),
            (deep, bf16),
            (deep, bf16),
            ((model_width, model_width), bf16),
            ((8, model_width), f32),
            ((1, inner), f32),
        ],
        [
            (square, f32),
            (square, bf16),
            (square, bf16),
            ((frame_count, inner), bf16),
            ((frame_count, inner), bf16),
            (square, bf16),
            (square, bf16),
        ],
    )
    clip_loss = 0.5 * jnp.sum(sums_b[0])
    grad_b_down, grad_gain_mlp, grad_bias_mlp, grad_b_out = (sums_b[i] for i in range(1, 5))
    grad_b_up = grad_b_up[0]
    group_ids = jnp.arange(GROUPS, dtype=jnp.int32)
    group_part = jnp.where(own_lang == group_ids, clip_loss, 0.0)

    *grads, sums_a = attend_back(joined, weights_t, inverse, grad_context, context)
    grad_b_query, grad_b_value = sums_a[0], sums_a[1]
    weight = (model_width, model_width)
    grad_w_qkv, grad_w_two_t, grad_w_one, back_mel, sums_c = run_whole(
        stem_back_kernel,
        "stem_back",
        (
            *grads,
            w_qkv,
            grad_middle,
            stem,
            normed_a,
            line(gain_attn),
            slope_two,
            w_conv2,
            act_even,
            act_odd,
            slope_even,
            slope_odd,
            w_conv1,
            taps,
        ),
        [
            ((model_width, 3 * model_width), bf16),
            ((3,) + weight, bf16),
            (w_conv1.shape, bf16),
            ((bins, mel_count), bf16),
            ((8, model_width), f32),
        ],
        [
            ((model_width, frame_count), bf16),
            (square, bf16),
            (square, bf16),
            ((model_width, frame_count), bf16),
            ((model_width, frame_count), bf16),
            (square, bf16),
            (square, bf16),
        ],
    )
    grad_gain_attn, grad_bias_attn, grad_b_two, grad_b_one = (sums_c[i] for i in range(4))
    grad_mel = lax.all_to_all(back_mel[:, None], "chan", split_axis=0, concat_axis=1, tiled=True)

    def scatter(values, dp_at, chan_at):
        part = lax.psum_scatter(values, "dp", scatter_dimension=dp_at, tiled=True)
        return lax.psum_scatter(part, "chan", scatter_dimension=chan_at, tiled=True).astype(f32)

    final_down = scatter(grad_w_down_t, 1, 0).T
    final_up = scatter(grad_w_up, 0, 1)
    final_out = scatter(grad_w_out, 0, 1)
    final_qkv = scatter(grad_w_qkv, 0, 1)
    part_two = scatter(grad_w_two_t, 1, 2).transpose(0, 2, 1)
    part_one = scatter(grad_w_one, 2, 1)
    totals_all = lax.psum(
        (
            group_part,
            grad_b_one,
            grad_b_two,
            grad_gain_attn,
            grad_bias_attn,
            grad_b_query,
            grad_b_value,
            grad_b_out,
            grad_gain_mlp,
            grad_bias_mlp,
            grad_b_up,
            grad_b_down,
        ),
        ("dp", "chan"),
    )
    member_all = language[:, None] == group_ids[None, :]
    frames_group = jnp.sum(jnp.where(member_all, lengths[:, None], 0), axis=0)
    group_loss = totals_all[0] / (model_width * jnp.maximum(frames_group, 1).astype(f32))
    return (
        block_rows.reshape(target.shape),
        group_loss,
        grad_mel,
        part_one,
        totals_all[1],
        part_two,
        totals_all[2],
        totals_all[3],
        totals_all[4],
        final_qkv,
        totals_all[5],
        totals_all[6],
        final_out,
        totals_all[7],
        totals_all[8],
        totals_all[9],
        final_up,
        totals_all[10],
        final_down,
        totals_all[11],
    )


def solution(mesh):
    whole = P()
    by_row = P(("dp", "chan"), None, None)
    return jax.shard_map(
        on_device,
        mesh=mesh,
        in_specs=(P("chan", "dp", None),) + (whole,) * 17 + (by_row,) + (whole,) * 3,
        out_specs=(
            by_row,
            whole,
            P("chan", "dp", None),
            P(None, "chan", "dp"),
            whole,
            P(None, "chan", "dp"),
            whole,
            whole,
            whole,
            P("dp", "chan"),
            whole,
            whole,
            P("dp", "chan"),
            whole,
            whole,
            whole,
            P("dp", "chan"),
            whole,
            P("dp", "chan"),
            whole,
        ),
        check_vma=False,
    )
```

```python
import math

import jax
import jax.numpy as jnp
import numpy as np
from jax import lax
from jax.experimental import pallas as pl
from jax.experimental.pallas import tpu as pltpu
from jax.sharding import PartitionSpec as P

HEAD_DIM = 64
GROUPS = 99

bf16 = jnp.bfloat16
f32 = jnp.float32
epsilon = 1e-05
masked_score = -1e30


def sinusoids(length, channels):
    half_width = channels // 2
    increment = math.log(10000.0) / (half_width - 1)
    inverse = np.exp(-increment * np.arange(half_width, dtype=np.float64))
    angles = np.arange(length, dtype=np.float64)[:, None] * inverse[None, :]
    return np.concatenate([np.sin(angles), np.cos(angles)], axis=1).astype(np.float32)


def lookup(row_id, table):
    matches = row_id == jnp.arange(table.shape[0], dtype=jnp.int32)
    return jnp.sum(jnp.where(matches, table, 0))


def mm(a, b):
    return jnp.dot(a, b, preferred_element_type=f32)


def mm_nt(a, b):
    return lax.dot_general(a, b, (((1,), (1,)), ((), ())), preferred_element_type=f32)


def mm_tn(a, b):
    return lax.dot_general(a, b, (((0,), (0,)), ((), ())), preferred_element_type=f32)


BLOCK = 256
VMEM_LIMIT = 60 * 1024 * 1024
TAIL_RATE = 0.31
TAIL = (
    0.12366556625478936,
    0.12390820374862553,
    0.10876305868035366,
    0.10683424297390944,
    -0.008837395578103507,
    0.14867850286492648,
    -0.13802626195746664,
    0.0350141511339579,
)


def gelu_pair(v):
    size = jnp.abs(v)
    base = 1.0 + TAIL_RATE * size
    rough = pl.reciprocal(base, approx=True)
    t = rough * (2.0 - base * rough)
    total = jnp.full_like(t, TAIL[-1])
    for coefficient in TAIL[-2::-1]:
        total = total * t + coefficient
    bell = jnp.exp(-0.5 * (v * v))
    tail = total * t * bell
    phi = jnp.where(v < 0.0, tail, 1.0 - tail)
    return v * phi, phi + v * (bell * (1.0 / math.sqrt(2.0 * math.pi)))


def turned(values):
    return values.astype(f32).T.astype(bf16)


def chunks(length, size):
    return [slice(at, min(at + size, length)) for at in range(0, length, size)]


def attend_kernel(len_ref, q_ref, k_ref, v_ref, ctx_ref, et_ref, inv_ref):
    length, width = q_ref.shape
    lane = lax.broadcasted_iota(jnp.int32, (length, width), 1)
    frame = lax.broadcasted_iota(jnp.int32, (length, width), 0)
    bias = jnp.where(frame < len_ref[0], 0.0, masked_score)
    q = q_ref[...].astype(f32) * HEAD_DIM ** (-0.5)
    k = k_ref[...].astype(f32)
    v_t = turned(v_ref[...])
    found = [[] for _ in chunks(length, BLOCK)]
    for h in range(2):
        mine = lane // HEAD_DIM == h
        spare = lane == HEAD_DIM * (1 - h)
        own_q = jnp.where(mine, q, jnp.where(spare, 1.0, 0.0)).astype(bf16)
        own_k = jnp.where(mine, k, jnp.where(spare, bias, 0.0)).astype(bf16)
        for at, cols in enumerate(chunks(length, BLOCK)):
            scores = mm_nt(own_k, own_q[cols])
            weight = jnp.exp(scores - jnp.max(scores, axis=0, keepdims=True))
            inverse = 1.0 / jnp.sum(weight, axis=0, keepdims=True)
            weight = weight.astype(bf16)
            et_ref[h, :, cols] = weight
            inv_ref[h, :, cols] = inverse
            found[at].append(mm(v_t[h * HEAD_DIM : (h + 1) * HEAD_DIM], weight) * inverse)
    for at, cols in enumerate(chunks(length, BLOCK)):
        ctx_ref[cols, :] = jnp.concatenate(found[at], axis=0).T.astype(bf16)


def attend_back_kernel(
    q_ref, k_ref, v_ref, et_ref, inv_ref, gctx_ref, ctx_ref, dq_ref, dk_ref, dv_ref, sums_ref, ds_ref
):
    length, width = q_ref.shape
    lane = lax.broadcasted_iota(jnp.int32, (length, width), 1)
    row = lax.broadcasted_iota(jnp.int32, (width, length), 0)
    scale = HEAD_DIM ** (-0.5)
    grad_t = gctx_ref[...].astype(f32).T * jnp.where(row < HEAD_DIM, inv_ref[0], inv_ref[1])
    grad_t = grad_t.astype(bf16).astype(f32)
    grad = grad_t.T
    inner_all = grad_t * ctx_ref[...].astype(f32).T
    k_t = turned(k_ref[...])
    q = q_ref[...].astype(f32) * scale
    v = v_ref[...].astype(f32)
    dq_t = []
    dk = jnp.zeros((length, width), f32)
    dv = jnp.zeros((length, width), f32)
    for h in range(2):
        at = HEAD_DIM * (1 - h)
        mine = lane // HEAD_DIM == h
        inner = jnp.sum(inner_all[h * HEAD_DIM : (h + 1) * HEAD_DIM], axis=0, keepdims=True)
        high = inner.astype(bf16).astype(f32)
        own_grad_t = jnp.where(row // HEAD_DIM == h, grad_t, 0.0)
        own_grad_t = jnp.where(row == at, -high, jnp.where(row == at + 1, high - inner, own_grad_t))
        own_grad_t = own_grad_t.astype(bf16)
        own_v = jnp.where(mine, v, jnp.where((lane == at) | (lane == at + 1), 1.0, 0.0)).astype(bf16)
        own_q = jnp.where(mine, q, 0.0).astype(bf16)
        own_grad = jnp.where(mine, grad, 0.0).astype(bf16)
        for cols in chunks(length, BLOCK):
            shifted = mm(own_v, own_grad_t[:, cols])
            ds_ref[:, cols] = (et_ref[h, :, cols].astype(f32) * shifted).astype(bf16)
        dk += mm(ds_ref[...], own_q)
        dv += mm(et_ref[h], own_grad)
        dq_t.append(mm(k_t[h * HEAD_DIM : (h + 1) * HEAD_DIM], ds_ref[...]))
    dq = (jnp.concatenate(dq_t, axis=0).T * scale).astype(bf16)
    dv = dv.astype(bf16)
    dq_ref[...] = dq
    dk_ref[...] = dk.astype(bf16)
    dv_ref[...] = dv
    sums_ref[0:1] = jnp.sum(dq.astype(f32), axis=0, keepdims=True)
    sums_ref[1:2] = jnp.sum(dv.astype(f32), axis=0, keepdims=True)


def attend(joined, valid_len):
    length, width = joined.shape[0], 2 * HEAD_DIM
    pairs = joined.shape[1] // (3 * width)
    block = lambda part: pl.BlockSpec((length, width), lambda p, n: (0, part * pairs + p))
    return pl.pallas_call(
        attend_kernel,
        grid_spec=pltpu.PrefetchScalarGridSpec(
            num_scalar_prefetch=1,
            grid=(pairs,),
            in_specs=[block(0), block(1), block(2)],
            out_specs=[
                block(0),
                pl.BlockSpec((2, length, length), lambda p, n: (p, 0, 0)),
                pl.BlockSpec((2, 1, length), lambda p, n: (p, 0, 0)),
            ],
        ),
        out_shape=[
            jax.ShapeDtypeStruct((length, pairs * width), bf16),
            jax.ShapeDtypeStruct((2 * pairs, length, length), bf16),
            jax.ShapeDtypeStruct((2 * pairs, 1, length), f32),
        ],
        compiler_params=pltpu.CompilerParams(vmem_limit_bytes=VMEM_LIMIT),
        name="attend",
    )(valid_len, joined, joined, joined)


def attend_back(joined, et, inverse, grad_context, context):
    length, width = joined.shape[0], 2 * HEAD_DIM
    pairs = joined.shape[1] // (3 * width)
    block = lambda part: pl.BlockSpec((length, width), lambda p: (0, part * pairs + p))
    one = jax.ShapeDtypeStruct((length, pairs * width), bf16)
    return pl.pallas_call(
        attend_back_kernel,
        grid=(pairs,),
        in_specs=[
            block(0),
            block(1),
            block(2),
            pl.BlockSpec((2, length, length), lambda p: (p, 0, 0)),
            pl.BlockSpec((2, 1, length), lambda p: (p, 0, 0)),
            block(0),
            block(0),
        ],
        out_specs=[block(0), block(0), block(0), pl.BlockSpec((8, width), lambda p: (0, p))],
        out_shape=[one, one, one, jax.ShapeDtypeStruct((8, pairs * width), f32)],
        scratch_shapes=[pltpu.VMEM((length, length), bf16)],
        compiler_params=pltpu.CompilerParams(vmem_limit_bytes=VMEM_LIMIT),
        name="attend_back",
    )(joined, joined, joined, et, inverse, grad_context, context)


def mean_of(values):
    return jnp.mean(values, axis=-1, keepdims=True)


def mlp_kernel(
    len_ref,
    ctx_ref,
    stem_ref,
    w_out_ref,
    b_out_ref,
    gain_ref,
    bias_ref,
    w_up_ref,
    b_up_ref,
    w_down_ref,
    b_down_ref,
    target_ref,
    out_ref,
    gctx_ref,
    gmid_ref,
    gw_up_ref,
    gw_down_ref,
    gw_out_ref,
    sums_ref,
    gb_up_ref,
    mid_ref,
    normed_ref,
    normed_t_ref,
    hidden_ref,
    slope_ref,
    branch_ref,
    branch_t_ref,
):
    length, width = ctx_ref.shape
    inner = w_up_ref.shape[1]
    row_steps, tile_steps = length // BLOCK, inner // BLOCK
    ones = lambda v: jnp.sum(v, axis=0, keepdims=True)
    sums_ref[...] = jnp.zeros_like(sums_ref)

    @pl.loop(0, row_steps)
    def _(i):
        rows = pl.ds(pl.multiple_of(i * BLOCK, BLOCK), BLOCK)
        middle = stem_ref[rows].astype(f32) + mm(ctx_ref[rows], w_out_ref[...]) + b_out_ref[...]
        mid_ref[rows] = middle
        centred = middle - mean_of(middle)
        scale = lax.rsqrt(mean_of(centred * centred) + epsilon)
        normed_ref[rows] = (centred * scale * gain_ref[...] + bias_ref[...]).astype(bf16)

    @pl.loop(0, tile_steps)
    def _(j):
        cols = pl.ds(pl.multiple_of(j * BLOCK, BLOCK), BLOCK)
        upward = mm(normed_ref[...], w_up_ref[:, cols]) + b_up_ref[:, cols]
        hidden, slope = gelu_pair(upward)
        hidden_ref[:, cols] = hidden.astype(bf16)
        slope_ref[:, cols] = slope.astype(bf16)

    @pl.loop(0, row_steps)
    def _(i):
        rows = pl.ds(pl.multiple_of(i * BLOCK, BLOCK), BLOCK)
        final = mid_ref[rows] + mm(hidden_ref[rows], w_down_ref[...]) + b_down_ref[...]
        out_ref[rows] = final.astype(bf16)
        frame = i * BLOCK + lax.broadcasted_iota(jnp.int32, final.shape, 0)
        mismatch = jnp.where(frame < len_ref[0], final - target_ref[rows].astype(f32), 0.0)
        gmid_ref[rows] = mismatch
        branch = mismatch.astype(bf16)
        branch_ref[rows] = branch
        branch_t_ref[:, rows] = turned(branch)
        normed_t_ref[:, rows] = turned(normed_ref[rows])
        sums_ref[0:1] += ones(mismatch * mismatch)
        sums_ref[1:2] += ones(branch.astype(f32))

    @pl.loop(0, tile_steps)
    def _(j):
        cols = pl.ds(pl.multiple_of(j * BLOCK, BLOCK), BLOCK)
        grad = mm_nt(branch_ref[...], w_down_ref[cols]) * slope_ref[:, cols].astype(f32)
        grad = grad.astype(bf16)
        gb_up_ref[:, cols] = ones(grad.astype(f32))
        gw_up_ref[:, cols] = mm(normed_t_ref[...], grad).astype(bf16)
        slope_ref[:, cols] = grad

    @pl.loop(0, inner // width)
    def _(j):
        cols = pl.ds(pl.multiple_of(j * width, width), width)
        found = mm(branch_t_ref[...], hidden_ref[:, cols]).astype(bf16)
        if len(gw_down_ref.shape) == 2:
            gw_down_ref[:, cols] = found
        else:
            part = gw_down_ref.shape[2]
            for k in range(width // part):
                gw_down_ref[j * (width // part) + k] = found[:, k * part : (k + 1) * part]

    @pl.loop(0, row_steps)
    def _(i):
        rows = pl.ds(pl.multiple_of(i * BLOCK, BLOCK), BLOCK)
        grad = mm_nt(slope_ref[rows], w_up_ref[...])
        middle = mid_ref[rows]
        centred = middle - mean_of(middle)
        scale = lax.rsqrt(mean_of(centred * centred) + epsilon)
        unit = centred * scale
        gained = grad * gain_ref[...]
        back = scale * (gained - mean_of(gained) - unit * mean_of(gained * unit))
        grad_middle = gmid_ref[rows] + back
        gmid_ref[rows] = grad_middle
        attended = grad_middle.astype(bf16)
        branch_ref[rows] = attended
        gctx_ref[rows] = mm_nt(attended, w_out_ref[...]).astype(bf16)
        normed_t_ref[:, rows] = turned(ctx_ref[rows])
        sums_ref[2:3] += ones(grad * unit)
        sums_ref[3:4] += ones(grad)
        sums_ref[4:5] += ones(attended.astype(f32))

    @pl.loop(0, width // BLOCK)
    def _(j):
        cols = pl.ds(pl.multiple_of(j * BLOCK, BLOCK), BLOCK)
        gw_out_ref[:, cols] = mm(normed_t_ref[...], branch_ref[:, cols]).astype(bf16)


def shifted(values, step, axis):
    length = values.shape[axis]
    moved = pltpu.roll(values, step % length, axis)
    place = lax.broadcasted_iota(jnp.int32, values.shape, axis)
    return jnp.where(place == (0 if step > 0 else length - 1), 0.0, moved)


def pick_frames(slots, frames, offset):
    slot = lax.broadcasted_iota(jnp.int32, (slots, frames), 0)
    frame = lax.broadcasted_iota(jnp.int32, (slots, frames), 1)
    return jnp.where(frame == 2 * slot + offset, 1.0, 0.0).astype(bf16)


def flat_taps(ref):
    return ref[...].reshape(-1, ref.shape[-1])


def stem_kernel(
    mel_ref,
    w_one_ref,
    b_one_ref,
    w_two_ref,
    b_two_ref,
    pos_ref,
    gain_ref,
    bias_ref,
    w_qkv_ref,
    b_query_ref,
    b_value_ref,
    taps_ref,
    act_even_ref,
    act_odd_ref,
    slope_even_ref,
    slope_odd_ref,
    slope_two_ref,
    stem_ref,
    normed_ref,
    joined_ref,
    behind_ref,
):
    length, width = stem_ref.shape
    steps = length // BLOCK
    mel = mel_ref[...].astype(f32)
    taps = jnp.concatenate([shifted(mel, 1, 1), mel, shifted(mel, -1, 1)], axis=0).astype(bf16)
    taps_ref[...] = taps
    w_one = flat_taps(w_one_ref)
    for offset, act_ref, slope_ref in (
        (0, act_even_ref, slope_even_ref),
        (1, act_odd_ref, slope_odd_ref),
    ):
        for i in range(steps):
            rows = slice(i * BLOCK, (i + 1) * BLOCK)
            frames = slice(2 * i * BLOCK, 2 * (i + 1) * BLOCK)
            picked = mm_nt(pick_frames(BLOCK, 2 * BLOCK, offset), taps[:, frames]).astype(bf16)
            act, slope = gelu_pair(mm(picked, w_one) + b_one_ref[...])
            act_ref[rows] = act.astype(bf16)
            slope_ref[rows] = slope.astype(bf16)
    for cols in chunks(width, BLOCK):
        behind_ref[:, cols] = shifted(act_odd_ref[:, cols].astype(f32), 1, 0).astype(bf16)

    @pl.loop(0, steps)
    def _(i):
        rows = pl.ds(pl.multiple_of(i * BLOCK, BLOCK), BLOCK)
        two = (
            mm(behind_ref[rows], w_two_ref[0])
            + mm(act_even_ref[rows], w_two_ref[1])
            + mm(act_odd_ref[rows], w_two_ref[2])
            + b_two_ref[...]
        )
        act, slope = gelu_pair(two)
        slope_two_ref[rows] = slope.astype(bf16)
        stem = (act + pos_ref[rows]).astype(bf16)
        stem_ref[rows] = stem
        stem = stem.astype(f32)
        centred = stem - mean_of(stem)
        scale = lax.rsqrt(mean_of(centred * centred) + epsilon)
        normed = (centred * scale * gain_ref[...] + bias_ref[...]).astype(bf16)
        normed_ref[rows] = normed
        query, key, value = (slice(part * width, (part + 1) * width) for part in range(3))
        joined_ref[rows, query] = (mm(normed, w_qkv_ref[:, query]) + b_query_ref[...]).astype(bf16)
        joined_ref[rows, key] = mm(normed, w_qkv_ref[:, key]).astype(bf16)
        joined_ref[rows, value] = (mm(normed, w_qkv_ref[:, value]) + b_value_ref[...]).astype(bf16)


def stem_back_kernel(
    gq_ref,
    gk_ref,
    gv_ref,
    w_qkv_ref,
    gmid_ref,
    stem_ref,
    normed_ref,
    gain_ref,
    slope_two_ref,
    w_two_ref,
    act_even_ref,
    act_odd_ref,
    slope_even_ref,
    slope_odd_ref,
    w_one_ref,
    taps_ref,
    gw_qkv_ref,
    gw_two_ref,
    gw_one_ref,
    gmel_ref,
    sums_ref,
    normed_t_ref,
    two_ref,
    two_ahead_ref,
    two_t_ref,
    two_ahead_t_ref,
    even_ref,
    odd_ref,
):
    length, width = stem_ref.shape
    steps = length // BLOCK
    ones = lambda v: jnp.sum(v, axis=0, keepdims=True)
    sums_ref[...] = jnp.zeros_like(sums_ref)

    @pl.loop(0, steps)
    def _(i):
        rows = pl.ds(pl.multiple_of(i * BLOCK, BLOCK), BLOCK)
        normed_t_ref[:, rows] = turned(normed_ref[rows])
        grad = (
            mm_nt(gq_ref[rows], w_qkv_ref[:, 0:width])
            + mm_nt(gk_ref[rows], w_qkv_ref[:, width : 2 * width])
            + mm_nt(gv_ref[rows], w_qkv_ref[:, 2 * width : 3 * width])
        )
        stem = stem_ref[rows].astype(f32)
        centred = stem - mean_of(stem)
        scale = lax.rsqrt(mean_of(centred * centred) + epsilon)
        unit = centred * scale
        gained = grad * gain_ref[...]
        back = scale * (gained - mean_of(gained) - unit * mean_of(gained * unit))
        grad_stem = (gmid_ref[rows] + back).astype(bf16).astype(f32)
        two = (grad_stem * slope_two_ref[rows].astype(f32)).astype(bf16)
        two_ref[rows] = two
        two_t_ref[:, rows] = turned(two)
        sums_ref[0:1] += ones(grad * unit)
        sums_ref[1:2] += ones(grad)
        sums_ref[2:3] += ones(two.astype(f32))

    for cols in chunks(width, BLOCK):
        two_ahead_ref[:, cols] = shifted(two_ref[:, cols].astype(f32), -1, 0).astype(bf16)

    @pl.loop(0, steps)
    def _(i):
        rows = pl.ds(pl.multiple_of(i * BLOCK, BLOCK), BLOCK)
        two_ahead_t_ref[:, rows] = turned(two_ahead_ref[rows])
        even = mm_nt(two_ref[rows], w_two_ref[1]) * slope_even_ref[rows].astype(f32)
        odd = mm_nt(two_ref[rows], w_two_ref[2]) + mm_nt(two_ahead_ref[rows], w_two_ref[0])
        odd = odd * slope_odd_ref[rows].astype(f32)
        even_ref[rows] = even.astype(bf16)
        odd_ref[rows] = odd.astype(bf16)
        sums_ref[3:4] += ones(even.astype(bf16).astype(f32)) + ones(odd.astype(bf16).astype(f32))

    @pl.loop(0, width // BLOCK)
    def _(j):
        cols = pl.ds(pl.multiple_of(j * BLOCK, BLOCK), BLOCK)
        for part, grad_ref in enumerate((gq_ref, gk_ref, gv_ref)):
            out = pl.ds(pl.multiple_of(part * width + j * BLOCK, BLOCK), BLOCK)
            gw_qkv_ref[:, out] = mm(normed_t_ref[...], grad_ref[:, cols]).astype(bf16)
        gw_two_ref[0, :, cols] = mm(two_ahead_t_ref[...], act_odd_ref[:, cols]).astype(bf16)
        gw_two_ref[1, :, cols] = mm(two_t_ref[...], act_even_ref[:, cols]).astype(bf16)
        gw_two_ref[2, :, cols] = mm(two_t_ref[...], act_odd_ref[:, cols]).astype(bf16)

    bins = w_one_ref.shape[1]
    gw_one = jnp.zeros((3 * bins, width), f32)
    for offset, grad_ref in ((0, even_ref), (1, odd_ref)):
        picked = [
            mm_nt(taps_ref[:, 2 * i * BLOCK : 2 * (i + 1) * BLOCK], pick_frames(BLOCK, 2 * BLOCK, offset))
            for i in range(steps)
        ]
        gw_one += mm(jnp.concatenate(picked, axis=1).astype(bf16), grad_ref[...])
    gw_one_ref[...] = jnp.zeros_like(gw_one_ref)
    gw_one_ref[:, 0 : 3 * bins] = gw_one.T.astype(bf16)
    even, odd = even_ref[...], odd_ref[...]
    mel_even = (
        mm_nt(odd, w_one_ref[0])
        + mm_nt(even, w_one_ref[1])
        + shifted(mm_nt(odd, w_one_ref[2]), 1, 0)
    )
    mel_odd = (
        shifted(mm_nt(even, w_one_ref[0]), -1, 0)
        + mm_nt(odd, w_one_ref[1])
        + mm_nt(even, w_one_ref[2])
    )
    mel_even, mel_odd = turned(mel_even), turned(mel_odd)
    for i in range(steps):
        cols = slice(i * BLOCK, (i + 1) * BLOCK)
        frames = slice(2 * i * BLOCK, 2 * (i + 1) * BLOCK)
        gmel_ref[:, frames] = (
            mm(mel_even[:, cols], pick_frames(BLOCK, 2 * BLOCK, 0))
            + mm(mel_odd[:, cols], pick_frames(BLOCK, 2 * BLOCK, 1))
        ).astype(bf16)


MESH = pl.DeviceIdType.MESH
SPAN = 640


def other(bit):
    return 1 - bit


def window(k, share):
    return k * share // 128 * 128


def reduce_kernel(*refs):
    down, up, out, qkv, two, one, small = refs[:7]
    down_z, up_z, out_z, qkv_z, two_z, one_z, small_z = refs[7:14]
    groups = [refs[14 + 5 * g : 19 + 5 * g] for g in range(4)]
    zi_down, zi_up, zi_out, zi_qkv, zi_two, zi_one, zo_all, small_buf, small_in = refs[34:43]
    send_c, recv_c, load, send_f, recv_f, send_s, recv_s, send_z, recv_z, send_m, recv_m = refs[43:]
    dp, chan = lax.axis_index("dp"), lax.axis_index("chan")
    core, at_x, at_y = dp % 2, (dp // 2) % 2, dp // 4
    device = lambda y, x, c: (4 * y + 2 * x + c, chan)
    by_core = device(at_y, at_x, other(core))
    by_x = device(at_y, other(at_x), core)
    by_y = device(other(at_y), at_x, core)
    by_z = [(dp, (chan + r) % 4) for r in (1, 2, 3)]
    block, width = up.shape[0] // 8, out.shape[1]
    share, qkv_share = width // 4, qkv.shape[1] // 4
    partners = [by_core, by_x, by_y] + by_z
    barrier = pltpu.get_barrier_semaphore()
    for partner in partners:
        pl.semaphore_signal(barrier, inc=1, device_id=partner, device_id_type=MESH)
    pl.semaphore_wait(barrier, len(partners))

    def rows(ref, start, count):
        return lambda d: ref.at[pl.ds(pl.multiple_of(d * block, block), block), pl.ds(start, count)]

    tasks = []
    piece = down.shape[1] // 4
    for k in range(4):
        tasks.append((lambda d, k=k: down.at[d, pl.ds(k * piece, piece)], groups[0], k, False, zi_down, k))
        tasks.append((rows(up, k * width, width), groups[1], k, True, zi_up, k))
    tasks.append((rows(out, 0, width), groups[1], 4, True, zi_out, 0))
    for k in range(4):
        tasks.append((rows(qkv, window(k, qkv_share), SPAN), groups[2], k, k % 2 == 1, zi_qkv, k))
    for k in range(3):
        tasks.append((rows(two.at[k], 0, width), groups[1], 5 + k, k % 2 == 0, zi_two, k))
    tasks.append((rows(one, 0, one.shape[1]), groups[3], 0, False, zi_one, 0))

    def copy(source, target, send, recv, to):
        pltpu.make_async_remote_copy(source, target, send, recv, device_id=to, device_id_type=MESH).start()

    def landed(ref, send, recv, to):
        return pltpu.make_async_remote_copy(ref, ref, send, recv, device_id=to, device_id_type=MESH)

    def ways(n):
        return (by_x, by_y) if tasks[n][3] else (by_y, by_x)

    def begin(n):
        source, (own, cin, _, _, _), at, x_first, _, _ = tasks[n]
        for slot in range(4):
            dx, dy = (slot // 2, slot % 2) if x_first else (slot % 2, slot // 2)
            x = other(at_x) if dx else at_x
            y = other(at_y) if dy else at_y
            d = 4 * y + 2 * x
            copy(source(d + other(core)), cin.at[at, slot], send_c.at[n], recv_c.at[n], by_core)
            pltpu.make_async_copy(source(d + core), own.at[at, slot], load.at[n]).start()

    def after_core(n):
        _, (own, cin, fin, _, _), at, _, _, _ = tasks[n]
        pltpu.make_async_copy(cin.at[at], own.at[at], load.at[n]).wait()
        landed(cin.at[at], send_c.at[n], recv_c.at[n], by_core).wait()
        for slot in (3, 2):
            own[at, slot] = (own[at, slot].astype(f32) + cin[at, slot].astype(f32)).astype(bf16)
            copy(own.at[at, slot], fin.at[at, slot - 2], send_f.at[n], recv_f.at[n], ways(n)[0])

    def after_first(n):
        _, (own, cin, fin, sin, _), at, _, _, _ = tasks[n]
        landed(fin.at[at], send_f.at[n], recv_f.at[n], ways(n)[0]).wait()
        total = own[at, 1].astype(f32) + cin[at, 1].astype(f32) + fin[at, 1].astype(f32)
        own[at, 1] = total.astype(bf16)
        copy(own.at[at, 1], sin.at[at], send_s.at[n], recv_s.at[n], ways(n)[1])

    def after_second(n):
        _, (own, cin, fin, sin, zo), at, _, z_in, k = tasks[n]
        landed(sin.at[at], send_s.at[n], recv_s.at[n], ways(n)[1]).wait()
        total = own[at, 0].astype(f32) + cin[at, 0].astype(f32) + fin[at, 0].astype(f32) + sin[at].astype(f32)
        if z_in is zi_out or z_in is zi_two:
            for z in range(4):
                first = window(z, share)
                taken = total[:, first : first + 256]
                taken = taken if z % 2 == 0 else pltpu.roll(taken, 256 - 64, 1)
                zo_all[k if z_in is zi_two else 3, z] = taken.astype(bf16)
            for r in (1, 2, 3):
                target = z_in.at[k, r - 1] if z_in is zi_two else z_in.at[r - 1]
                source = zo_all.at[k if z_in is zi_two else 3, (chan + r) % 4]
                copy(source, target, send_z.at[n, r - 1], recv_z.at[n, r - 1], by_z[r - 1])
        else:
            zo[at] = total.astype(bf16)
            for r in (1, 2, 3):
                send = lambda: copy(zo.at[at], z_in.at[r - 1], send_z.at[n, r - 1], recv_z.at[n, r - 1], by_z[r - 1])
                if z_in is zi_one:
                    send()
                else:
                    pl.when((chan + r) % 4 == k)(send)

    def summed(first, z_in):
        return first.astype(f32) + z_in[0].astype(f32) + z_in[1].astype(f32) + z_in[2].astype(f32)

    def finish(n):
        _, (_, _, _, _, zo), at, _, z_in, k = tasks[n]
        if z_in is zi_out or z_in is zi_two or z_in is zi_one:
            for r in (1, 2, 3):
                target = z_in.at[k, r - 1] if z_in is zi_two else z_in.at[r - 1]
                landed(target, send_z.at[n, r - 1], recv_z.at[n, r - 1], by_z[r - 1]).wait()
            if z_in is zi_one:
                one_z[...] = summed(zo[at], z_in)
            elif z_in is zi_two:
                two_z[k] = summed(zo_all[k, chan], z_in.at[k])[:, 0:share]
            else:
                out_z[...] = summed(zo_all[3, chan], z_in)[:, 0:share]
            return

        @pl.when(chan != k)
        def _():
            for r in (1, 2, 3):

                @pl.when((chan + r) % 4 == k)
                def _():
                    landed(zo.at[at], send_z.at[n, r - 1], recv_z.at[n, r - 1], by_z[r - 1]).wait_send()

        @pl.when(chan == k)
        def _():
            for r in (1, 2, 3):
                landed(z_in.at[r - 1], send_z.at[n, r - 1], recv_z.at[n, r - 1], by_z[r - 1]).wait_recv()
            total = summed(zo[at], z_in)
            if z_in is zi_down:
                down_z[...] = total
            elif z_in is zi_up:
                up_z[...] = total
            else:
                skip = k * qkv_share - window(k, qkv_share)
                qkv_z[...] = total[:, skip : skip + qkv_share]

    small_ways = [by_core, by_x, by_y]

    def small_send(i):
        if i == 0:
            small_buf[0] = small[...]
        else:
            landed(small_in.at[i - 1], send_m.at[i - 1], recv_m.at[i - 1], small_ways[i - 1]).wait()
            small_buf[i] = small_buf[i - 1] + small_in[i - 1]
        if i < 3:
            copy(small_buf.at[i], small_in.at[i], send_m.at[i], recv_m.at[i], small_ways[i])
        else:
            for r in range(3):
                copy(small_buf.at[3], small_in.at[3 + r], send_m.at[3 + r], recv_m.at[3 + r], by_z[r])

    def small_end():
        for r in range(3):
            landed(small_in.at[3 + r], send_m.at[3 + r], recv_m.at[3 + r], by_z[r]).wait()
        small_z[...] = small_buf[3] + small_in[3] + small_in[4] + small_in[5]

    count = len(tasks)
    small_send(0)
    for n in range(count):
        begin(n)
    for t in range(count + 4):
        if t < count:
            after_core(t)
        if t in (2, 4, 6):
            small_send(t // 2)
        if 0 <= t - 2 < count:
            after_first(t - 2)
        if 0 <= t - 4 < count:
            after_second(t - 4)
    small_end()
    for n in range(count):
        finish(n)


def reduce_all(down, up, out, qkv, two, one, small):
    block, width, share = up.shape[0] // 8, out.shape[1], out.shape[1] // 4
    piece, part = down.shape[1] // 4, down.shape[2]
    qkv_share, tail = qkv.shape[1] // 4, one.shape[1]
    held = pl.BlockSpec(memory_space=pltpu.VMEM)
    far = pl.BlockSpec(memory_space=pl.ANY)
    scratch = []
    for count, shape in ((4, (piece, part)), (8, (block, width)), (4, (block, SPAN)), (1, (block, tail))):
        for lead in ((count, 4), (count, 4), (count, 2), (count,), (count,)):
            scratch.append(pltpu.VMEM(lead + shape, bf16))
    scratch += [
        pltpu.VMEM((3, piece, part), bf16),
        pltpu.VMEM((3, block, width), bf16),
        pltpu.VMEM((3, block, 256), bf16),
        pltpu.VMEM((3, block, SPAN), bf16),
        pltpu.VMEM((3, 3, block, 256), bf16),
        pltpu.VMEM((3, block, tail), bf16),
        pltpu.VMEM((4, 4, block, 256), bf16),
        pltpu.VMEM((4,) + small.shape, f32),
        pltpu.VMEM((6,) + small.shape, f32),
    ]
    count = 17
    sems = [(count,)] * 7 + [(count, 3)] * 2 + [(6,)] * 2
    scratch += [pltpu.SemaphoreType.DMA(s) for s in sems]
    return pl.pallas_call(
        reduce_kernel,
        in_specs=[far] * 6 + [held],
        out_specs=[held] * 7,
        out_shape=[
            jax.ShapeDtypeStruct(s, f32)
            for s in (
                (piece, part),
                (block, width),
                (block, share),
                (block, qkv_share),
                (3, block, share),
                (block, tail),
                small.shape,
            )
        ],
        scratch_shapes=scratch,
        compiler_params=pltpu.CompilerParams(
            vmem_limit_bytes=VMEM_LIMIT, collective_id=1, has_side_effects=True
        ),
        name="reduce_all",
    )(down, up, out, qkv, two, one, small)


def run_whole(kernel, name, operands, results, scratch):
    held = pl.BlockSpec(memory_space=pltpu.VMEM)
    scalar = pl.BlockSpec(memory_space=pltpu.SMEM)
    return pl.pallas_call(
        kernel,
        in_specs=[scalar if o.dtype == jnp.int32 else held for o in operands],
        out_specs=[held] * len(results),
        out_shape=[jax.ShapeDtypeStruct(*r) for r in results],
        scratch_shapes=[pltpu.VMEM(*s) for s in scratch],
        compiler_params=pltpu.CompilerParams(vmem_limit_bytes=VMEM_LIMIT),
        name=name,
    )(*operands)


def on_device(
    mel_input,
    w_conv1,
    b_conv1,
    w_conv2,
    b_conv2,
    gain_attn,
    bias_attn,
    w_qkv,
    b_query,
    b_value,
    w_out,
    b_out,
    gain_mlp,
    bias_mlp,
    w_up,
    b_up,
    w_down,
    b_down,
    target,
    lengths,
    row_clip,
    language,
):
    clip_count, frame_count, model_width = target.shape
    mel_count = mel_input.shape[2]
    row_at = lax.axis_index("dp") * lax.axis_size("chan") + lax.axis_index("chan")
    own_id = lax.dynamic_index_in_dim(row_clip, row_at * clip_count, keepdims=False)
    valid_len = lookup(own_id, lengths)
    own_lang = lookup(own_id, language)

    mel = lax.all_to_all(mel_input, "chan", split_axis=1, concat_axis=0, tiled=True)[:, 0]
    bins = w_conv1.shape[1]
    fast = lax.axis_size("dp") == 8 and lax.axis_size("chan") == 4
    line = lambda v: v.astype(f32).reshape(1, -1)
    square = (frame_count, model_width)
    (
        taps,
        act_even,
        act_odd,
        slope_even,
        slope_odd,
        slope_two,
        stem,
        normed_a,
        joined,
    ) = run_whole(
        stem_kernel,
        "stem",
        (
            mel,
            w_conv1,
            line(b_conv1),
            w_conv2,
            line(b_conv2),
            sinusoids(frame_count, model_width),
            line(gain_attn),
            line(bias_attn),
            w_qkv,
            line(b_query),
            line(b_value),
        ),
        [((3 * bins, mel_count), bf16)] + [(square, bf16)] * 7 + [((frame_count, 3 * model_width), bf16)],
        [(square, bf16)],
    )
    valid = valid_len.reshape(1)
    context, weights_t, inverse = attend(joined, valid)
    inner = w_up.shape[1]
    deep = (model_width, inner)
    (
        block_rows,
        grad_context,
        grad_middle,
        grad_w_up,
        grad_w_down_t,
        grad_w_out,
        sums_b,
        grad_b_up,
    ) = run_whole(
        mlp_kernel,
        "mlp",
        (
            valid,
            context,
            stem,
            w_out,
            line(b_out),
            line(gain_mlp),
            line(bias_mlp),
            w_up,
            line(b_up),
            w_down,
            line(b_down),
            target[0],
        ),
        [
            (square, bf16),
            (square, bf16),
            (square, f32),
            (deep, bf16),
            ((8, model_width, inner // 8) if fast else deep, bf16),
            ((model_width, model_width), bf16),
            ((8, model_width), f32),
            ((1, inner), f32),
        ],
        [
            (square, f32),
            (square, bf16),
            (square, bf16),
            ((frame_count, inner), bf16),
            ((frame_count, inner), bf16),
            (square, bf16),
            (square, bf16),
        ],
    )
    clip_loss = 0.5 * jnp.sum(sums_b[0])
    group_ids = jnp.arange(GROUPS, dtype=jnp.int32)
    group_part = jnp.where(own_lang == group_ids, clip_loss, 0.0)

    *grads, sums_a = attend_back(joined, weights_t, inverse, grad_context, context)
    weight = (model_width, model_width)
    grad_w_qkv, grad_w_two_t, grad_w_one_t, back_mel, sums_c = run_whole(
        stem_back_kernel,
        "stem_back",
        (
            *grads,
            w_qkv,
            grad_middle,
            stem,
            normed_a,
            line(gain_attn),
            slope_two,
            w_conv2,
            act_even,
            act_odd,
            slope_even,
            slope_odd,
            w_conv1,
            taps,
        ),
        [
            ((model_width, 3 * model_width), bf16),
            ((3,) + weight, bf16),
            ((model_width, 256), bf16),
            ((bins, mel_count), bf16),
            ((8, model_width), f32),
        ],
        [
            ((model_width, frame_count), bf16),
            (square, bf16),
            (square, bf16),
            ((model_width, frame_count), bf16),
            ((model_width, frame_count), bf16),
            (square, bf16),
            (square, bf16),
        ],
    )
    grad_mel = lax.all_to_all(back_mel[:, None], "chan", split_axis=0, concat_axis=1, tiled=True)

    padded = jnp.pad(group_part, (0, model_width - GROUPS))
    small = jnp.concatenate(
        [
            padded[None],
            sums_c[3:4],
            sums_c[2:3],
            sums_c[0:2],
            sums_a[0:2],
            sums_b[4:5],
            sums_b[2:4],
            sums_b[1:2],
            grad_b_up.reshape(-1, model_width),
            jnp.zeros((1, model_width), f32),
        ]
    )
    if fast:
        down_z, final_up, final_out, final_qkv, two_z, one_z, small = reduce_all(
            grad_w_down_t, grad_w_up, grad_w_out, grad_w_qkv, grad_w_two_t, grad_w_one_t, small
        )
        final_down = down_z.T
        part_two = two_z.transpose(0, 2, 1)
        one_z = one_z[:, : 3 * bins].reshape(-1, 3, bins).transpose(1, 2, 0)
        part = bins // lax.axis_size("chan")
        part_one = lax.dynamic_slice_in_dim(one_z, lax.axis_index("chan") * part, part, 1)
    else:

        def scatter(values, dp_at, chan_at):
            part = lax.psum_scatter(values, "dp", scatter_dimension=dp_at, tiled=True)
            return lax.psum_scatter(part, "chan", scatter_dimension=chan_at, tiled=True).astype(f32)

        final_down = scatter(grad_w_down_t, 1, 0).T
        final_up = scatter(grad_w_up, 0, 1)
        final_out = scatter(grad_w_out, 0, 1)
        final_qkv = scatter(grad_w_qkv, 0, 1)
        part_two = scatter(grad_w_two_t, 1, 2).transpose(0, 2, 1)
        one_rows = grad_w_one_t[:, : 3 * bins].reshape(-1, 3, bins).transpose(1, 2, 0)
        part_one = scatter(one_rows, 2, 1)
        small = lax.psum(small, ("dp", "chan"))
    totals_all = [small[0, :GROUPS]] + [small[i] for i in range(1, 11)]
    totals_all.insert(10, small[11:15].reshape(-1))
    member_all = language[:, None] == group_ids[None, :]
    frames_group = jnp.sum(jnp.where(member_all, lengths[:, None], 0), axis=0)
    group_loss = totals_all[0] / (model_width * jnp.maximum(frames_group, 1).astype(f32))
    return (
        block_rows.reshape(target.shape),
        group_loss,
        grad_mel,
        part_one,
        totals_all[1],
        part_two,
        totals_all[2],
        totals_all[3],
        totals_all[4],
        final_qkv,
        totals_all[5],
        totals_all[6],
        final_out,
        totals_all[7],
        totals_all[8],
        totals_all[9],
        final_up,
        totals_all[10],
        final_down,
        totals_all[11],
    )


def solution(mesh):
    whole = P()
    by_row = P(("dp", "chan"), None, None)
    return jax.shard_map(
        on_device,
        mesh=mesh,
        in_specs=(P("chan", "dp", None),) + (whole,) * 17 + (by_row,) + (whole,) * 3,
        out_specs=(
            by_row,
            whole,
            P("chan", "dp", None),
            P(None, "chan", "dp"),
            whole,
            P(None, "chan", "dp"),
            whole,
            whole,
            whole,
            P("dp", "chan"),
            whole,
            whole,
            P("dp", "chan"),
            whole,
            whole,
            whole,
            P("dp", "chan"),
            whole,
            P("dp", "chan"),
            whole,
        ),
        check_vma=False,
    )
```

```python
import math

import jax
import jax.numpy as jnp
import numpy as np
from jax import lax
from jax.experimental import pallas as pl
from jax.experimental.pallas import tpu as pltpu
from jax.sharding import PartitionSpec as P

HEAD_DIM = 64
GROUPS = 99

bf16 = jnp.bfloat16
f32 = jnp.float32
epsilon = 1e-05
masked_score = -1e30


def sinusoids(length, channels):
    half_width = channels // 2
    increment = math.log(10000.0) / (half_width - 1)
    inverse = np.exp(-increment * np.arange(half_width, dtype=np.float64))
    angles = np.arange(length, dtype=np.float64)[:, None] * inverse[None, :]
    return np.concatenate([np.sin(angles), np.cos(angles)], axis=1).astype(np.float32)


def lookup(row_id, table):
    matches = row_id == jnp.arange(table.shape[0], dtype=jnp.int32)
    return jnp.sum(jnp.where(matches, table, 0))


def mm(a, b):
    return jnp.dot(a, b, preferred_element_type=f32)


def mm_nt(a, b):
    return lax.dot_general(a, b, (((1,), (1,)), ((), ())), preferred_element_type=f32)


def mm_tn(a, b):
    return lax.dot_general(a, b, (((0,), (0,)), ((), ())), preferred_element_type=f32)


BLOCK = 256
VMEM_LIMIT = 60 * 1024 * 1024
TAIL_RATE = 0.31
TAIL = (
    0.12366556625478936,
    0.12390820374862553,
    0.10876305868035366,
    0.10683424297390944,
    -0.008837395578103507,
    0.14867850286492648,
    -0.13802626195746664,
    0.0350141511339579,
)


def gelu_pair(v):
    size = jnp.abs(v)
    base = 1.0 + TAIL_RATE * size
    rough = pl.reciprocal(base, approx=True)
    t = rough * (2.0 - base * rough)
    total = jnp.full_like(t, TAIL[-1])
    for coefficient in TAIL[-2::-1]:
        total = total * t + coefficient
    bell = jnp.exp(-0.5 * (v * v))
    tail = total * t * bell
    phi = jnp.where(v < 0.0, tail, 1.0 - tail)
    return v * phi, phi + v * (bell * (1.0 / math.sqrt(2.0 * math.pi)))


def turned(values):
    return values.astype(f32).T.astype(bf16)


def chunks(length, size):
    return [slice(at, min(at + size, length)) for at in range(0, length, size)]


def attend_kernel(len_ref, q_ref, k_ref, v_ref, ctx_ref, et_ref, inv_ref):
    length, width = q_ref.shape
    lane = lax.broadcasted_iota(jnp.int32, (length, width), 1)
    frame = lax.broadcasted_iota(jnp.int32, (length, width), 0)
    bias = jnp.where(frame < len_ref[0], 0.0, masked_score)
    q = q_ref[...].astype(f32) * HEAD_DIM ** (-0.5)
    k = k_ref[...].astype(f32)
    v_t = turned(v_ref[...])
    found = [[] for _ in chunks(length, BLOCK)]
    for h in range(2):
        mine = lane // HEAD_DIM == h
        spare = lane == HEAD_DIM * (1 - h)
        own_q = jnp.where(mine, q, jnp.where(spare, 1.0, 0.0)).astype(bf16)
        own_k = jnp.where(mine, k, jnp.where(spare, bias, 0.0)).astype(bf16)
        for at, cols in enumerate(chunks(length, BLOCK)):
            scores = mm_nt(own_k, own_q[cols])
            weight = jnp.exp(scores - jnp.max(scores, axis=0, keepdims=True))
            inverse = 1.0 / jnp.sum(weight, axis=0, keepdims=True)
            weight = weight.astype(bf16)
            et_ref[h, :, cols] = weight
            inv_ref[h, :, cols] = inverse
            found[at].append(mm(v_t[h * HEAD_DIM : (h + 1) * HEAD_DIM], weight) * inverse)
    for at, cols in enumerate(chunks(length, BLOCK)):
        ctx_ref[cols, :] = jnp.concatenate(found[at], axis=0).T.astype(bf16)


def attend_back_kernel(
    q_ref, k_ref, v_ref, et_ref, inv_ref, gctx_ref, ctx_ref, dq_ref, dk_ref, dv_ref, sums_ref, ds_ref
):
    length, width = q_ref.shape
    lane = lax.broadcasted_iota(jnp.int32, (length, width), 1)
    row = lax.broadcasted_iota(jnp.int32, (width, length), 0)
    scale = HEAD_DIM ** (-0.5)
    grad_t = gctx_ref[...].astype(f32).T * jnp.where(row < HEAD_DIM, inv_ref[0], inv_ref[1])
    grad_t = grad_t.astype(bf16).astype(f32)
    grad = grad_t.T
    inner_all = grad_t * ctx_ref[...].astype(f32).T
    k_t = turned(k_ref[...])
    q = q_ref[...].astype(f32) * scale
    v = v_ref[...].astype(f32)
    dq_t = []
    dk = jnp.zeros((length, width), f32)
    dv = jnp.zeros((length, width), f32)
    for h in range(2):
        at = HEAD_DIM * (1 - h)
        mine = lane // HEAD_DIM == h
        inner = jnp.sum(inner_all[h * HEAD_DIM : (h + 1) * HEAD_DIM], axis=0, keepdims=True)
        high = inner.astype(bf16).astype(f32)
        own_grad_t = jnp.where(row // HEAD_DIM == h, grad_t, 0.0)
        own_grad_t = jnp.where(row == at, -high, jnp.where(row == at + 1, high - inner, own_grad_t))
        own_grad_t = own_grad_t.astype(bf16)
        own_v = jnp.where(mine, v, jnp.where((lane == at) | (lane == at + 1), 1.0, 0.0)).astype(bf16)
        own_q = jnp.where(mine, q, 0.0).astype(bf16)
        own_grad = jnp.where(mine, grad, 0.0).astype(bf16)
        for cols in chunks(length, BLOCK):
            shifted = mm(own_v, own_grad_t[:, cols])
            ds_ref[:, cols] = (et_ref[h, :, cols].astype(f32) * shifted).astype(bf16)
        dk += mm(ds_ref[...], own_q)
        dv += mm(et_ref[h], own_grad)
        dq_t.append(mm(k_t[h * HEAD_DIM : (h + 1) * HEAD_DIM], ds_ref[...]))
    dq = (jnp.concatenate(dq_t, axis=0).T * scale).astype(bf16)
    dv = dv.astype(bf16)
    dq_ref[...] = dq
    dk_ref[...] = dk.astype(bf16)
    dv_ref[...] = dv
    sums_ref[0:1] = jnp.sum(dq.astype(f32), axis=0, keepdims=True)
    sums_ref[1:2] = jnp.sum(dv.astype(f32), axis=0, keepdims=True)


def attend(joined, valid_len):
    length, width = joined.shape[0], 2 * HEAD_DIM
    pairs = joined.shape[1] // (3 * width)
    block = lambda part: pl.BlockSpec((length, width), lambda p, n: (0, part * pairs + p))
    return pl.pallas_call(
        attend_kernel,
        grid_spec=pltpu.PrefetchScalarGridSpec(
            num_scalar_prefetch=1,
            grid=(pairs,),
            in_specs=[block(0), block(1), block(2)],
            out_specs=[
                block(0),
                pl.BlockSpec((2, length, length), lambda p, n: (p, 0, 0)),
                pl.BlockSpec((2, 1, length), lambda p, n: (p, 0, 0)),
            ],
        ),
        out_shape=[
            jax.ShapeDtypeStruct((length, pairs * width), bf16),
            jax.ShapeDtypeStruct((2 * pairs, length, length), bf16),
            jax.ShapeDtypeStruct((2 * pairs, 1, length), f32),
        ],
        compiler_params=pltpu.CompilerParams(vmem_limit_bytes=VMEM_LIMIT),
        name="attend",
    )(valid_len, joined, joined, joined)


def attend_back(joined, et, inverse, grad_context, context):
    length, width = joined.shape[0], 2 * HEAD_DIM
    pairs = joined.shape[1] // (3 * width)
    block = lambda part: pl.BlockSpec((length, width), lambda p: (0, part * pairs + p))
    one = jax.ShapeDtypeStruct((length, pairs * width), bf16)
    return pl.pallas_call(
        attend_back_kernel,
        grid=(pairs,),
        in_specs=[
            block(0),
            block(1),
            block(2),
            pl.BlockSpec((2, length, length), lambda p: (p, 0, 0)),
            pl.BlockSpec((2, 1, length), lambda p: (p, 0, 0)),
            block(0),
            block(0),
        ],
        out_specs=[block(0), block(0), block(0), pl.BlockSpec((8, width), lambda p: (0, p))],
        out_shape=[one, one, one, jax.ShapeDtypeStruct((8, pairs * width), f32)],
        scratch_shapes=[pltpu.VMEM((length, length), bf16)],
        compiler_params=pltpu.CompilerParams(vmem_limit_bytes=VMEM_LIMIT),
        name="attend_back",
    )(joined, joined, joined, et, inverse, grad_context, context)


def mean_of(values):
    return jnp.mean(values, axis=-1, keepdims=True)


def store_all(ref, value):
    ref[...] = value


def mlp_kernel(
    len_ref,
    ctx_ref,
    stem_ref,
    w_out_ref,
    b_out_ref,
    gain_ref,
    bias_ref,
    w_up_ref,
    b_up_ref,
    w_down_ref,
    b_down_ref,
    target_ref,
    out_ref,
    gctx_ref,
    gmid_ref,
    gw_up_ref,
    gw_down_ref,
    gw_out_ref,
    sums_ref,
    gb_up_ref,
    mid_ref,
    normed_ref,
    normed_t_ref,
    hidden_ref,
    slope_ref,
    branch_ref,
    branch_t_ref,
    *shared,
):
    length, width = ctx_ref.shape
    if shared:
        gw_blocks, cin, fin, sin, z_out, z_in, *sems = shared
        links, sems = Links(), dict(zip(SEMS, sems))
        piece = width // 4
        tasks = [
            Task(
                links,
                lambda d, k=k: gw_blocks.at[d, pl.ds(k * piece, piece)],
                None,
                (cin, fin, sin),
                k,
                k % 2 == 1,
                sems,
                k,
                "own",
                k,
                z_out,
                z_in,
            )
            for k in range(4)
        ]
        links.greet()
    inner = w_up_ref.shape[1]
    row_steps, tile_steps = length // BLOCK, inner // BLOCK
    ones = lambda v: jnp.sum(v, axis=0, keepdims=True)
    sums_ref[...] = jnp.zeros_like(sums_ref)

    @pl.loop(0, row_steps)
    def _(i):
        rows = pl.ds(pl.multiple_of(i * BLOCK, BLOCK), BLOCK)
        middle = stem_ref[rows].astype(f32) + mm(ctx_ref[rows], w_out_ref[...]) + b_out_ref[...]
        mid_ref[rows] = middle
        centred = middle - mean_of(middle)
        scale = lax.rsqrt(mean_of(centred * centred) + epsilon)
        normed_ref[rows] = (centred * scale * gain_ref[...] + bias_ref[...]).astype(bf16)

    @pl.loop(0, tile_steps)
    def _(j):
        cols = pl.ds(pl.multiple_of(j * BLOCK, BLOCK), BLOCK)
        upward = mm(normed_ref[...], w_up_ref[:, cols]) + b_up_ref[:, cols]
        hidden, slope = gelu_pair(upward)
        hidden_ref[:, cols] = hidden.astype(bf16)
        slope_ref[:, cols] = slope.astype(bf16)

    @pl.loop(0, row_steps)
    def _(i):
        rows = pl.ds(pl.multiple_of(i * BLOCK, BLOCK), BLOCK)
        final = mid_ref[rows] + mm(hidden_ref[rows], w_down_ref[...]) + b_down_ref[...]
        out_ref[rows] = final.astype(bf16)
        frame = i * BLOCK + lax.broadcasted_iota(jnp.int32, final.shape, 0)
        mismatch = jnp.where(frame < len_ref[0], final - target_ref[rows].astype(f32), 0.0)
        gmid_ref[rows] = mismatch
        branch = mismatch.astype(bf16)
        branch_ref[rows] = branch
        branch_t_ref[:, rows] = turned(branch)
        normed_t_ref[:, rows] = turned(normed_ref[rows])
        sums_ref[5:6] += ones(mismatch * mismatch)
        sums_ref[1:2] += ones(branch.astype(f32))

    group = lax.broadcasted_iota(jnp.int32, (1, width), 1)
    loss = 0.5 * jnp.sum(sums_ref[5:6], axis=1, keepdims=True)
    sums_ref[0:1] = jnp.where(group == len_ref[1], loss, 0.0)

    @pl.loop(0, inner // width)
    def _(j):
        cols = pl.ds(pl.multiple_of(j * width, width), width)
        found = mm(branch_t_ref[...], hidden_ref[:, cols]).astype(bf16)
        if shared:
            part = gw_blocks.shape[2]
            for k in range(width // part):
                gw_blocks[j * (width // part) + k] = found[:, k * part : (k + 1) * part]
        else:
            gw_down_ref[:, cols] = found

    if shared:
        links.met()
        for task in tasks:
            task.begin()

    @pl.loop(0, tile_steps)
    def _(j):
        cols = pl.ds(pl.multiple_of(j * BLOCK, BLOCK), BLOCK)
        grad = mm_nt(branch_ref[...], w_down_ref[cols]) * slope_ref[:, cols].astype(f32)
        grad = grad.astype(bf16)
        gb_up_ref[:, cols] = ones(grad.astype(f32))
        gw_up_ref[:, cols] = mm(normed_t_ref[...], grad).astype(bf16)
        slope_ref[:, cols] = grad
        if shared:
            for step, run in (
                (1, tasks[0].after_core),
                (2, tasks[1].after_core),
                (3, tasks[2].after_core),
                (4, tasks[3].after_core),
                (9, tasks[0].after_first),
                (10, tasks[1].after_first),
            ):
                pl.when(j == step)(run)

    @pl.loop(0, row_steps)
    def _(i):
        rows = pl.ds(pl.multiple_of(i * BLOCK, BLOCK), BLOCK)
        grad = mm_nt(slope_ref[rows], w_up_ref[...])
        middle = mid_ref[rows]
        centred = middle - mean_of(middle)
        scale = lax.rsqrt(mean_of(centred * centred) + epsilon)
        unit = centred * scale
        gained = grad * gain_ref[...]
        back = scale * (gained - mean_of(gained) - unit * mean_of(gained * unit))
        grad_middle = gmid_ref[rows] + back
        gmid_ref[rows] = grad_middle
        attended = grad_middle.astype(bf16)
        branch_ref[rows] = attended
        gctx_ref[rows] = mm_nt(attended, w_out_ref[...]).astype(bf16)
        normed_t_ref[:, rows] = turned(ctx_ref[rows])
        sums_ref[2:3] += ones(grad * unit)
        sums_ref[3:4] += ones(grad)
        sums_ref[4:5] += ones(attended.astype(f32))
        if shared:
            for step, runs in (
                (0, (tasks[2].after_first,)),
                (1, (tasks[3].after_first, tasks[0].after_second)),
                (2, (tasks[1].after_second,)),
            ):
                for run in runs:
                    pl.when(i == step)(run)

    @pl.loop(0, width // BLOCK)
    def _(j):
        cols = pl.ds(pl.multiple_of(j * BLOCK, BLOCK), BLOCK)
        gw_out_ref[:, cols] = mm(normed_t_ref[...], branch_ref[:, cols]).astype(bf16)

    if shared:
        tasks[2].after_second()
        tasks[3].after_second()
        for task in tasks:
            task.finish(lambda total: store_all(gw_down_ref, total))


def shifted(values, step, axis):
    length = values.shape[axis]
    moved = pltpu.roll(values, step % length, axis)
    place = lax.broadcasted_iota(jnp.int32, values.shape, axis)
    return jnp.where(place == (0 if step > 0 else length - 1), 0.0, moved)


def pick_frames(slots, frames, offset):
    slot = lax.broadcasted_iota(jnp.int32, (slots, frames), 0)
    frame = lax.broadcasted_iota(jnp.int32, (slots, frames), 1)
    return jnp.where(frame == 2 * slot + offset, 1.0, 0.0).astype(bf16)


def flat_taps(ref):
    return ref[...].reshape(-1, ref.shape[-1])


def stem_kernel(
    mel_ref,
    w_one_ref,
    b_one_ref,
    w_two_ref,
    b_two_ref,
    pos_ref,
    gain_ref,
    bias_ref,
    w_qkv_ref,
    b_query_ref,
    b_value_ref,
    taps_ref,
    act_even_ref,
    act_odd_ref,
    slope_even_ref,
    slope_odd_ref,
    slope_two_ref,
    stem_ref,
    normed_ref,
    joined_ref,
    behind_ref,
):
    length, width = stem_ref.shape
    steps = length // BLOCK
    mel = mel_ref[...].astype(f32)
    taps = jnp.concatenate([shifted(mel, 1, 1), mel, shifted(mel, -1, 1)], axis=0).astype(bf16)
    taps_ref[...] = taps
    w_one = flat_taps(w_one_ref)
    for offset, act_ref, slope_ref in (
        (0, act_even_ref, slope_even_ref),
        (1, act_odd_ref, slope_odd_ref),
    ):
        for i in range(steps):
            rows = slice(i * BLOCK, (i + 1) * BLOCK)
            frames = slice(2 * i * BLOCK, 2 * (i + 1) * BLOCK)
            picked = mm_nt(pick_frames(BLOCK, 2 * BLOCK, offset), taps[:, frames]).astype(bf16)
            act, slope = gelu_pair(mm(picked, w_one) + b_one_ref[...])
            act_ref[rows] = act.astype(bf16)
            slope_ref[rows] = slope.astype(bf16)
    for cols in chunks(width, BLOCK):
        behind_ref[:, cols] = shifted(act_odd_ref[:, cols].astype(f32), 1, 0).astype(bf16)

    @pl.loop(0, steps)
    def _(i):
        rows = pl.ds(pl.multiple_of(i * BLOCK, BLOCK), BLOCK)
        two = (
            mm(behind_ref[rows], w_two_ref[0])
            + mm(act_even_ref[rows], w_two_ref[1])
            + mm(act_odd_ref[rows], w_two_ref[2])
            + b_two_ref[...]
        )
        act, slope = gelu_pair(two)
        slope_two_ref[rows] = slope.astype(bf16)
        stem = (act + pos_ref[rows]).astype(bf16)
        stem_ref[rows] = stem
        stem = stem.astype(f32)
        centred = stem - mean_of(stem)
        scale = lax.rsqrt(mean_of(centred * centred) + epsilon)
        normed = (centred * scale * gain_ref[...] + bias_ref[...]).astype(bf16)
        normed_ref[rows] = normed
        query, key, value = (slice(part * width, (part + 1) * width) for part in range(3))
        joined_ref[rows, query] = (mm(normed, w_qkv_ref[:, query]) + b_query_ref[...]).astype(bf16)
        joined_ref[rows, key] = mm(normed, w_qkv_ref[:, key]).astype(bf16)
        joined_ref[rows, value] = (mm(normed, w_qkv_ref[:, value]) + b_value_ref[...]).astype(bf16)


def stem_back_kernel(
    gq_ref,
    gk_ref,
    gv_ref,
    w_qkv_ref,
    gmid_ref,
    stem_ref,
    normed_ref,
    gain_ref,
    slope_two_ref,
    w_two_ref,
    act_even_ref,
    act_odd_ref,
    slope_even_ref,
    slope_odd_ref,
    w_one_ref,
    taps_ref,
    gw_qkv_ref,
    gw_two_ref,
    gw_one_ref,
    gmel_ref,
    sums_ref,
    normed_t_ref,
    two_ref,
    two_ahead_ref,
    two_t_ref,
    two_ahead_t_ref,
    even_ref,
    odd_ref,
):
    length, width = stem_ref.shape
    steps = length // BLOCK
    ones = lambda v: jnp.sum(v, axis=0, keepdims=True)
    sums_ref[...] = jnp.zeros_like(sums_ref)

    @pl.loop(0, steps)
    def _(i):
        rows = pl.ds(pl.multiple_of(i * BLOCK, BLOCK), BLOCK)
        normed_t_ref[:, rows] = turned(normed_ref[rows])
        grad = (
            mm_nt(gq_ref[rows], w_qkv_ref[:, 0:width])
            + mm_nt(gk_ref[rows], w_qkv_ref[:, width : 2 * width])
            + mm_nt(gv_ref[rows], w_qkv_ref[:, 2 * width : 3 * width])
        )
        stem = stem_ref[rows].astype(f32)
        centred = stem - mean_of(stem)
        scale = lax.rsqrt(mean_of(centred * centred) + epsilon)
        unit = centred * scale
        gained = grad * gain_ref[...]
        back = scale * (gained - mean_of(gained) - unit * mean_of(gained * unit))
        grad_stem = (gmid_ref[rows] + back).astype(bf16).astype(f32)
        two = (grad_stem * slope_two_ref[rows].astype(f32)).astype(bf16)
        two_ref[rows] = two
        two_t_ref[:, rows] = turned(two)
        sums_ref[0:1] += ones(grad * unit)
        sums_ref[1:2] += ones(grad)
        sums_ref[2:3] += ones(two.astype(f32))

    for cols in chunks(width, BLOCK):
        two_ahead_ref[:, cols] = shifted(two_ref[:, cols].astype(f32), -1, 0).astype(bf16)

    @pl.loop(0, steps)
    def _(i):
        rows = pl.ds(pl.multiple_of(i * BLOCK, BLOCK), BLOCK)
        two_ahead_t_ref[:, rows] = turned(two_ahead_ref[rows])
        even = mm_nt(two_ref[rows], w_two_ref[1]) * slope_even_ref[rows].astype(f32)
        odd = mm_nt(two_ref[rows], w_two_ref[2]) + mm_nt(two_ahead_ref[rows], w_two_ref[0])
        odd = odd * slope_odd_ref[rows].astype(f32)
        even_ref[rows] = even.astype(bf16)
        odd_ref[rows] = odd.astype(bf16)
        sums_ref[3:4] += ones(even.astype(bf16).astype(f32)) + ones(odd.astype(bf16).astype(f32))

    @pl.loop(0, width // BLOCK)
    def _(j):
        cols = pl.ds(pl.multiple_of(j * BLOCK, BLOCK), BLOCK)
        for part, grad_ref in enumerate((gq_ref, gk_ref, gv_ref)):
            out = pl.ds(pl.multiple_of(part * width + j * BLOCK, BLOCK), BLOCK)
            gw_qkv_ref[:, out] = mm(normed_t_ref[...], grad_ref[:, cols]).astype(bf16)
        gw_two_ref[0, :, cols] = mm(two_ahead_t_ref[...], act_odd_ref[:, cols]).astype(bf16)
        gw_two_ref[1, :, cols] = mm(two_t_ref[...], act_even_ref[:, cols]).astype(bf16)
        gw_two_ref[2, :, cols] = mm(two_t_ref[...], act_odd_ref[:, cols]).astype(bf16)

    bins = w_one_ref.shape[1]
    gw_one = jnp.zeros((3 * bins, width), f32)
    for offset, grad_ref in ((0, even_ref), (1, odd_ref)):
        picked = [
            mm_nt(taps_ref[:, 2 * i * BLOCK : 2 * (i + 1) * BLOCK], pick_frames(BLOCK, 2 * BLOCK, offset))
            for i in range(steps)
        ]
        gw_one += mm(jnp.concatenate(picked, axis=1).astype(bf16), grad_ref[...])
    gw_one_ref[...] = jnp.zeros_like(gw_one_ref)
    gw_one_ref[:, 0 : 3 * bins] = gw_one.T.astype(bf16)
    even, odd = even_ref[...], odd_ref[...]
    mel_even = (
        mm_nt(odd, w_one_ref[0])
        + mm_nt(even, w_one_ref[1])
        + shifted(mm_nt(odd, w_one_ref[2]), 1, 0)
    )
    mel_odd = (
        shifted(mm_nt(even, w_one_ref[0]), -1, 0)
        + mm_nt(odd, w_one_ref[1])
        + mm_nt(even, w_one_ref[2])
    )
    mel_even, mel_odd = turned(mel_even), turned(mel_odd)
    for i in range(steps):
        cols = slice(i * BLOCK, (i + 1) * BLOCK)
        frames = slice(2 * i * BLOCK, 2 * (i + 1) * BLOCK)
        gmel_ref[:, frames] = (
            mm(mel_even[:, cols], pick_frames(BLOCK, 2 * BLOCK, 0))
            + mm(mel_odd[:, cols], pick_frames(BLOCK, 2 * BLOCK, 1))
        ).astype(bf16)


MESH = pl.DeviceIdType.MESH
SPAN = 640


def window(k, share):
    return k * share // 128 * 128


def remote(source, target, send, recv, to):
    return pltpu.make_async_remote_copy(source, target, send, recv, device_id=to, device_id_type=MESH)


class Links:
    def __init__(self):
        dp, chan = lax.axis_index("dp"), lax.axis_index("chan")
        self.chan = chan
        self.core, self.x, self.y = dp % 2, (dp // 2) % 2, dp // 4
        self.by_core = (self.dest(0, 0, 1), chan)
        self.by_x = (self.dest(0, 1, 0), chan)
        self.by_y = (self.dest(1, 0, 0), chan)
        self.by_z = [(dp, (chan + r) % 4) for r in (1, 2, 3)]
        self.partners = [self.by_core, self.by_x, self.by_y] + self.by_z

    def dest(self, dy, dx, dc):
        flip = lambda bit, turn: 1 - bit if turn else bit
        return 4 * flip(self.y, dy) + 2 * flip(self.x, dx) + flip(self.core, dc)

    def greet(self):
        for partner in self.partners:
            pl.semaphore_signal(pltpu.get_barrier_semaphore(), inc=1, device_id=partner, device_id_type=MESH)

    def met(self):
        pl.semaphore_wait(pltpu.get_barrier_semaphore(), len(self.partners))


class Task:
    def __init__(self, links, source, own, bufs, at, x_first, sems, n, kind, k, z_out, z_in):
        self.links, self.source, self.own, self.bufs, self.at = links, source, own, bufs, at
        self.x_first, self.sems, self.n, self.kind, self.k = x_first, sems, n, kind, k
        self.z_out, self.z_in = z_out, z_in
        self.ways = (links.by_x, links.by_y) if x_first else (links.by_y, links.by_x)

    def sem(self, name):
        return self.sems[name].at[self.n]

    def dest(self, slot, dc):
        dx, dy = (slot // 2, slot % 2) if self.x_first else (slot % 2, slot // 2)
        return self.links.dest(dy, dx, dc)

    def begin(self):
        cin = self.bufs[0]
        for slot in (3, 2, 1, 0):
            source = self.source(self.dest(slot, 1))
            remote(source, cin.at[self.at, slot], self.sem("send_c"), self.sem("recv_c"), self.links.by_core).start()
        if self.own is not None:
            for slot in (3, 2, 1, 0):
                source = self.source(self.dest(slot, 0))
                pltpu.make_async_copy(source, self.own.at[self.at, slot], self.sem("load")).start()

    def mine(self, slot):
        if self.own is not None:
            return self.own[self.at, slot].astype(f32)
        return self.source(self.dest(slot, 0))[...].astype(f32)

    def wait(self, ref, name, to):
        remote(ref, ref, self.sem("send_" + name), self.sem("recv_" + name), to).wait()

    def after_core(self):
        cin, fin, _ = self.bufs
        if self.own is not None:
            held = self.own.at[self.at]
            pltpu.make_async_copy(held, held, self.sem("load")).wait()
        self.wait(cin.at[self.at], "c", self.links.by_core)
        for slot in (3, 2):
            cin[self.at, slot] = (self.mine(slot) + cin[self.at, slot].astype(f32)).astype(bf16)
            target = fin.at[self.at, slot - 2]
            remote(cin.at[self.at, slot], target, self.sem("send_f"), self.sem("recv_f"), self.ways[0]).start()

    def after_first(self):
        cin, fin, sin = self.bufs
        self.wait(fin.at[self.at], "f", self.ways[0])
        total = self.mine(1) + cin[self.at, 1].astype(f32) + fin[self.at, 1].astype(f32)
        cin[self.at, 1] = total.astype(bf16)
        remote(cin.at[self.at, 1], sin.at[self.at], self.sem("send_s"), self.sem("recv_s"), self.ways[1]).start()

    def z_copy(self, r):
        if self.kind == "split":
            source = self.z_out.at[self.k, (self.links.chan + r) % 4]
        else:
            source = self.z_out.at[self.at]
        target = self.z_in.at[self.k, r - 1] if self.kind == "split" else self.z_in.at[r - 1]
        sems = self.sems["send_z"].at[self.n, r - 1], self.sems["recv_z"].at[self.n, r - 1]
        return remote(source, target, *sems, self.links.by_z[r - 1])

    def after_second(self):
        cin, fin, sin = self.bufs
        self.wait(sin.at[self.at], "s", self.ways[1])
        total = self.mine(0) + cin[self.at, 0].astype(f32)
        total = total + fin[self.at, 0].astype(f32) + sin[self.at].astype(f32)
        if self.kind == "split":
            share = total.shape[1] // 4
            for z in range(4):
                first = window(z, share)
                taken = total[:, first : first + 256]
                skip = z * share - first
                self.z_out[self.k, z] = (pltpu.roll(taken, 256 - skip, 1) if skip else taken).astype(bf16)
        else:
            self.z_out[self.at] = total.astype(bf16)
        for r in (1, 2, 3):
            if self.kind == "own":
                pl.when((self.links.chan + r) % 4 == self.k)(lambda r=r: self.z_copy(r).start())
            else:
                self.z_copy(r).start()

    def finish(self, store):
        chan = self.links.chan

        def total():
            first = self.z_out[self.k, chan] if self.kind == "split" else self.z_out[self.at]
            rest = self.z_in.at[self.k] if self.kind == "split" else self.z_in
            store(first.astype(f32) + rest[0].astype(f32) + rest[1].astype(f32) + rest[2].astype(f32))

        if self.kind != "own":
            for r in (1, 2, 3):
                self.z_copy(r).wait()
            total()
            return

        for r in (1, 2, 3):
            pl.when((chan + r) % 4 == self.k)(lambda r=r: self.z_copy(r).wait_send())

        @pl.when(chan == self.k)
        def _():
            for r in (1, 2, 3):
                self.z_copy(r).wait_recv()
            total()


SEMS = ("send_c", "recv_c", "load", "send_f", "recv_f", "send_s", "recv_s", "send_z", "recv_z")


def sems_for(count):
    return [pltpu.SemaphoreType.DMA((count, 3) if name.endswith("_z") else (count,)) for name in SEMS]


def bufs_for(count, shape):
    return [pltpu.VMEM(lead + shape, bf16) for lead in ((count, 4), (count, 2), (count,))]


def rows_of(ref, block, start, count):
    return lambda d: ref.at[pl.ds(pl.multiple_of(d * block, block), block), pl.ds(start, count)]


def pair_back(p, q_ref, k_ref, v_ref, et_of, inverse_ref, gctx_ref, ctx_ref, dq_ref, dk_ref, dv_ref, sums_ref, ds_ref):
    length, width = q_ref.shape[0], 2 * HEAD_DIM
    cols = pl.ds(pl.multiple_of(p * width, width), width)
    lane = lax.broadcasted_iota(jnp.int32, (length, width), 1)
    row = lax.broadcasted_iota(jnp.int32, (width, length), 0)
    scale = HEAD_DIM ** (-0.5)
    grad_t = gctx_ref[:, cols].astype(f32).T
    grad_t = grad_t * jnp.where(row < HEAD_DIM, inverse_ref[2 * p], inverse_ref[2 * p + 1])
    grad_t = grad_t.astype(bf16).astype(f32)
    grad = grad_t.T
    inner_all = grad_t * ctx_ref[:, cols].astype(f32).T
    k_t = turned(k_ref[:, cols])
    q = q_ref[:, cols].astype(f32) * scale
    v = v_ref[:, cols].astype(f32)
    dq_t = []
    dk = jnp.zeros((length, width), f32)
    dv = jnp.zeros((length, width), f32)
    for h in range(2):
        at = HEAD_DIM * (1 - h)
        mine = lane // HEAD_DIM == h
        inner = jnp.sum(inner_all[h * HEAD_DIM : (h + 1) * HEAD_DIM], axis=0, keepdims=True)
        high = inner.astype(bf16).astype(f32)
        own_grad_t = jnp.where(row // HEAD_DIM == h, grad_t, 0.0)
        own_grad_t = jnp.where(row == at, -high, jnp.where(row == at + 1, high - inner, own_grad_t))
        own_grad_t = own_grad_t.astype(bf16)
        own_v = jnp.where(mine, v, jnp.where((lane == at) | (lane == at + 1), 1.0, 0.0)).astype(bf16)
        own_q = jnp.where(mine, q, 0.0).astype(bf16)
        own_grad = jnp.where(mine, grad, 0.0).astype(bf16)
        et_ref = et_of(h)
        for part in chunks(length, BLOCK):
            moved = mm(own_v, own_grad_t[:, part])
            ds_ref[:, part] = (et_ref[:, part].astype(f32) * moved).astype(bf16)
        dk += mm(ds_ref[...], own_q)
        dv += mm(et_ref[...], own_grad)
        dq_t.append(mm(k_t[h * HEAD_DIM : (h + 1) * HEAD_DIM], ds_ref[...]))
    dq = (jnp.concatenate(dq_t, axis=0).T * scale).astype(bf16)
    dv = dv.astype(bf16)
    dq_ref[:, cols] = dq
    dk_ref[:, cols] = dk.astype(bf16)
    dv_ref[:, cols] = dv
    sums_ref[0:1, cols] = jnp.sum(dq.astype(f32), axis=0, keepdims=True)
    sums_ref[1:2, cols] = jnp.sum(dv.astype(f32), axis=0, keepdims=True)


def back_kernel(*refs):
    joined, et, inverse, gctx, ctx, w_qkv, gmid, stem, normed, gain_ref, slope_two = refs[:11]
    w_two, act_even, act_odd, slope_even, slope_odd, w_one_ref, taps_ref = refs[11:18]
    gw_up, gw_out, sums_b_ref, gb_up_ref = refs[18:22]
    up_z, out_z, qkv_z, two_z, one_z, small_z, gmel_z = refs[22:29]
    pool, d_ref, w_qkv_v, gmid_v, stem_v, normed_v, slope_two_v, w_two_v, act_v, gw_qkv = refs[29:39]
    gw_one, sums_a_ref, sums_ref = refs[39:42]
    own_a, cin_a, fin_a, sin_a, cin_q, fin_q, sin_q, cin_t, fin_t, sin_t, cin_n, fin_n, sin_n = refs[42:55]
    zo_up, zo_qkv, zo_split, zo_one, zi_up, zi_split, zi_qkv, zi_one = refs[55:63]
    small_buf, small_in, gmel_out, gmel_in = refs[63:67]
    sems = dict(zip(SEMS, refs[67:76]))
    loads, et_loads, send_m, recv_m, send_g, recv_g = refs[76:]
    length, width = ctx.shape
    steps, pairs, block = length // BLOCK, width // (2 * HEAD_DIM), width // 8
    bins = w_one_ref.shape[1]
    links = Links()
    links.greet()

    q_v, k_v, v_v = (pool.at[i] for i in range(3))
    ctx_v, gctx_v, ds_v = pool.at[7], pool.at[8], pool.at[9]
    started = []

    def load(source, target):
        copy = pltpu.make_async_copy(source, target, loads.at[len(started)])
        copy.start()
        started.append(copy)
        return copy

    def et_load(head, slot):
        return pltpu.make_async_copy(et.at[head], pool.at[3 + slot], et_loads.at[slot])

    first = [load(joined.at[:, pl.ds(i * width, width)], pool.at[i]) for i in range(3)]
    first += [load(gctx, gctx_v), load(ctx, ctx_v)]
    for head in range(4):
        et_load(head, head).start()

    tasks = {}

    def add(name, *args):
        tasks[name] = Task(links, *args[:5], sems, len(tasks), *args[5:])

    bufs_a, bufs_q = (cin_a, fin_a, sin_a), (cin_q, fin_q, sin_q)
    bufs_t, bufs_n = (cin_t, fin_t, sin_t), (cin_n, fin_n, sin_n)
    for k in range(4):
        add(f"u{k}", rows_of(gw_up, block, k * width, width), own_a, bufs_a, k, k % 2 == 0, "own", k, zo_up, zi_up)
    add("o", rows_of(gw_out, block, 0, width), own_a, bufs_a, 4, True, "split", 3, zo_split, zi_split)
    for k in range(4):
        at = window(k, 3 * width // 4)
        add(f"q{k}", rows_of(gw_qkv, block, at, SPAN), None, bufs_q, k, k % 2 == 1, "own", k, zo_qkv, zi_qkv)
    for k in range(3):
        source = rows_of(pool.at[7 + k], block, 0, width)
        add(f"t{k}", source, None, bufs_t, k, k % 2 == 0, "split", k, zo_split, zi_split)
    add("n", rows_of(gw_one, block, 0, gw_one.shape[1]), None, bufs_n, 0, False, "all", 0, zo_one, zi_one)

    def run(step, *names):
        for name in names:
            getattr(tasks[name], step)()

    links.met()
    run("begin", "u0", "u1", "u2", "u3", "o")
    late = [
        load(normed, normed_v),
        load(w_qkv, w_qkv_v),
        load(gmid, gmid_v),
        load(stem, stem_v),
        load(slope_two, slope_two_v),
        load(act_even, act_v.at[0]),
        load(act_odd, act_v.at[1]),
        load(w_two, w_two_v),
    ]
    for copy in first:
        copy.wait()

    @pl.loop(0, pairs)
    def _(p):
        for h in range(2):
            et_load(2 * p + h, (2 * p + h) % 4).wait()
        pair_back(
            p,
            q_v,
            k_v,
            v_v,
            lambda h: pool.at[3 + (2 * p + h) % 4],
            inverse,
            gctx_v,
            ctx_v,
            d_ref.at[0],
            d_ref.at[1],
            d_ref.at[2],
            sums_a_ref,
            ds_v,
        )

        @pl.when(p + 2 < pairs)
        def _():
            for h in range(2):
                et_load(2 * p + 4 + h, (2 * p + h) % 4).start()

        for at, step, names in (
            (0, "after_core", ("u0", "u1")),
            (1, "after_core", ("u2", "u3", "o")),
            (3, "after_first", ("u0", "u1")),
            (5, "after_first", ("u2", "u3")),
        ):
            pl.when(p == at)(lambda step=step, names=names: run(step, *names))

    for copy in late:
        copy.wait()
    ones = lambda v: jnp.sum(v, axis=0, keepdims=True)
    normed_t, two_v, two_ahead, two_t, two_ahead_t, even_v, odd_v = (pool.at[i] for i in range(7))
    gw_two = [pool.at[7 + k] for k in range(3)]
    sums_ref[...] = jnp.zeros_like(sums_ref)

    @pl.loop(0, steps)
    def _(i):
        rows = pl.ds(pl.multiple_of(i * BLOCK, BLOCK), BLOCK)
        normed_t[:, rows] = turned(normed_v[rows])

    @pl.loop(0, width // BLOCK)
    def _(j):
        cols = pl.ds(pl.multiple_of(j * BLOCK, BLOCK), BLOCK)
        for part in range(3):
            out = pl.ds(pl.multiple_of(part * width + j * BLOCK, BLOCK), BLOCK)
            gw_qkv[:, out] = mm(normed_t[...], d_ref[part, :, cols]).astype(bf16)

    run("begin", "q0", "q1", "q2", "q3")
    run("after_first", "o")

    @pl.loop(0, steps)
    def _(i):
        rows = pl.ds(pl.multiple_of(i * BLOCK, BLOCK), BLOCK)
        grad = (
            mm_nt(d_ref[0, rows], w_qkv_v[:, 0:width])
            + mm_nt(d_ref[1, rows], w_qkv_v[:, width : 2 * width])
            + mm_nt(d_ref[2, rows], w_qkv_v[:, 2 * width : 3 * width])
        )
        stem = stem_v[rows].astype(f32)
        centred = stem - mean_of(stem)
        scale = lax.rsqrt(mean_of(centred * centred) + epsilon)
        unit = centred * scale
        gained = grad * gain_ref[...]
        back = scale * (gained - mean_of(gained) - unit * mean_of(gained * unit))
        grad_stem = (gmid_v[rows] + back).astype(bf16).astype(f32)
        two = (grad_stem * slope_two_v[rows].astype(f32)).astype(bf16)
        two_v[rows] = two
        two_t[:, rows] = turned(two)
        sums_ref[0:1] += ones(grad * unit)
        sums_ref[1:2] += ones(grad)
        sums_ref[2:3] += ones(two.astype(f32))
        for at, step, names in (
            (0, "after_second", ("u0", "u1")),
            (1, "after_core", ("q0", "q1", "q2", "q3")),
            (2, "after_second", ("u2", "u3", "o")),
        ):
            pl.when(i == at)(lambda step=step, names=names: run(step, *names))

    slope_v = d_ref
    slopes = [load(slope_even, slope_v.at[0]), load(slope_odd, slope_v.at[1])]
    for cols in chunks(width, BLOCK):
        two_ahead[:, cols] = shifted(two_v[:, cols].astype(f32), -1, 0).astype(bf16)

    @pl.loop(0, steps)
    def _(i):
        rows = pl.ds(pl.multiple_of(i * BLOCK, BLOCK), BLOCK)
        two_ahead_t[:, rows] = turned(two_ahead[rows])

    @pl.loop(0, width // BLOCK)
    def _(j):
        cols = pl.ds(pl.multiple_of(j * BLOCK, BLOCK), BLOCK)
        gw_two[0][:, cols] = mm(two_ahead_t[...], act_v[1, :, cols]).astype(bf16)
        gw_two[1][:, cols] = mm(two_t[...], act_v[0, :, cols]).astype(bf16)
        gw_two[2][:, cols] = mm(two_t[...], act_v[1, :, cols]).astype(bf16)

    run("begin", "t0", "t1", "t2")
    run("after_first", "q0", "q1")
    for copy in slopes:
        copy.wait()

    @pl.loop(0, steps)
    def _(i):
        rows = pl.ds(pl.multiple_of(i * BLOCK, BLOCK), BLOCK)
        even = mm_nt(two_v[rows], w_two_v[1]) * slope_v[0, rows].astype(f32)
        odd = mm_nt(two_v[rows], w_two_v[2]) + mm_nt(two_ahead[rows], w_two_v[0])
        odd = odd * slope_v[1, rows].astype(f32)
        even, odd = even.astype(bf16), odd.astype(bf16)
        even_v[rows] = even
        odd_v[rows] = odd
        sums_ref[3:4] += ones(even.astype(f32)) + ones(odd.astype(f32))

    run("after_core", "t0", "t1", "t2")

    small_ways = [links.by_core, links.by_x, links.by_y]

    def small_send(i):
        if i == 0:
            small_buf[0, 0:1] = sums_b_ref[0:1]
            small_buf[0, 1:2] = sums_ref[3:4]
            small_buf[0, 2:3] = sums_ref[2:3]
            small_buf[0, 3:5] = sums_ref[0:2]
            small_buf[0, 5:7] = sums_a_ref[0:2]
            small_buf[0, 7:8] = sums_b_ref[4:5]
            small_buf[0, 8:10] = sums_b_ref[2:4]
            small_buf[0, 10:11] = sums_b_ref[1:2]
            for k in range(4):
                small_buf[0, 11 + k : 12 + k] = gb_up_ref[:, k * width : (k + 1) * width]
            small_buf[0, 15:16] = jnp.zeros((1, width), f32)
        else:
            got = small_in.at[i - 1]
            remote(got, got, send_m.at[i - 1], recv_m.at[i - 1], small_ways[i - 1]).wait()
            small_buf[i] = small_buf[i - 1] + small_in[i - 1]
        if i < 3:
            remote(small_buf.at[i], small_in.at[i], send_m.at[i], recv_m.at[i], small_ways[i]).start()
        else:
            for r in range(3):
                sem = 3 + r
                remote(small_buf.at[3], small_in.at[sem], send_m.at[sem], recv_m.at[sem], links.by_z[r]).start()

    small_send(0)

    total_one = jnp.zeros((3 * bins, width), f32)
    for offset, grad_ref in ((0, even_v), (1, odd_v)):
        picked = [
            mm_nt(taps_ref[:, 2 * i * BLOCK : 2 * (i + 1) * BLOCK], pick_frames(BLOCK, 2 * BLOCK, offset))
            for i in range(steps)
        ]
        total_one += mm(jnp.concatenate(picked, axis=1).astype(bf16), grad_ref[...])
    gw_one[...] = jnp.zeros_like(gw_one)
    gw_one[:, 0 : 3 * bins] = total_one.T.astype(bf16)
    run("begin", "n")
    run("after_first", "q2", "q3")
    small_send(1)

    even, odd = even_v[...], odd_v[...]
    mel_even = (
        mm_nt(odd, w_one_ref[0])
        + mm_nt(even, w_one_ref[1])
        + shifted(mm_nt(odd, w_one_ref[2]), 1, 0)
    )
    mel_odd = (
        shifted(mm_nt(even, w_one_ref[0]), -1, 0)
        + mm_nt(odd, w_one_ref[1])
        + mm_nt(even, w_one_ref[2])
    )
    mel_even, mel_odd = turned(mel_even), turned(mel_odd)
    share = bins // 4
    tall = gmel_out.shape[1]
    for i in range(steps):
        cols = slice(i * BLOCK, (i + 1) * BLOCK)
        frames = slice(2 * i * BLOCK, 2 * (i + 1) * BLOCK)
        gmel = mm(mel_even[:, cols], pick_frames(BLOCK, 2 * BLOCK, 0))
        gmel += mm(mel_odd[:, cols], pick_frames(BLOCK, 2 * BLOCK, 1))
        for z in range(4):
            part = gmel[z * share : (z + 1) * share]
            part = jnp.concatenate([part, jnp.zeros((tall - share, 2 * BLOCK), f32)], axis=0)
            gmel_out[z, :, frames] = part.astype(bf16)
    gmel_copies = [
        remote(gmel_out.at[(links.chan + r) % 4], gmel_in.at[r - 1], send_g.at[r - 1], recv_g.at[r - 1], links.by_z[r - 1])
        for r in (1, 2, 3)
    ]
    for copy in gmel_copies:
        copy.start()

    run("after_second", "q0", "q1")
    run("after_core", "n")
    small_send(2)
    run("after_first", "t0", "t1", "t2")
    run("after_second", "q2", "q3")
    small_send(3)
    run("after_first", "n")
    run("after_second", "t0", "t1", "t2", "n")

    for copy in gmel_copies:
        copy.wait()
    parts = [gmel_out[links.chan], gmel_in[0], gmel_in[1], gmel_in[2]]
    parts = [part.astype(f32)[0:share] for part in parts]
    placed = []
    for z in range(4):
        value = parts[0]
        for r in (1, 2, 3):
            value = jnp.where((links.chan + 4 - r) % 4 == z, parts[r], value)
        placed.append(value[:, None])
    gmel_z[...] = jnp.concatenate(placed, axis=1).astype(bf16)
    for r in range(3):
        got = small_in.at[3 + r]
        remote(got, got, send_m.at[3 + r], recv_m.at[3 + r], links.by_z[r]).wait()
    small_z[...] = small_buf[3] + small_in[3] + small_in[4] + small_in[5]

    for k in range(4):
        tasks[f"u{k}"].finish(lambda total: store_all(up_z, total))
    quarter = width // 4
    tasks["o"].finish(lambda total: store_all(out_z, total[:, 0:quarter]))
    for k in range(4):
        skip = k * 3 * quarter - window(k, 3 * quarter)
        tasks[f"q{k}"].finish(lambda total, skip=skip: store_all(qkv_z, total[:, skip : skip + 3 * quarter]))
    for k in range(3):
        tasks[f"t{k}"].finish(lambda total, k=k: store_all(two_z.at[k], total[:, 0:quarter]))
    tasks["n"].finish(lambda total: store_all(one_z, total))


def run_back(operands):
    joined, et, w_one, taps = operands[0], operands[1], operands[16], operands[17]
    length, width = operands[4].shape
    block, quarter = width // 8, width // 4
    bins, frames = w_one.shape[1], taps.shape[1]
    held = pl.BlockSpec(memory_space=pltpu.VMEM)
    far = pl.BlockSpec(memory_space=pl.ANY)
    near = (2, 9, 16, 17, 20, 21)
    square = (length, width)
    vmem = lambda *shape: pltpu.VMEM(shape, bf16)
    scratch = [
        vmem(10, *square),
        vmem(3, *square),
        vmem(width, 3 * width),
        pltpu.VMEM(square, f32),
        vmem(*square),
        vmem(*square),
        vmem(*square),
        vmem(3, width, width),
        vmem(2, *square),
        vmem(width, 3 * width),
        vmem(width, 256),
        pltpu.VMEM((8, width), f32),
        pltpu.VMEM((8, width), f32),
        vmem(5, 4, block, width),
        *bufs_for(5, (block, width)),
        *bufs_for(4, (block, SPAN)),
        *bufs_for(3, (block, width)),
        *bufs_for(1, (block, 256)),
        vmem(4, block, width),
        vmem(4, block, SPAN),
        vmem(4, 4, block, 256),
        vmem(1, block, 256),
        vmem(3, block, width),
        vmem(4, 3, block, 256),
        vmem(3, block, SPAN),
        vmem(3, block, 256),
        pltpu.VMEM((4, 16, width), f32),
        pltpu.VMEM((6, 16, width), f32),
        vmem(4, 32, frames),
        vmem(3, 32, frames),
        *sems_for(13),
        pltpu.SemaphoreType.DMA((15,)),
        pltpu.SemaphoreType.DMA((4,)),
        pltpu.SemaphoreType.DMA((6,)),
        pltpu.SemaphoreType.DMA((6,)),
        pltpu.SemaphoreType.DMA((3,)),
        pltpu.SemaphoreType.DMA((3,)),
    ]
    shapes = (
        (block, width),
        (block, quarter),
        (block, 3 * quarter),
        (3, block, quarter),
        (block, 256),
        (16, width),
    )
    return pl.pallas_call(
        back_kernel,
        in_specs=[held if i in near else far for i in range(len(operands))],
        out_specs=[held] * 7,
        out_shape=[jax.ShapeDtypeStruct(s, f32) for s in shapes]
        + [jax.ShapeDtypeStruct((bins // 4, 4, frames), bf16)],
        scratch_shapes=scratch,
        compiler_params=pltpu.CompilerParams(
            vmem_limit_bytes=VMEM_LIMIT, collective_id=2, has_side_effects=True
        ),
        name="back",
    )(*operands)


def run_whole(kernel, name, operands, results, scratch, more=(), **params):
    held = pl.BlockSpec(memory_space=pltpu.VMEM)
    scalar = pl.BlockSpec(memory_space=pltpu.SMEM)
    return pl.pallas_call(
        kernel,
        in_specs=[scalar if o.dtype == jnp.int32 else held for o in operands],
        out_specs=[held] * len(results),
        out_shape=[jax.ShapeDtypeStruct(*r) for r in results],
        scratch_shapes=[pltpu.VMEM(*s) for s in scratch] + list(more),
        compiler_params=pltpu.CompilerParams(vmem_limit_bytes=VMEM_LIMIT, **params),
        name=name,
    )(*operands)


def on_device(
    mel_input,
    w_conv1,
    b_conv1,
    w_conv2,
    b_conv2,
    gain_attn,
    bias_attn,
    w_qkv,
    b_query,
    b_value,
    w_out,
    b_out,
    gain_mlp,
    bias_mlp,
    w_up,
    b_up,
    w_down,
    b_down,
    target,
    lengths,
    row_clip,
    language,
):
    clip_count, frame_count, model_width = target.shape
    mel_count = mel_input.shape[2]
    row_at = lax.axis_index("dp") * lax.axis_size("chan") + lax.axis_index("chan")
    own_id = lax.dynamic_index_in_dim(row_clip, row_at * clip_count, keepdims=False)
    valid_len = lookup(own_id, lengths)
    own_lang = lookup(own_id, language)

    mel = lax.all_to_all(mel_input, "chan", split_axis=1, concat_axis=0, tiled=True)[:, 0]
    bins = w_conv1.shape[1]
    fast = lax.axis_size("dp") == 8 and lax.axis_size("chan") == 4
    line = lambda v: v.astype(f32).reshape(1, -1)
    square = (frame_count, model_width)
    (
        taps,
        act_even,
        act_odd,
        slope_even,
        slope_odd,
        slope_two,
        stem,
        normed_a,
        joined,
    ) = run_whole(
        stem_kernel,
        "stem",
        (
            mel,
            w_conv1,
            line(b_conv1),
            w_conv2,
            line(b_conv2),
            sinusoids(frame_count, model_width),
            line(gain_attn),
            line(bias_attn),
            w_qkv,
            line(b_query),
            line(b_value),
        ),
        [((3 * bins, mel_count), bf16)] + [(square, bf16)] * 7 + [((frame_count, 3 * model_width), bf16)],
        [(square, bf16)],
    )
    valid = valid_len.reshape(1)
    context, weights_t, inverse = attend(joined, valid)
    inner = w_up.shape[1]
    deep = (model_width, inner)
    (
        block_rows,
        grad_context,
        grad_middle,
        grad_w_up,
        grad_w_down_t,
        grad_w_out,
        sums_b,
        grad_b_up,
    ) = run_whole(
        mlp_kernel,
        "mlp",
        (
            jnp.stack([valid_len, own_lang]),
            context,
            stem,
            w_out,
            line(b_out),
            line(gain_mlp),
            line(bias_mlp),
            w_up,
            line(b_up),
            w_down,
            line(b_down),
            target[0],
        ),
        [
            (square, bf16),
            (square, bf16),
            (square, f32),
            (deep, bf16),
            ((model_width // 4, inner // 8), f32) if fast else (deep, bf16),
            ((model_width, model_width), bf16),
            ((8, model_width), f32),
            ((1, inner), f32),
        ],
        [
            (square, f32),
            (square, bf16),
            (square, bf16),
            ((frame_count, inner), bf16),
            ((frame_count, inner), bf16),
            (square, bf16),
            (square, bf16),
        ],
        [
            pltpu.VMEM((8, model_width, inner // 8), bf16),
            *bufs_for(4, (model_width // 4, inner // 8)),
            pltpu.VMEM((4, model_width // 4, inner // 8), bf16),
            pltpu.VMEM((3, model_width // 4, inner // 8), bf16),
            *sems_for(4),
        ]
        if fast
        else [],
        **(dict(collective_id=1, has_side_effects=True) if fast else {}),
    )
    if fast:
        final_up, final_out, final_qkv, two_z, one_z, small, grad_mel = run_back(
            (
                joined,
                weights_t,
                inverse,
                grad_context,
                context,
                w_qkv,
                grad_middle,
                stem,
                normed_a,
                line(gain_attn),
                slope_two,
                w_conv2,
                act_even,
                act_odd,
                slope_even,
                slope_odd,
                w_conv1,
                taps,
                grad_w_up,
                grad_w_out,
                sums_b,
                grad_b_up,
            )
        )
        final_down = grad_w_down_t.T
        part_two = two_z.transpose(0, 2, 1)
        one_z = one_z[:, : 3 * bins].reshape(-1, 3, bins).transpose(1, 2, 0)
        part = bins // lax.axis_size("chan")
        part_one = lax.dynamic_slice_in_dim(one_z, lax.axis_index("chan") * part, part, 1)
    else:
        *grads, sums_a = attend_back(joined, weights_t, inverse, grad_context, context)
        weight = (model_width, model_width)
        grad_w_qkv, grad_w_two_t, grad_w_one_t, back_mel, sums_c = run_whole(
            stem_back_kernel,
            "stem_back",
            (
                *grads,
                w_qkv,
                grad_middle,
                stem,
                normed_a,
                line(gain_attn),
                slope_two,
                w_conv2,
                act_even,
                act_odd,
                slope_even,
                slope_odd,
                w_conv1,
                taps,
            ),
            [
                ((model_width, 3 * model_width), bf16),
                ((3,) + weight, bf16),
                ((model_width, 256), bf16),
                ((bins, mel_count), bf16),
                ((8, model_width), f32),
            ],
            [
                ((model_width, frame_count), bf16),
                (square, bf16),
                (square, bf16),
                ((model_width, frame_count), bf16),
                ((model_width, frame_count), bf16),
                (square, bf16),
                (square, bf16),
            ],
        )
        grad_mel = lax.all_to_all(back_mel[:, None], "chan", split_axis=0, concat_axis=1, tiled=True)

        small = jnp.concatenate(
            [
                sums_b[0:1],
                sums_c[3:4],
                sums_c[2:3],
                sums_c[0:2],
                sums_a[0:2],
                sums_b[4:5],
                sums_b[2:4],
                sums_b[1:2],
                grad_b_up.reshape(-1, model_width),
                jnp.zeros((1, model_width), f32),
            ]
        )

        def scatter(values, dp_at, chan_at):
            part = lax.psum_scatter(values, "dp", scatter_dimension=dp_at, tiled=True)
            return lax.psum_scatter(part, "chan", scatter_dimension=chan_at, tiled=True).astype(f32)

        final_down = scatter(grad_w_down_t, 1, 0).T
        final_up = scatter(grad_w_up, 0, 1)
        final_out = scatter(grad_w_out, 0, 1)
        final_qkv = scatter(grad_w_qkv, 0, 1)
        part_two = scatter(grad_w_two_t, 1, 2).transpose(0, 2, 1)
        one_rows = grad_w_one_t[:, : 3 * bins].reshape(-1, 3, bins).transpose(1, 2, 0)
        part_one = scatter(one_rows, 2, 1)
        small = lax.psum(small, ("dp", "chan"))
    totals_all = [small[0, :GROUPS]] + [small[i] for i in range(1, 11)]
    totals_all.insert(10, small[11:15].reshape(-1))
    group_ids = jnp.arange(GROUPS, dtype=jnp.int32)
    member_all = language[:, None] == group_ids[None, :]
    frames_group = jnp.sum(jnp.where(member_all, lengths[:, None], 0), axis=0)
    group_loss = totals_all[0] / (model_width * jnp.maximum(frames_group, 1).astype(f32))
    return (
        block_rows.reshape(target.shape),
        group_loss,
        grad_mel,
        part_one,
        totals_all[1],
        part_two,
        totals_all[2],
        totals_all[3],
        totals_all[4],
        final_qkv,
        totals_all[5],
        totals_all[6],
        final_out,
        totals_all[7],
        totals_all[8],
        totals_all[9],
        final_up,
        totals_all[10],
        final_down,
        totals_all[11],
    )


def solution(mesh):
    whole = P()
    by_row = P(("dp", "chan"), None, None)
    return jax.shard_map(
        on_device,
        mesh=mesh,
        in_specs=(P("chan", "dp", None),) + (whole,) * 17 + (by_row,) + (whole,) * 3,
        out_specs=(
            by_row,
            whole,
            P("chan", "dp", None),
            P(None, "chan", "dp"),
            whole,
            P(None, "chan", "dp"),
            whole,
            whole,
            whole,
            P("dp", "chan"),
            whole,
            whole,
            P("dp", "chan"),
            whole,
            whole,
            whole,
            P("dp", "chan"),
            whole,
            P("dp", "chan"),
            whole,
        ),
        check_vma=False,
    )
```

```python
import math
from types import SimpleNamespace

import jax
import jax.numpy as jnp
import numpy as np
from jax import lax
from jax.experimental import pallas as pl
from jax.experimental.pallas import tpu as pltpu
from jax.sharding import PartitionSpec as P

HEAD_DIM = 64
GROUPS = 99

bf16 = jnp.bfloat16
f32 = jnp.float32
epsilon = 1e-05
masked_score = -1e30


def sinusoids(length, channels):
    half_width = channels // 2
    increment = math.log(10000.0) / (half_width - 1)
    inverse = np.exp(-increment * np.arange(half_width, dtype=np.float64))
    angles = np.arange(length, dtype=np.float64)[:, None] * inverse[None, :]
    return np.concatenate([np.sin(angles), np.cos(angles)], axis=1).astype(np.float32)


def lookup(row_id, table):
    matches = row_id == jnp.arange(table.shape[0], dtype=jnp.int32)
    return jnp.sum(jnp.where(matches, table, 0))


def mm(a, b):
    return jnp.dot(a, b, preferred_element_type=f32)


def mm_nt(a, b):
    return lax.dot_general(a, b, (((1,), (1,)), ((), ())), preferred_element_type=f32)


def mm_tn(a, b):
    return lax.dot_general(a, b, (((0,), (0,)), ((), ())), preferred_element_type=f32)


BLOCK = 256
VMEM_LIMIT = 61 * 1024 * 1024


def gelu_pair(v):
    phi = 0.5 + 0.5 * lax.erf(v * math.sqrt(0.5))
    return v * phi, phi + v * (jnp.exp(-0.5 * (v * v)) * (1.0 / math.sqrt(2.0 * math.pi)))


def unrolled(count):
    def run(body):
        for i in range(count):
            body(i)

    return run


def row_of(ref):
    return ref[...].astype(f32).reshape(1, -1)


def own_clip(row_clip_ref):
    return row_clip_ref[lax.axis_index("dp") * lax.axis_size("chan") + lax.axis_index("chan")]


def turned(values):
    return values.astype(f32).T.astype(bf16)


def chunks(length, size):
    return [slice(at, min(at + size, length)) for at in range(0, length, size)]


def attend_kernel(row_clip_ref, lengths_ref, q_ref, k_ref, v_ref, ctx_ref, et_ref, inv_ref):
    length, width = q_ref.shape[0], 2 * HEAD_DIM
    lane = lax.broadcasted_iota(jnp.int32, (length, width), 1)
    frame = lax.broadcasted_iota(jnp.int32, (length, width), 0)
    bias = jnp.where(frame < lengths_ref[own_clip(row_clip_ref)], 0.0, masked_score)
    for pair in range(q_ref.shape[1] // width):
        cols = slice(pair * width, (pair + 1) * width)
        q = q_ref[:, cols].astype(f32) * HEAD_DIM ** (-0.5)
        k = k_ref[:, cols].astype(f32)
        v_t = turned(v_ref[:, cols])
        for h in range(2):
            mine = lane // HEAD_DIM == h
            spare = lane == HEAD_DIM * (1 - h)
            own_q = jnp.where(mine, q, jnp.where(spare, 1.0, 0.0)).astype(bf16)
            own_k = jnp.where(mine, k, jnp.where(spare, bias, 0.0)).astype(bf16)
            scores = mm_nt(own_k, own_q)
            weight = jnp.exp(scores - jnp.max(scores, axis=0, keepdims=True))
            et_ref[2 * pair + h] = weight.astype(bf16)
            inv_ref[2 * pair + h] = 1.0 / jnp.sum(weight, axis=0, keepdims=True)
        found = [
            mm(v_t[h * HEAD_DIM : (h + 1) * HEAD_DIM], et_ref[2 * pair + h]) * inv_ref[2 * pair + h]
            for h in range(2)
        ]
        ctx_ref[:, cols] = jnp.concatenate(found, axis=0).T.astype(bf16)


def attend_back_kernel(
    q_ref, k_ref, v_ref, et_ref, inv_ref, gctx_ref, ctx_ref, dq_ref, dk_ref, dv_ref, sums_ref, ds_ref
):
    length, width = q_ref.shape
    lane = lax.broadcasted_iota(jnp.int32, (length, width), 1)
    row = lax.broadcasted_iota(jnp.int32, (width, length), 0)
    scale = HEAD_DIM ** (-0.5)
    grad_t = gctx_ref[...].astype(f32).T * jnp.where(row < HEAD_DIM, inv_ref[0], inv_ref[1])
    grad_t = grad_t.astype(bf16).astype(f32)
    grad = grad_t.T
    inner_all = grad_t * ctx_ref[...].astype(f32).T
    k_t = turned(k_ref[...])
    q = q_ref[...].astype(f32) * scale
    v = v_ref[...].astype(f32)
    dq_t = []
    dk = jnp.zeros((length, width), f32)
    dv = jnp.zeros((length, width), f32)
    for h in range(2):
        at = HEAD_DIM * (1 - h)
        mine = lane // HEAD_DIM == h
        inner = jnp.sum(inner_all[h * HEAD_DIM : (h + 1) * HEAD_DIM], axis=0, keepdims=True)
        high = inner.astype(bf16).astype(f32)
        own_grad_t = jnp.where(row // HEAD_DIM == h, grad_t, 0.0)
        own_grad_t = jnp.where(row == at, -high, jnp.where(row == at + 1, high - inner, own_grad_t))
        own_grad_t = own_grad_t.astype(bf16)
        own_v = jnp.where(mine, v, jnp.where((lane == at) | (lane == at + 1), 1.0, 0.0)).astype(bf16)
        own_q = jnp.where(mine, q, 0.0).astype(bf16)
        own_grad = jnp.where(mine, grad, 0.0).astype(bf16)
        for cols in chunks(length, BLOCK):
            shifted = mm(own_v, own_grad_t[:, cols])
            ds_ref[:, cols] = (et_ref[h, :, cols].astype(f32) * shifted).astype(bf16)
        dk += mm(ds_ref[...], own_q)
        dv += mm(et_ref[h], own_grad)
        dq_t.append(mm(k_t[h * HEAD_DIM : (h + 1) * HEAD_DIM], ds_ref[...]))
    dq = (jnp.concatenate(dq_t, axis=0).T * scale).astype(bf16)
    dv = dv.astype(bf16)
    dq_ref[...] = dq
    dk_ref[...] = dk.astype(bf16)
    dv_ref[...] = dv
    sums_ref[0:1] = jnp.sum(dq.astype(f32), axis=0, keepdims=True)
    sums_ref[1:2] = jnp.sum(dv.astype(f32), axis=0, keepdims=True)


def attend(joined, row_clip, lengths):
    length, width = joined.shape[0], 4 * HEAD_DIM
    pairs = joined.shape[1] // (3 * width)
    block = lambda part: pl.BlockSpec((length, width), lambda p, *_: (0, part * pairs + p))
    return pl.pallas_call(
        attend_kernel,
        grid_spec=pltpu.PrefetchScalarGridSpec(
            num_scalar_prefetch=2,
            grid=(pairs,),
            in_specs=[block(0), block(1), block(2)],
            out_specs=[
                block(0),
                pl.BlockSpec((4, length, length), lambda p, *_: (p, 0, 0)),
                pl.BlockSpec((4, 1, length), lambda p, *_: (p, 0, 0)),
            ],
        ),
        out_shape=[
            jax.ShapeDtypeStruct((length, pairs * width), bf16),
            jax.ShapeDtypeStruct((4 * pairs, length, length), bf16),
            jax.ShapeDtypeStruct((4 * pairs, 1, length), f32),
        ],
        compiler_params=pltpu.CompilerParams(vmem_limit_bytes=VMEM_LIMIT),
        name="attend",
    )(row_clip, lengths, joined, joined, joined)


def attend_back(joined, et, inverse, grad_context, context):
    length, width = joined.shape[0], 2 * HEAD_DIM
    pairs = joined.shape[1] // (3 * width)
    block = lambda part: pl.BlockSpec((length, width), lambda p: (0, part * pairs + p))
    one = jax.ShapeDtypeStruct((length, pairs * width), bf16)
    return pl.pallas_call(
        attend_back_kernel,
        grid=(pairs,),
        in_specs=[
            block(0),
            block(1),
            block(2),
            pl.BlockSpec((2, length, length), lambda p: (p, 0, 0)),
            pl.BlockSpec((2, 1, length), lambda p: (p, 0, 0)),
            block(0),
            block(0),
        ],
        out_specs=[block(0), block(0), block(0), pl.BlockSpec((8, width), lambda p: (0, p))],
        out_shape=[one, one, one, jax.ShapeDtypeStruct((8, pairs * width), f32)],
        scratch_shapes=[pltpu.VMEM((length, length), bf16)],
        compiler_params=pltpu.CompilerParams(vmem_limit_bytes=VMEM_LIMIT),
        name="attend_back",
    )(joined, joined, joined, et, inverse, grad_context, context)


def mean_of(values):
    return jnp.mean(values, axis=-1, keepdims=True)


def mlp_body(v, live, spoken, wait, done, tick):
    length, width = v.stem.shape
    inner = v.w_up.shape[1]
    row_steps, wide_steps = length // BLOCK, inner // width
    ones = lambda values: jnp.sum(values, axis=0, keepdims=True)
    v.sums[...] = jnp.zeros_like(v.sums)
    v.b_up_line[...] = row_of(v.b_up)
    wait("ctx", "w_out", "stem")

    @unrolled(row_steps)
    def _(i):
        rows = pl.ds(i * BLOCK, BLOCK)
        middle = v.stem[rows].astype(f32) + mm(v.ctx[rows], v.w_out[...]) + row_of(v.b_out)
        v.mid[rows] = middle
        centred = middle - mean_of(middle)
        scale = lax.rsqrt(mean_of(centred * centred) + epsilon)
        v.normed[rows] = (centred * scale * row_of(v.gain) + row_of(v.bias)).astype(bf16)

    wait("w_up")

    @unrolled(wide_steps)
    def _(j):
        cols = pl.ds(j * width, width)
        upward = mm(v.normed[...], v.w_up[:, cols]) + v.b_up_line[:, cols]
        hidden, slope = gelu_pair(upward)
        v.hidden[:, cols] = hidden.astype(bf16)
        v.slope[:, cols] = slope.astype(bf16)

    wait("w_down", "target")

    @unrolled(row_steps)
    def _(i):
        rows = pl.ds(i * BLOCK, BLOCK)
        final = v.mid[rows] + mm(v.hidden[rows], v.w_down[...]) + row_of(v.b_down)
        v.out[rows] = final.astype(bf16)
        frame = i * BLOCK + lax.broadcasted_iota(jnp.int32, final.shape, 0)
        mismatch = jnp.where(frame < live, final - v.target[rows].astype(f32), 0.0)
        v.gmid[rows] = mismatch
        branch = mismatch.astype(bf16)
        v.branch[rows] = branch
        v.branch_t[:, rows] = turned(branch)
        v.normed_t[:, rows] = turned(v.normed[rows])
        v.sums[5:6] += ones(mismatch * mismatch)
        v.sums[1:2] += ones(branch.astype(f32))

    done("out")
    group = lax.broadcasted_iota(jnp.int32, (1, width), 1)
    loss = 0.5 * jnp.sum(v.sums[5:6], axis=1, keepdims=True)
    v.sums[0:1] = jnp.where(group == spoken, loss, 0.0)

    @unrolled(wide_steps)
    def _(j):
        cols = pl.ds(j * width, width)
        v.put_down(j, cols, mm(v.branch_t[...], v.hidden[:, cols]).astype(bf16))

    tick("down")

    @unrolled(wide_steps)
    def _(j):
        cols = pl.ds(j * width, width)
        grad = mm_nt(v.branch[...], v.w_down[cols]) * v.slope[:, cols].astype(f32)
        grad = grad.astype(bf16)
        v.gb_up[:, cols] = ones(grad.astype(f32))
        v.slope[:, cols] = grad
        v.put_up(j, cols, mm(v.normed_t[...], grad).astype(bf16))
        tick("tiles", j)

    tick("up")

    @unrolled(row_steps)
    def _(i):
        rows = pl.ds(i * BLOCK, BLOCK)
        grad = mm_nt(v.slope[rows], v.w_up[...])
        middle = v.mid[rows]
        centred = middle - mean_of(middle)
        scale = lax.rsqrt(mean_of(centred * centred) + epsilon)
        unit = centred * scale
        gained = grad * row_of(v.gain)
        back = scale * (gained - mean_of(gained) - unit * mean_of(gained * unit))
        grad_middle = v.gmid[rows] + back
        v.gmid[rows] = grad_middle
        attended = grad_middle.astype(bf16)
        v.branch[rows] = attended
        v.gctx[rows] = mm_nt(attended, v.w_out[...]).astype(bf16)
        v.normed_t[:, rows] = turned(v.ctx[rows])
        v.sums[2:3] += ones(grad * unit)
        v.sums[3:4] += ones(grad)
        v.sums[4:5] += ones(attended.astype(f32))
        done("gmid", i)
        done("gctx", i)
        tick("rows", i)

    v.gw_out[...] = mm(v.normed_t[...], v.branch[...]).astype(bf16)
    done("gw_out")
    tick("end")


def own_scalars(row_clip_ref, lengths_ref, language_ref):
    clip = own_clip(row_clip_ref)
    return lengths_ref[clip], language_ref[clip]


def mlp_kernel(row_clip, lengths, language, *refs):
    names = ("ctx", "stem", "w_out", "b_out", "gain", "bias", "w_up", "b_up", "w_down", "b_down", "target")
    names += ("out", "gctx", "gmid", "gw_up", "gw_down", "gw_out", "sums", "gb_up", "mid", "normed", "normed_t")
    names += ("hidden", "slope", "branch", "branch_t", "b_up_line")
    v = SimpleNamespace(**dict(zip(names, refs)))

    def put_down(j, cols, values):
        v.gw_down[:, cols] = values

    def put_up(j, cols, values):
        v.gw_up[:, cols] = values

    v.put_down, v.put_up = put_down, put_up
    nothing = lambda *_: None
    mlp_body(v, *own_scalars(row_clip, lengths, language), nothing, nothing, nothing)


def mlp_send_kernel(row_clip, lengths, language, *refs):
    far_in = ("ctx", "stem", "w_out", "w_up", "w_down", "target")
    far_out = ("out", "gctx", "gmid", "gw_out")
    near = ("b_out", "gain", "bias", "b_up", "b_down")
    names = far_in + near + far_out + ("half_down", "core_down", "core_up", "sums", "gb_up")
    given = SimpleNamespace(**dict(zip(names, refs)))
    held = far_in + far_out + ("mid", "normed", "normed_t", "hidden", "slope", "branch", "branch_t", "b_up_line")
    held += ("gw_up", "gw_blocks", "cin_d", "fin_d", "cin_u")
    rest = refs[len(names) :]
    v = SimpleNamespace(**dict(zip(held, rest)))
    for name in near + ("sums", "gb_up"):
        setattr(v, name, getattr(given, name))
    in_sems, out_sems = rest[len(held) : len(held) + 2]
    sems = dict(zip(SEMS, rest[len(held) + 2 :]))
    links = Links()
    links.greet([links.by_core, links.by_x, links.by_y])
    loads = {}
    for i, name in enumerate(far_in):
        loads[name] = pltpu.make_async_copy(getattr(given, name), getattr(v, name), in_sems.at[i])
        loads[name].start()
    width = v.stem.shape[1]
    part, third, block = given.half_down.shape[3], given.core_up.shape[3], given.core_up.shape[2]
    tasks = {}
    for k in range(3):
        source = lambda d, k=k: v.gw_blocks.at[d, :, pl.ds(k * part, part)]
        tasks[f"d{k}"] = Task(links, k != 0, sems, k, None, source, None, v.cin_d.at[k], v.fin_d.at[k], None, None, None)
    for k in range(3):
        source = rows_of(v.gw_up, block, k * third, third)
        tasks[f"u{k}"] = Task(links, k == 1, sems, 3 + k, None, source, None, v.cin_u.at[k], None, None, None, None)

    def put_down(j, cols, values):
        wide = v.gw_blocks.shape[2]
        for k in range(width // wide):
            v.gw_blocks[j * (width // wide) + k] = values[:, k * wide : (k + 1) * wide]

    def put_up(j, cols, values):
        for k in range(width // BLOCK):
            out = pl.ds((k * 4 + j) * BLOCK, BLOCK)
            v.gw_up[:, out] = values[:, k * BLOCK : (k + 1) * BLOCK]

    v.put_down, v.put_up = put_down, put_up
    leaving = []

    def leave(source, target):
        copy = pltpu.make_async_copy(source, target, out_sems.at[len(leaving)])
        copy.start()
        leaving.append(copy)

    steps = v.stem.shape[0] // BLOCK
    pieces = {"gmid": 8, "gctx": 8 + steps}

    def row_copy(name, i):
        rows = pl.ds(i * BLOCK, BLOCK)
        return pltpu.make_async_copy(getattr(v, name).at[rows], getattr(given, name).at[rows], out_sems.at[pieces[name] + i])

    def wait(*names):
        for name in names:
            loads[name].wait()

    def done(name, i=None):
        if i is None:
            leave(getattr(v, name), getattr(given, name))
        else:
            row_copy(name, i).start()

    def tick(place, i=None):
        if place == "down":
            links.met([links.by_core, links.by_x, links.by_y])
            for k in range(3):
                tasks[f"d{k}"].begin()
        elif place == "tiles":
            pl.when(i == 1)(tasks["d0"].after_core)
            pl.when(i == 1)(tasks["d1"].after_core)
            pl.when(i == 3)(tasks["d2"].stop_at_core)
        elif place == "up":
            for k in range(3):
                tasks[f"u{k}"].begin()
            leave(v.cin_d.at[2], given.core_down)
        elif place == "rows":
            pl.when(i == 1)(tasks["u0"].stop_at_core)
            pl.when(i == 2)(tasks["u1"].stop_at_core)
        else:
            tasks["u2"].stop_at_core()
            leave(v.cin_u, given.core_up)
            for k in range(2):
                tasks[f"d{k}"].stop_at_first()
                leave(v.cin_d.at[k, pl.ds(0, 2)], given.half_down.at[k])

    mlp_body(v, *own_scalars(row_clip, lengths, language), wait, done, tick)
    for copy in leaving:
        copy.wait()
    for name in pieces:
        for i in range(steps):
            row_copy(name, i).wait()


def run_mlp_send(scalars, far, near):
    square, deep = far[0].shape, far[3].shape
    width, inner = deep
    block, part, third = width // 8, inner // 24, inner // 3
    in_smem = pl.BlockSpec(memory_space=pltpu.SMEM)
    in_vmem = pl.BlockSpec(memory_space=pltpu.VMEM)
    anywhere = pl.BlockSpec(memory_space=pl.ANY)
    whole = lambda x: pltpu.VMEM(x.shape, x.dtype)
    results = [
        (square, bf16),
        (square, bf16),
        (square, f32),
        ((width, width), bf16),
        ((2, 2, width, part), bf16),
        ((4, width, part), bf16),
        ((3, 4, block, third), bf16),
        ((8, width), f32),
        ((1, inner), f32),
    ]
    return pl.pallas_call(
        mlp_send_kernel,
        in_specs=[in_smem] * 3 + [anywhere] * len(far) + [in_vmem] * len(near),
        out_specs=[anywhere] * 7 + [in_vmem] * 2,
        out_shape=[jax.ShapeDtypeStruct(*r) for r in results],
        scratch_shapes=[whole(x) for x in far]
        + [pltpu.VMEM(*r) for r in results[:4]]
        + [
            pltpu.VMEM(square, f32),
            pltpu.VMEM(square, bf16),
            pltpu.VMEM(square, bf16),
            pltpu.VMEM((square[0], inner), bf16),
            pltpu.VMEM((square[0], inner), bf16),
            pltpu.VMEM(square, bf16),
            pltpu.VMEM(square, bf16),
            pltpu.VMEM((1, inner), f32),
            pltpu.VMEM(deep, bf16),
            pltpu.VMEM((8, width, inner // 8), bf16),
            *bufs_for(3, (width, part), 4, 2),
            *bufs_for(3, (block, third), 4),
            pltpu.SemaphoreType.DMA((len(far),)),
            pltpu.SemaphoreType.DMA((8 + 2 * (square[0] // BLOCK),)),
            *sems_for(6),
        ],
        compiler_params=pltpu.CompilerParams(
            vmem_limit_bytes=VMEM_LIMIT, collective_id=1, has_side_effects=True
        ),
        name="mlp",
    )(*scalars, *far, *near)


def shifted(values, step, axis):
    length = values.shape[axis]
    moved = pltpu.roll(values, step % length, axis)
    place = lax.broadcasted_iota(jnp.int32, values.shape, axis)
    return jnp.where(place == (0 if step > 0 else length - 1), 0.0, moved)


def pick_frames(slots, frames, offset):
    slot = lax.broadcasted_iota(jnp.int32, (slots, frames), 0)
    frame = lax.broadcasted_iota(jnp.int32, (slots, frames), 1)
    return jnp.where(frame == 2 * slot + offset, 1.0, 0.0).astype(bf16)


def flat_taps(ref):
    return ref[...].reshape(-1, ref.shape[-1])


def stem_kernel(*refs):
    near = ("mel", "w_one", "b_one", "b_two", "gain", "bias", "b_query", "b_value")
    far_in = ("w_two", "pos", "w_qkv")
    whole_out = ("taps", "act_even", "act_odd", "slope_even", "slope_odd")
    row_out = ("slope_two", "stem", "normed", "joined")
    far_out = whole_out + row_out
    names = near + far_in + far_out
    given = SimpleNamespace(**dict(zip(names, refs)))
    rest = refs[len(names) :]
    held = far_in + far_out + ("behind", "mel_out", "mel_in")
    v = SimpleNamespace(**dict(zip(held, rest)))
    in_sems, out_sems, send_g, recv_g = rest[len(held) :]
    loads = {}
    for i, name in enumerate(far_in):
        loads[name] = pltpu.make_async_copy(getattr(given, name), getattr(v, name), in_sems.at[i])
        loads[name].start()
    leaving = []

    def leave(source, target):
        copy = pltpu.make_async_copy(source, target, out_sems.at[len(leaving)])
        copy.start()
        leaving.append(copy)

    length, width = v.stem.shape
    steps = length // BLOCK
    links = Links()
    links.greet(links.by_z)
    bins_given = given.mel[...].astype(f32)
    share, tall = bins_given.shape[0], v.mel_out.shape[1]
    empty = jnp.zeros((tall - share, bins_given.shape[2]), f32)
    for z in range(4):
        v.mel_out[z] = jnp.concatenate([bins_given[:, z], empty], axis=0).astype(bf16)
    links.met(links.by_z)
    copies = [
        remote(v.mel_out.at[(links.chan + r) % 4], v.mel_in.at[r - 1], send_g.at[r - 1], recv_g.at[r - 1], links.by_z[r - 1])
        for r in (1, 2, 3)
    ]
    for copy in copies:
        copy.start()
    picks = [pick_frames(BLOCK, 2 * BLOCK, offset) for offset in range(2)]
    for copy in copies:
        copy.wait()
    mel = jnp.concatenate(by_place(links, v.mel_out, v.mel_in, share), axis=0)
    taps = jnp.concatenate([shifted(mel, 1, 1), mel, shifted(mel, -1, 1)], axis=0).astype(bf16)
    v.taps[...] = taps
    leave(v.taps, given.taps)
    w_one = flat_taps(given.w_one)
    for pick, act_ref, slope_ref in (
        (picks[1], v.act_odd, v.slope_odd),
        (picks[0], v.act_even, v.slope_even),
    ):
        for i in range(steps):
            rows = slice(i * BLOCK, (i + 1) * BLOCK)
            frames = slice(2 * i * BLOCK, 2 * (i + 1) * BLOCK)
            picked = mm_nt(pick, taps[:, frames]).astype(bf16)
            act, slope = gelu_pair(mm(picked, w_one) + row_of(given.b_one))
            act_ref[rows] = act.astype(bf16)
            slope_ref[rows] = slope.astype(bf16)
    for name in whole_out[1:]:
        leave(getattr(v, name), getattr(given, name))
    for cols in chunks(width, BLOCK):
        v.behind[:, cols] = shifted(v.act_odd[:, cols].astype(f32), 1, 0).astype(bf16)
    for name in far_in:
        loads[name].wait()
    query, key, value = (slice(part * width, (part + 1) * width) for part in range(3))
    for i in range(steps):
        rows = slice(i * BLOCK, (i + 1) * BLOCK)
        two = (
            mm(v.behind[rows], v.w_two[0])
            + mm(v.act_even[rows], v.w_two[1])
            + mm(v.act_odd[rows], v.w_two[2])
            + row_of(given.b_two)
        )
        act, slope = gelu_pair(two)
        v.slope_two[rows] = slope.astype(bf16)
        stem = (act + v.pos[rows]).astype(bf16)
        v.stem[rows] = stem
        stem = stem.astype(f32)
        centred = stem - mean_of(stem)
        scale = lax.rsqrt(mean_of(centred * centred) + epsilon)
        normed = (centred * scale * row_of(given.gain) + row_of(given.bias)).astype(bf16)
        v.normed[rows] = normed
        v.joined[rows, query] = (mm(normed, v.w_qkv[:, query]) + row_of(given.b_query)).astype(bf16)
        v.joined[rows, key] = mm(normed, v.w_qkv[:, key]).astype(bf16)
        v.joined[rows, value] = (mm(normed, v.w_qkv[:, value]) + row_of(given.b_value)).astype(bf16)
        for name in row_out:
            leave(getattr(v, name).at[pl.ds(i * BLOCK, BLOCK)], getattr(given, name).at[pl.ds(i * BLOCK, BLOCK)])
    for copy in leaving:
        copy.wait()


def run_stem(near, far, length):
    width, frames = near[1].shape[2], near[0].shape[2]
    square = (length, width)
    results = [(3 * near[1].shape[1], frames)] + [square] * 7 + [(length, 3 * width)]
    in_vmem = pl.BlockSpec(memory_space=pltpu.VMEM)
    anywhere = pl.BlockSpec(memory_space=pl.ANY)
    return pl.pallas_call(
        stem_kernel,
        in_specs=[in_vmem] * len(near) + [anywhere] * len(far),
        out_specs=[anywhere] * len(results),
        out_shape=[jax.ShapeDtypeStruct(r, bf16) for r in results],
        scratch_shapes=[pltpu.VMEM(x.shape, x.dtype) for x in far]
        + [pltpu.VMEM(r, bf16) for r in results]
        + [
            pltpu.VMEM(square, bf16),
            pltpu.VMEM((4, 32, frames), bf16),
            pltpu.VMEM((3, 32, frames), bf16),
            pltpu.SemaphoreType.DMA((len(far),)),
            pltpu.SemaphoreType.DMA((5 + 4 * (length // BLOCK),)),
            pltpu.SemaphoreType.DMA((3,)),
            pltpu.SemaphoreType.DMA((3,)),
        ],
        compiler_params=pltpu.CompilerParams(
            vmem_limit_bytes=VMEM_LIMIT, collective_id=3, has_side_effects=True
        ),
        name="stem",
    )(*near, *far)


def stem_back_kernel(
    gq_ref,
    gk_ref,
    gv_ref,
    w_qkv_ref,
    gmid_ref,
    stem_ref,
    normed_ref,
    gain_ref,
    slope_two_ref,
    w_two_ref,
    act_even_ref,
    act_odd_ref,
    slope_even_ref,
    slope_odd_ref,
    w_one_ref,
    taps_ref,
    gw_qkv_ref,
    gw_two_ref,
    gw_one_ref,
    gmel_ref,
    sums_ref,
    normed_t_ref,
    two_ref,
    two_ahead_ref,
    two_t_ref,
    two_ahead_t_ref,
    even_ref,
    odd_ref,
):
    length, width = stem_ref.shape
    steps = length // BLOCK
    ones = lambda v: jnp.sum(v, axis=0, keepdims=True)
    sums_ref[...] = jnp.zeros_like(sums_ref)

    @pl.loop(0, steps)
    def _(i):
        rows = pl.ds(pl.multiple_of(i * BLOCK, BLOCK), BLOCK)
        normed_t_ref[:, rows] = turned(normed_ref[rows])
        grad = (
            mm_nt(gq_ref[rows], w_qkv_ref[:, 0:width])
            + mm_nt(gk_ref[rows], w_qkv_ref[:, width : 2 * width])
            + mm_nt(gv_ref[rows], w_qkv_ref[:, 2 * width : 3 * width])
        )
        stem = stem_ref[rows].astype(f32)
        centred = stem - mean_of(stem)
        scale = lax.rsqrt(mean_of(centred * centred) + epsilon)
        unit = centred * scale
        gained = grad * row_of(gain_ref)
        back = scale * (gained - mean_of(gained) - unit * mean_of(gained * unit))
        grad_stem = (gmid_ref[rows] + back).astype(bf16).astype(f32)
        two = (grad_stem * slope_two_ref[rows].astype(f32)).astype(bf16)
        two_ref[rows] = two
        two_t_ref[:, rows] = turned(two)
        sums_ref[0:1] += ones(grad * unit)
        sums_ref[1:2] += ones(grad)
        sums_ref[2:3] += ones(two.astype(f32))

    for cols in chunks(width, BLOCK):
        two_ahead_ref[:, cols] = shifted(two_ref[:, cols].astype(f32), -1, 0).astype(bf16)

    @pl.loop(0, steps)
    def _(i):
        rows = pl.ds(pl.multiple_of(i * BLOCK, BLOCK), BLOCK)
        two_ahead_t_ref[:, rows] = turned(two_ahead_ref[rows])
        even = mm_nt(two_ref[rows], w_two_ref[1]) * slope_even_ref[rows].astype(f32)
        odd = mm_nt(two_ref[rows], w_two_ref[2]) + mm_nt(two_ahead_ref[rows], w_two_ref[0])
        odd = odd * slope_odd_ref[rows].astype(f32)
        even_ref[rows] = even.astype(bf16)
        odd_ref[rows] = odd.astype(bf16)
        sums_ref[3:4] += ones(even.astype(bf16).astype(f32)) + ones(odd.astype(bf16).astype(f32))

    @pl.loop(0, width // BLOCK)
    def _(j):
        cols = pl.ds(pl.multiple_of(j * BLOCK, BLOCK), BLOCK)
        for part, grad_ref in enumerate((gq_ref, gk_ref, gv_ref)):
            out = pl.ds(pl.multiple_of(part * width + j * BLOCK, BLOCK), BLOCK)
            gw_qkv_ref[:, out] = mm(normed_t_ref[...], grad_ref[:, cols]).astype(bf16)
        gw_two_ref[0, :, cols] = mm(two_ahead_t_ref[...], act_odd_ref[:, cols]).astype(bf16)
        gw_two_ref[1, :, cols] = mm(two_t_ref[...], act_even_ref[:, cols]).astype(bf16)
        gw_two_ref[2, :, cols] = mm(two_t_ref[...], act_odd_ref[:, cols]).astype(bf16)

    bins = w_one_ref.shape[1]
    gw_one = jnp.zeros((3 * bins, width), f32)
    for offset, grad_ref in ((0, even_ref), (1, odd_ref)):
        picked = [
            mm_nt(taps_ref[:, 2 * i * BLOCK : 2 * (i + 1) * BLOCK], pick_frames(BLOCK, 2 * BLOCK, offset))
            for i in range(steps)
        ]
        gw_one += mm(jnp.concatenate(picked, axis=1).astype(bf16), grad_ref[...])
    gw_one_ref[...] = jnp.zeros_like(gw_one_ref)
    gw_one_ref[:, 0 : 3 * bins] = gw_one.T.astype(bf16)
    even, odd = even_ref[...], odd_ref[...]
    mel_even = (
        mm_nt(odd, w_one_ref[0])
        + mm_nt(even, w_one_ref[1])
        + shifted(mm_nt(odd, w_one_ref[2]), 1, 0)
    )
    mel_odd = (
        shifted(mm_nt(even, w_one_ref[0]), -1, 0)
        + mm_nt(odd, w_one_ref[1])
        + mm_nt(even, w_one_ref[2])
    )
    mel_even, mel_odd = turned(mel_even), turned(mel_odd)
    for i in range(steps):
        cols = slice(i * BLOCK, (i + 1) * BLOCK)
        frames = slice(2 * i * BLOCK, 2 * (i + 1) * BLOCK)
        gmel_ref[:, frames] = (
            mm(mel_even[:, cols], pick_frames(BLOCK, 2 * BLOCK, 0))
            + mm(mel_odd[:, cols], pick_frames(BLOCK, 2 * BLOCK, 1))
        ).astype(bf16)


MESH = pl.DeviceIdType.MESH


def remote(source, target, send, recv, to):
    return pltpu.make_async_remote_copy(source, target, send, recv, device_id=to, device_id_type=MESH)


class Links:
    def __init__(self):
        dp, chan = lax.axis_index("dp"), lax.axis_index("chan")
        self.chan = chan
        self.core, self.x, self.y = dp % 2, (dp // 2) % 2, dp // 4
        self.by_core = (self.dest(0, 0, 1), chan)
        self.by_x = (self.dest(0, 1, 0), chan)
        self.by_y = (self.dest(1, 0, 0), chan)
        self.by_z = [(dp, (chan + r) % 4) for r in (1, 2, 3)]
        self.by_next = (dp, chan + 1 - 2 * (chan % 2))
        self.by_far = (dp, (chan + 2) % 4)
        self.partners = [self.by_core, self.by_x, self.by_y] + self.by_z

    def dest(self, dy, dx, dc):
        flip = lambda bit, turn: 1 - bit if turn else bit
        return 4 * flip(self.y, dy) + 2 * flip(self.x, dx) + flip(self.core, dc)

    def greet(self, partners):
        for partner in partners:
            pl.semaphore_signal(pltpu.get_barrier_semaphore(), inc=1, device_id=partner, device_id_type=MESH)

    def met(self, partners):
        pl.semaphore_wait(pltpu.get_barrier_semaphore(), len(partners))


def by_place(links, out_ref, in_ref, share):
    parts = [out_ref[links.chan], in_ref[0], in_ref[1], in_ref[2]]
    parts = [part.astype(f32)[0:share] for part in parts]
    placed = []
    for z in range(4):
        value = parts[0]
        for r in (1, 2, 3):
            value = jnp.where((links.chan + 4 - r) % 4 == z, parts[r], value)
        placed.append(value)
    return placed


class Task:
    def __init__(self, links, x_first, sems, n, cut, source, own, cin, fin, sin, z_out, z_in, stage=0):
        self.links, self.x_first, self.sems, self.n, self.cut = links, x_first, sems, n, cut
        self.source, self.own, self.cin, self.fin, self.sin = source, own, cin, fin, sin
        self.z_out, self.z_in, self.stage = z_out, z_in, stage
        self.ways = (links.by_x, links.by_y) if x_first else (links.by_y, links.by_x)

    def sem(self, name):
        return self.sems[name].at[self.n]

    def dest(self, slot, dc):
        dx, dy = (slot // 2, slot % 2) if self.x_first else (slot % 2, slot // 2)
        return self.links.dest(dy, dx, dc)

    def begin(self):
        if self.stage == 0:
            for slot in (3, 2, 1, 0):
                source = self.source(self.dest(slot, 1))
                remote(source, self.cin.at[slot], self.sem("send_c"), self.sem("recv_c"), self.links.by_core).start()
                if self.own is not None:
                    source = self.source(self.dest(slot, 0))
                    pltpu.make_async_copy(source, self.own.at[slot], self.sem("load")).start()
            return
        if self.stage == 1:
            for slot in (3, 2):
                self.to_first(self.source.at[slot], slot)
        else:
            self.to_second(self.source.at[1])
        held = self.own.shape[0]
        pltpu.make_async_copy(self.source.at[pl.ds(0, held)], self.own, self.sem("load")).start()

    def to_first(self, ref, slot):
        remote(ref, self.fin.at[slot - 2], self.sem("send_f"), self.sem("recv_f"), self.ways[0]).start()

    def to_second(self, ref):
        remote(ref, self.sin, self.sem("send_s"), self.sem("recv_s"), self.ways[1]).start()

    def loaded(self, stage):
        if self.own is not None and self.stage == stage:
            pltpu.make_async_copy(self.own, self.own, self.sem("load")).wait()

    def wait(self, ref, name, to):
        remote(ref, ref, self.sem("send_" + name), self.sem("recv_" + name), to).wait()

    def held(self, slot):
        if self.stage:
            return self.own[slot].astype(f32)
        own = self.own[slot] if self.own is not None else self.source(self.dest(slot, 0))[...]
        return own.astype(f32) + self.cin[slot].astype(f32)

    def core_done(self):
        self.loaded(0)
        self.wait(self.cin, "c", self.links.by_core)

    def after_core(self):
        self.core_done()
        for slot in (3, 2):
            self.cin[slot] = self.held(slot).astype(bf16)
            self.to_first(self.cin.at[slot], slot)

    def stop_at_core(self):
        self.core_done()
        for slot in (3, 2, 1, 0):
            self.cin[slot] = self.held(slot).astype(bf16)

    def stop_at_first(self):
        self.wait(self.fin, "f", self.ways[0])
        for slot in (1, 0):
            self.cin[slot] = (self.held(slot) + self.fin[slot].astype(f32)).astype(bf16)

    def after_first(self):
        self.loaded(1)
        self.wait(self.fin, "f", self.ways[0])
        leaving = self.own if self.stage else self.cin
        leaving[1] = (self.held(1) + self.fin[1].astype(f32)).astype(bf16)
        self.to_second(leaving.at[1])

    def z_copies(self):
        theirs = 1 - self.links.chan % 2
        sems = self.sem("send_z"), self.sem("recv_z")
        return [remote(self.z_out.at[2 * a + theirs], self.z_in.at[a], *sems, self.links.by_next) for a in range(2)]

    def after_second(self):
        self.loaded(2)
        self.wait(self.sin, "s", self.ways[1])
        total = self.held(0) + self.sin[...].astype(f32)
        if self.stage < 2:
            total = total + self.fin[0].astype(f32)
        for z in range(4):
            self.z_out[z] = self.cut(total, z).astype(bf16)
        for copy in self.z_copies():
            copy.start()

    def after_third(self):
        chan = self.links.chan
        self.wait(self.z_in.at[pl.ds(0, 2)], "z", self.links.by_next)
        far = (chan + 2) % 4
        self.z_out[far] = (self.z_out[far].astype(f32) + self.z_in[far // 2].astype(f32)).astype(bf16)
        remote(self.z_out.at[far], self.z_in.at[2], self.sem("send_w"), self.sem("recv_w"), self.links.by_far).start()

    def finish(self):
        chan = self.links.chan
        self.wait(self.z_in.at[2], "w", self.links.by_far)
        return self.z_out[chan].astype(f32) + self.z_in[chan // 2].astype(f32) + self.z_in[2].astype(f32)


def cut_rows(block, z):
    share = block.shape[0] // 4
    return block[z * share : (z + 1) * share]


def cut_columns(block, z):
    share = block.shape[1] // 4
    first = z * share // 128 * 128
    taken = block[:, first : first + (share + 127) // 128 * 128]
    skip = z * share - first
    return pltpu.roll(taken, taken.shape[1] - skip, 1) if skip else taken


def cut_half_tiles(block, z):
    taken = block[:, z // 2 * 128 : (z // 2 + 1) * 128]
    return pltpu.roll(taken, 64, 1) if z % 2 else taken


SEMS = ("send_c", "recv_c", "load", "send_f", "recv_f", "send_s", "recv_s", "send_z", "recv_z", "send_w", "recv_w")


def sems_for(count):
    return [pltpu.SemaphoreType.DMA((count,)) for _ in SEMS]


def bufs_for(count, shape, *slots):
    return [pltpu.VMEM((count,) + ((slot,) if slot else ()) + shape, bf16) for slot in slots]


def rows_of(ref, block, start, count):
    return lambda d: ref.at[pl.ds(pl.multiple_of(d * block, block), block), pl.ds(start, count)]


def pair_back(p, q_ref, k_ref, v_ref, et_of, inverse_ref, gctx_ref, ctx_ref, dq_ref, dk_ref, dv_ref, sums_ref, ds_ref, between):
    length, width = q_ref.shape[0], 2 * HEAD_DIM
    cols = pl.ds(pl.multiple_of(p * width, width), width)
    lane = lax.broadcasted_iota(jnp.int32, (length, width), 1)
    row = lax.broadcasted_iota(jnp.int32, (width, length), 0)
    scale = HEAD_DIM ** (-0.5)
    grad_t = gctx_ref[:, cols].astype(f32).T
    grad_t = grad_t * jnp.where(row < HEAD_DIM, inverse_ref[2 * p], inverse_ref[2 * p + 1])
    grad_t = grad_t.astype(bf16).astype(f32)
    grad = grad_t.T
    inner_all = grad_t * ctx_ref[:, cols].astype(f32).T
    k_t = turned(k_ref[:, cols])
    q = q_ref[:, cols].astype(f32) * scale
    v = v_ref[:, cols].astype(f32)
    dq_t = []
    dk = jnp.zeros((length, width), f32)
    dv = jnp.zeros((length, width), f32)
    for h in range(2):
        at = HEAD_DIM * (1 - h)
        mine = lane // HEAD_DIM == h
        inner = jnp.sum(inner_all[h * HEAD_DIM : (h + 1) * HEAD_DIM], axis=0, keepdims=True)
        high = inner.astype(bf16).astype(f32)
        own_grad_t = jnp.where(row // HEAD_DIM == h, grad_t, 0.0)
        own_grad_t = jnp.where(row == at, -high, jnp.where(row == at + 1, high - inner, own_grad_t))
        own_grad_t = own_grad_t.astype(bf16)
        own_v = jnp.where(mine, v, jnp.where((lane == at) | (lane == at + 1), 1.0, 0.0)).astype(bf16)
        own_q = jnp.where(mine, q, 0.0).astype(bf16)
        own_grad = jnp.where(mine, grad, 0.0).astype(bf16)
        et_ref = et_of(h)
        ds_ref[...] = (et_ref[...].astype(f32) * mm(own_v, own_grad_t)).astype(bf16)
        dk += mm(ds_ref[...], own_q)
        dv += mm(et_ref[...], own_grad)
        dq_t.append(mm(k_t[h * HEAD_DIM : (h + 1) * HEAD_DIM], ds_ref[...]))
        if h == 0:
            between()
    dq = (jnp.concatenate(dq_t, axis=0).T * scale).astype(bf16)
    dv = dv.astype(bf16)
    dq_ref[:, cols] = dq
    dk_ref[:, cols] = dk.astype(bf16)
    dv_ref[:, cols] = dv
    sums_ref[0:1, cols] = jnp.sum(dq.astype(f32), axis=0, keepdims=True)
    sums_ref[1:2, cols] = jnp.sum(dv.astype(f32), axis=0, keepdims=True)


SCHEDULE = {
    "middle": (
        (0, "after_core o"),
        (2, "after_third d0"),
        (4, "finish d1"),
        (5, "after_first u1"),
        (5, "after_first u2"),
    ),
    "pairs": (
        (0, "after_second d0"),
        (0, "after_second d1"),
        (2, "after_first d2"),
        (2, "after_third d1"),
        (2, "after_first u0"),
        (3, "finish d0"),
    ),
    "turn": (
        (0, "after_second d2"),
    ),
    "qkv": (
        (1, "after_first o"),
    ),
    "rows": (
        (0, "after_third d2"),
        (0, "after_second u1"),
        (0, "after_second u0"),
        (1, "after_core q0"),
        (2, "after_second o"),
        (2, "after_second u2"),
        (2, "after_core q1"),
        (2, "after_core q2"),
    ),
    "ahead": (
        (0, "finish d2"),
        (0, "after_third u1"),
    ),
    "two": (
        (1, "after_third u0"),
    ),
    "convs": (
        (0, "after_third o"),
        (1, "after_first q0"),
        (1, "after_core t0"),
        (1, "after_third u2"),
        (1, "after_core t1"),
        (1, "finish u1"),
        (1, "after_core t2"),
        (2, "after_first q1"),
        (2, "after_core t3"),
        (2, "after_core t4"),
        (2, "after_core t5"),
        (2, "finish u0"),
    ),
    "one": (
        (0, "after_first q2"),
        (0, "after_core m"),
        (0, "after_second q0"),
        (0, "finish o"),
    ),
    "mel": (
        (0, "after_first t1"),
        (0, "after_core n"),
        (0, "finish u2"),
        (0, "after_first t0"),
    ),
    "tail": (
        (0, "after_second q1"),
        (0, "after_third q0"),
        (0, "after_first t2"),
        (0, "after_first t3"),
        (0, "after_first t4"),
        (0, "after_third q1"),
        (0, "after_first t5"),
        (0, "after_second q2"),
        (0, "finish q0"),
        (0, "after_first m"),
        (0, "after_first n"),
        (0, "after_second t1"),
        (0, "after_second t0"),
        (0, "after_second t3"),
        (0, "after_second t2"),
        (0, "after_third q2"),
        (0, "finish q1"),
        (0, "after_second t5"),
        (0, "after_second t4"),
        (0, "after_third t1"),
        (0, "after_second n"),
        (0, "after_second m"),
        (0, "after_third t0"),
        (0, "after_third t3"),
        (0, "after_third t2"),
        (0, "after_third t5"),
        (0, "finish q2"),
        (0, "after_third t4"),
        (0, "finish t1"),
        (0, "after_third n"),
        (0, "finish t0"),
        (0, "after_third m"),
        (0, "finish t3"),
        (0, "finish t2"),
        (0, "finish t5"),
        (0, "finish t4"),
        (0, "finish n"),
        (0, "finish m"),
    ),
}


def back_kernel(*refs):
    joined, et, inverse, gctx, ctx, w_qkv, gmid, stem, normed, gain_ref, slope_two = refs[:11]
    w_two, act_even, act_odd, slope_even, slope_odd, w_one_ref, taps_ref = refs[11:18]
    half_down, core_down, core_up, gw_out, sums_b_ref, gb_up_ref = refs[18:24]
    up_z, down_z, out_z, qkv_z, two_z, one_z, small_z, gmel_z = refs[24:32]
    pool, d_ref, w_qkv_v, gmid_v, stem_v, normed_v, slope_two_v, w_two_v, gw_qkv = refs[32:41]
    gw_one, sums_a_ref, sums_ref = refs[41:44]
    rest = list(refs[44:])
    take = lambda count: [rest.pop(0) for _ in range(count)]
    own_h, sin_h, zo_h, zi_h = take(4)
    own_c, fin_c, sin_c, zo_c, zi_c = take(5)
    own_u, fin_u, sin_u, zo_u, zi_u = take(5)
    own_o, cin_o, fin_o, sin_o, zo_o, zi_o = take(6)
    bufs_q, bufs_t, bufs_n = take(5), take(5), take(5)
    small_buf, small_in, gmel_out, gmel_in = take(4)
    sems = dict(zip(SEMS, take(len(SEMS))))
    loads, et_loads, send_m, recv_m, send_g, recv_g = rest
    length, width = ctx.shape
    steps, pairs, block = length // BLOCK, width // (2 * HEAD_DIM), width // 8
    bins = w_one_ref.shape[1]
    links = Links()
    links.greet(links.partners)

    q_v, k_v, v_v = (pool.at[i] for i in range(3))
    ctx_v, gctx_v, ds_v = pool.at[7], pool.at[8], pool.at[9]
    started = []

    def load(source, target):
        copy = pltpu.make_async_copy(source, target, loads.at[len(started)])
        copy.start()
        started.append(copy)
        return copy

    def et_load(head, slot):
        return pltpu.make_async_copy(et.at[head], pool.at[3 + slot], et_loads.at[slot])

    first = [load(joined.at[:, pl.ds(i * width, width)], pool.at[i]) for i in range(3)]
    first += [load(gctx, gctx_v), load(ctx, ctx_v)]
    for head in range(4):
        et_load(head, head).start()

    tasks = {}

    def add(name, x_first, cut, source, own, cin, fin, sin, z_out, z_in, stage=0):
        tasks[name] = Task(
            links, x_first, sems, len(tasks), cut, source, own, cin, fin, sin, z_out, z_in, stage
        )

    at = lambda k, *bufs: [ref.at[k] for ref in bufs]
    part, third, rest_rows, half = core_down.shape[2], core_up.shape[3], block // 3, block // 2
    for k in range(2):
        own, sin, z_out, z_in = at(k, own_h, sin_h, zo_h, zi_h)
        add(f"d{k}", k != 0, cut_rows, half_down.at[k], own, None, None, sin, z_out, z_in, 2)
    own, *bufs = at(0, own_c, fin_c, sin_c, zo_c, zi_c)
    add("d2", True, cut_rows, core_down, own, None, *bufs, 1)
    for k in range(3):
        own, *bufs = at(k, own_u, fin_u, sin_u, zo_u, zi_u)
        add(f"u{k}", k == 1, cut_columns, core_up.at[k], own, None, *bufs, 1)
    own, *bufs = at(0, own_o, cin_o, fin_o, sin_o, zo_o, zi_o)
    add("o", True, cut_columns, rows_of(gw_out, block, 0, width), own, *bufs)
    for k in range(3):
        source = lambda d, k=k: gw_qkv.at[pl.ds(pl.multiple_of(d * block + k * rest_rows, rest_rows), rest_rows)]
        add(f"q{k}", k == 1, cut_columns, source, None, *at(k, *bufs_q))
    for k in range(6):
        source = lambda d, k=k: pool.at[7 + k // 2, pl.ds(pl.multiple_of(d * block + k % 2 * half, half), half)]
        add(f"t{k}", k % 2 == 0, cut_columns, source, None, *at(k, *bufs_t))
    add("n", False, cut_half_tiles, rows_of(gw_one, block, 0, gw_one.shape[1]), None, *at(0, *bufs_n))
    quarter = width // 4

    def store(name):
        total = tasks[name].finish()
        k = int(name[1:] or 0)
        if name[0] == "d":
            down_z[:, k * part : (k + 1) * part] = total
        elif name[0] == "u":
            up_z[:, k * third // 4 : (k + 1) * third // 4] = total
        elif name == "o":
            out_z[...] = total[:, 0:quarter]
        elif name[0] == "q":
            qkv_z[k * rest_rows : (k + 1) * rest_rows] = total[:, 0 : 3 * quarter]
        elif name[0] == "t":
            two_z[k // 2, k % 2 * half : (k % 2 + 1) * half] = total[:, 0:quarter]
        else:
            one_z[...] = total

    small_ways = [links.by_core, links.by_x, links.by_y, links.by_next, links.by_far]

    def small_step(step):
        i = ("begin", "after_core", "after_first", "after_second", "after_third", "finish").index(step)
        if i == 0:
            small_buf[0, 0:1] = sums_b_ref[0:1]
            small_buf[0, 1:2] = sums_ref[3:4]
            small_buf[0, 2:3] = sums_ref[2:3]
            small_buf[0, 3:5] = sums_ref[0:2]
            small_buf[0, 5:7] = sums_a_ref[0:2]
            small_buf[0, 7:8] = sums_b_ref[4:5]
            small_buf[0, 8:10] = sums_b_ref[2:4]
            small_buf[0, 10:11] = sums_b_ref[1:2]
            for k in range(4):
                small_buf[0, 11 + k : 12 + k] = gb_up_ref[:, k * width : (k + 1) * width]
            small_buf[0, 15:16] = jnp.zeros((1, width), f32)
        else:
            got = small_in.at[i - 1]
            remote(got, got, send_m.at[i - 1], recv_m.at[i - 1], small_ways[i - 1]).wait()
            total = small_buf[i - 1] + small_in[i - 1]
            if i == 5:
                small_z[...] = total
                return
            small_buf[i] = total
        remote(small_buf.at[i], small_in.at[i], send_m.at[i], recv_m.at[i], small_ways[i]).start()

    def run(step, *names):
        for name in names:
            if name == "m":
                small_step(step)
            elif step == "finish":
                store(name)
            else:
                getattr(tasks[name], step)()

    def ticks(place, at=None):
        for index, steps_there in SCHEDULE.get(place, ()):
            work = lambda steps_there=steps_there: run(*steps_there.split())
            if at is None or isinstance(at, int):
                if at in (None, index):
                    work()
            else:
                pl.when(at == index)(work)

    links.met(links.partners)
    run("begin", "d0", "d1", "d2", "u0", "u1", "u2", "o")
    late = [
        load(normed, normed_v),
        load(w_qkv, w_qkv_v),
        load(gmid, gmid_v),
        load(stem, stem_v),
        load(slope_two, slope_two_v),
        load(w_two, w_two_v),
    ]
    for copy in first:
        copy.wait()

    @pl.loop(0, pairs)
    def _(p):
        for h in range(2):
            et_load(2 * p + h, (2 * p + h) % 4).wait()
        pair_back(
            p,
            q_v,
            k_v,
            v_v,
            lambda h: pool.at[3 + (2 * p + h) % 4],
            inverse,
            gctx_v,
            ctx_v,
            d_ref.at[0],
            d_ref.at[1],
            d_ref.at[2],
            sums_a_ref,
            ds_v,
            lambda: ticks("middle", p),
        )

        @pl.when(p + 2 < pairs)
        def _():
            for h in range(2):
                et_load(2 * p + 4 + h, (2 * p + h) % 4).start()

        ticks("pairs", p)

    acts = [load(act_even, pool.at[5]), load(act_odd, pool.at[6])]
    for copy in late:
        copy.wait()
    ones = lambda v: jnp.sum(v, axis=0, keepdims=True)
    normed_t, two_v, two_ahead, two_t, two_ahead_t = (pool.at[i] for i in range(5))
    act_v = [pool.at[5], pool.at[6]]
    even_v, odd_v = pool.at[0], pool.at[5]
    gw_two = [pool.at[7 + k] for k in range(3)]
    sums_ref[...] = jnp.zeros_like(sums_ref)

    @unrolled(steps)
    def _(i):
        rows = pl.ds(i * BLOCK, BLOCK)
        normed_t[:, rows] = turned(normed_v[rows])

    ticks("turn")

    @unrolled(3)
    def _(j):
        cols = pl.ds(j * width, width)
        gw_qkv[:, cols] = mm(normed_t[...], d_ref[j]).astype(bf16)
        ticks("qkv", j)

    run("begin", "q0", "q1", "q2")

    @unrolled(steps)
    def _(i):
        rows = pl.ds(i * BLOCK, BLOCK)
        grad = (
            mm_nt(d_ref[0, rows], w_qkv_v[:, 0:width])
            + mm_nt(d_ref[1, rows], w_qkv_v[:, width : 2 * width])
            + mm_nt(d_ref[2, rows], w_qkv_v[:, 2 * width : 3 * width])
        )
        stem = stem_v[rows].astype(f32)
        centred = stem - mean_of(stem)
        scale = lax.rsqrt(mean_of(centred * centred) + epsilon)
        unit = centred * scale
        gained = grad * row_of(gain_ref)
        back = scale * (gained - mean_of(gained) - unit * mean_of(gained * unit))
        grad_stem = (gmid_v[rows] + back).astype(bf16).astype(f32)
        two = (grad_stem * slope_two_v[rows].astype(f32)).astype(bf16)
        two_v[rows] = two
        two_t[:, rows] = turned(two)
        sums_ref[0:1] += ones(grad * unit)
        sums_ref[1:2] += ones(grad)
        sums_ref[2:3] += ones(two.astype(f32))
        ticks("rows", i)

    slope_v = d_ref
    for copy in acts:
        copy.wait()
    slopes = [load(slope_even, slope_v.at[0]), load(slope_odd, slope_v.at[1])]
    for cols in chunks(width, BLOCK):
        two_ahead[:, cols] = shifted(two_v[:, cols].astype(f32), -1, 0).astype(bf16)

    @unrolled(steps)
    def _(i):
        rows = pl.ds(i * BLOCK, BLOCK)
        two_ahead_t[:, rows] = turned(two_ahead[rows])

    ticks("ahead")

    gw_two[0][...] = mm(two_ahead_t[...], act_v[1][...]).astype(bf16)
    ticks("two", 0)
    gw_two[1][...] = mm(two_t[...], act_v[0][...]).astype(bf16)
    ticks("two", 1)
    gw_two[2][...] = mm(two_t[...], act_v[1][...]).astype(bf16)

    run("begin", "t0", "t1", "t2", "t3", "t4", "t5")
    for copy in slopes:
        copy.wait()

    @unrolled(steps)
    def _(i):
        rows = pl.ds(i * BLOCK, BLOCK)
        even = mm_nt(two_v[rows], w_two_v[1]) * slope_v[0, rows].astype(f32)
        odd = mm_nt(two_v[rows], w_two_v[2]) + mm_nt(two_ahead[rows], w_two_v[0])
        odd = odd * slope_v[1, rows].astype(f32)
        even, odd = even.astype(bf16), odd.astype(bf16)
        even_v[rows] = even
        odd_v[rows] = odd
        sums_ref[3:4] += ones(even.astype(f32)) + ones(odd.astype(f32))
        ticks("convs", i)

    run("begin", "m")

    total_one = jnp.zeros((3 * bins, width), f32)
    for offset, grad_ref in ((0, even_v), (1, odd_v)):
        picked = [
            mm_nt(taps_ref[:, 2 * i * BLOCK : 2 * (i + 1) * BLOCK], pick_frames(BLOCK, 2 * BLOCK, offset))
            for i in range(steps)
        ]
        total_one += mm(jnp.concatenate(picked, axis=1).astype(bf16), grad_ref[...])
    share = bins // 4
    spread = []
    for z in range(4):
        spread += [total_one[(4 * j + z) * share : (4 * j + z + 1) * share] for j in range(3)]
        spread.append(jnp.zeros((64 - 3 * share, width), f32))
    gw_one[...] = jnp.concatenate(spread, axis=0).T.astype(bf16)
    run("begin", "n")
    ticks("one")

    even, odd = even_v[...], odd_v[...]
    mel_even = (
        mm_nt(odd, w_one_ref[0])
        + mm_nt(even, w_one_ref[1])
        + shifted(mm_nt(odd, w_one_ref[2]), 1, 0)
    )
    mel_odd = (
        shifted(mm_nt(even, w_one_ref[0]), -1, 0)
        + mm_nt(odd, w_one_ref[1])
        + mm_nt(even, w_one_ref[2])
    )
    mel_even, mel_odd = turned(mel_even), turned(mel_odd)
    share = bins // 4
    tall = gmel_out.shape[1]
    for i in range(steps):
        cols = slice(i * BLOCK, (i + 1) * BLOCK)
        frames = slice(2 * i * BLOCK, 2 * (i + 1) * BLOCK)
        gmel = mm(mel_even[:, cols], pick_frames(BLOCK, 2 * BLOCK, 0))
        gmel += mm(mel_odd[:, cols], pick_frames(BLOCK, 2 * BLOCK, 1))
        for z in range(4):
            part = gmel[z * share : (z + 1) * share]
            part = jnp.concatenate([part, jnp.zeros((tall - share, 2 * BLOCK), f32)], axis=0)
            gmel_out[z, :, frames] = part.astype(bf16)
    gmel_copies = [
        remote(gmel_out.at[(links.chan + r) % 4], gmel_in.at[r - 1], send_g.at[r - 1], recv_g.at[r - 1], links.by_z[r - 1])
        for r in (1, 2, 3)
    ]
    for copy in gmel_copies:
        copy.start()

    ticks("mel")
    ticks("tail")

    for copy in gmel_copies:
        copy.wait()
    placed = by_place(links, gmel_out, gmel_in, share)
    gmel_z[...] = jnp.concatenate([part[:, None] for part in placed], axis=1).astype(bf16)
    ticks("end")


def run_back(operands):
    joined, et, w_one, taps = operands[0], operands[1], operands[16], operands[17]
    length, width = operands[4].shape
    block, quarter = width // 8, width // 4
    bins, frames = w_one.shape[1], taps.shape[1]
    held = pl.BlockSpec(memory_space=pltpu.VMEM)
    far = pl.BlockSpec(memory_space=pl.ANY)
    near = (2, 9, 16, 17, 22, 23)
    part, third = operands[19].shape[2], operands[20].shape[3]
    square = (length, width)
    vmem = lambda *shape: pltpu.VMEM(shape, bf16)
    scratch = [
        vmem(10, *square),
        vmem(3, *square),
        vmem(width, 3 * width),
        pltpu.VMEM(square, f32),
        vmem(*square),
        vmem(*square),
        vmem(*square),
        vmem(3, width, width),
        vmem(width, 3 * width),
        vmem(width, 256),
        pltpu.VMEM((8, width), f32),
        pltpu.VMEM((8, width), f32),
        *bufs_for(2, (width, part), 1, 0),
        *bufs_for(2, (quarter, part), 4, 3),
        *bufs_for(1, (width, part), 2, 2, 0),
        *bufs_for(1, (quarter, part), 4, 3),
        *bufs_for(3, (block, third), 2, 2, 0),
        *bufs_for(3, (block, third // 4), 4, 3),
        *bufs_for(1, (block, width), 4, 4, 2, 0),
        *bufs_for(1, (block, 256), 4, 3),
        *bufs_for(3, (block // 3, 3 * width), 4, 2, 0),
        *bufs_for(3, (block // 3, 640), 4, 3),
        *bufs_for(6, (block // 2, width), 4, 2, 0),
        *bufs_for(6, (block // 2, 256), 4, 3),
        *bufs_for(1, (block, 256), 4, 2, 0),
        *bufs_for(1, (block, 128), 4, 3),
        pltpu.VMEM((5, 16, width), f32),
        pltpu.VMEM((5, 16, width), f32),
        vmem(4, 32, frames),
        vmem(3, 32, frames),
        *sems_for(17),
        pltpu.SemaphoreType.DMA((15,)),
        pltpu.SemaphoreType.DMA((4,)),
        pltpu.SemaphoreType.DMA((6,)),
        pltpu.SemaphoreType.DMA((6,)),
        pltpu.SemaphoreType.DMA((3,)),
        pltpu.SemaphoreType.DMA((3,)),
    ]
    shapes = (
        (block, width),
        (quarter, 3 * part),
        (block, quarter),
        (block, 3 * quarter),
        (3, block, quarter),
        (block, 128),
        (16, width),
    )
    return pl.pallas_call(
        back_kernel,
        in_specs=[held if i in near else far for i in range(len(operands))],
        out_specs=[held] * 8,
        out_shape=[jax.ShapeDtypeStruct(s, f32) for s in shapes]
        + [jax.ShapeDtypeStruct((bins // 4, 4, frames), bf16)],
        scratch_shapes=scratch,
        compiler_params=pltpu.CompilerParams(
            vmem_limit_bytes=VMEM_LIMIT, collective_id=2, has_side_effects=True
        ),
        name="back",
    )(*operands)


def last_kernel(*refs):
    lengths_ref, language_ref, down, up, out, qkv, two, one, small, gmel = refs[:10]
    outs = refs[10:]
    group_z, gmel_z, one_z, b_one_z, two_z, b_two_z, gain_a_z, bias_a_z, qkv_z, b_query_z = outs[:10]
    b_value_z, out_z, b_out_z, gain_b_z, bias_b_z, up_z, b_up_z, down_z, b_down_z = outs[10:]
    group = lax.broadcasted_iota(jnp.int32, (1, 128), 1)

    def count(c, total):
        return total + jnp.where(group == language_ref[c], lengths_ref[c], 0)

    frames = lax.fori_loop(0, lengths_ref.shape[0], count, jnp.zeros((1, 128), jnp.int32))
    width = small.shape[1]
    loss = small[0:1, 0:128] / (width * jnp.maximum(frames, 1).astype(f32))
    group_z[...] = loss.reshape(-1)[: group_z.shape[0]]
    gmel_z[...] = gmel[...]
    vectors = (b_one_z, b_two_z, gain_a_z, bias_a_z, b_query_z, b_value_z, b_out_z, gain_b_z, bias_b_z, b_down_z)
    for i, ref in enumerate(vectors):
        ref[...] = small[1 + i]
    for k in range(b_up_z.shape[0] // width):
        b_up_z[pl.ds(k * width, width)] = small[11 + k]
    up_z[...] = up[...]
    out_z[...] = out[...]
    qkv_z[...] = qkv[...]
    down_z[...] = down[...]
    for j in range(3):
        two_z[j] = two[j].T
    bins = one_z.shape[1]
    turned_one = one[...].T
    for j in range(3):
        one_z[j] = turned_one[j * bins : (j + 1) * bins]


def run_whole(kernel, name, operands, results, scratch):
    held = pl.BlockSpec(memory_space=pltpu.VMEM)
    scalar = pl.BlockSpec(memory_space=pltpu.SMEM)
    return pl.pallas_call(
        kernel,
        in_specs=[scalar if o.dtype == jnp.int32 else held for o in operands],
        out_specs=[held] * len(results),
        out_shape=[jax.ShapeDtypeStruct(*r) for r in results],
        scratch_shapes=[pltpu.VMEM(*s) for s in scratch],
        compiler_params=pltpu.CompilerParams(vmem_limit_bytes=VMEM_LIMIT),
        name=name,
    )(*operands)


def on_device(
    mel_input,
    w_conv1,
    b_conv1,
    w_conv2,
    b_conv2,
    gain_attn,
    bias_attn,
    w_qkv,
    b_query,
    b_value,
    w_out,
    b_out,
    gain_mlp,
    bias_mlp,
    w_up,
    b_up,
    w_down,
    b_down,
    target,
    lengths,
    row_clip,
    language,
):
    clip_count, frame_count, model_width = target.shape
    mel_count = mel_input.shape[2]
    bins = w_conv1.shape[1]
    fast = lax.axis_size("dp") == 8 and lax.axis_size("chan") == 4
    square = (frame_count, model_width)
    (
        taps,
        act_even,
        act_odd,
        slope_even,
        slope_odd,
        slope_two,
        stem,
        normed_a,
        joined,
    ) = run_stem(
        (mel_input, w_conv1, b_conv1, b_conv2, gain_attn, bias_attn, b_query, b_value),
        (w_conv2, jnp.asarray(sinusoids(frame_count, model_width)), w_qkv),
        frame_count,
    )
    context, weights_t, inverse = attend(joined, row_clip, lengths)
    inner = w_up.shape[1]
    deep = (model_width, inner)
    vectors = (b_out, gain_mlp, bias_mlp, b_up, b_down)
    if fast:
        (
            block_rows,
            grad_context,
            grad_middle,
            grad_w_out,
            half_down,
            core_down,
            core_up,
            sums_b,
            grad_b_up,
        ) = run_mlp_send((row_clip, lengths, language), (context, stem, w_out, w_up, w_down, target[0]), vectors)
    else:
        (
            block_rows,
            grad_context,
            grad_middle,
            grad_w_up,
            grad_w_down_t,
            grad_w_out,
            sums_b,
            grad_b_up,
        ) = run_whole(
            mlp_kernel,
            "mlp",
            (
                row_clip,
                lengths,
                language,
                context,
                stem,
                w_out,
                b_out,
                gain_mlp,
                bias_mlp,
                w_up,
                b_up,
                w_down,
                b_down,
                target[0],
            ),
            [
                (square, bf16),
                (square, bf16),
                (square, f32),
                (deep, bf16),
                (deep, bf16),
                ((model_width, model_width), bf16),
                ((8, model_width), f32),
                ((1, inner), f32),
            ],
            [
                (square, f32),
                (square, bf16),
                (square, bf16),
                ((frame_count, inner), bf16),
                ((frame_count, inner), bf16),
                (square, bf16),
                (square, bf16),
                ((1, inner), f32),
            ],
        )
    if fast:
        final_up, down_z, final_out, final_qkv, two_z, one_z, small, grad_mel = run_back(
            (
                joined,
                weights_t,
                inverse,
                grad_context,
                context,
                w_qkv,
                grad_middle,
                stem,
                normed_a,
                gain_attn,
                slope_two,
                w_conv2,
                act_even,
                act_odd,
                slope_even,
                slope_odd,
                w_conv1,
                taps,
                half_down,
                core_down,
                core_up,
                grad_w_out,
                sums_b,
                grad_b_up,
            )
        )
        part = bins // lax.axis_size("chan")
        vector = ((model_width,), f32)
        share = model_width // 4
        block = model_width // 8
        finals = run_whole(
            last_kernel,
            "last",
            (
                lengths,
                language,
                down_z,
                final_up,
                final_out,
                final_qkv,
                two_z,
                one_z,
                small,
                grad_mel,
            ),
            [
                ((GROUPS,), f32),
                (mel_input.shape, bf16),
                ((3, part, block), f32),
                vector,
                ((3, share, block), f32),
                vector,
                vector,
                vector,
                ((block, 3 * share), f32),
                vector,
                vector,
                ((block, share), f32),
                vector,
                vector,
                vector,
                ((block, inner // 4), f32),
                ((inner,), f32),
                ((share, inner // 8), f32),
                vector,
            ],
            [],
        )
        return (block_rows.reshape(target.shape), *finals[:17], finals[17].T, finals[18])
    else:
        *grads, sums_a = attend_back(joined, weights_t, inverse, grad_context, context)
        weight = (model_width, model_width)
        grad_w_qkv, grad_w_two_t, grad_w_one_t, back_mel, sums_c = run_whole(
            stem_back_kernel,
            "stem_back",
            (
                *grads,
                w_qkv,
                grad_middle,
                stem,
                normed_a,
                gain_attn,
                slope_two,
                w_conv2,
                act_even,
                act_odd,
                slope_even,
                slope_odd,
                w_conv1,
                taps,
            ),
            [
                ((model_width, 3 * model_width), bf16),
                ((3,) + weight, bf16),
                ((model_width, 256), bf16),
                ((bins, mel_count), bf16),
                ((8, model_width), f32),
            ],
            [
                ((model_width, frame_count), bf16),
                (square, bf16),
                (square, bf16),
                ((model_width, frame_count), bf16),
                ((model_width, frame_count), bf16),
                (square, bf16),
                (square, bf16),
            ],
        )
        grad_mel = lax.all_to_all(back_mel[:, None], "chan", split_axis=0, concat_axis=1, tiled=True)

        small = jnp.concatenate(
            [
                sums_b[0:1],
                sums_c[3:4],
                sums_c[2:3],
                sums_c[0:2],
                sums_a[0:2],
                sums_b[4:5],
                sums_b[2:4],
                sums_b[1:2],
                grad_b_up.reshape(-1, model_width),
                jnp.zeros((1, model_width), f32),
            ]
        )

        def scatter(values, dp_at, chan_at):
            part = lax.psum_scatter(values, "dp", scatter_dimension=dp_at, tiled=True)
            return lax.psum_scatter(part, "chan", scatter_dimension=chan_at, tiled=True).astype(f32)

        final_down = scatter(grad_w_down_t, 1, 0).T
        final_up = scatter(grad_w_up, 0, 1)
        final_out = scatter(grad_w_out, 0, 1)
        final_qkv = scatter(grad_w_qkv, 0, 1)
        part_two = scatter(grad_w_two_t, 1, 2).transpose(0, 2, 1)
        one_rows = grad_w_one_t[:, : 3 * bins].reshape(-1, 3, bins).transpose(1, 2, 0)
        part_one = scatter(one_rows, 2, 1)
        small = lax.psum(small, ("dp", "chan"))
    totals_all = [small[0, :GROUPS]] + [small[i] for i in range(1, 11)]
    totals_all.insert(10, small[11:15].reshape(-1))
    group_ids = jnp.arange(GROUPS, dtype=jnp.int32)
    member_all = language[:, None] == group_ids[None, :]
    frames_group = jnp.sum(jnp.where(member_all, lengths[:, None], 0), axis=0)
    group_loss = totals_all[0] / (model_width * jnp.maximum(frames_group, 1).astype(f32))
    return (
        block_rows.reshape(target.shape),
        group_loss,
        grad_mel,
        part_one,
        totals_all[1],
        part_two,
        totals_all[2],
        totals_all[3],
        totals_all[4],
        final_qkv,
        totals_all[5],
        totals_all[6],
        final_out,
        totals_all[7],
        totals_all[8],
        totals_all[9],
        final_up,
        totals_all[10],
        final_down,
        totals_all[11],
    )


def solution(mesh):
    whole = P()
    by_row = P(("dp", "chan"), None, None)
    return jax.shard_map(
        on_device,
        mesh=mesh,
        in_specs=(P("chan", "dp", None),) + (whole,) * 17 + (by_row,) + (whole,) * 3,
        out_specs=(
            by_row,
            whole,
            P("chan", "dp", None),
            P(None, "chan", "dp"),
            whole,
            P(None, "chan", "dp"),
            whole,
            whole,
            whole,
            P("dp", "chan"),
            whole,
            whole,
            P("dp", "chan"),
            whole,
            whole,
            whole,
            P("dp", "chan"),
            whole,
            P("dp", "chan"),
            whole,
        ),
        check_vma=False,
    )
```

```python
import math
from types import SimpleNamespace

import jax
import jax.numpy as jnp
import numpy as np
from jax import lax
from jax.experimental import pallas as pl
from jax.experimental.pallas import tpu as pltpu
from jax.sharding import PartitionSpec as P

HEAD_DIM = 64
GROUPS = 99
DP, CHAN = "dp", "chan"

bf16 = jnp.bfloat16
f32 = jnp.float32
epsilon = 1e-05
masked_score = -1e30


def sinusoids(length, channels):
    half_width = channels // 2
    increment = math.log(10000.0) / (half_width - 1)
    inverse = np.exp(-increment * np.arange(half_width, dtype=np.float64))
    angles = np.arange(length, dtype=np.float64)[:, None] * inverse[None, :]
    return np.concatenate([np.sin(angles), np.cos(angles)], axis=1).astype(np.float32)


def lookup(row_id, table):
    matches = row_id == jnp.arange(table.shape[0], dtype=jnp.int32)
    return jnp.sum(jnp.where(matches, table, 0))


def mm(a, b):
    return jnp.dot(a, b, preferred_element_type=f32)


def mm_nt(a, b):
    return lax.dot_general(a, b, (((1,), (1,)), ((), ())), preferred_element_type=f32)


def mm_tn(a, b):
    return lax.dot_general(a, b, (((0,), (0,)), ((), ())), preferred_element_type=f32)


BLOCK = 256
VMEM_LIMIT = 61 * 1024 * 1024


def gelu_pair(v):
    phi = 0.5 + 0.5 * lax.erf(v * math.sqrt(0.5))
    return v * phi, phi + v * (jnp.exp(-0.5 * (v * v)) * (1.0 / math.sqrt(2.0 * math.pi)))


def unrolled(count):
    def run(body):
        for i in range(count):
            body(i)

    return run


def row_of(ref):
    return ref[...].astype(f32).reshape(1, -1)


def own_clip(row_clip_ref):
    return row_clip_ref[lax.axis_index(DP) * lax.axis_size(CHAN) + lax.axis_index(CHAN)]


def turned(values):
    return values.astype(f32).T.astype(bf16)


def chunks(length, size):
    return [slice(at, min(at + size, length)) for at in range(0, length, size)]


def attend_kernel(row_clip_ref, lengths_ref, q_ref, k_ref, v_ref, ctx_ref, et_ref, inv_ref):
    length, width = q_ref.shape[0], 2 * HEAD_DIM
    lane = lax.broadcasted_iota(jnp.int32, (length, width), 1)
    frame = lax.broadcasted_iota(jnp.int32, (length, width), 0)
    bias = jnp.where(frame < lengths_ref[own_clip(row_clip_ref)], 0.0, masked_score)
    for pair in range(q_ref.shape[1] // width):
        cols = slice(pair * width, (pair + 1) * width)
        q = q_ref[:, cols].astype(f32) * HEAD_DIM ** (-0.5)
        k = k_ref[:, cols].astype(f32)
        v_t = turned(v_ref[:, cols])
        for h in range(2):
            mine = lane // HEAD_DIM == h
            spare = lane == HEAD_DIM * (1 - h)
            own_q = jnp.where(mine, q, jnp.where(spare, 1.0, 0.0)).astype(bf16)
            own_k = jnp.where(mine, k, jnp.where(spare, bias, 0.0)).astype(bf16)
            scores = mm_nt(own_k, own_q)
            weight = jnp.exp(scores - jnp.max(scores, axis=0, keepdims=True))
            et_ref[2 * pair + h] = weight.astype(bf16)
            inv_ref[2 * pair + h] = 1.0 / jnp.sum(weight, axis=0, keepdims=True)
        found = [
            mm(v_t[h * HEAD_DIM : (h + 1) * HEAD_DIM], et_ref[2 * pair + h]) * inv_ref[2 * pair + h]
            for h in range(2)
        ]
        ctx_ref[:, cols] = jnp.concatenate(found, axis=0).T.astype(bf16)


def attend_back_kernel(
    q_ref, k_ref, v_ref, et_ref, inv_ref, gctx_ref, ctx_ref, dq_ref, dk_ref, dv_ref, sums_ref, ds_ref
):
    length, width = q_ref.shape
    lane = lax.broadcasted_iota(jnp.int32, (length, width), 1)
    row = lax.broadcasted_iota(jnp.int32, (width, length), 0)
    scale = HEAD_DIM ** (-0.5)
    grad_t = gctx_ref[...].astype(f32).T * jnp.where(row < HEAD_DIM, inv_ref[0], inv_ref[1])
    grad_t = grad_t.astype(bf16).astype(f32)
    grad = grad_t.T
    inner_all = grad_t * ctx_ref[...].astype(f32).T
    k_t = turned(k_ref[...])
    q = q_ref[...].astype(f32) * scale
    v = v_ref[...].astype(f32)
    dq_t = []
    dk = jnp.zeros((length, width), f32)
    dv = jnp.zeros((length, width), f32)
    for h in range(2):
        at = HEAD_DIM * (1 - h)
        mine = lane // HEAD_DIM == h
        inner = jnp.sum(inner_all[h * HEAD_DIM : (h + 1) * HEAD_DIM], axis=0, keepdims=True)
        high = inner.astype(bf16).astype(f32)
        own_grad_t = jnp.where(row // HEAD_DIM == h, grad_t, 0.0)
        own_grad_t = jnp.where(row == at, -high, jnp.where(row == at + 1, high - inner, own_grad_t))
        own_grad_t = own_grad_t.astype(bf16)
        own_v = jnp.where(mine, v, jnp.where((lane == at) | (lane == at + 1), 1.0, 0.0)).astype(bf16)
        own_q = jnp.where(mine, q, 0.0).astype(bf16)
        own_grad = jnp.where(mine, grad, 0.0).astype(bf16)
        for cols in chunks(length, BLOCK):
            shifted = mm(own_v, own_grad_t[:, cols])
            ds_ref[:, cols] = (et_ref[h, :, cols].astype(f32) * shifted).astype(bf16)
        dk += mm(ds_ref[...], own_q)
        dv += mm(et_ref[h], own_grad)
        dq_t.append(mm(k_t[h * HEAD_DIM : (h + 1) * HEAD_DIM], ds_ref[...]))
    dq = (jnp.concatenate(dq_t, axis=0).T * scale).astype(bf16)
    dv = dv.astype(bf16)
    dq_ref[...] = dq
    dk_ref[...] = dk.astype(bf16)
    dv_ref[...] = dv
    sums_ref[0:1] = jnp.sum(dq.astype(f32), axis=0, keepdims=True)
    sums_ref[1:2] = jnp.sum(dv.astype(f32), axis=0, keepdims=True)


def attend(joined, row_clip, lengths):
    length, width = joined.shape[0], 4 * HEAD_DIM
    pairs = joined.shape[1] // (3 * width)
    block = lambda part: pl.BlockSpec((length, width), lambda p, *_: (0, part * pairs + p))
    return pl.pallas_call(
        attend_kernel,
        grid_spec=pltpu.PrefetchScalarGridSpec(
            num_scalar_prefetch=2,
            grid=(pairs,),
            in_specs=[block(0), block(1), block(2)],
            out_specs=[
                block(0),
                pl.BlockSpec((4, length, length), lambda p, *_: (p, 0, 0)),
                pl.BlockSpec((4, 1, length), lambda p, *_: (p, 0, 0)),
            ],
        ),
        out_shape=[
            jax.ShapeDtypeStruct((length, pairs * width), bf16),
            jax.ShapeDtypeStruct((4 * pairs, length, length), bf16),
            jax.ShapeDtypeStruct((4 * pairs, 1, length), f32),
        ],
        compiler_params=pltpu.CompilerParams(vmem_limit_bytes=VMEM_LIMIT),
        name="attend",
    )(row_clip, lengths, joined, joined, joined)


def attend_back(joined, et, inverse, grad_context, context):
    length, width = joined.shape[0], 2 * HEAD_DIM
    pairs = joined.shape[1] // (3 * width)
    block = lambda part: pl.BlockSpec((length, width), lambda p: (0, part * pairs + p))
    one = jax.ShapeDtypeStruct((length, pairs * width), bf16)
    return pl.pallas_call(
        attend_back_kernel,
        grid=(pairs,),
        in_specs=[
            block(0),
            block(1),
            block(2),
            pl.BlockSpec((2, length, length), lambda p: (p, 0, 0)),
            pl.BlockSpec((2, 1, length), lambda p: (p, 0, 0)),
            block(0),
            block(0),
        ],
        out_specs=[block(0), block(0), block(0), pl.BlockSpec((8, width), lambda p: (0, p))],
        out_shape=[one, one, one, jax.ShapeDtypeStruct((8, pairs * width), f32)],
        scratch_shapes=[pltpu.VMEM((length, length), bf16)],
        compiler_params=pltpu.CompilerParams(vmem_limit_bytes=VMEM_LIMIT),
        name="attend_back",
    )(joined, joined, joined, et, inverse, grad_context, context)


def mean_of(values):
    return jnp.mean(values, axis=-1, keepdims=True)


def mlp_body(v, live, spoken, wait, done, tick):
    length, width = v.stem.shape
    inner = v.w_up.shape[1]
    row_steps, wide_steps = length // BLOCK, inner // width
    ones = lambda values: jnp.sum(values, axis=0, keepdims=True)
    v.sums[...] = jnp.zeros_like(v.sums)
    v.b_up_line[...] = row_of(v.b_up)
    wait(0, 3, 1)

    @unrolled(row_steps)
    def _(i):
        rows = pl.ds(i * BLOCK, BLOCK)
        middle = v.stem[rows].astype(f32) + mm(v.ctx[rows], v.w_out[...]) + row_of(v.b_out)
        v.mid[rows] = middle
        centred = middle - mean_of(middle)
        scale = lax.rsqrt(mean_of(centred * centred) + epsilon)
        v.normed[rows] = (centred * scale * row_of(v.gain) + row_of(v.bias)).astype(bf16)

    wait(3, 1, 2)

    @unrolled(wide_steps)
    def _(j):
        cols = pl.ds(j * width, width)
        upward = mm(v.normed[...], v.w_up[:, cols]) + v.b_up_line[:, cols]
        hidden, slope = gelu_pair(upward)
        v.hidden[:, cols] = hidden.astype(bf16)
        v.slope[:, cols] = slope.astype(bf16)

    wait(4, 2, 0)

    @unrolled(row_steps)
    def _(i):
        rows = pl.ds(i * BLOCK, BLOCK)
        final = v.mid[rows] + mm(v.hidden[rows], v.w_down[...]) + row_of(v.b_down)
        v.out[rows] = final.astype(bf16)
        frame = i * BLOCK + lax.broadcasted_iota(jnp.int32, final.shape, 0)
        mismatch = jnp.where(frame < live, final - v.target[rows].astype(f32), 0.0)
        v.gmid[rows] = mismatch
        branch = mismatch.astype(bf16)
        v.branch[rows] = branch
        v.branch_t[:, rows] = turned(branch)
        v.normed_t[:, rows] = turned(v.normed[rows])
        v.sums[5:6] += ones(mismatch * mismatch)
        v.sums[1:2] += ones(branch.astype(f32))

    done("out")
    group = lax.broadcasted_iota(jnp.int32, (1, width), 1)
    loss = 0.5 * jnp.sum(v.sums[5:6], axis=1, keepdims=True)
    v.sums[0:1] = jnp.where(group == spoken, loss, 0.0)

    @unrolled(wide_steps)
    def _(j):
        cols = pl.ds(j * width, width)
        v.put_down(j, cols, mm(v.branch_t[...], v.hidden[:, cols]).astype(bf16))

    tick("down")

    @unrolled(wide_steps)
    def _(j):
        cols = pl.ds(j * width, width)
        grad = mm_nt(v.branch[...], v.w_down[cols]) * v.slope[:, cols].astype(f32)
        grad = grad.astype(bf16)
        v.gb_up[:, cols] = ones(grad.astype(f32))
        v.slope[:, cols] = grad
        v.put_up(j, cols, mm(v.normed_t[...], grad).astype(bf16))
        tick("tiles", j)

    tick("up")

    @unrolled(row_steps)
    def _(i):
        rows = pl.ds(i * BLOCK, BLOCK)
        grad = mm_nt(v.slope[rows], v.w_up[...])
        middle = v.mid[rows]
        centred = middle - mean_of(middle)
        scale = lax.rsqrt(mean_of(centred * centred) + epsilon)
        unit = centred * scale
        gained = grad * row_of(v.gain)
        back = scale * (gained - mean_of(gained) - unit * mean_of(gained * unit))
        grad_middle = v.gmid[rows] + back
        v.gmid[rows] = grad_middle
        attended = grad_middle.astype(bf16)
        v.branch[rows] = attended
        v.gctx[rows] = mm_nt(attended, v.w_out[...]).astype(bf16)
        v.normed_t[:, rows] = turned(v.ctx[rows])
        v.sums[2:3] += ones(grad * unit)
        v.sums[3:4] += ones(grad)
        v.sums[4:5] += ones(attended.astype(f32))
        done("gmid", i)
        done("gctx", i)
        tick("rows", i)

    v.gw_out[...] = mm(v.normed_t[...], v.branch[...]).astype(bf16)
    done("gw_out")
    tick("end")


def own_scalars(row_clip_ref, lengths_ref, language_ref):
    clip = own_clip(row_clip_ref)
    return lengths_ref[clip], language_ref[clip]


def mlp_kernel(row_clip, lengths, language, *refs):
    names = ("ctx", "stem", "w_out", "b_out", "gain", "bias", "w_up", "b_up", "w_down", "b_down", "target")
    names += ("out", "gctx", "gmid", "gw_up", "gw_down", "gw_out", "sums", "gb_up", "mid", "normed", "normed_t")
    names += ("hidden", "slope", "branch", "branch_t", "b_up_line")
    v = SimpleNamespace(**dict(zip(names, refs)))

    def put_down(j, cols, values):
        v.gw_down[:, cols] = values

    def put_up(j, cols, values):
        v.gw_up[:, cols] = values

    v.put_down, v.put_up = put_down, put_up
    nothing = lambda *_: None
    mlp_body(v, *own_scalars(row_clip, lengths, language), nothing, nothing, nothing)


def mlp_send_kernel(row_clip, lengths, language, *refs):
    far_in = ("ctx", "stem", "w_out", "w_up", "w_down", "target")
    far_out = ("out", "gctx", "gmid", "gw_out")
    near = ("b_out", "gain", "bias", "b_up", "b_down")
    names = far_in + near + far_out + ("half_down", "core_down", "core_up", "sums", "gb_up")
    given = SimpleNamespace(**dict(zip(names, refs)))
    held = far_in + far_out + ("mid", "normed", "normed_t", "hidden", "slope", "branch", "branch_t", "b_up_line")
    held += ("gw_up", "gw_blocks", "cin_d", "fin_d", "cin_u")
    rest = refs[len(names) :]
    v = SimpleNamespace(**dict(zip(held, rest)))
    for name in near + ("sums", "gb_up"):
        setattr(v, name, getattr(given, name))
    in_sems, out_sems = rest[len(held) : len(held) + 2]
    sems = SimpleNamespace(**dict(zip(SEMS, rest[len(held) + 2 :])))
    links = Links()
    links.greet([links.by_core, links.by_x, links.by_y])
    loads = [pltpu.make_async_copy(getattr(given, n), getattr(v, n), in_sems.at[i]) for i, n in enumerate(far_in)]
    for copy in loads[:3]:
        copy.start()
    width = v.stem.shape[1]
    part, third, block = given.half_down.shape[3], given.core_up.shape[3], given.core_up.shape[2]
    tasks = {}
    for k in range(3):
        source = lambda d, k=k: v.gw_blocks.at[d, :, pl.ds(k * part, part)]
        tasks[f"d{k}"] = Task(links, k != 0, sems, k, None, source, None, v.cin_d.at[k], v.fin_d.at[k], None, None, None)
    for k in range(3):
        source = rows_of(v.gw_up, block, k * third, third)
        tasks[f"u{k}"] = Task(links, k == 1, sems, 3 + k, None, source, None, v.cin_u.at[k], None, None, None, None)

    def put_down(j, cols, values):
        wide = v.gw_blocks.shape[2]
        for k in range(width // wide):
            v.gw_blocks[j * (width // wide) + k] = values[:, k * wide : (k + 1) * wide]

    def put_up(j, cols, values):
        for k in range(width // BLOCK):
            out = pl.ds((k * 4 + j) * BLOCK, BLOCK)
            v.gw_up[:, out] = values[:, k * BLOCK : (k + 1) * BLOCK]

    v.put_down, v.put_up = put_down, put_up
    leaving = []

    def leave(source, target):
        copy = pltpu.make_async_copy(source, target, out_sems.at[len(leaving)])
        copy.start()
        leaving.append(copy)

    steps = v.stem.shape[0] // BLOCK
    pieces = {"gmid": 8, "gctx": 8 + steps}

    def row_copy(name, i):
        rows = pl.ds(i * BLOCK, BLOCK)
        return pltpu.make_async_copy(getattr(v, name).at[rows], getattr(given, name).at[rows], out_sems.at[pieces[name] + i])

    def wait(first, count, ahead):
        for copy in loads[first : first + count]:
            copy.wait()
        for copy in loads[first + count : first + count + ahead]:
            copy.start()

    def done(name, i=None):
        if i is None:
            leave(getattr(v, name), getattr(given, name))
        else:
            row_copy(name, i).start()

    def tick(place, i=None):
        if place == "down":
            links.met([links.by_core, links.by_x, links.by_y])
            for k in range(3):
                tasks[f"d{k}"].begin()
        elif place == "tiles":
            pl.when(i == 1)(tasks["d0"].after_core)
            pl.when(i == 1)(tasks["d1"].after_core)
            pl.when(i == 3)(tasks["d2"].stop_at_core)
        elif place == "up":
            for k in range(3):
                tasks[f"u{k}"].begin()
            leave(v.cin_d.at[2], given.core_down)
        elif place == "rows":
            pl.when(i == 1)(tasks["u0"].stop_at_core)
            pl.when(i == 2)(tasks["u1"].stop_at_core)
        else:
            tasks["u2"].stop_at_core()
            leave(v.cin_u, given.core_up)
            for k in range(2):
                tasks[f"d{k}"].stop_at_first()
                leave(v.cin_d.at[k, pl.ds(0, 2)], given.half_down.at[k])

    mlp_body(v, *own_scalars(row_clip, lengths, language), wait, done, tick)
    for copy in leaving:
        copy.wait()
    for name in pieces:
        for i in range(steps):
            row_copy(name, i).wait()


def run_mlp_send(scalars, far, near):
    square, deep = far[0].shape, far[3].shape
    width, inner = deep
    block, part, third = width // 8, inner // 24, inner // 3
    in_smem = pl.BlockSpec(memory_space=pltpu.SMEM)
    in_vmem = pl.BlockSpec(memory_space=pltpu.VMEM)
    anywhere = pl.BlockSpec(memory_space=pl.ANY)
    whole = lambda x: pltpu.VMEM(x.shape, x.dtype)
    results = [
        (square, bf16),
        (square, bf16),
        (square, f32),
        ((width, width), bf16),
        ((2, 2, width, part), bf16),
        ((4, width, part), bf16),
        ((3, 4, block, third), bf16),
        ((8, width), f32),
        ((1, inner), f32),
    ]
    return pl.pallas_call(
        mlp_send_kernel,
        in_specs=[in_smem] * 3 + [anywhere] * len(far) + [in_vmem] * len(near),
        out_specs=[anywhere] * 7 + [in_vmem] * 2,
        out_shape=[jax.ShapeDtypeStruct(*r) for r in results],
        scratch_shapes=[whole(x) for x in far]
        + [pltpu.VMEM(*r) for r in results[:4]]
        + [
            pltpu.VMEM(square, f32),
            pltpu.VMEM(square, bf16),
            pltpu.VMEM(square, bf16),
            pltpu.VMEM((square[0], inner), bf16),
            pltpu.VMEM((square[0], inner), bf16),
            pltpu.VMEM(square, bf16),
            pltpu.VMEM(square, bf16),
            pltpu.VMEM((1, inner), f32),
            pltpu.VMEM(deep, bf16),
            pltpu.VMEM((8, width, inner // 8), bf16),
            *bufs_for(3, (width, part), 4, 2),
            *bufs_for(3, (block, third), 4),
            pltpu.SemaphoreType.DMA((len(far),)),
            pltpu.SemaphoreType.DMA((8 + 2 * (square[0] // BLOCK),)),
            *sems_for(6),
        ],
        compiler_params=pltpu.CompilerParams(
            vmem_limit_bytes=VMEM_LIMIT, collective_id=1, has_side_effects=True
        ),
        name="mlp",
    )(*scalars, *far, *near)


def shifted(values, step, axis):
    length = values.shape[axis]
    moved = pltpu.roll(values, step % length, axis)
    place = lax.broadcasted_iota(jnp.int32, values.shape, axis)
    return jnp.where(place == (0 if step > 0 else length - 1), 0.0, moved)


def pick_frames(slots, frames, offset):
    slot = lax.broadcasted_iota(jnp.int32, (slots, frames), 0)
    frame = lax.broadcasted_iota(jnp.int32, (slots, frames), 1)
    return jnp.where(frame == 2 * slot + offset, 1.0, 0.0).astype(bf16)


def flat_taps(ref):
    return ref[...].reshape(-1, ref.shape[-1])


def stem_kernel(*refs):
    near = ("mel", "w_one", "b_one", "b_two", "gain", "bias", "b_query", "b_value")
    far_in = ("w_two", "pos", "w_qkv")
    whole_out = ("taps", "act_even", "act_odd", "slope_even", "slope_odd")
    row_out = ("slope_two", "stem", "normed", "joined")
    far_out = whole_out + row_out
    names = near + far_in + far_out
    given = SimpleNamespace(**dict(zip(names, refs)))
    rest = refs[len(names) :]
    held = far_in + far_out + ("behind", "mel_out", "mel_in")
    v = SimpleNamespace(**dict(zip(held, rest)))
    in_sems, out_sems, send_g, recv_g = rest[len(held) :]
    loads = {}
    for i, name in enumerate(far_in):
        loads[name] = pltpu.make_async_copy(getattr(given, name), getattr(v, name), in_sems.at[i])
        loads[name].start()
    leaving = []

    def leave(source, target):
        copy = pltpu.make_async_copy(source, target, out_sems.at[len(leaving)])
        copy.start()
        leaving.append(copy)

    length, width = v.stem.shape
    steps = length // BLOCK
    links = Links()
    links.greet(links.by_z)
    bins_given = given.mel[...].astype(f32)
    share, tall = bins_given.shape[0], v.mel_out.shape[1]
    empty = jnp.zeros((tall - share, bins_given.shape[2]), f32)
    for z in range(4):
        v.mel_out[z] = jnp.concatenate([bins_given[:, z], empty], axis=0).astype(bf16)
    links.met(links.by_z)
    copies = [
        remote(v.mel_out.at[(links.chan + r) % 4], v.mel_in.at[r - 1], send_g.at[r - 1], recv_g.at[r - 1], links.by_z[r - 1])
        for r in (1, 2, 3)
    ]
    for copy in copies:
        copy.start()
    picks = [pick_frames(BLOCK, 2 * BLOCK, offset) for offset in range(2)]
    for copy in copies:
        copy.wait()
    mel = jnp.concatenate(by_place(links, v.mel_out, v.mel_in, share), axis=0)
    taps = jnp.concatenate([shifted(mel, 1, 1), mel, shifted(mel, -1, 1)], axis=0).astype(bf16)
    v.taps[...] = taps
    leave(v.taps, given.taps)
    w_one = flat_taps(given.w_one)
    for pick, act_ref, slope_ref in (
        (picks[1], v.act_odd, v.slope_odd),
        (picks[0], v.act_even, v.slope_even),
    ):
        for i in range(steps):
            rows = slice(i * BLOCK, (i + 1) * BLOCK)
            frames = slice(2 * i * BLOCK, 2 * (i + 1) * BLOCK)
            picked = mm_nt(pick, taps[:, frames]).astype(bf16)
            act, slope = gelu_pair(mm(picked, w_one) + row_of(given.b_one))
            act_ref[rows] = act.astype(bf16)
            slope_ref[rows] = slope.astype(bf16)
    for name in whole_out[1:]:
        leave(getattr(v, name), getattr(given, name))
    for cols in chunks(width, BLOCK):
        v.behind[:, cols] = shifted(v.act_odd[:, cols].astype(f32), 1, 0).astype(bf16)
    for name in far_in:
        loads[name].wait()
    query, key, value = (slice(part * width, (part + 1) * width) for part in range(3))
    for i in range(steps):
        rows = slice(i * BLOCK, (i + 1) * BLOCK)
        two = (
            mm(v.behind[rows], v.w_two[0])
            + mm(v.act_even[rows], v.w_two[1])
            + mm(v.act_odd[rows], v.w_two[2])
            + row_of(given.b_two)
        )
        act, slope = gelu_pair(two)
        v.slope_two[rows] = slope.astype(bf16)
        stem = (act + v.pos[rows]).astype(bf16)
        v.stem[rows] = stem
        stem = stem.astype(f32)
        centred = stem - mean_of(stem)
        scale = lax.rsqrt(mean_of(centred * centred) + epsilon)
        normed = (centred * scale * row_of(given.gain) + row_of(given.bias)).astype(bf16)
        v.normed[rows] = normed
        v.joined[rows, query] = (mm(normed, v.w_qkv[:, query]) + row_of(given.b_query)).astype(bf16)
        v.joined[rows, key] = mm(normed, v.w_qkv[:, key]).astype(bf16)
        v.joined[rows, value] = (mm(normed, v.w_qkv[:, value]) + row_of(given.b_value)).astype(bf16)
        for name in row_out:
            leave(getattr(v, name).at[pl.ds(i * BLOCK, BLOCK)], getattr(given, name).at[pl.ds(i * BLOCK, BLOCK)])
    for copy in leaving:
        copy.wait()


def run_stem(near, far, length):
    width, frames = near[1].shape[2], near[0].shape[2]
    square = (length, width)
    results = [(3 * near[1].shape[1], frames)] + [square] * 7 + [(length, 3 * width)]
    in_vmem = pl.BlockSpec(memory_space=pltpu.VMEM)
    anywhere = pl.BlockSpec(memory_space=pl.ANY)
    return pl.pallas_call(
        stem_kernel,
        in_specs=[in_vmem] * len(near) + [anywhere] * len(far),
        out_specs=[anywhere] * len(results),
        out_shape=[jax.ShapeDtypeStruct(r, bf16) for r in results],
        scratch_shapes=[pltpu.VMEM(x.shape, x.dtype) for x in far]
        + [pltpu.VMEM(r, bf16) for r in results]
        + [
            pltpu.VMEM(square, bf16),
            pltpu.VMEM((4, 32, frames), bf16),
            pltpu.VMEM((3, 32, frames), bf16),
            pltpu.SemaphoreType.DMA((len(far),)),
            pltpu.SemaphoreType.DMA((5 + 4 * (length // BLOCK),)),
            pltpu.SemaphoreType.DMA((3,)),
            pltpu.SemaphoreType.DMA((3,)),
        ],
        compiler_params=pltpu.CompilerParams(
            vmem_limit_bytes=VMEM_LIMIT, collective_id=3, has_side_effects=True
        ),
        name="stem",
    )(*near, *far)


def stem_back_kernel(
    gq_ref,
    gk_ref,
    gv_ref,
    w_qkv_ref,
    gmid_ref,
    stem_ref,
    normed_ref,
    gain_ref,
    slope_two_ref,
    w_two_ref,
    act_even_ref,
    act_odd_ref,
    slope_even_ref,
    slope_odd_ref,
    w_one_ref,
    taps_ref,
    gw_qkv_ref,
    gw_two_ref,
    gw_one_ref,
    gmel_ref,
    sums_ref,
    normed_t_ref,
    two_ref,
    two_ahead_ref,
    two_t_ref,
    two_ahead_t_ref,
    even_ref,
    odd_ref,
):
    length, width = stem_ref.shape
    steps = length // BLOCK
    ones = lambda v: jnp.sum(v, axis=0, keepdims=True)
    sums_ref[...] = jnp.zeros_like(sums_ref)

    @pl.loop(0, steps)
    def _(i):
        rows = pl.ds(pl.multiple_of(i * BLOCK, BLOCK), BLOCK)
        normed_t_ref[:, rows] = turned(normed_ref[rows])
        grad = (
            mm_nt(gq_ref[rows], w_qkv_ref[:, 0:width])
            + mm_nt(gk_ref[rows], w_qkv_ref[:, width : 2 * width])
            + mm_nt(gv_ref[rows], w_qkv_ref[:, 2 * width : 3 * width])
        )
        stem = stem_ref[rows].astype(f32)
        centred = stem - mean_of(stem)
        scale = lax.rsqrt(mean_of(centred * centred) + epsilon)
        unit = centred * scale
        gained = grad * row_of(gain_ref)
        back = scale * (gained - mean_of(gained) - unit * mean_of(gained * unit))
        grad_stem = (gmid_ref[rows] + back).astype(bf16).astype(f32)
        two = (grad_stem * slope_two_ref[rows].astype(f32)).astype(bf16)
        two_ref[rows] = two
        two_t_ref[:, rows] = turned(two)
        sums_ref[0:1] += ones(grad * unit)
        sums_ref[1:2] += ones(grad)
        sums_ref[2:3] += ones(two.astype(f32))

    for cols in chunks(width, BLOCK):
        two_ahead_ref[:, cols] = shifted(two_ref[:, cols].astype(f32), -1, 0).astype(bf16)

    @pl.loop(0, steps)
    def _(i):
        rows = pl.ds(pl.multiple_of(i * BLOCK, BLOCK), BLOCK)
        two_ahead_t_ref[:, rows] = turned(two_ahead_ref[rows])
        even = mm_nt(two_ref[rows], w_two_ref[1]) * slope_even_ref[rows].astype(f32)
        odd = mm_nt(two_ref[rows], w_two_ref[2]) + mm_nt(two_ahead_ref[rows], w_two_ref[0])
        odd = odd * slope_odd_ref[rows].astype(f32)
        even_ref[rows] = even.astype(bf16)
        odd_ref[rows] = odd.astype(bf16)
        sums_ref[3:4] += ones(even.astype(bf16).astype(f32)) + ones(odd.astype(bf16).astype(f32))

    @pl.loop(0, width // BLOCK)
    def _(j):
        cols = pl.ds(pl.multiple_of(j * BLOCK, BLOCK), BLOCK)
        for part, grad_ref in enumerate((gq_ref, gk_ref, gv_ref)):
            out = pl.ds(pl.multiple_of(part * width + j * BLOCK, BLOCK), BLOCK)
            gw_qkv_ref[:, out] = mm(normed_t_ref[...], grad_ref[:, cols]).astype(bf16)
        gw_two_ref[0, :, cols] = mm(two_ahead_t_ref[...], act_odd_ref[:, cols]).astype(bf16)
        gw_two_ref[1, :, cols] = mm(two_t_ref[...], act_even_ref[:, cols]).astype(bf16)
        gw_two_ref[2, :, cols] = mm(two_t_ref[...], act_odd_ref[:, cols]).astype(bf16)

    bins = w_one_ref.shape[1]
    gw_one = jnp.zeros((3 * bins, width), f32)
    for offset, grad_ref in ((0, even_ref), (1, odd_ref)):
        picked = [
            mm_nt(taps_ref[:, 2 * i * BLOCK : 2 * (i + 1) * BLOCK], pick_frames(BLOCK, 2 * BLOCK, offset))
            for i in range(steps)
        ]
        gw_one += mm(jnp.concatenate(picked, axis=1).astype(bf16), grad_ref[...])
    gw_one_ref[...] = jnp.zeros_like(gw_one_ref)
    gw_one_ref[:, 0 : 3 * bins] = gw_one.T.astype(bf16)
    even, odd = even_ref[...], odd_ref[...]
    mel_even = (
        mm_nt(odd, w_one_ref[0])
        + mm_nt(even, w_one_ref[1])
        + shifted(mm_nt(odd, w_one_ref[2]), 1, 0)
    )
    mel_odd = (
        shifted(mm_nt(even, w_one_ref[0]), -1, 0)
        + mm_nt(odd, w_one_ref[1])
        + mm_nt(even, w_one_ref[2])
    )
    mel_even, mel_odd = turned(mel_even), turned(mel_odd)
    for i in range(steps):
        cols = slice(i * BLOCK, (i + 1) * BLOCK)
        frames = slice(2 * i * BLOCK, 2 * (i + 1) * BLOCK)
        gmel_ref[:, frames] = (
            mm(mel_even[:, cols], pick_frames(BLOCK, 2 * BLOCK, 0))
            + mm(mel_odd[:, cols], pick_frames(BLOCK, 2 * BLOCK, 1))
        ).astype(bf16)


MESH = pl.DeviceIdType.MESH


def remote(source, target, send, recv, to):
    return pltpu.make_async_remote_copy(source, target, send, recv, device_id=to, device_id_type=MESH)


class Links:
    def __init__(self):
        dp, chan = lax.axis_index(DP), lax.axis_index(CHAN)
        self.chan = chan
        self.core, self.x, self.y = dp % 2, (dp // 2) % 2, dp // 4
        self.by_core = (self.dest(0, 0, 1), chan)
        self.by_x = (self.dest(0, 1, 0), chan)
        self.by_y = (self.dest(1, 0, 0), chan)
        self.by_z = [(dp, (chan + r) % 4) for r in (1, 2, 3)]
        self.by_next = (dp, chan + 1 - 2 * (chan % 2))
        self.by_far = (dp, (chan + 2) % 4)
        self.partners = [self.by_core, self.by_x, self.by_y] + self.by_z

    def dest(self, dy, dx, dc):
        flip = lambda bit, turn: 1 - bit if turn else bit
        return 4 * flip(self.y, dy) + 2 * flip(self.x, dx) + flip(self.core, dc)

    def greet(self, partners):
        for partner in partners:
            pl.semaphore_signal(pltpu.get_barrier_semaphore(), inc=1, device_id=partner, device_id_type=MESH)

    def met(self, partners):
        pl.semaphore_wait(pltpu.get_barrier_semaphore(), len(partners))


def by_place(links, out_ref, in_ref, share):
    parts = [out_ref[links.chan], in_ref[0], in_ref[1], in_ref[2]]
    parts = [part.astype(f32)[0:share] for part in parts]
    placed = []
    for z in range(4):
        value = parts[0]
        for r in (1, 2, 3):
            value = jnp.where((links.chan + 4 - r) % 4 == z, parts[r], value)
        placed.append(value)
    return placed


class Task:
    def __init__(self, links, x_first, sems, n, cut, source, own, cin, fin, sin, z_out, z_in, stage=0):
        self.links, self.x_first, self.sems, self.n, self.cut = links, x_first, sems, n, cut
        self.source, self.own, self.cin, self.fin, self.sin = source, own, cin, fin, sin
        self.z_out, self.z_in, self.stage = z_out, z_in, stage
        self.ways = (links.by_x, links.by_y) if x_first else (links.by_y, links.by_x)

    def dest(self, slot, dc):
        dx, dy = (slot // 2, slot % 2) if self.x_first else (slot % 2, slot // 2)
        return self.links.dest(dy, dx, dc)

    def begin(self):
        if self.stage == 0:
            for slot in (3, 2, 1, 0):
                source = self.source(self.dest(slot, 1))
                remote(source, self.cin.at[slot], self.sems.send_c.at[self.n], self.sems.recv_c.at[self.n], self.links.by_core).start()
                if self.own is not None:
                    source = self.source(self.dest(slot, 0))
                    pltpu.make_async_copy(source, self.own.at[slot], self.sems.load.at[self.n]).start()
            return
        if self.stage == 1:
            for slot in (3, 2):
                self.to_first(self.source.at[slot], slot)
        else:
            self.to_second(self.source.at[1])
        held = self.own.shape[0]
        pltpu.make_async_copy(self.source.at[pl.ds(0, held)], self.own, self.sems.load.at[self.n]).start()

    def to_first(self, ref, slot):
        remote(ref, self.fin.at[slot - 2], self.sems.send_f.at[self.n], self.sems.recv_f.at[self.n], self.ways[0]).start()

    def to_second(self, ref):
        remote(ref, self.sin, self.sems.send_s.at[self.n], self.sems.recv_s.at[self.n], self.ways[1]).start()

    def loaded(self, stage):
        if self.own is not None and self.stage == stage:
            pltpu.make_async_copy(self.own, self.own, self.sems.load.at[self.n]).wait()

    def wait(self, ref, send, recv, to):
        remote(ref, ref, send.at[self.n], recv.at[self.n], to).wait()

    def held(self, slot):
        if self.stage:
            return self.own[slot].astype(f32)
        own = self.own[slot] if self.own is not None else self.source(self.dest(slot, 0))[...]
        return own.astype(f32) + self.cin[slot].astype(f32)

    def core_done(self):
        self.loaded(0)
        self.wait(self.cin, self.sems.send_c, self.sems.recv_c, self.links.by_core)

    def after_core(self):
        self.core_done()
        for slot in (3, 2):
            self.cin[slot] = self.held(slot).astype(bf16)
            self.to_first(self.cin.at[slot], slot)

    def stop_at_core(self):
        self.core_done()
        for slot in (3, 2, 1, 0):
            self.cin[slot] = self.held(slot).astype(bf16)

    def stop_at_first(self):
        self.wait(self.fin, self.sems.send_f, self.sems.recv_f, self.ways[0])
        for slot in (1, 0):
            self.cin[slot] = (self.held(slot) + self.fin[slot].astype(f32)).astype(bf16)

    def after_first(self):
        self.loaded(1)
        self.wait(self.fin, self.sems.send_f, self.sems.recv_f, self.ways[0])
        leaving = self.own if self.stage else self.cin
        leaving[1] = (self.held(1) + self.fin[1].astype(f32)).astype(bf16)
        self.to_second(leaving.at[1])

    def z_copies(self):
        theirs = 1 - self.links.chan % 2
        sems = self.sems.send_z.at[self.n], self.sems.recv_z.at[self.n]
        return [remote(self.z_out.at[2 * a + theirs], self.z_in.at[a], *sems, self.links.by_next) for a in range(2)]

    def after_second(self):
        self.loaded(2)
        self.wait(self.sin, self.sems.send_s, self.sems.recv_s, self.ways[1])
        total = self.held(0) + self.sin[...].astype(f32)
        if self.stage < 2:
            total = total + self.fin[0].astype(f32)
        for z in range(4):
            self.z_out[z] = self.cut(total, z).astype(bf16)
        for copy in self.z_copies():
            copy.start()

    def after_third(self):
        chan = self.links.chan
        self.wait(self.z_in.at[pl.ds(0, 2)], self.sems.send_z, self.sems.recv_z, self.links.by_next)
        far = (chan + 2) % 4
        self.z_out[far] = (self.z_out[far].astype(f32) + self.z_in[far // 2].astype(f32)).astype(bf16)
        remote(self.z_out.at[far], self.z_in.at[2], self.sems.send_w.at[self.n], self.sems.recv_w.at[self.n], self.links.by_far).start()

    def finish(self):
        chan = self.links.chan
        self.wait(self.z_in.at[2], self.sems.send_w, self.sems.recv_w, self.links.by_far)
        return self.z_out[chan].astype(f32) + self.z_in[chan // 2].astype(f32) + self.z_in[2].astype(f32)


def cut_rows(block, z):
    share = block.shape[0] // 4
    return block[z * share : (z + 1) * share]


def cut_columns(block, z):
    share = block.shape[1] // 4
    first = z * share // 128 * 128
    taken = block[:, first : first + (share + 127) // 128 * 128]
    skip = z * share - first
    return pltpu.roll(taken, taken.shape[1] - skip, 1) if skip else taken


def cut_half_tiles(block, z):
    taken = block[:, z // 2 * 128 : (z // 2 + 1) * 128]
    return pltpu.roll(taken, 64, 1) if z % 2 else taken


SEMS = ("send_c", "recv_c", "load", "send_f", "recv_f", "send_s", "recv_s", "send_z", "recv_z", "send_w", "recv_w")


def sems_for(count):
    return [pltpu.SemaphoreType.DMA((count,)) for _ in SEMS]


def bufs_for(count, shape, *slots):
    return [pltpu.VMEM((count,) + ((slot,) if slot else ()) + shape, bf16) for slot in slots]


def rows_of(ref, block, start, count):
    return lambda d: ref.at[pl.ds(pl.multiple_of(d * block, block), block), pl.ds(start, count)]


def pair_back(p, q_ref, k_ref, v_ref, et_of, inverse_ref, gctx_ref, ctx_ref, dq_ref, dk_ref, dv_ref, sums_ref, ds_ref, between):
    length, width = q_ref.shape[0], 2 * HEAD_DIM
    cols = pl.ds(pl.multiple_of(p * width, width), width)
    lane = lax.broadcasted_iota(jnp.int32, (length, width), 1)
    row = lax.broadcasted_iota(jnp.int32, (width, length), 0)
    scale = HEAD_DIM ** (-0.5)
    grad_t = gctx_ref[:, cols].astype(f32).T
    grad_t = grad_t * jnp.where(row < HEAD_DIM, inverse_ref[2 * p], inverse_ref[2 * p + 1])
    grad_t = grad_t.astype(bf16).astype(f32)
    grad = grad_t.T
    inner_all = grad_t * ctx_ref[:, cols].astype(f32).T
    k_t = turned(k_ref[:, cols])
    q = q_ref[:, cols].astype(f32) * scale
    v = v_ref[:, cols].astype(f32)
    dq_t = []
    dk = jnp.zeros((length, width), f32)
    dv = jnp.zeros((length, width), f32)
    for h in range(2):
        at = HEAD_DIM * (1 - h)
        mine = lane // HEAD_DIM == h
        inner = jnp.sum(inner_all[h * HEAD_DIM : (h + 1) * HEAD_DIM], axis=0, keepdims=True)
        high = inner.astype(bf16).astype(f32)
        own_grad_t = jnp.where(row // HEAD_DIM == h, grad_t, 0.0)
        own_grad_t = jnp.where(row == at, -high, jnp.where(row == at + 1, high - inner, own_grad_t))
        own_grad_t = own_grad_t.astype(bf16)
        own_v = jnp.where(mine, v, jnp.where((lane == at) | (lane == at + 1), 1.0, 0.0)).astype(bf16)
        own_q = jnp.where(mine, q, 0.0).astype(bf16)
        own_grad = jnp.where(mine, grad, 0.0).astype(bf16)
        et_ref = et_of(h)
        ds_ref[...] = (et_ref[...].astype(f32) * mm(own_v, own_grad_t)).astype(bf16)
        dk += mm(ds_ref[...], own_q)
        dv += mm(et_ref[...], own_grad)
        dq_t.append(mm(k_t[h * HEAD_DIM : (h + 1) * HEAD_DIM], ds_ref[...]))
        if h == 0:
            between()
    dq = (jnp.concatenate(dq_t, axis=0).T * scale).astype(bf16)
    dv = dv.astype(bf16)
    dq_ref[:, cols] = dq
    dk_ref[:, cols] = dk.astype(bf16)
    dv_ref[:, cols] = dv
    sums_ref[0:1, cols] = jnp.sum(dq.astype(f32), axis=0, keepdims=True)
    sums_ref[1:2, cols] = jnp.sum(dv.astype(f32), axis=0, keepdims=True)


STEPS = ("begin", "after_core", "after_first", "after_second", "after_third", "finish")
TASKS = ("d0", "d1", "d2", "u0", "u1", "u2", "o", "q0", "q1", "q2", "t0", "t1", "t2", "t3", "t4", "t5", "n", "m")
SCHEDULE = {
    "middle": (
        (0, 1, 6),
        (2, 4, 0),
        (4, 5, 1),
        (5, 2, 4),
        (5, 2, 5),
    ),
    "pairs": (
        (0, 3, 0),
        (0, 3, 1),
        (2, 2, 2),
        (2, 4, 1),
        (2, 2, 3),
        (3, 5, 0),
    ),
    "turn": (
        (0, 3, 2),
    ),
    "qkv": (
        (1, 2, 6),
    ),
    "rows": (
        (0, 4, 2),
        (0, 3, 4),
        (0, 3, 3),
        (1, 1, 7),
        (2, 3, 6),
        (2, 3, 5),
        (2, 1, 8),
        (2, 1, 9),
    ),
    "ahead": (
        (0, 5, 2),
        (0, 4, 4),
    ),
    "two": (
        (1, 4, 3),
    ),
    "convs": (
        (0, 4, 6),
        (1, 2, 7),
        (1, 1, 10),
        (1, 4, 5),
        (1, 1, 11),
        (1, 5, 4),
        (1, 1, 12),
        (2, 2, 8),
        (2, 1, 13),
        (2, 1, 14),
        (2, 1, 15),
        (2, 5, 3),
    ),
    "one": (
        (0, 2, 9),
        (0, 1, 17),
        (0, 3, 7),
        (0, 5, 6),
    ),
    "mel": (
        (0, 2, 11),
        (0, 1, 16),
        (0, 5, 5),
        (0, 2, 10),
    ),
    "tail": (
        (0, 3, 8),
        (0, 4, 7),
        (0, 2, 12),
        (0, 2, 13),
        (0, 2, 14),
        (0, 4, 8),
        (0, 2, 15),
        (0, 3, 9),
        (0, 5, 7),
        (0, 2, 17),
        (0, 2, 16),
        (0, 3, 11),
        (0, 3, 10),
        (0, 3, 13),
        (0, 3, 12),
        (0, 4, 9),
        (0, 5, 8),
        (0, 3, 15),
        (0, 3, 14),
        (0, 4, 11),
        (0, 3, 16),
        (0, 3, 17),
        (0, 4, 10),
        (0, 4, 13),
        (0, 4, 12),
        (0, 4, 15),
        (0, 5, 9),
        (0, 4, 14),
        (0, 5, 11),
        (0, 4, 16),
        (0, 5, 10),
        (0, 4, 17),
        (0, 5, 13),
        (0, 5, 12),
        (0, 5, 15),
        (0, 5, 14),
        (0, 5, 16),
        (0, 5, 17),
    ),
}


def back_kernel(*refs):
    joined, et, inverse, gctx, ctx, w_qkv, gmid, stem, normed, gain_ref, slope_two = refs[:11]
    w_two, act_even, act_odd, slope_even, slope_odd, w_one_ref, taps_ref = refs[11:18]
    half_down, core_down, core_up, gw_out, sums_b_ref, gb_up_ref = refs[18:24]
    up_z, down_z, out_z, qkv_z, two_z, one_z, small_z, gmel_z = refs[24:32]
    pool, d_ref, w_qkv_v, gmid_v, stem_v, normed_v, slope_two_v, w_two_v, gw_qkv = refs[32:41]
    gw_one, sums_a_ref, sums_ref = refs[41:44]
    rest = list(refs[44:])
    take = lambda count: [rest.pop(0) for _ in range(count)]
    own_h, sin_h, zo_h, zi_h = take(4)
    own_c, fin_c, sin_c, zo_c, zi_c = take(5)
    own_u, fin_u, sin_u, zo_u, zi_u = take(5)
    own_o, cin_o, fin_o, sin_o, zo_o, zi_o = take(6)
    bufs_q, bufs_t, bufs_n = take(5), take(5), take(5)
    small_buf, small_in, gmel_out, gmel_in = take(4)
    sems = SimpleNamespace(**dict(zip(SEMS, take(len(SEMS)))))
    loads, et_loads, send_m, recv_m, send_g, recv_g = rest
    length, width = ctx.shape
    steps, pairs, block = length // BLOCK, width // (2 * HEAD_DIM), width // 8
    bins = w_one_ref.shape[1]
    links = Links()
    links.greet(links.partners)

    q_v, k_v, v_v = (pool.at[i] for i in range(3))
    ctx_v, gctx_v, ds_v = pool.at[7], pool.at[8], pool.at[9]
    started = []

    def later(source, target):
        copy = pltpu.make_async_copy(source, target, loads.at[len(started)])
        started.append(copy)
        return copy

    def load(source, target):
        copy = later(source, target)
        copy.start()
        return copy

    def et_load(head, slot):
        return pltpu.make_async_copy(et.at[head], pool.at[3 + slot], et_loads.at[slot])

    first = [load(joined.at[:, pl.ds(i * width, width)], pool.at[i]) for i in range(3)]
    first += [load(gctx, gctx_v), load(ctx, ctx_v)]
    for head in range(2):
        et_load(head, head).start()

    tasks = {}

    def add(name, x_first, cut, source, own, cin, fin, sin, z_out, z_in, stage=0):
        tasks[name] = Task(
            links, x_first, sems, len(tasks), cut, source, own, cin, fin, sin, z_out, z_in, stage
        )

    at = lambda k, *bufs: [ref.at[k] for ref in bufs]
    part, third, rest_rows, half = core_down.shape[2], core_up.shape[3], block // 3, block // 2
    for k in range(2):
        own, sin, z_out, z_in = at(k, own_h, sin_h, zo_h, zi_h)
        add(f"d{k}", k != 0, cut_rows, half_down.at[k], own, None, None, sin, z_out, z_in, 2)
    own, *bufs = at(0, own_c, fin_c, sin_c, zo_c, zi_c)
    add("d2", True, cut_rows, core_down, own, None, *bufs, 1)
    for k in range(3):
        own, *bufs = at(k, own_u, fin_u, sin_u, zo_u, zi_u)
        add(f"u{k}", k == 1, cut_columns, core_up.at[k], own, None, *bufs, 1)
    own, *bufs = at(0, own_o, cin_o, fin_o, sin_o, zo_o, zi_o)
    add("o", True, cut_columns, rows_of(gw_out, block, 0, width), own, *bufs)
    for k in range(3):
        source = lambda d, k=k: gw_qkv.at[pl.ds(pl.multiple_of(d * block + k * rest_rows, rest_rows), rest_rows)]
        add(f"q{k}", k == 1, cut_columns, source, None, *at(k, *bufs_q))
    for k in range(6):
        source = lambda d, k=k: pool.at[7 + k // 2, pl.ds(pl.multiple_of(d * block + k % 2 * half, half), half)]
        add(f"t{k}", k % 2 == 0, cut_columns, source, None, *at(k, *bufs_t))
    add("n", False, cut_half_tiles, rows_of(gw_one, block, 0, gw_one.shape[1]), None, *at(0, *bufs_n))
    quarter = width // 4

    def store(name):
        total = tasks[name].finish()
        k = int(name[1:] or 0)
        if name[0] == "d":
            down_z[:, k * part : (k + 1) * part] = total
        elif name[0] == "u":
            up_z[:, k * third // 4 : (k + 1) * third // 4] = total
        elif name == "o":
            out_z[...] = total[:, 0:quarter]
        elif name[0] == "q":
            qkv_z[k * rest_rows : (k + 1) * rest_rows] = total[:, 0 : 3 * quarter]
        elif name[0] == "t":
            two_z[k // 2, k % 2 * half : (k % 2 + 1) * half] = total[:, 0:quarter]
        else:
            one_z[...] = total

    small_ways = [links.by_core, links.by_x, links.by_y, links.by_next, links.by_far]

    def small_step(step):
        i = STEPS.index(step)
        if i == 0:
            small_buf[0, 0:1] = sums_b_ref[0:1]
            small_buf[0, 1:2] = sums_ref[3:4]
            small_buf[0, 2:3] = sums_ref[2:3]
            small_buf[0, 3:5] = sums_ref[0:2]
            small_buf[0, 5:7] = sums_a_ref[0:2]
            small_buf[0, 7:8] = sums_b_ref[4:5]
            small_buf[0, 8:10] = sums_b_ref[2:4]
            small_buf[0, 10:11] = sums_b_ref[1:2]
            for k in range(4):
                small_buf[0, 11 + k : 12 + k] = gb_up_ref[:, k * width : (k + 1) * width]
            small_buf[0, 15:16] = jnp.zeros((1, width), f32)
        else:
            got = small_in.at[i - 1]
            remote(got, got, send_m.at[i - 1], recv_m.at[i - 1], small_ways[i - 1]).wait()
            total = small_buf[i - 1] + small_in[i - 1]
            if i == 5:
                small_z[...] = total
                return
            small_buf[i] = total
        remote(small_buf.at[i], small_in.at[i], send_m.at[i], recv_m.at[i], small_ways[i]).start()

    def run(step, *names):
        for name in names:
            if name == "m":
                small_step(step)
            elif step == STEPS[5]:
                store(name)
            else:
                getattr(tasks[name], step)()

    def ticks(place, at=None):
        for index, step, task in SCHEDULE.get(place, ()):
            work = lambda step=step, task=task: run(STEPS[step], TASKS[task])
            if at is None or isinstance(at, int):
                if at in (None, index):
                    work()
            else:
                pl.when(at == index)(work)

    links.met(links.partners)
    run(STEPS[0], "d0", "d1", "d2", "u0", "u1", "u2", "o")
    late = [
        later(normed, normed_v),
        later(w_qkv, w_qkv_v),
        later(gmid, gmid_v),
        later(stem, stem_v),
        later(slope_two, slope_two_v),
        later(w_two, w_two_v),
    ]
    for copy in first:
        copy.wait()
    for head in range(2, 4):
        et_load(head, head).start()

    @pl.loop(0, pairs)
    def _(p):
        for h in range(2):
            et_load(2 * p + h, (2 * p + h) % 4).wait()
        pair_back(
            p,
            q_v,
            k_v,
            v_v,
            lambda h: pool.at[3 + (2 * p + h) % 4],
            inverse,
            gctx_v,
            ctx_v,
            d_ref.at[0],
            d_ref.at[1],
            d_ref.at[2],
            sums_a_ref,
            ds_v,
            lambda: ticks("middle", p),
        )

        @pl.when(p == 0)
        def _():
            for copy in late:
                copy.start()

        @pl.when(p + 2 < pairs)
        def _():
            for h in range(2):
                et_load(2 * p + 4 + h, (2 * p + h) % 4).start()

        ticks("pairs", p)

    acts = [load(act_even, pool.at[5]), load(act_odd, pool.at[6])]
    for copy in late:
        copy.wait()
    ones = lambda v: jnp.sum(v, axis=0, keepdims=True)
    normed_t, two_v, two_ahead, two_t, two_ahead_t = (pool.at[i] for i in range(5))
    act_v = [pool.at[5], pool.at[6]]
    even_v, odd_v = pool.at[0], pool.at[5]
    gw_two = [pool.at[7 + k] for k in range(3)]
    sums_ref[...] = jnp.zeros_like(sums_ref)

    @unrolled(steps)
    def _(i):
        rows = pl.ds(i * BLOCK, BLOCK)
        normed_t[:, rows] = turned(normed_v[rows])

    ticks("turn")

    @unrolled(3)
    def _(j):
        cols = pl.ds(j * width, width)
        gw_qkv[:, cols] = mm(normed_t[...], d_ref[j]).astype(bf16)
        ticks("qkv", j)

    run(STEPS[0], "q0", "q1", "q2")

    @unrolled(steps)
    def _(i):
        rows = pl.ds(i * BLOCK, BLOCK)
        grad = (
            mm_nt(d_ref[0, rows], w_qkv_v[:, 0:width])
            + mm_nt(d_ref[1, rows], w_qkv_v[:, width : 2 * width])
            + mm_nt(d_ref[2, rows], w_qkv_v[:, 2 * width : 3 * width])
        )
        stem = stem_v[rows].astype(f32)
        centred = stem - mean_of(stem)
        scale = lax.rsqrt(mean_of(centred * centred) + epsilon)
        unit = centred * scale
        gained = grad * row_of(gain_ref)
        back = scale * (gained - mean_of(gained) - unit * mean_of(gained * unit))
        grad_stem = (gmid_v[rows] + back).astype(bf16).astype(f32)
        two = (grad_stem * slope_two_v[rows].astype(f32)).astype(bf16)
        two_v[rows] = two
        two_t[:, rows] = turned(two)
        sums_ref[0:1] += ones(grad * unit)
        sums_ref[1:2] += ones(grad)
        sums_ref[2:3] += ones(two.astype(f32))
        ticks("rows", i)

    slope_v = d_ref
    for copy in acts:
        copy.wait()
    slopes = [load(slope_even, slope_v.at[0]), load(slope_odd, slope_v.at[1])]
    for cols in chunks(width, BLOCK):
        two_ahead[:, cols] = shifted(two_v[:, cols].astype(f32), -1, 0).astype(bf16)

    @unrolled(steps)
    def _(i):
        rows = pl.ds(i * BLOCK, BLOCK)
        two_ahead_t[:, rows] = turned(two_ahead[rows])

    ticks("ahead")

    gw_two[0][...] = mm(two_ahead_t[...], act_v[1][...]).astype(bf16)
    ticks("two", 0)
    gw_two[1][...] = mm(two_t[...], act_v[0][...]).astype(bf16)
    ticks("two", 1)
    gw_two[2][...] = mm(two_t[...], act_v[1][...]).astype(bf16)

    run(STEPS[0], "t0", "t1", "t2", "t3", "t4", "t5")
    for copy in slopes:
        copy.wait()

    @unrolled(steps)
    def _(i):
        rows = pl.ds(i * BLOCK, BLOCK)
        even = mm_nt(two_v[rows], w_two_v[1]) * slope_v[0, rows].astype(f32)
        odd = mm_nt(two_v[rows], w_two_v[2]) + mm_nt(two_ahead[rows], w_two_v[0])
        odd = odd * slope_v[1, rows].astype(f32)
        even, odd = even.astype(bf16), odd.astype(bf16)
        even_v[rows] = even
        odd_v[rows] = odd
        sums_ref[3:4] += ones(even.astype(f32)) + ones(odd.astype(f32))
        ticks("convs", i)

    run(STEPS[0], "m")

    total_one = jnp.zeros((3 * bins, width), f32)
    for offset, grad_ref in ((0, even_v), (1, odd_v)):
        picked = [
            mm_nt(taps_ref[:, 2 * i * BLOCK : 2 * (i + 1) * BLOCK], pick_frames(BLOCK, 2 * BLOCK, offset))
            for i in range(steps)
        ]
        total_one += mm(jnp.concatenate(picked, axis=1).astype(bf16), grad_ref[...])
    share = bins // 4
    spread = []
    for z in range(4):
        spread += [total_one[(4 * j + z) * share : (4 * j + z + 1) * share] for j in range(3)]
        spread.append(jnp.zeros((64 - 3 * share, width), f32))
    gw_one[...] = jnp.concatenate(spread, axis=0).T.astype(bf16)
    run(STEPS[0], "n")
    ticks("one")

    even, odd = even_v[...], odd_v[...]
    mel_even = (
        mm_nt(odd, w_one_ref[0])
        + mm_nt(even, w_one_ref[1])
        + shifted(mm_nt(odd, w_one_ref[2]), 1, 0)
    )
    mel_odd = (
        shifted(mm_nt(even, w_one_ref[0]), -1, 0)
        + mm_nt(odd, w_one_ref[1])
        + mm_nt(even, w_one_ref[2])
    )
    mel_even, mel_odd = turned(mel_even), turned(mel_odd)
    share = bins // 4
    tall = gmel_out.shape[1]
    for i in range(steps):
        cols = slice(i * BLOCK, (i + 1) * BLOCK)
        frames = slice(2 * i * BLOCK, 2 * (i + 1) * BLOCK)
        gmel = mm(mel_even[:, cols], pick_frames(BLOCK, 2 * BLOCK, 0))
        gmel += mm(mel_odd[:, cols], pick_frames(BLOCK, 2 * BLOCK, 1))
        for z in range(4):
            part = gmel[z * share : (z + 1) * share]
            part = jnp.concatenate([part, jnp.zeros((tall - share, 2 * BLOCK), f32)], axis=0)
            gmel_out[z, :, frames] = part.astype(bf16)
    gmel_copies = [
        remote(gmel_out.at[(links.chan + r) % 4], gmel_in.at[r - 1], send_g.at[r - 1], recv_g.at[r - 1], links.by_z[r - 1])
        for r in (1, 2, 3)
    ]
    for copy in gmel_copies:
        copy.start()

    ticks("mel")
    ticks("tail")

    for copy in gmel_copies:
        copy.wait()
    placed = by_place(links, gmel_out, gmel_in, share)
    gmel_z[...] = jnp.concatenate([part[:, None] for part in placed], axis=1).astype(bf16)
    ticks("end")


def run_back(operands):
    joined, et, w_one, taps = operands[0], operands[1], operands[16], operands[17]
    length, width = operands[4].shape
    block, quarter = width // 8, width // 4
    bins, frames = w_one.shape[1], taps.shape[1]
    held = pl.BlockSpec(memory_space=pltpu.VMEM)
    far = pl.BlockSpec(memory_space=pl.ANY)
    near = (2, 9, 16, 17, 22, 23)
    part, third = operands[19].shape[2], operands[20].shape[3]
    square = (length, width)
    vmem = lambda *shape: pltpu.VMEM(shape, bf16)
    scratch = [
        vmem(10, *square),
        vmem(3, *square),
        vmem(width, 3 * width),
        pltpu.VMEM(square, f32),
        vmem(*square),
        vmem(*square),
        vmem(*square),
        vmem(3, width, width),
        vmem(width, 3 * width),
        vmem(width, 256),
        pltpu.VMEM((8, width), f32),
        pltpu.VMEM((8, width), f32),
        *bufs_for(2, (width, part), 1, 0),
        *bufs_for(2, (quarter, part), 4, 3),
        *bufs_for(1, (width, part), 2, 2, 0),
        *bufs_for(1, (quarter, part), 4, 3),
        *bufs_for(3, (block, third), 2, 2, 0),
        *bufs_for(3, (block, third // 4), 4, 3),
        *bufs_for(1, (block, width), 4, 4, 2, 0),
        *bufs_for(1, (block, 256), 4, 3),
        *bufs_for(3, (block // 3, 3 * width), 4, 2, 0),
        *bufs_for(3, (block // 3, 640), 4, 3),
        *bufs_for(6, (block // 2, width), 4, 2, 0),
        *bufs_for(6, (block // 2, 256), 4, 3),
        *bufs_for(1, (block, 256), 4, 2, 0),
        *bufs_for(1, (block, 128), 4, 3),
        pltpu.VMEM((5, 16, width), f32),
        pltpu.VMEM((5, 16, width), f32),
        vmem(4, 32, frames),
        vmem(3, 32, frames),
        *sems_for(17),
        pltpu.SemaphoreType.DMA((15,)),
        pltpu.SemaphoreType.DMA((4,)),
        pltpu.SemaphoreType.DMA((6,)),
        pltpu.SemaphoreType.DMA((6,)),
        pltpu.SemaphoreType.DMA((3,)),
        pltpu.SemaphoreType.DMA((3,)),
    ]
    shapes = (
        (block, width),
        (quarter, 3 * part),
        (block, quarter),
        (block, 3 * quarter),
        (3, block, quarter),
        (block, 128),
        (16, width),
    )
    return pl.pallas_call(
        back_kernel,
        in_specs=[held if i in near else far for i in range(len(operands))],
        out_specs=[held] * 8,
        out_shape=[jax.ShapeDtypeStruct(s, f32) for s in shapes]
        + [jax.ShapeDtypeStruct((bins // 4, 4, frames), bf16)],
        scratch_shapes=scratch,
        compiler_params=pltpu.CompilerParams(
            vmem_limit_bytes=VMEM_LIMIT, collective_id=2, has_side_effects=True
        ),
        name="back",
    )(*operands)


def last_kernel(*refs):
    lengths_ref, language_ref, down, up, out, qkv, two, one, small, gmel = refs[:10]
    outs = refs[10:]
    group_z, gmel_z, one_z, b_one_z, two_z, b_two_z, gain_a_z, bias_a_z, qkv_z, b_query_z = outs[:10]
    b_value_z, out_z, b_out_z, gain_b_z, bias_b_z, up_z, b_up_z, down_z, b_down_z = outs[10:]
    group = lax.broadcasted_iota(jnp.int32, (1, 128), 1)

    def count(c, total):
        return total + jnp.where(group == language_ref[c], lengths_ref[c], 0)

    frames = lax.fori_loop(0, lengths_ref.shape[0], count, jnp.zeros((1, 128), jnp.int32))
    width = small.shape[1]
    loss = small[0:1, 0:128] / (width * jnp.maximum(frames, 1).astype(f32))
    group_z[...] = loss.reshape(-1)[: group_z.shape[0]]
    gmel_z[...] = gmel[...]
    vectors = (b_one_z, b_two_z, gain_a_z, bias_a_z, b_query_z, b_value_z, b_out_z, gain_b_z, bias_b_z, b_down_z)
    for i, ref in enumerate(vectors):
        ref[...] = small[1 + i]
    for k in range(b_up_z.shape[0] // width):
        b_up_z[pl.ds(k * width, width)] = small[11 + k]
    up_z[...] = up[...]
    out_z[...] = out[...]
    qkv_z[...] = qkv[...]
    down_z[...] = down[...]
    for j in range(3):
        two_z[j] = two[j].T
    bins = one_z.shape[1]
    turned_one = one[...].T
    for j in range(3):
        one_z[j] = turned_one[j * bins : (j + 1) * bins]


def run_whole(kernel, name, operands, results, scratch):
    held = pl.BlockSpec(memory_space=pltpu.VMEM)
    scalar = pl.BlockSpec(memory_space=pltpu.SMEM)
    return pl.pallas_call(
        kernel,
        in_specs=[scalar if o.dtype == jnp.int32 else held for o in operands],
        out_specs=[held] * len(results),
        out_shape=[jax.ShapeDtypeStruct(*r) for r in results],
        scratch_shapes=[pltpu.VMEM(*s) for s in scratch],
        compiler_params=pltpu.CompilerParams(vmem_limit_bytes=VMEM_LIMIT),
        name=name,
    )(*operands)


def on_device(
    mel_input,
    w_conv1,
    b_conv1,
    w_conv2,
    b_conv2,
    gain_attn,
    bias_attn,
    w_qkv,
    b_query,
    b_value,
    w_out,
    b_out,
    gain_mlp,
    bias_mlp,
    w_up,
    b_up,
    w_down,
    b_down,
    target,
    lengths,
    row_clip,
    language,
):
    clip_count, frame_count, model_width = target.shape
    mel_count = mel_input.shape[2]
    bins = w_conv1.shape[1]
    fast = lax.axis_size(DP) == 8 and lax.axis_size(CHAN) == 4
    square = (frame_count, model_width)
    (
        taps,
        act_even,
        act_odd,
        slope_even,
        slope_odd,
        slope_two,
        stem,
        normed_a,
        joined,
    ) = run_stem(
        (mel_input, w_conv1, b_conv1, b_conv2, gain_attn, bias_attn, b_query, b_value),
        (w_conv2, jnp.asarray(sinusoids(frame_count, model_width)), w_qkv),
        frame_count,
    )
    context, weights_t, inverse = attend(joined, row_clip, lengths)
    inner = w_up.shape[1]
    deep = (model_width, inner)
    vectors = (b_out, gain_mlp, bias_mlp, b_up, b_down)
    if fast:
        (
            block_rows,
            grad_context,
            grad_middle,
            grad_w_out,
            half_down,
            core_down,
            core_up,
            sums_b,
            grad_b_up,
        ) = run_mlp_send((row_clip, lengths, language), (context, stem, w_out, w_up, w_down, target[0]), vectors)
    else:
        (
            block_rows,
            grad_context,
            grad_middle,
            grad_w_up,
            grad_w_down_t,
            grad_w_out,
            sums_b,
            grad_b_up,
        ) = run_whole(
            mlp_kernel,
            "mlp",
            (
                row_clip,
                lengths,
                language,
                context,
                stem,
                w_out,
                b_out,
                gain_mlp,
                bias_mlp,
                w_up,
                b_up,
                w_down,
                b_down,
                target[0],
            ),
            [
                (square, bf16),
                (square, bf16),
                (square, f32),
                (deep, bf16),
                (deep, bf16),
                ((model_width, model_width), bf16),
                ((8, model_width), f32),
                ((1, inner), f32),
            ],
            [
                (square, f32),
                (square, bf16),
                (square, bf16),
                ((frame_count, inner), bf16),
                ((frame_count, inner), bf16),
                (square, bf16),
                (square, bf16),
                ((1, inner), f32),
            ],
        )
    if fast:
        final_up, down_z, final_out, final_qkv, two_z, one_z, small, grad_mel = run_back(
            (
                joined,
                weights_t,
                inverse,
                grad_context,
                context,
                w_qkv,
                grad_middle,
                stem,
                normed_a,
                gain_attn,
                slope_two,
                w_conv2,
                act_even,
                act_odd,
                slope_even,
                slope_odd,
                w_conv1,
                taps,
                half_down,
                core_down,
                core_up,
                grad_w_out,
                sums_b,
                grad_b_up,
            )
        )
        part = bins // lax.axis_size(CHAN)
        vector = ((model_width,), f32)
        share = model_width // 4
        block = model_width // 8
        finals = run_whole(
            last_kernel,
            "last",
            (
                lengths,
                language,
                down_z,
                final_up,
                final_out,
                final_qkv,
                two_z,
                one_z,
                small,
                grad_mel,
            ),
            [
                ((GROUPS,), f32),
                (mel_input.shape, bf16),
                ((3, part, block), f32),
                vector,
                ((3, share, block), f32),
                vector,
                vector,
                vector,
                ((block, 3 * share), f32),
                vector,
                vector,
                ((block, share), f32),
                vector,
                vector,
                vector,
                ((block, inner // 4), f32),
                ((inner,), f32),
                ((share, inner // 8), f32),
                vector,
            ],
            [],
        )
        return (block_rows.reshape(target.shape), *finals[:17], finals[17].T, finals[18])
    else:
        *grads, sums_a = attend_back(joined, weights_t, inverse, grad_context, context)
        weight = (model_width, model_width)
        grad_w_qkv, grad_w_two_t, grad_w_one_t, back_mel, sums_c = run_whole(
            stem_back_kernel,
            "stem_back",
            (
                *grads,
                w_qkv,
                grad_middle,
                stem,
                normed_a,
                gain_attn,
                slope_two,
                w_conv2,
                act_even,
                act_odd,
                slope_even,
                slope_odd,
                w_conv1,
                taps,
            ),
            [
                ((model_width, 3 * model_width), bf16),
                ((3,) + weight, bf16),
                ((model_width, 256), bf16),
                ((bins, mel_count), bf16),
                ((8, model_width), f32),
            ],
            [
                ((model_width, frame_count), bf16),
                (square, bf16),
                (square, bf16),
                ((model_width, frame_count), bf16),
                ((model_width, frame_count), bf16),
                (square, bf16),
                (square, bf16),
            ],
        )
        grad_mel = lax.all_to_all(back_mel[:, None], CHAN, split_axis=0, concat_axis=1, tiled=True)

        small = jnp.concatenate(
            [
                sums_b[0:1],
                sums_c[3:4],
                sums_c[2:3],
                sums_c[0:2],
                sums_a[0:2],
                sums_b[4:5],
                sums_b[2:4],
                sums_b[1:2],
                grad_b_up.reshape(-1, model_width),
                jnp.zeros((1, model_width), f32),
            ]
        )

        def scatter(values, dp_at, chan_at):
            part = lax.psum_scatter(values, DP, scatter_dimension=dp_at, tiled=True)
            return lax.psum_scatter(part, CHAN, scatter_dimension=chan_at, tiled=True).astype(f32)

        final_down = scatter(grad_w_down_t, 1, 0).T
        final_up = scatter(grad_w_up, 0, 1)
        final_out = scatter(grad_w_out, 0, 1)
        final_qkv = scatter(grad_w_qkv, 0, 1)
        part_two = scatter(grad_w_two_t, 1, 2).transpose(0, 2, 1)
        one_rows = grad_w_one_t[:, : 3 * bins].reshape(-1, 3, bins).transpose(1, 2, 0)
        part_one = scatter(one_rows, 2, 1)
        small = lax.psum(small, (DP, CHAN))
    totals_all = [small[0, :GROUPS]] + [small[i] for i in range(1, 11)]
    totals_all.insert(10, small[11:15].reshape(-1))
    group_ids = jnp.arange(GROUPS, dtype=jnp.int32)
    member_all = language[:, None] == group_ids[None, :]
    frames_group = jnp.sum(jnp.where(member_all, lengths[:, None], 0), axis=0)
    group_loss = totals_all[0] / (model_width * jnp.maximum(frames_group, 1).astype(f32))
    return (
        block_rows.reshape(target.shape),
        group_loss,
        grad_mel,
        part_one,
        totals_all[1],
        part_two,
        totals_all[2],
        totals_all[3],
        totals_all[4],
        final_qkv,
        totals_all[5],
        totals_all[6],
        final_out,
        totals_all[7],
        totals_all[8],
        totals_all[9],
        final_up,
        totals_all[10],
        final_down,
        totals_all[11],
    )


def solution(mesh):
    whole = P()
    by_row = P((DP, CHAN), None, None)
    return jax.shard_map(
        on_device,
        mesh=mesh,
        in_specs=(P(CHAN, DP, None),) + (whole,) * 17 + (by_row,) + (whole,) * 3,
        out_specs=(
            by_row,
            whole,
            P(CHAN, DP, None),
            P(None, CHAN, DP),
            whole,
            P(None, CHAN, DP),
            whole,
            whole,
            whole,
            P(DP, CHAN),
            whole,
            whole,
            P(DP, CHAN),
            whole,
            whole,
            whole,
            P(DP, CHAN),
            whole,
            P(DP, CHAN),
            whole,
        ),
        check_vma=False,
    )
```

```python
import math
from types import SimpleNamespace

import jax
import jax.numpy as jnp
import numpy as np
from jax import lax
from jax.experimental import pallas as pl
from jax.experimental.pallas import tpu as pltpu
from jax.sharding import PartitionSpec as P

HEAD_DIM = 64
GROUPS = 99
DP, CHAN = "dp", "chan"

bf16 = jnp.bfloat16
f32 = jnp.float32
epsilon = 1e-05
masked_score = -1e30


def sinusoids(length, channels):
    half_width = channels // 2
    increment = math.log(10000.0) / (half_width - 1)
    inverse = np.exp(-increment * np.arange(half_width, dtype=np.float64))
    angles = np.arange(length, dtype=np.float64)[:, None] * inverse[None, :]
    return np.concatenate([np.sin(angles), np.cos(angles)], axis=1).astype(np.float32)


def lookup(row_id, table):
    matches = row_id == jnp.arange(table.shape[0], dtype=jnp.int32)
    return jnp.sum(jnp.where(matches, table, 0))


def mm(a, b):
    return jnp.dot(a, b, preferred_element_type=f32)


def mm_nt(a, b):
    return lax.dot_general(a, b, (((1,), (1,)), ((), ())), preferred_element_type=f32)


def mm_tn(a, b):
    return lax.dot_general(a, b, (((0,), (0,)), ((), ())), preferred_element_type=f32)


BLOCK = 256
VMEM_LIMIT = 61 * 1024 * 1024


def gelu_pair(v):
    phi = 0.5 + 0.5 * lax.erf(v * math.sqrt(0.5))
    return v * phi, phi + v * (jnp.exp(-0.5 * (v * v)) * (1.0 / math.sqrt(2.0 * math.pi)))


def unrolled(count):
    def run(body):
        for i in range(count):
            body(i)

    return run


def row_of(ref):
    return ref[...].astype(f32).reshape(1, -1)


def own_clip(row_clip_ref):
    return row_clip_ref[lax.axis_index(DP) * lax.axis_size(CHAN) + lax.axis_index(CHAN)]


def turned(values):
    return values.astype(f32).T.astype(bf16)


def chunks(length, size):
    return [slice(at, min(at + size, length)) for at in range(0, length, size)]


def attend_kernel(row_clip_ref, lengths_ref, q_ref, k_ref, v_ref, ctx_ref, et_ref, inv_ref):
    length, width = q_ref.shape[0], 2 * HEAD_DIM
    lane = lax.broadcasted_iota(jnp.int32, (length, width), 1)
    frame = lax.broadcasted_iota(jnp.int32, (length, width), 0)
    bias = jnp.where(frame < lengths_ref[own_clip(row_clip_ref)], 0.0, masked_score)
    for pair in range(q_ref.shape[1] // width):
        cols = slice(pair * width, (pair + 1) * width)
        q = q_ref[:, cols].astype(f32) * HEAD_DIM ** (-0.5)
        k = k_ref[:, cols].astype(f32)
        v_t = turned(v_ref[:, cols])
        for h in range(2):
            mine = lane // HEAD_DIM == h
            spare = lane == HEAD_DIM * (1 - h)
            own_q = jnp.where(mine, q, jnp.where(spare, 1.0, 0.0)).astype(bf16)
            own_k = jnp.where(mine, k, jnp.where(spare, bias, 0.0)).astype(bf16)
            scores = mm_nt(own_k, own_q)
            weight = jnp.exp(scores - jnp.max(scores, axis=0, keepdims=True))
            et_ref[2 * pair + h] = weight.astype(bf16)
            inv_ref[2 * pair + h] = 1.0 / jnp.sum(weight, axis=0, keepdims=True)
        found = [
            mm(v_t[h * HEAD_DIM : (h + 1) * HEAD_DIM], et_ref[2 * pair + h]) * inv_ref[2 * pair + h]
            for h in range(2)
        ]
        ctx_ref[:, cols] = jnp.concatenate(found, axis=0).T.astype(bf16)


def attend_back_kernel(
    q_ref, k_ref, v_ref, et_ref, inv_ref, gctx_ref, ctx_ref, dq_ref, dk_ref, dv_ref, sums_ref, ds_ref
):
    length, width = q_ref.shape
    lane = lax.broadcasted_iota(jnp.int32, (length, width), 1)
    row = lax.broadcasted_iota(jnp.int32, (width, length), 0)
    scale = HEAD_DIM ** (-0.5)
    grad_t = gctx_ref[...].astype(f32).T * jnp.where(row < HEAD_DIM, inv_ref[0], inv_ref[1])
    grad_t = grad_t.astype(bf16).astype(f32)
    grad = grad_t.T
    inner_all = grad_t * ctx_ref[...].astype(f32).T
    k_t = turned(k_ref[...])
    q = q_ref[...].astype(f32) * scale
    v = v_ref[...].astype(f32)
    dq_t = []
    dk = jnp.zeros((length, width), f32)
    dv = jnp.zeros((length, width), f32)
    for h in range(2):
        at = HEAD_DIM * (1 - h)
        mine = lane // HEAD_DIM == h
        inner = jnp.sum(inner_all[h * HEAD_DIM : (h + 1) * HEAD_DIM], axis=0, keepdims=True)
        high = inner.astype(bf16).astype(f32)
        own_grad_t = jnp.where(row // HEAD_DIM == h, grad_t, 0.0)
        own_grad_t = jnp.where(row == at, -high, jnp.where(row == at + 1, high - inner, own_grad_t))
        own_grad_t = own_grad_t.astype(bf16)
        own_v = jnp.where(mine, v, jnp.where((lane == at) | (lane == at + 1), 1.0, 0.0)).astype(bf16)
        own_q = jnp.where(mine, q, 0.0).astype(bf16)
        own_grad = jnp.where(mine, grad, 0.0).astype(bf16)
        for cols in chunks(length, BLOCK):
            shifted = mm(own_v, own_grad_t[:, cols])
            ds_ref[:, cols] = (et_ref[h, :, cols].astype(f32) * shifted).astype(bf16)
        dk += mm(ds_ref[...], own_q)
        dv += mm(et_ref[h], own_grad)
        dq_t.append(mm(k_t[h * HEAD_DIM : (h + 1) * HEAD_DIM], ds_ref[...]))
    dq = (jnp.concatenate(dq_t, axis=0).T * scale).astype(bf16)
    dv = dv.astype(bf16)
    dq_ref[...] = dq
    dk_ref[...] = dk.astype(bf16)
    dv_ref[...] = dv
    sums_ref[0:1] = jnp.sum(dq.astype(f32), axis=0, keepdims=True)
    sums_ref[1:2] = jnp.sum(dv.astype(f32), axis=0, keepdims=True)


def attend(joined, row_clip, lengths):
    length, width = joined.shape[0], 4 * HEAD_DIM
    pairs = joined.shape[1] // (3 * width)
    block = lambda part: pl.BlockSpec((length, width), lambda p, *_: (0, part * pairs + p))
    return pl.pallas_call(
        attend_kernel,
        grid_spec=pltpu.PrefetchScalarGridSpec(
            num_scalar_prefetch=2,
            grid=(pairs,),
            in_specs=[block(0), block(1), block(2)],
            out_specs=[
                block(0),
                pl.BlockSpec((4, length, length), lambda p, *_: (p, 0, 0)),
                pl.BlockSpec((4, 1, length), lambda p, *_: (p, 0, 0)),
            ],
        ),
        out_shape=[
            jax.ShapeDtypeStruct((length, pairs * width), bf16),
            jax.ShapeDtypeStruct((4 * pairs, length, length), bf16),
            jax.ShapeDtypeStruct((4 * pairs, 1, length), f32),
        ],
        compiler_params=pltpu.CompilerParams(vmem_limit_bytes=VMEM_LIMIT),
        name="attend",
    )(row_clip, lengths, joined, joined, joined)


def attend_back(joined, et, inverse, grad_context, context):
    length, width = joined.shape[0], 2 * HEAD_DIM
    pairs = joined.shape[1] // (3 * width)
    block = lambda part: pl.BlockSpec((length, width), lambda p: (0, part * pairs + p))
    one = jax.ShapeDtypeStruct((length, pairs * width), bf16)
    return pl.pallas_call(
        attend_back_kernel,
        grid=(pairs,),
        in_specs=[
            block(0),
            block(1),
            block(2),
            pl.BlockSpec((2, length, length), lambda p: (p, 0, 0)),
            pl.BlockSpec((2, 1, length), lambda p: (p, 0, 0)),
            block(0),
            block(0),
        ],
        out_specs=[block(0), block(0), block(0), pl.BlockSpec((8, width), lambda p: (0, p))],
        out_shape=[one, one, one, jax.ShapeDtypeStruct((8, pairs * width), f32)],
        scratch_shapes=[pltpu.VMEM((length, length), bf16)],
        compiler_params=pltpu.CompilerParams(vmem_limit_bytes=VMEM_LIMIT),
        name="attend_back",
    )(joined, joined, joined, et, inverse, grad_context, context)


def mean_of(values):
    return jnp.mean(values, axis=-1, keepdims=True)


def mlp_body(v, live, spoken, wait, done, tick):
    length, width = v.stem.shape
    inner = v.w_up.shape[1]
    row_steps, wide_steps = length // BLOCK, inner // width
    ones = lambda values: jnp.sum(values, axis=0, keepdims=True)
    v.sums[...] = jnp.zeros_like(v.sums)
    v.b_up_line[...] = row_of(v.b_up)
    wait(0, 3, 1)

    @unrolled(row_steps)
    def _(i):
        rows = pl.ds(i * BLOCK, BLOCK)
        middle = v.stem[rows].astype(f32) + mm(v.ctx[rows], v.w_out[...]) + row_of(v.b_out)
        v.mid[rows] = middle
        centred = middle - mean_of(middle)
        scale = lax.rsqrt(mean_of(centred * centred) + epsilon)
        v.normed[rows] = (centred * scale * row_of(v.gain) + row_of(v.bias)).astype(bf16)

    wait(3, 1, 2)

    @unrolled(wide_steps)
    def _(j):
        cols = pl.ds(j * width, width)
        upward = mm(v.normed[...], v.w_up[:, cols]) + v.b_up_line[:, cols]
        hidden, slope = gelu_pair(upward)
        v.hidden[:, cols] = hidden.astype(bf16)
        v.slope[:, cols] = slope.astype(bf16)

    wait(4, 2, 0)

    @unrolled(row_steps)
    def _(i):
        rows = pl.ds(i * BLOCK, BLOCK)
        final = v.mid[rows] + mm(v.hidden[rows], v.w_down[...]) + row_of(v.b_down)
        v.out[rows] = final.astype(bf16)
        frame = i * BLOCK + lax.broadcasted_iota(jnp.int32, final.shape, 0)
        mismatch = jnp.where(frame < live, final - v.target[rows].astype(f32), 0.0)
        v.gmid[rows] = mismatch
        branch = mismatch.astype(bf16)
        v.branch[rows] = branch
        v.branch_t[:, rows] = turned(branch)
        v.normed_t[:, rows] = turned(v.normed[rows])
        v.sums[5:6] += ones(mismatch * mismatch)
        v.sums[1:2] += ones(branch.astype(f32))

    done("out")
    group = lax.broadcasted_iota(jnp.int32, (1, width), 1)
    loss = 0.5 * jnp.sum(v.sums[5:6], axis=1, keepdims=True)
    v.sums[0:1] = jnp.where(group == spoken, loss, 0.0)

    @unrolled(wide_steps)
    def _(j):
        cols = pl.ds(j * width, width)
        v.put_down(j, cols, mm(v.branch_t[...], v.hidden[:, cols]).astype(bf16))

    tick("down")

    @unrolled(wide_steps)
    def _(j):
        cols = pl.ds(j * width, width)
        grad = mm_nt(v.branch[...], v.w_down[cols]) * v.slope[:, cols].astype(f32)
        grad = grad.astype(bf16)
        v.gb_up[:, cols] = ones(grad.astype(f32))
        v.slope[:, cols] = grad
        v.put_up(j, cols, mm(v.normed_t[...], grad).astype(bf16))
        tick("tiles", j)

    tick("up")

    @unrolled(row_steps)
    def _(i):
        rows = pl.ds(i * BLOCK, BLOCK)
        grad = mm_nt(v.slope[rows], v.w_up[...])
        middle = v.mid[rows]
        centred = middle - mean_of(middle)
        scale = lax.rsqrt(mean_of(centred * centred) + epsilon)
        unit = centred * scale
        gained = grad * row_of(v.gain)
        back = scale * (gained - mean_of(gained) - unit * mean_of(gained * unit))
        grad_middle = v.gmid[rows] + back
        v.gmid[rows] = grad_middle
        attended = grad_middle.astype(bf16)
        v.branch[rows] = attended
        v.gctx[rows] = mm_nt(attended, v.w_out[...]).astype(bf16)
        v.normed_t[:, rows] = turned(v.ctx[rows])
        v.sums[2:3] += ones(grad * unit)
        v.sums[3:4] += ones(grad)
        v.sums[4:5] += ones(attended.astype(f32))
        done("gmid", i)
        done("gctx", i)
        tick("rows", i)

    v.gw_out[...] = mm(v.normed_t[...], v.branch[...]).astype(bf16)
    done("gw_out")
    tick("end")


def own_scalars(row_clip_ref, lengths_ref, language_ref):
    clip = own_clip(row_clip_ref)
    return lengths_ref[clip], language_ref[clip]


def mlp_kernel(row_clip, lengths, language, *refs):
    names = ("ctx", "stem", "w_out", "b_out", "gain", "bias", "w_up", "b_up", "w_down", "b_down", "target")
    names += ("out", "gctx", "gmid", "gw_up", "gw_down", "gw_out", "sums", "gb_up", "mid", "normed", "normed_t")
    names += ("hidden", "slope", "branch", "branch_t", "b_up_line")
    v = SimpleNamespace(**dict(zip(names, refs)))

    def put_down(j, cols, values):
        v.gw_down[:, cols] = values

    def put_up(j, cols, values):
        v.gw_up[:, cols] = values

    v.put_down, v.put_up = put_down, put_up
    nothing = lambda *_: None
    mlp_body(v, *own_scalars(row_clip, lengths, language), nothing, nothing, nothing)


def mlp_send_kernel(row_clip, lengths, language, *refs):
    far_in = ("ctx", "stem", "w_out", "w_up", "w_down", "target")
    far_out = ("out", "gctx", "gmid", "gw_out")
    near = ("b_out", "gain", "bias", "b_up", "b_down")
    names = far_in + near + far_out + ("half_down", "core_down", "core_up", "sums", "gb_up")
    given = SimpleNamespace(**dict(zip(names, refs)))
    held = far_in + far_out + ("mid", "normed", "normed_t", "hidden", "slope", "branch", "branch_t", "b_up_line")
    held += ("gw_up", "gw_blocks", "cin_d", "fin_d", "cin_u")
    rest = refs[len(names) :]
    v = SimpleNamespace(**dict(zip(held, rest)))
    for name in near + ("sums", "gb_up"):
        setattr(v, name, getattr(given, name))
    in_sems, out_sems = rest[len(held) : len(held) + 2]
    sems = SimpleNamespace(**dict(zip(SEMS, rest[len(held) + 2 :])))
    links = Links()
    links.greet([links.by_core, links.by_x, links.by_y])
    loads = [pltpu.make_async_copy(getattr(given, n), getattr(v, n), in_sems.at[i]) for i, n in enumerate(far_in)]
    for copy in loads[:3]:
        copy.start()
    width = v.stem.shape[1]
    part, third, block = given.half_down.shape[3], given.core_up.shape[3], given.core_up.shape[2]
    tasks = {}
    for k in range(3):
        source = lambda d, k=k: v.gw_blocks.at[d, :, pl.ds(k * part, part)]
        tasks[f"d{k}"] = Task(links, k != 0, sems, k, None, source, None, v.cin_d.at[k], v.fin_d.at[k], None, None, None)
    for k in range(3):
        source = rows_of(v.gw_up, block, k * third, third)
        tasks[f"u{k}"] = Task(links, k == 1, sems, 3 + k, None, source, None, v.cin_u.at[k], None, None, None, None)

    def put_down(j, cols, values):
        wide = v.gw_blocks.shape[2]
        for k in range(width // wide):
            v.gw_blocks[j * (width // wide) + k] = values[:, k * wide : (k + 1) * wide]

    def put_up(j, cols, values):
        for k in range(width // BLOCK):
            out = pl.ds((k * 4 + j) * BLOCK, BLOCK)
            v.gw_up[:, out] = values[:, k * BLOCK : (k + 1) * BLOCK]

    v.put_down, v.put_up = put_down, put_up
    leaving = []

    def leave(source, target):
        copy = pltpu.make_async_copy(source, target, out_sems.at[len(leaving)])
        copy.start()
        leaving.append(copy)

    steps = v.stem.shape[0] // BLOCK
    pieces = {"gmid": 8, "gctx": 8 + steps}

    def row_copy(name, i):
        rows = pl.ds(i * BLOCK, BLOCK)
        return pltpu.make_async_copy(getattr(v, name).at[rows], getattr(given, name).at[rows], out_sems.at[pieces[name] + i])

    def wait(first, count, ahead):
        for copy in loads[first : first + count]:
            copy.wait()
        for copy in loads[first + count : first + count + ahead]:
            copy.start()

    def done(name, i=None):
        if i is None:
            leave(getattr(v, name), getattr(given, name))
        else:
            row_copy(name, i).start()

    def tick(place, i=None):
        if place == "down":
            links.met([links.by_core, links.by_x, links.by_y])
            for k in range(3):
                tasks[f"d{k}"].begin()
        elif place == "tiles":
            pl.when(i == 1)(tasks["d0"].after_core)
            pl.when(i == 1)(tasks["d1"].after_core)
            pl.when(i == 3)(tasks["d2"].stop_at_core)
        elif place == "up":
            for k in range(3):
                tasks[f"u{k}"].begin()
            leave(v.cin_d.at[2], given.core_down)
        elif place == "rows":
            pl.when(i == 1)(tasks["u0"].stop_at_core)
            pl.when(i == 2)(tasks["u1"].stop_at_core)
        else:
            tasks["u2"].stop_at_core()
            leave(v.cin_u, given.core_up)
            for k in range(2):
                tasks[f"d{k}"].stop_at_first()
                leave(v.cin_d.at[k, pl.ds(0, 2)], given.half_down.at[k])

    mlp_body(v, *own_scalars(row_clip, lengths, language), wait, done, tick)
    for copy in leaving:
        copy.wait()
    for name in pieces:
        for i in range(steps):
            row_copy(name, i).wait()


def run_mlp_send(scalars, far, near):
    square, deep = far[0].shape, far[3].shape
    width, inner = deep
    block, part, third = width // 8, inner // 24, inner // 3
    in_smem = pl.BlockSpec(memory_space=pltpu.SMEM)
    in_vmem = pl.BlockSpec(memory_space=pltpu.VMEM)
    anywhere = pl.BlockSpec(memory_space=pl.ANY)
    whole = lambda x: pltpu.VMEM(x.shape, x.dtype)
    results = [
        (square, bf16),
        (square, bf16),
        (square, f32),
        ((width, width), bf16),
        ((2, 2, width, part), bf16),
        ((4, width, part), bf16),
        ((3, 4, block, third), bf16),
        ((8, width), f32),
        ((1, inner), f32),
    ]
    return pl.pallas_call(
        mlp_send_kernel,
        in_specs=[in_smem] * 3 + [anywhere] * len(far) + [in_vmem] * len(near),
        out_specs=[anywhere] * 7 + [in_vmem] * 2,
        out_shape=[jax.ShapeDtypeStruct(*r) for r in results],
        scratch_shapes=[whole(x) for x in far]
        + [pltpu.VMEM(*r) for r in results[:4]]
        + [
            pltpu.VMEM(square, f32),
            pltpu.VMEM(square, bf16),
            pltpu.VMEM(square, bf16),
            pltpu.VMEM((square[0], inner), bf16),
            pltpu.VMEM((square[0], inner), bf16),
            pltpu.VMEM(square, bf16),
            pltpu.VMEM(square, bf16),
            pltpu.VMEM((1, inner), f32),
            pltpu.VMEM(deep, bf16),
            pltpu.VMEM((8, width, inner // 8), bf16),
            *bufs_for(3, (width, part), 4, 2),
            *bufs_for(3, (block, third), 4),
            pltpu.SemaphoreType.DMA((len(far),)),
            pltpu.SemaphoreType.DMA((8 + 2 * (square[0] // BLOCK),)),
            *sems_for(6),
        ],
        compiler_params=pltpu.CompilerParams(
            vmem_limit_bytes=VMEM_LIMIT, collective_id=1, has_side_effects=True
        ),
        name="mlp",
    )(*scalars, *far, *near)


def shifted(values, step, axis):
    length = values.shape[axis]
    moved = pltpu.roll(values, step % length, axis)
    place = lax.broadcasted_iota(jnp.int32, values.shape, axis)
    return jnp.where(place == (0 if step > 0 else length - 1), 0.0, moved)


def pick_frames(slots, frames, offset):
    slot = lax.broadcasted_iota(jnp.int32, (slots, frames), 0)
    frame = lax.broadcasted_iota(jnp.int32, (slots, frames), 1)
    return jnp.where(frame == 2 * slot + offset, 1.0, 0.0).astype(bf16)


def flat_taps(ref):
    return ref[...].reshape(-1, ref.shape[-1])


def stem_kernel(*refs):
    near = ("mel", "w_one", "b_one", "b_two", "gain", "bias", "b_query", "b_value")
    far_in = ("w_two", "pos", "w_qkv")
    whole_out = ("taps", "act_even", "act_odd", "slope_even", "slope_odd")
    row_out = ("slope_two", "stem", "normed", "joined")
    far_out = whole_out + row_out
    names = near + far_in + far_out
    given = SimpleNamespace(**dict(zip(names, refs)))
    rest = refs[len(names) :]
    held = far_in + far_out + ("behind", "mel_out", "mel_in")
    v = SimpleNamespace(**dict(zip(held, rest)))
    in_sems, out_sems, send_g, recv_g = rest[len(held) :]
    loads = {}
    for i, name in enumerate(far_in):
        loads[name] = pltpu.make_async_copy(getattr(given, name), getattr(v, name), in_sems.at[i])
        loads[name].start()
    leaving = []

    def leave(source, target):
        copy = pltpu.make_async_copy(source, target, out_sems.at[len(leaving)])
        copy.start()
        leaving.append(copy)

    length, width = v.stem.shape
    steps = length // BLOCK
    links = Links()
    links.greet(links.by_z)
    bins_given = given.mel[...].astype(f32)
    share = bins_given.shape[0]
    for z in range(4):
        v.mel_out[z] = stacked(bins_given[:, z]).astype(bf16)
    links.met(links.by_z)
    copies = [
        remote(v.mel_out.at[(links.chan + r) % 4], v.mel_in.at[r - 1], send_g.at[r - 1], recv_g.at[r - 1], links.by_z[r - 1])
        for r in (1, 2, 3)
    ]
    for copy in copies:
        copy.start()
    picks = [pick_frames(BLOCK, 2 * BLOCK, offset) for offset in range(2)]
    for copy in copies:
        copy.wait()
    mel = jnp.concatenate(by_place(links, v.mel_out, v.mel_in, share), axis=0)
    taps = jnp.concatenate([shifted(mel, 1, 1), mel, shifted(mel, -1, 1)], axis=0).astype(bf16)
    v.taps[...] = taps
    leave(v.taps, given.taps)
    w_one = flat_taps(given.w_one)
    for pick, act_ref, slope_ref in (
        (picks[1], v.act_odd, v.slope_odd),
        (picks[0], v.act_even, v.slope_even),
    ):
        for i in range(steps):
            rows = slice(i * BLOCK, (i + 1) * BLOCK)
            frames = slice(2 * i * BLOCK, 2 * (i + 1) * BLOCK)
            picked = mm_nt(pick, taps[:, frames]).astype(bf16)
            act, slope = gelu_pair(mm(picked, w_one) + row_of(given.b_one))
            act_ref[rows] = act.astype(bf16)
            slope_ref[rows] = slope.astype(bf16)
    for name in whole_out[1:]:
        leave(getattr(v, name), getattr(given, name))
    for cols in chunks(width, BLOCK):
        v.behind[:, cols] = shifted(v.act_odd[:, cols].astype(f32), 1, 0).astype(bf16)
    for name in far_in:
        loads[name].wait()
    query, key, value = (slice(part * width, (part + 1) * width) for part in range(3))
    for i in range(steps):
        rows = slice(i * BLOCK, (i + 1) * BLOCK)
        two = (
            mm(v.behind[rows], v.w_two[0])
            + mm(v.act_even[rows], v.w_two[1])
            + mm(v.act_odd[rows], v.w_two[2])
            + row_of(given.b_two)
        )
        act, slope = gelu_pair(two)
        v.slope_two[rows] = slope.astype(bf16)
        stem = (act + v.pos[rows]).astype(bf16)
        v.stem[rows] = stem
        stem = stem.astype(f32)
        centred = stem - mean_of(stem)
        scale = lax.rsqrt(mean_of(centred * centred) + epsilon)
        normed = (centred * scale * row_of(given.gain) + row_of(given.bias)).astype(bf16)
        v.normed[rows] = normed
        v.joined[rows, query] = (mm(normed, v.w_qkv[:, query]) + row_of(given.b_query)).astype(bf16)
        v.joined[rows, key] = mm(normed, v.w_qkv[:, key]).astype(bf16)
        v.joined[rows, value] = (mm(normed, v.w_qkv[:, value]) + row_of(given.b_value)).astype(bf16)
        for name in row_out:
            leave(getattr(v, name).at[pl.ds(i * BLOCK, BLOCK)], getattr(given, name).at[pl.ds(i * BLOCK, BLOCK)])
    for copy in leaving:
        copy.wait()


def run_stem(near, far, length):
    width, frames = near[1].shape[2], near[0].shape[2]
    square = (length, width)
    results = [(3 * near[1].shape[1], frames)] + [square] * 7 + [(length, 3 * width)]
    in_vmem = pl.BlockSpec(memory_space=pltpu.VMEM)
    anywhere = pl.BlockSpec(memory_space=pl.ANY)
    return pl.pallas_call(
        stem_kernel,
        in_specs=[in_vmem] * len(near) + [anywhere] * len(far),
        out_specs=[anywhere] * len(results),
        out_shape=[jax.ShapeDtypeStruct(r, bf16) for r in results],
        scratch_shapes=[pltpu.VMEM(x.shape, x.dtype) for x in far]
        + [pltpu.VMEM(r, bf16) for r in results]
        + [
            pltpu.VMEM(square, bf16),
            pltpu.VMEM((4, near[0].shape[0] * frames // 128, 128), bf16),
            pltpu.VMEM((3, near[0].shape[0] * frames // 128, 128), bf16),
            pltpu.SemaphoreType.DMA((len(far),)),
            pltpu.SemaphoreType.DMA((5 + 4 * (length // BLOCK),)),
            pltpu.SemaphoreType.DMA((3,)),
            pltpu.SemaphoreType.DMA((3,)),
        ],
        compiler_params=pltpu.CompilerParams(
            vmem_limit_bytes=VMEM_LIMIT, collective_id=3, has_side_effects=True
        ),
        name="stem",
    )(*near, *far)


def stem_back_kernel(
    gq_ref,
    gk_ref,
    gv_ref,
    w_qkv_ref,
    gmid_ref,
    stem_ref,
    normed_ref,
    gain_ref,
    slope_two_ref,
    w_two_ref,
    act_even_ref,
    act_odd_ref,
    slope_even_ref,
    slope_odd_ref,
    w_one_ref,
    taps_ref,
    gw_qkv_ref,
    gw_two_ref,
    gw_one_ref,
    gmel_ref,
    sums_ref,
    normed_t_ref,
    two_ref,
    two_ahead_ref,
    two_t_ref,
    two_ahead_t_ref,
    even_ref,
    odd_ref,
):
    length, width = stem_ref.shape
    steps = length // BLOCK
    ones = lambda v: jnp.sum(v, axis=0, keepdims=True)
    sums_ref[...] = jnp.zeros_like(sums_ref)

    @pl.loop(0, steps)
    def _(i):
        rows = pl.ds(pl.multiple_of(i * BLOCK, BLOCK), BLOCK)
        normed_t_ref[:, rows] = turned(normed_ref[rows])
        grad = (
            mm_nt(gq_ref[rows], w_qkv_ref[:, 0:width])
            + mm_nt(gk_ref[rows], w_qkv_ref[:, width : 2 * width])
            + mm_nt(gv_ref[rows], w_qkv_ref[:, 2 * width : 3 * width])
        )
        stem = stem_ref[rows].astype(f32)
        centred = stem - mean_of(stem)
        scale = lax.rsqrt(mean_of(centred * centred) + epsilon)
        unit = centred * scale
        gained = grad * row_of(gain_ref)
        back = scale * (gained - mean_of(gained) - unit * mean_of(gained * unit))
        grad_stem = (gmid_ref[rows] + back).astype(bf16).astype(f32)
        two = (grad_stem * slope_two_ref[rows].astype(f32)).astype(bf16)
        two_ref[rows] = two
        two_t_ref[:, rows] = turned(two)
        sums_ref[0:1] += ones(grad * unit)
        sums_ref[1:2] += ones(grad)
        sums_ref[2:3] += ones(two.astype(f32))

    for cols in chunks(width, BLOCK):
        two_ahead_ref[:, cols] = shifted(two_ref[:, cols].astype(f32), -1, 0).astype(bf16)

    @pl.loop(0, steps)
    def _(i):
        rows = pl.ds(pl.multiple_of(i * BLOCK, BLOCK), BLOCK)
        two_ahead_t_ref[:, rows] = turned(two_ahead_ref[rows])
        even = mm_nt(two_ref[rows], w_two_ref[1]) * slope_even_ref[rows].astype(f32)
        odd = mm_nt(two_ref[rows], w_two_ref[2]) + mm_nt(two_ahead_ref[rows], w_two_ref[0])
        odd = odd * slope_odd_ref[rows].astype(f32)
        even_ref[rows] = even.astype(bf16)
        odd_ref[rows] = odd.astype(bf16)
        sums_ref[3:4] += ones(even.astype(bf16).astype(f32)) + ones(odd.astype(bf16).astype(f32))

    @pl.loop(0, width // BLOCK)
    def _(j):
        cols = pl.ds(pl.multiple_of(j * BLOCK, BLOCK), BLOCK)
        for part, grad_ref in enumerate((gq_ref, gk_ref, gv_ref)):
            out = pl.ds(pl.multiple_of(part * width + j * BLOCK, BLOCK), BLOCK)
            gw_qkv_ref[:, out] = mm(normed_t_ref[...], grad_ref[:, cols]).astype(bf16)
        gw_two_ref[0, :, cols] = mm(two_ahead_t_ref[...], act_odd_ref[:, cols]).astype(bf16)
        gw_two_ref[1, :, cols] = mm(two_t_ref[...], act_even_ref[:, cols]).astype(bf16)
        gw_two_ref[2, :, cols] = mm(two_t_ref[...], act_odd_ref[:, cols]).astype(bf16)

    bins = w_one_ref.shape[1]
    gw_one = jnp.zeros((3 * bins, width), f32)
    for offset, grad_ref in ((0, even_ref), (1, odd_ref)):
        picked = [
            mm_nt(taps_ref[:, 2 * i * BLOCK : 2 * (i + 1) * BLOCK], pick_frames(BLOCK, 2 * BLOCK, offset))
            for i in range(steps)
        ]
        gw_one += mm(jnp.concatenate(picked, axis=1).astype(bf16), grad_ref[...])
    gw_one_ref[...] = jnp.zeros_like(gw_one_ref)
    gw_one_ref[:, 0 : 3 * bins] = gw_one.T.astype(bf16)
    even, odd = even_ref[...], odd_ref[...]
    mel_even = (
        mm_nt(odd, w_one_ref[0])
        + mm_nt(even, w_one_ref[1])
        + shifted(mm_nt(odd, w_one_ref[2]), 1, 0)
    )
    mel_odd = (
        shifted(mm_nt(even, w_one_ref[0]), -1, 0)
        + mm_nt(odd, w_one_ref[1])
        + mm_nt(even, w_one_ref[2])
    )
    mel_even, mel_odd = turned(mel_even), turned(mel_odd)
    for i in range(steps):
        cols = slice(i * BLOCK, (i + 1) * BLOCK)
        frames = slice(2 * i * BLOCK, 2 * (i + 1) * BLOCK)
        gmel_ref[:, frames] = (
            mm(mel_even[:, cols], pick_frames(BLOCK, 2 * BLOCK, 0))
            + mm(mel_odd[:, cols], pick_frames(BLOCK, 2 * BLOCK, 1))
        ).astype(bf16)


MESH = pl.DeviceIdType.MESH


def remote(source, target, send, recv, to):
    return pltpu.make_async_remote_copy(source, target, send, recv, device_id=to, device_id_type=MESH)


class Links:
    def __init__(self):
        dp, chan = lax.axis_index(DP), lax.axis_index(CHAN)
        self.chan = chan
        self.core, self.x, self.y = dp % 2, (dp // 2) % 2, dp // 4
        self.by_core = (self.dest(0, 0, 1), chan)
        self.by_x = (self.dest(0, 1, 0), chan)
        self.by_y = (self.dest(1, 0, 0), chan)
        self.by_z = [(dp, (chan + r) % 4) for r in (1, 2, 3)]
        self.by_next = (dp, chan + 1 - 2 * (chan % 2))
        self.by_far = (dp, (chan + 2) % 4)
        self.partners = [self.by_core, self.by_x, self.by_y] + self.by_z

    def dest(self, dy, dx, dc):
        flip = lambda bit, turn: 1 - bit if turn else bit
        return 4 * flip(self.y, dy) + 2 * flip(self.x, dx) + flip(self.core, dc)

    def greet(self, partners):
        for partner in partners:
            pl.semaphore_signal(pltpu.get_barrier_semaphore(), inc=1, device_id=partner, device_id_type=MESH)

    def met(self, partners):
        pl.semaphore_wait(pltpu.get_barrier_semaphore(), len(partners))


def stacked(bins):
    return jnp.concatenate([bins[:, at : at + 128] for at in range(0, bins.shape[1], 128)], axis=0)


def by_place(links, out_ref, in_ref, share):
    parts = [out_ref[links.chan], in_ref[0], in_ref[1], in_ref[2]]
    parts = [part.astype(f32) for part in parts]
    parts = [jnp.concatenate([p[at : at + share] for at in range(0, p.shape[0], share)], axis=1) for p in parts]
    placed = []
    for z in range(4):
        value = parts[0]
        for r in (1, 2, 3):
            value = jnp.where((links.chan + 4 - r) % 4 == z, parts[r], value)
        placed.append(value)
    return placed


class Task:
    def __init__(self, links, x_first, sems, n, cut, source, own, cin, fin, sin, z_out, z_in, stage=0):
        self.links, self.x_first, self.sems, self.n, self.cut = links, x_first, sems, n, cut
        self.source, self.own, self.cin, self.fin, self.sin = source, own, cin, fin, sin
        self.z_out, self.z_in, self.stage = z_out, z_in, stage
        self.ways = (links.by_x, links.by_y) if x_first else (links.by_y, links.by_x)

    def dest(self, slot, dc):
        dx, dy = (slot // 2, slot % 2) if self.x_first else (slot % 2, slot // 2)
        return self.links.dest(dy, dx, dc)

    def begin(self):
        if self.stage == 0:
            for slot in (3, 2, 1, 0):
                source = self.source(self.dest(slot, 1))
                remote(source, self.cin.at[slot], self.sems.send_c.at[self.n], self.sems.recv_c.at[self.n], self.links.by_core).start()
                if self.own is not None:
                    source = self.source(self.dest(slot, 0))
                    pltpu.make_async_copy(source, self.own.at[slot], self.sems.load.at[self.n]).start()
            return
        if self.stage == 1:
            for slot in (3, 2):
                self.to_first(self.source.at[slot], slot)
        else:
            self.to_second(self.source.at[1])
        held = self.own.shape[0]
        pltpu.make_async_copy(self.source.at[pl.ds(0, held)], self.own, self.sems.load.at[self.n]).start()

    def to_first(self, ref, slot):
        remote(ref, self.fin.at[slot - 2], self.sems.send_f.at[self.n], self.sems.recv_f.at[self.n], self.ways[0]).start()

    def to_second(self, ref):
        remote(ref, self.sin, self.sems.send_s.at[self.n], self.sems.recv_s.at[self.n], self.ways[1]).start()

    def loaded(self, stage):
        if self.own is not None and self.stage == stage:
            pltpu.make_async_copy(self.own, self.own, self.sems.load.at[self.n]).wait()

    def wait(self, ref, send, recv, to):
        remote(ref, ref, send.at[self.n], recv.at[self.n], to).wait()

    def held(self, slot):
        if self.stage:
            return self.own[slot].astype(f32)
        own = self.own[slot] if self.own is not None else self.source(self.dest(slot, 0))[...]
        return own.astype(f32) + self.cin[slot].astype(f32)

    def core_done(self):
        self.loaded(0)
        self.wait(self.cin, self.sems.send_c, self.sems.recv_c, self.links.by_core)

    def after_core(self):
        self.core_done()
        for slot in (3, 2):
            self.cin[slot] = self.held(slot).astype(bf16)
            self.to_first(self.cin.at[slot], slot)

    def stop_at_core(self):
        self.core_done()
        for slot in (3, 2, 1, 0):
            self.cin[slot] = self.held(slot).astype(bf16)

    def stop_at_first(self):
        self.wait(self.fin, self.sems.send_f, self.sems.recv_f, self.ways[0])
        for slot in (1, 0):
            self.cin[slot] = (self.held(slot) + self.fin[slot].astype(f32)).astype(bf16)

    def after_first(self):
        self.loaded(1)
        self.wait(self.fin, self.sems.send_f, self.sems.recv_f, self.ways[0])
        leaving = self.own if self.stage else self.cin
        leaving[1] = (self.held(1) + self.fin[1].astype(f32)).astype(bf16)
        self.to_second(leaving.at[1])

    def z_copies(self):
        theirs = 1 - self.links.chan % 2
        sems = self.sems.send_z.at[self.n], self.sems.recv_z.at[self.n]
        return [remote(self.z_out.at[2 * a + theirs], self.z_in.at[a], *sems, self.links.by_next) for a in range(2)]

    def after_second(self):
        self.loaded(2)
        self.wait(self.sin, self.sems.send_s, self.sems.recv_s, self.ways[1])
        total = self.held(0) + self.sin[...].astype(f32)
        if self.stage < 2:
            total = total + self.fin[0].astype(f32)
        for z in range(4):
            self.z_out[z] = self.cut(total, z).astype(bf16)
        for copy in self.z_copies():
            copy.start()

    def after_third(self):
        chan = self.links.chan
        self.wait(self.z_in.at[pl.ds(0, 2)], self.sems.send_z, self.sems.recv_z, self.links.by_next)
        far = (chan + 2) % 4
        self.z_out[far] = (self.z_out[far].astype(f32) + self.z_in[far // 2].astype(f32)).astype(bf16)
        remote(self.z_out.at[far], self.z_in.at[2], self.sems.send_w.at[self.n], self.sems.recv_w.at[self.n], self.links.by_far).start()

    def finish(self):
        chan = self.links.chan
        self.wait(self.z_in.at[2], self.sems.send_w, self.sems.recv_w, self.links.by_far)
        return self.z_out[chan].astype(f32) + self.z_in[chan // 2].astype(f32) + self.z_in[2].astype(f32)


def cut_rows(block, z):
    share = block.shape[0] // 4
    return block[z * share : (z + 1) * share]


def cut_columns(block, z):
    share = block.shape[1] // 4
    first = z * share // 128 * 128
    taken = block[:, first : first + (share + 127) // 128 * 128]
    skip = z * share - first
    return pltpu.roll(taken, taken.shape[1] - skip, 1) if skip else taken


def cut_half_tiles(block, z):
    taken = block[:, z // 2 * 128 : (z // 2 + 1) * 128]
    return pltpu.roll(taken, 64, 1) if z % 2 else taken


SEMS = ("send_c", "recv_c", "load", "send_f", "recv_f", "send_s", "recv_s", "send_z", "recv_z", "send_w", "recv_w")


def sems_for(count):
    return [pltpu.SemaphoreType.DMA((count,)) for _ in SEMS]


def bufs_for(count, shape, *slots):
    return [pltpu.VMEM((count,) + ((slot,) if slot else ()) + shape, bf16) for slot in slots]


def rows_of(ref, block, start, count):
    return lambda d: ref.at[pl.ds(pl.multiple_of(d * block, block), block), pl.ds(start, count)]


def pair_back(p, q_ref, k_ref, v_ref, et_of, inverse_ref, gctx_ref, ctx_ref, dq_ref, dk_ref, dv_ref, sums_ref, ds_ref, between):
    length, width = q_ref.shape[0], 2 * HEAD_DIM
    cols = pl.ds(pl.multiple_of(p * width, width), width)
    lane = lax.broadcasted_iota(jnp.int32, (length, width), 1)
    row = lax.broadcasted_iota(jnp.int32, (width, length), 0)
    scale = HEAD_DIM ** (-0.5)
    grad_t = gctx_ref[:, cols].astype(f32).T
    grad_t = grad_t * jnp.where(row < HEAD_DIM, inverse_ref[2 * p], inverse_ref[2 * p + 1])
    grad_t = grad_t.astype(bf16).astype(f32)
    grad = grad_t.T
    inner_all = grad_t * ctx_ref[:, cols].astype(f32).T
    k_t = turned(k_ref[:, cols])
    q = q_ref[:, cols].astype(f32) * scale
    v = v_ref[:, cols].astype(f32)
    dq_t = []
    dk = jnp.zeros((length, width), f32)
    dv = jnp.zeros((length, width), f32)
    for h in range(2):
        at = HEAD_DIM * (1 - h)
        mine = lane // HEAD_DIM == h
        inner = jnp.sum(inner_all[h * HEAD_DIM : (h + 1) * HEAD_DIM], axis=0, keepdims=True)
        high = inner.astype(bf16).astype(f32)
        own_grad_t = jnp.where(row // HEAD_DIM == h, grad_t, 0.0)
        own_grad_t = jnp.where(row == at, -high, jnp.where(row == at + 1, high - inner, own_grad_t))
        own_grad_t = own_grad_t.astype(bf16)
        own_v = jnp.where(mine, v, jnp.where((lane == at) | (lane == at + 1), 1.0, 0.0)).astype(bf16)
        own_q = jnp.where(mine, q, 0.0).astype(bf16)
        own_grad = jnp.where(mine, grad, 0.0).astype(bf16)
        et_ref = et_of(h)
        ds_ref[...] = (et_ref[...].astype(f32) * mm(own_v, own_grad_t)).astype(bf16)
        dk += mm(ds_ref[...], own_q)
        dv += mm(et_ref[...], own_grad)
        dq_t.append(mm(k_t[h * HEAD_DIM : (h + 1) * HEAD_DIM], ds_ref[...]))
        if h == 0:
            between()
    dq = (jnp.concatenate(dq_t, axis=0).T * scale).astype(bf16)
    dv = dv.astype(bf16)
    dq_ref[:, cols] = dq
    dk_ref[:, cols] = dk.astype(bf16)
    dv_ref[:, cols] = dv
    sums_ref[0:1, cols] = jnp.sum(dq.astype(f32), axis=0, keepdims=True)
    sums_ref[1:2, cols] = jnp.sum(dv.astype(f32), axis=0, keepdims=True)


STEPS = ("begin", "after_core", "after_first", "after_second", "after_third", "finish")
TASKS = ("d0", "d1", "d2", "u0", "u1", "u2", "o", "q0", "q1", "q2", "t0", "t1", "t2", "t3", "t4", "t5", "n", "m")
SCHEDULE = {
    "middle": (
        (0, 1, 6),
        (2, 4, 0),
        (4, 5, 1),
        (5, 2, 4),
        (5, 2, 5),
    ),
    "pairs": (
        (0, 3, 0),
        (0, 3, 1),
        (2, 4, 1),
        (2, 2, 2),
        (2, 2, 3),
        (3, 5, 0),
    ),
    "turn": (
        (0, 3, 2),
    ),
    "qkv": (
        (1, 2, 6),
    ),
    "rows": (
        (0, 4, 2),
        (0, 3, 4),
        (0, 3, 3),
        (1, 1, 7),
        (2, 3, 6),
        (2, 3, 5),
        (2, 1, 8),
        (2, 1, 9),
    ),
    "ahead": (
        (0, 5, 2),
        (0, 4, 4),
    ),
    "convs": (
        (1, 4, 3),
    ),
    "one": (
        (0, 4, 6),
        (0, 2, 7),
        (0, 4, 5),
        (0, 5, 4),
        (0, 1, 17),
    ),
    "mel": (
        (0, 2, 8),
        (0, 1, 16),
        (0, 5, 3),
    ),
    "two": (
        (1, 2, 9),
        (1, 3, 7),
        (1, 5, 6),
        (2, 2, 17),
        (2, 1, 10),
        (2, 5, 5),
        (2, 1, 11),
    ),
    "tail": (
        (0, 1, 12),
        (0, 3, 8),
        (0, 1, 13),
        (0, 1, 14),
        (0, 1, 15),
        (0, 2, 16),
        (0, 4, 7),
        (0, 3, 9),
        (0, 3, 17),
        (0, 4, 8),
        (0, 2, 10),
        (0, 2, 11),
        (0, 4, 9),
        (0, 4, 17),
        (0, 2, 12),
        (0, 2, 13),
        (0, 5, 7),
        (0, 2, 14),
        (0, 5, 8),
        (0, 2, 15),
        (0, 3, 16),
        (0, 3, 10),
        (0, 3, 11),
        (0, 5, 9),
        (0, 3, 12),
        (0, 3, 13),
        (0, 5, 17),
        (0, 4, 16),
        (0, 3, 14),
        (0, 3, 15),
        (0, 4, 10),
        (0, 4, 11),
        (0, 4, 12),
        (0, 4, 13),
        (0, 4, 14),
        (0, 5, 16),
        (0, 4, 15),
        (0, 5, 10),
        (0, 5, 11),
        (0, 5, 12),
        (0, 5, 13),
        (0, 5, 14),
        (0, 5, 15),
    ),
}


def back_kernel(*refs):
    joined, et, inverse, gctx, ctx, w_qkv, gmid, stem, normed, gain_ref, slope_two = refs[:11]
    w_two, act_even, act_odd, slope_even, slope_odd, w_one_ref, taps_ref = refs[11:18]
    half_down, core_down, core_up, gw_out, sums_b_ref, gb_up_ref = refs[18:24]
    up_z, down_z, out_z, qkv_z, two_z, one_z, small_z, gmel_z = refs[24:32]
    pool, d_ref, w_qkv_v, gmid_v, stem_v, normed_v, slope_two_v, w_two_v, gw_qkv = refs[32:41]
    gw_one, sums_a_ref, sums_ref = refs[41:44]
    rest = list(refs[44:])
    take = lambda count: [rest.pop(0) for _ in range(count)]
    own_h, sin_h, zo_h, zi_h = take(4)
    own_c, fin_c, sin_c, zo_c, zi_c = take(5)
    own_u, fin_u, sin_u, zo_u, zi_u = take(5)
    own_o, cin_o, fin_o, sin_o, zo_o, zi_o = take(6)
    bufs_q, bufs_t, bufs_n = take(5), take(5), take(5)
    small_buf, small_in, gmel_out, gmel_in = take(4)
    sems = SimpleNamespace(**dict(zip(SEMS, take(len(SEMS)))))
    loads, et_loads, send_m, recv_m, send_g, recv_g = rest
    length, width = ctx.shape
    steps, pairs, block = length // BLOCK, width // (2 * HEAD_DIM), width // 8
    bins = w_one_ref.shape[1]
    links = Links()
    links.greet(links.partners)

    q_v, k_v, v_v = (pool.at[i] for i in range(3))
    ctx_v, gctx_v, ds_v = pool.at[7], pool.at[8], pool.at[9]
    started = []

    def later(source, target):
        copy = pltpu.make_async_copy(source, target, loads.at[len(started)])
        started.append(copy)
        return copy

    def load(source, target):
        copy = later(source, target)
        copy.start()
        return copy

    def et_load(head, slot):
        return pltpu.make_async_copy(et.at[head], pool.at[3 + slot], et_loads.at[slot])

    first = [load(joined.at[:, pl.ds(i * width, width)], pool.at[i]) for i in range(3)]
    first += [load(gctx, gctx_v), load(ctx, ctx_v)]
    for head in range(2):
        et_load(head, head).start()

    tasks = {}

    def add(name, x_first, cut, source, own, cin, fin, sin, z_out, z_in, stage=0):
        tasks[name] = Task(
            links, x_first, sems, len(tasks), cut, source, own, cin, fin, sin, z_out, z_in, stage
        )

    at = lambda k, *bufs: [ref.at[k] for ref in bufs]
    part, third, rest_rows, half = core_down.shape[2], core_up.shape[3], block // 3, block // 2
    for k in range(2):
        own, sin, z_out, z_in = at(k, own_h, sin_h, zo_h, zi_h)
        add(f"d{k}", k != 0, cut_rows, half_down.at[k], own, None, None, sin, z_out, z_in, 2)
    own, *bufs = at(0, own_c, fin_c, sin_c, zo_c, zi_c)
    add("d2", True, cut_rows, core_down, own, None, *bufs, 1)
    for k in range(3):
        own, *bufs = at(k, own_u, fin_u, sin_u, zo_u, zi_u)
        add(f"u{k}", k == 1, cut_columns, core_up.at[k], own, None, *bufs, 1)
    own, *bufs = at(0, own_o, cin_o, fin_o, sin_o, zo_o, zi_o)
    add("o", True, cut_columns, rows_of(gw_out, block, 0, width), own, *bufs)
    for k in range(3):
        source = lambda d, k=k: gw_qkv.at[pl.ds(pl.multiple_of(d * block + k * rest_rows, rest_rows), rest_rows)]
        add(f"q{k}", k == 1, cut_columns, source, None, *at(k, *bufs_q))
    for k in range(6):
        source = lambda d, k=k: pool.at[7 + k // 2, pl.ds(pl.multiple_of(d * block + k % 2 * half, half), half)]
        add(f"t{k}", k % 2 == 0, cut_columns, source, None, *at(k, *bufs_t))
    add("n", False, cut_half_tiles, rows_of(gw_one, block, 0, gw_one.shape[1]), None, *at(0, *bufs_n))
    quarter = width // 4

    def store(name):
        total = tasks[name].finish()
        k = int(name[1:] or 0)
        if name[0] == "d":
            down_z[:, k * part : (k + 1) * part] = total
        elif name[0] == "u":
            up_z[:, k * third // 4 : (k + 1) * third // 4] = total
        elif name == "o":
            out_z[...] = total[:, 0:quarter]
        elif name[0] == "q":
            qkv_z[k * rest_rows : (k + 1) * rest_rows] = total[:, 0 : 3 * quarter]
        elif name[0] == "t":
            two_z[k // 2, k % 2 * half : (k % 2 + 1) * half] = total[:, 0:quarter]
        else:
            one_z[...] = total

    small_ways = [links.by_core, links.by_x, links.by_y, links.by_next, links.by_far]

    def small_step(step):
        i = STEPS.index(step)
        if i == 0:
            small_buf[0, 0:1] = sums_b_ref[0:1]
            small_buf[0, 1:2] = sums_ref[3:4]
            small_buf[0, 2:3] = sums_ref[2:3]
            small_buf[0, 3:5] = sums_ref[0:2]
            small_buf[0, 5:7] = sums_a_ref[0:2]
            small_buf[0, 7:8] = sums_b_ref[4:5]
            small_buf[0, 8:10] = sums_b_ref[2:4]
            small_buf[0, 10:11] = sums_b_ref[1:2]
            for k in range(4):
                small_buf[0, 11 + k : 12 + k] = gb_up_ref[:, k * width : (k + 1) * width]
            small_buf[0, 15:16] = jnp.zeros((1, width), f32)
        else:
            got = small_in.at[i - 1]
            remote(got, got, send_m.at[i - 1], recv_m.at[i - 1], small_ways[i - 1]).wait()
            total = small_buf[i - 1] + small_in[i - 1]
            if i == 5:
                small_z[...] = total
                return
            small_buf[i] = total
        remote(small_buf.at[i], small_in.at[i], send_m.at[i], recv_m.at[i], small_ways[i]).start()

    def run(step, *names):
        for name in names:
            if name == "m":
                small_step(step)
            elif step == STEPS[5]:
                store(name)
            else:
                getattr(tasks[name], step)()

    def ticks(place, at=None):
        for index, step, task in SCHEDULE.get(place, ()):
            work = lambda step=step, task=task: run(STEPS[step], TASKS[task])
            if at is None or isinstance(at, int):
                if at in (None, index):
                    work()
            else:
                pl.when(at == index)(work)

    links.met(links.partners)
    run(STEPS[0], "d0", "d1", "d2", "u0", "u1", "u2", "o")
    late = [
        later(normed, normed_v),
        later(w_qkv, w_qkv_v),
        later(gmid, gmid_v),
        later(stem, stem_v),
        later(slope_two, slope_two_v),
        later(w_two, w_two_v),
    ]
    for copy in first:
        copy.wait()
    for head in range(2, 4):
        et_load(head, head).start()

    @pl.loop(0, pairs)
    def _(p):
        for h in range(2):
            et_load(2 * p + h, (2 * p + h) % 4).wait()
        pair_back(
            p,
            q_v,
            k_v,
            v_v,
            lambda h: pool.at[3 + (2 * p + h) % 4],
            inverse,
            gctx_v,
            ctx_v,
            d_ref.at[0],
            d_ref.at[1],
            d_ref.at[2],
            sums_a_ref,
            ds_v,
            lambda: ticks("middle", p),
        )

        @pl.when(p == 0)
        def _():
            for copy in late:
                copy.start()

        @pl.when(p + 2 < pairs)
        def _():
            for h in range(2):
                et_load(2 * p + 4 + h, (2 * p + h) % 4).start()

        ticks("pairs", p)

    acts = [load(act_even, pool.at[5]), load(act_odd, pool.at[6])]
    for copy in late:
        copy.wait()
    ones = lambda v: jnp.sum(v, axis=0, keepdims=True)
    normed_t, two_v, two_ahead, two_t, two_ahead_t = (pool.at[i] for i in range(5))
    act_v = [pool.at[5], pool.at[6]]
    even_v, odd_v = pool.at[0], d_ref.at[2]
    gw_two = [pool.at[7 + k] for k in range(3)]
    sums_ref[...] = jnp.zeros_like(sums_ref)

    @unrolled(steps)
    def _(i):
        rows = pl.ds(i * BLOCK, BLOCK)
        normed_t[:, rows] = turned(normed_v[rows])

    ticks("turn")

    @unrolled(3)
    def _(j):
        cols = pl.ds(j * width, width)
        gw_qkv[:, cols] = mm(normed_t[...], d_ref[j]).astype(bf16)
        ticks("qkv", j)

    run(STEPS[0], "q0", "q1", "q2")

    @unrolled(steps)
    def _(i):
        rows = pl.ds(i * BLOCK, BLOCK)
        grad = (
            mm_nt(d_ref[0, rows], w_qkv_v[:, 0:width])
            + mm_nt(d_ref[1, rows], w_qkv_v[:, width : 2 * width])
            + mm_nt(d_ref[2, rows], w_qkv_v[:, 2 * width : 3 * width])
        )
        stem = stem_v[rows].astype(f32)
        centred = stem - mean_of(stem)
        scale = lax.rsqrt(mean_of(centred * centred) + epsilon)
        unit = centred * scale
        gained = grad * row_of(gain_ref)
        back = scale * (gained - mean_of(gained) - unit * mean_of(gained * unit))
        grad_stem = (gmid_v[rows] + back).astype(bf16).astype(f32)
        two = (grad_stem * slope_two_v[rows].astype(f32)).astype(bf16)
        two_v[rows] = two
        two_t[:, rows] = turned(two)
        sums_ref[0:1] += ones(grad * unit)
        sums_ref[1:2] += ones(grad)
        sums_ref[2:3] += ones(two.astype(f32))
        ticks("rows", i)

    slope_v = d_ref
    for copy in acts:
        copy.wait()
    slopes = [load(slope_even, slope_v.at[0]), load(slope_odd, slope_v.at[1])]
    for cols in chunks(width, BLOCK):
        two_ahead[:, cols] = shifted(two_v[:, cols].astype(f32), -1, 0).astype(bf16)

    @unrolled(steps)
    def _(i):
        rows = pl.ds(i * BLOCK, BLOCK)
        two_ahead_t[:, rows] = turned(two_ahead[rows])

    ticks("ahead")

    for copy in slopes:
        copy.wait()

    @unrolled(steps)
    def _(i):
        rows = pl.ds(i * BLOCK, BLOCK)
        even = mm_nt(two_v[rows], w_two_v[1]) * slope_v[0, rows].astype(f32)
        odd = mm_nt(two_v[rows], w_two_v[2]) + mm_nt(two_ahead[rows], w_two_v[0])
        odd = odd * slope_v[1, rows].astype(f32)
        even, odd = even.astype(bf16), odd.astype(bf16)
        even_v[rows] = even
        odd_v[rows] = odd
        sums_ref[3:4] += ones(even.astype(f32)) + ones(odd.astype(f32))
        ticks("convs", i)

    run(STEPS[0], "m")

    total_one = jnp.zeros((3 * bins, width), f32)
    for offset, grad_ref in ((0, even_v), (1, odd_v)):
        picked = [
            mm_nt(taps_ref[:, 2 * i * BLOCK : 2 * (i + 1) * BLOCK], pick_frames(BLOCK, 2 * BLOCK, offset))
            for i in range(steps)
        ]
        total_one += mm(jnp.concatenate(picked, axis=1).astype(bf16), grad_ref[...])
    share = bins // 4
    spread = []
    for z in range(4):
        spread += [total_one[(4 * j + z) * share : (4 * j + z + 1) * share] for j in range(3)]
        spread.append(jnp.zeros((64 - 3 * share, width), f32))
    gw_one[...] = jnp.concatenate(spread, axis=0).T.astype(bf16)
    run(STEPS[0], "n")
    ticks("one")

    even, odd = even_v[...], odd_v[...]
    mel_even = (
        mm_nt(odd, w_one_ref[0])
        + mm_nt(even, w_one_ref[1])
        + shifted(mm_nt(odd, w_one_ref[2]), 1, 0)
    )
    mel_odd = (
        shifted(mm_nt(even, w_one_ref[0]), -1, 0)
        + mm_nt(odd, w_one_ref[1])
        + mm_nt(even, w_one_ref[2])
    )
    mel_even, mel_odd = turned(mel_even), turned(mel_odd)
    share = bins // 4
    given = [[] for _ in range(4)]
    for i in range(steps):
        cols = slice(i * BLOCK, (i + 1) * BLOCK)
        frames = slice(2 * i * BLOCK, 2 * (i + 1) * BLOCK)
        gmel = mm(mel_even[:, cols], pick_frames(BLOCK, 2 * BLOCK, 0))
        gmel += mm(mel_odd[:, cols], pick_frames(BLOCK, 2 * BLOCK, 1))
        for z in range(4):
            given[z].append(gmel[z * share : (z + 1) * share])
    for z in range(4):
        gmel_out[z] = stacked(jnp.concatenate(given[z], axis=1)).astype(bf16)
    gmel_copies = [
        remote(gmel_out.at[(links.chan + r) % 4], gmel_in.at[r - 1], send_g.at[r - 1], recv_g.at[r - 1], links.by_z[r - 1])
        for r in (1, 2, 3)
    ]
    for copy in gmel_copies:
        copy.start()
    ticks("mel")
    for k, (left, right) in enumerate(((two_ahead_t, 1), (two_t, 0), (two_t, 1))):
        gw_two[k][...] = mm(left[...], act_v[right][...]).astype(bf16)
        run(STEPS[0], f"t{2 * k}", f"t{2 * k + 1}")
        ticks("two", k)
    ticks("tail")

    for copy in gmel_copies:
        copy.wait()
    placed = by_place(links, gmel_out, gmel_in, share)
    gmel_z[...] = jnp.concatenate([part[:, None] for part in placed], axis=1).astype(bf16)
    ticks("end")


def run_back(operands):
    joined, et, w_one, taps = operands[0], operands[1], operands[16], operands[17]
    length, width = operands[4].shape
    block, quarter = width // 8, width // 4
    bins, frames = w_one.shape[1], taps.shape[1]
    held = pl.BlockSpec(memory_space=pltpu.VMEM)
    far = pl.BlockSpec(memory_space=pl.ANY)
    near = (2, 9, 16, 17, 22, 23)
    part, third = operands[19].shape[2], operands[20].shape[3]
    square = (length, width)
    vmem = lambda *shape: pltpu.VMEM(shape, bf16)
    scratch = [
        vmem(10, *square),
        vmem(3, *square),
        vmem(width, 3 * width),
        pltpu.VMEM(square, f32),
        vmem(*square),
        vmem(*square),
        vmem(*square),
        vmem(3, width, width),
        vmem(width, 3 * width),
        vmem(width, 256),
        pltpu.VMEM((8, width), f32),
        pltpu.VMEM((8, width), f32),
        *bufs_for(2, (width, part), 1, 0),
        *bufs_for(2, (quarter, part), 4, 3),
        *bufs_for(1, (width, part), 2, 2, 0),
        *bufs_for(1, (quarter, part), 4, 3),
        *bufs_for(3, (block, third), 2, 2, 0),
        *bufs_for(3, (block, third // 4), 4, 3),
        *bufs_for(1, (block, width), 4, 4, 2, 0),
        *bufs_for(1, (block, 256), 4, 3),
        *bufs_for(3, (block // 3, 3 * width), 4, 2, 0),
        *bufs_for(3, (block // 3, 640), 4, 3),
        *bufs_for(6, (block // 2, width), 4, 2, 0),
        *bufs_for(6, (block // 2, 256), 4, 3),
        *bufs_for(1, (block, 256), 4, 2, 0),
        *bufs_for(1, (block, 128), 4, 3),
        pltpu.VMEM((5, 16, width), f32),
        pltpu.VMEM((5, 16, width), f32),
        vmem(4, bins // 4 * frames // 128, 128),
        vmem(3, bins // 4 * frames // 128, 128),
        *sems_for(17),
        pltpu.SemaphoreType.DMA((15,)),
        pltpu.SemaphoreType.DMA((4,)),
        pltpu.SemaphoreType.DMA((6,)),
        pltpu.SemaphoreType.DMA((6,)),
        pltpu.SemaphoreType.DMA((3,)),
        pltpu.SemaphoreType.DMA((3,)),
    ]
    shapes = (
        (block, width),
        (quarter, 3 * part),
        (block, quarter),
        (block, 3 * quarter),
        (3, block, quarter),
        (block, 128),
        (16, width),
    )
    return pl.pallas_call(
        back_kernel,
        in_specs=[held if i in near else far for i in range(len(operands))],
        out_specs=[held] * 8,
        out_shape=[jax.ShapeDtypeStruct(s, f32) for s in shapes]
        + [jax.ShapeDtypeStruct((bins // 4, 4, frames), bf16)],
        scratch_shapes=scratch,
        compiler_params=pltpu.CompilerParams(
            vmem_limit_bytes=VMEM_LIMIT, collective_id=2, has_side_effects=True
        ),
        name="back",
    )(*operands)


def last_kernel(*refs):
    lengths_ref, language_ref, down, up, out, qkv, two, one, small, gmel = refs[:10]
    outs = refs[10:]
    group_z, gmel_z, one_z, b_one_z, two_z, b_two_z, gain_a_z, bias_a_z, qkv_z, b_query_z = outs[:10]
    b_value_z, out_z, b_out_z, gain_b_z, bias_b_z, up_z, b_up_z, down_z, b_down_z = outs[10:]
    group = lax.broadcasted_iota(jnp.int32, (1, 128), 1)

    def count(c, total):
        return total + jnp.where(group == language_ref[c], lengths_ref[c], 0)

    frames = lax.fori_loop(0, lengths_ref.shape[0], count, jnp.zeros((1, 128), jnp.int32))
    width = small.shape[1]
    loss = small[0:1, 0:128] / (width * jnp.maximum(frames, 1).astype(f32))
    group_z[...] = loss.reshape(-1)[: group_z.shape[0]]
    gmel_z[...] = gmel[...]
    vectors = (b_one_z, b_two_z, gain_a_z, bias_a_z, b_query_z, b_value_z, b_out_z, gain_b_z, bias_b_z, b_down_z)
    for i, ref in enumerate(vectors):
        ref[...] = small[1 + i]
    for k in range(b_up_z.shape[0] // width):
        b_up_z[pl.ds(k * width, width)] = small[11 + k]
    up_z[...] = up[...]
    out_z[...] = out[...]
    qkv_z[...] = qkv[...]
    down_z[...] = down[...]
    for j in range(3):
        two_z[j] = two[j].T
    bins = one_z.shape[1]
    turned_one = one[...].T
    for j in range(3):
        one_z[j] = turned_one[j * bins : (j + 1) * bins]


def run_whole(kernel, name, operands, results, scratch):
    held = pl.BlockSpec(memory_space=pltpu.VMEM)
    scalar = pl.BlockSpec(memory_space=pltpu.SMEM)
    return pl.pallas_call(
        kernel,
        in_specs=[scalar if o.dtype == jnp.int32 else held for o in operands],
        out_specs=[held] * len(results),
        out_shape=[jax.ShapeDtypeStruct(*r) for r in results],
        scratch_shapes=[pltpu.VMEM(*s) for s in scratch],
        compiler_params=pltpu.CompilerParams(vmem_limit_bytes=VMEM_LIMIT),
        name=name,
    )(*operands)


def on_device(
    mel_input,
    w_conv1,
    b_conv1,
    w_conv2,
    b_conv2,
    gain_attn,
    bias_attn,
    w_qkv,
    b_query,
    b_value,
    w_out,
    b_out,
    gain_mlp,
    bias_mlp,
    w_up,
    b_up,
    w_down,
    b_down,
    target,
    lengths,
    row_clip,
    language,
):
    clip_count, frame_count, model_width = target.shape
    mel_count = mel_input.shape[2]
    bins = w_conv1.shape[1]
    fast = lax.axis_size(DP) == 8 and lax.axis_size(CHAN) == 4
    square = (frame_count, model_width)
    (
        taps,
        act_even,
        act_odd,
        slope_even,
        slope_odd,
        slope_two,
        stem,
        normed_a,
        joined,
    ) = run_stem(
        (mel_input, w_conv1, b_conv1, b_conv2, gain_attn, bias_attn, b_query, b_value),
        (w_conv2, jnp.asarray(sinusoids(frame_count, model_width)), w_qkv),
        frame_count,
    )
    context, weights_t, inverse = attend(joined, row_clip, lengths)
    inner = w_up.shape[1]
    deep = (model_width, inner)
    vectors = (b_out, gain_mlp, bias_mlp, b_up, b_down)
    if fast:
        (
            block_rows,
            grad_context,
            grad_middle,
            grad_w_out,
            half_down,
            core_down,
            core_up,
            sums_b,
            grad_b_up,
        ) = run_mlp_send((row_clip, lengths, language), (context, stem, w_out, w_up, w_down, target[0]), vectors)
    else:
        (
            block_rows,
            grad_context,
            grad_middle,
            grad_w_up,
            grad_w_down_t,
            grad_w_out,
            sums_b,
            grad_b_up,
        ) = run_whole(
            mlp_kernel,
            "mlp",
            (
                row_clip,
                lengths,
                language,
                context,
                stem,
                w_out,
                b_out,
                gain_mlp,
                bias_mlp,
                w_up,
                b_up,
                w_down,
                b_down,
                target[0],
            ),
            [
                (square, bf16),
                (square, bf16),
                (square, f32),
                (deep, bf16),
                (deep, bf16),
                ((model_width, model_width), bf16),
                ((8, model_width), f32),
                ((1, inner), f32),
            ],
            [
                (square, f32),
                (square, bf16),
                (square, bf16),
                ((frame_count, inner), bf16),
                ((frame_count, inner), bf16),
                (square, bf16),
                (square, bf16),
                ((1, inner), f32),
            ],
        )
    if fast:
        final_up, down_z, final_out, final_qkv, two_z, one_z, small, grad_mel = run_back(
            (
                joined,
                weights_t,
                inverse,
                grad_context,
                context,
                w_qkv,
                grad_middle,
                stem,
                normed_a,
                gain_attn,
                slope_two,
                w_conv2,
                act_even,
                act_odd,
                slope_even,
                slope_odd,
                w_conv1,
                taps,
                half_down,
                core_down,
                core_up,
                grad_w_out,
                sums_b,
                grad_b_up,
            )
        )
        part = bins // lax.axis_size(CHAN)
        vector = ((model_width,), f32)
        share = model_width // 4
        block = model_width // 8
        finals = run_whole(
            last_kernel,
            "last",
            (
                lengths,
                language,
                down_z,
                final_up,
                final_out,
                final_qkv,
                two_z,
                one_z,
                small,
                grad_mel,
            ),
            [
                ((GROUPS,), f32),
                (mel_input.shape, bf16),
                ((3, part, block), f32),
                vector,
                ((3, share, block), f32),
                vector,
                vector,
                vector,
                ((block, 3 * share), f32),
                vector,
                vector,
                ((block, share), f32),
                vector,
                vector,
                vector,
                ((block, inner // 4), f32),
                ((inner,), f32),
                ((share, inner // 8), f32),
                vector,
            ],
            [],
        )
        return (block_rows.reshape(target.shape), *finals[:17], finals[17].T, finals[18])
    else:
        *grads, sums_a = attend_back(joined, weights_t, inverse, grad_context, context)
        weight = (model_width, model_width)
        grad_w_qkv, grad_w_two_t, grad_w_one_t, back_mel, sums_c = run_whole(
            stem_back_kernel,
            "stem_back",
            (
                *grads,
                w_qkv,
                grad_middle,
                stem,
                normed_a,
                gain_attn,
                slope_two,
                w_conv2,
                act_even,
                act_odd,
                slope_even,
                slope_odd,
                w_conv1,
                taps,
            ),
            [
                ((model_width, 3 * model_width), bf16),
                ((3,) + weight, bf16),
                ((model_width, 256), bf16),
                ((bins, mel_count), bf16),
                ((8, model_width), f32),
            ],
            [
                ((model_width, frame_count), bf16),
                (square, bf16),
                (square, bf16),
                ((model_width, frame_count), bf16),
                ((model_width, frame_count), bf16),
                (square, bf16),
                (square, bf16),
            ],
        )
        grad_mel = lax.all_to_all(back_mel[:, None], CHAN, split_axis=0, concat_axis=1, tiled=True)

        small = jnp.concatenate(
            [
                sums_b[0:1],
                sums_c[3:4],
                sums_c[2:3],
                sums_c[0:2],
                sums_a[0:2],
                sums_b[4:5],
                sums_b[2:4],
                sums_b[1:2],
                grad_b_up.reshape(-1, model_width),
                jnp.zeros((1, model_width), f32),
            ]
        )

        def scatter(values, dp_at, chan_at):
            part = lax.psum_scatter(values, DP, scatter_dimension=dp_at, tiled=True)
            return lax.psum_scatter(part, CHAN, scatter_dimension=chan_at, tiled=True).astype(f32)

        final_down = scatter(grad_w_down_t, 1, 0).T
        final_up = scatter(grad_w_up, 0, 1)
        final_out = scatter(grad_w_out, 0, 1)
        final_qkv = scatter(grad_w_qkv, 0, 1)
        part_two = scatter(grad_w_two_t, 1, 2).transpose(0, 2, 1)
        one_rows = grad_w_one_t[:, : 3 * bins].reshape(-1, 3, bins).transpose(1, 2, 0)
        part_one = scatter(one_rows, 2, 1)
        small = lax.psum(small, (DP, CHAN))
    totals_all = [small[0, :GROUPS]] + [small[i] for i in range(1, 11)]
    totals_all.insert(10, small[11:15].reshape(-1))
    group_ids = jnp.arange(GROUPS, dtype=jnp.int32)
    member_all = language[:, None] == group_ids[None, :]
    frames_group = jnp.sum(jnp.where(member_all, lengths[:, None], 0), axis=0)
    group_loss = totals_all[0] / (model_width * jnp.maximum(frames_group, 1).astype(f32))
    return (
        block_rows.reshape(target.shape),
        group_loss,
        grad_mel,
        part_one,
        totals_all[1],
        part_two,
        totals_all[2],
        totals_all[3],
        totals_all[4],
        final_qkv,
        totals_all[5],
        totals_all[6],
        final_out,
        totals_all[7],
        totals_all[8],
        totals_all[9],
        final_up,
        totals_all[10],
        final_down,
        totals_all[11],
    )


def solution(mesh):
    whole = P()
    by_row = P((DP, CHAN), None, None)
    return jax.shard_map(
        on_device,
        mesh=mesh,
        in_specs=(P(CHAN, DP, None),) + (whole,) * 17 + (by_row,) + (whole,) * 3,
        out_specs=(
            by_row,
            whole,
            P(CHAN, DP, None),
            P(None, CHAN, DP),
            whole,
            P(None, CHAN, DP),
            whole,
            whole,
            whole,
            P(DP, CHAN),
            whole,
            whole,
            P(DP, CHAN),
            whole,
            whole,
            whole,
            P(DP, CHAN),
            whole,
            P(DP, CHAN),
            whole,
        ),
        check_vma=False,
    )
```

```python
import math
from types import SimpleNamespace

import jax
import jax.numpy as jnp
import numpy as np
from jax import lax
from jax.experimental import pallas as pl
from jax.experimental.pallas import tpu as pltpu
from jax.sharding import PartitionSpec as P

HEAD_DIM = 64
GROUPS = 99
DP, CHAN = "dp", "chan"

bf16 = jnp.bfloat16
f32 = jnp.float32
epsilon = 1e-05
masked_score = -1e30


def sinusoids(length, channels):
    half_width = channels // 2
    increment = math.log(10000.0) / (half_width - 1)
    inverse = np.exp(-increment * np.arange(half_width, dtype=np.float64))
    angles = np.arange(length, dtype=np.float64)[:, None] * inverse[None, :]
    return np.concatenate([np.sin(angles), np.cos(angles)], axis=1).astype(np.float32)


def lookup(row_id, table):
    matches = row_id == jnp.arange(table.shape[0], dtype=jnp.int32)
    return jnp.sum(jnp.where(matches, table, 0))


def mm(a, b):
    return jnp.dot(a, b, preferred_element_type=f32)


def mm_nt(a, b):
    return lax.dot_general(a, b, (((1,), (1,)), ((), ())), preferred_element_type=f32)


def mm_tn(a, b):
    return lax.dot_general(a, b, (((0,), (0,)), ((), ())), preferred_element_type=f32)


BLOCK = 256
VMEM_LIMIT = 61 * 1024 * 1024


def gelu_pair(v):
    phi = 0.5 + 0.5 * lax.erf(v * math.sqrt(0.5))
    return v * phi, phi + v * (jnp.exp(-0.5 * (v * v)) * (1.0 / math.sqrt(2.0 * math.pi)))


def unrolled(count):
    def run(body):
        for i in range(count):
            body(i)

    return run


def row_of(ref):
    return ref[...].astype(f32).reshape(1, -1)


def own_clip(row_clip_ref):
    return row_clip_ref[lax.axis_index(DP) * lax.axis_size(CHAN) + lax.axis_index(CHAN)]


def turned(values):
    return values.astype(f32).T.astype(bf16)


def chunks(length, size):
    return [slice(at, min(at + size, length)) for at in range(0, length, size)]


def attend_kernel(row_clip_ref, lengths_ref, q_ref, k_ref, v_ref, ctx_ref, et_ref, inv_ref):
    length, width = q_ref.shape[0], 2 * HEAD_DIM
    lane = lax.broadcasted_iota(jnp.int32, (length, width), 1)
    frame = lax.broadcasted_iota(jnp.int32, (length, width), 0)
    bias = jnp.where(frame < lengths_ref[own_clip(row_clip_ref)], 0.0, masked_score)
    for pair in range(q_ref.shape[1] // width):
        cols = slice(pair * width, (pair + 1) * width)
        q = q_ref[:, cols].astype(f32) * HEAD_DIM ** (-0.5)
        k = k_ref[:, cols].astype(f32)
        v_t = turned(v_ref[:, cols])
        for h in range(2):
            mine = lane // HEAD_DIM == h
            spare = lane == HEAD_DIM * (1 - h)
            own_q = jnp.where(mine, q, jnp.where(spare, 1.0, 0.0)).astype(bf16)
            own_k = jnp.where(mine, k, jnp.where(spare, bias, 0.0)).astype(bf16)
            scores = mm_nt(own_k, own_q)
            weight = jnp.exp(scores - jnp.max(scores, axis=0, keepdims=True))
            et_ref[2 * pair + h] = weight.astype(bf16)
            inv_ref[2 * pair + h] = 1.0 / jnp.sum(weight, axis=0, keepdims=True)
        found = [
            mm(v_t[h * HEAD_DIM : (h + 1) * HEAD_DIM], et_ref[2 * pair + h]) * inv_ref[2 * pair + h]
            for h in range(2)
        ]
        ctx_ref[:, cols] = jnp.concatenate(found, axis=0).T.astype(bf16)


def attend_back_kernel(
    q_ref, k_ref, v_ref, et_ref, inv_ref, gctx_ref, ctx_ref, dq_ref, dk_ref, dv_ref, sums_ref, ds_ref
):
    length, width = q_ref.shape
    lane = lax.broadcasted_iota(jnp.int32, (length, width), 1)
    row = lax.broadcasted_iota(jnp.int32, (width, length), 0)
    scale = HEAD_DIM ** (-0.5)
    grad_t = gctx_ref[...].astype(f32).T * jnp.where(row < HEAD_DIM, inv_ref[0], inv_ref[1])
    grad_t = grad_t.astype(bf16).astype(f32)
    grad = grad_t.T
    inner_all = grad_t * ctx_ref[...].astype(f32).T
    k_t = turned(k_ref[...])
    q = q_ref[...].astype(f32) * scale
    v = v_ref[...].astype(f32)
    dq_t = []
    dk = jnp.zeros((length, width), f32)
    dv = jnp.zeros((length, width), f32)
    for h in range(2):
        at = HEAD_DIM * (1 - h)
        mine = lane // HEAD_DIM == h
        inner = jnp.sum(inner_all[h * HEAD_DIM : (h + 1) * HEAD_DIM], axis=0, keepdims=True)
        high = inner.astype(bf16).astype(f32)
        own_grad_t = jnp.where(row // HEAD_DIM == h, grad_t, 0.0)
        own_grad_t = jnp.where(row == at, -high, jnp.where(row == at + 1, high - inner, own_grad_t))
        own_grad_t = own_grad_t.astype(bf16)
        own_v = jnp.where(mine, v, jnp.where((lane == at) | (lane == at + 1), 1.0, 0.0)).astype(bf16)
        own_q = jnp.where(mine, q, 0.0).astype(bf16)
        own_grad = jnp.where(mine, grad, 0.0).astype(bf16)
        for cols in chunks(length, BLOCK):
            shifted = mm(own_v, own_grad_t[:, cols])
            ds_ref[:, cols] = (et_ref[h, :, cols].astype(f32) * shifted).astype(bf16)
        dk += mm(ds_ref[...], own_q)
        dv += mm(et_ref[h], own_grad)
        dq_t.append(mm(k_t[h * HEAD_DIM : (h + 1) * HEAD_DIM], ds_ref[...]))
    dq = (jnp.concatenate(dq_t, axis=0).T * scale).astype(bf16)
    dv = dv.astype(bf16)
    dq_ref[...] = dq
    dk_ref[...] = dk.astype(bf16)
    dv_ref[...] = dv
    sums_ref[0:1] = jnp.sum(dq.astype(f32), axis=0, keepdims=True)
    sums_ref[1:2] = jnp.sum(dv.astype(f32), axis=0, keepdims=True)


def attend(joined, row_clip, lengths):
    length, width = joined.shape[0], 4 * HEAD_DIM
    pairs = joined.shape[1] // (3 * width)
    block = lambda part: pl.BlockSpec((length, width), lambda p, *_: (0, part * pairs + p))
    return pl.pallas_call(
        attend_kernel,
        grid_spec=pltpu.PrefetchScalarGridSpec(
            num_scalar_prefetch=2,
            grid=(pairs,),
            in_specs=[block(0), block(1), block(2)],
            out_specs=[
                block(0),
                pl.BlockSpec((4, length, length), lambda p, *_: (p, 0, 0)),
                pl.BlockSpec((4, 1, length), lambda p, *_: (p, 0, 0)),
            ],
        ),
        out_shape=[
            jax.ShapeDtypeStruct((length, pairs * width), bf16),
            jax.ShapeDtypeStruct((4 * pairs, length, length), bf16),
            jax.ShapeDtypeStruct((4 * pairs, 1, length), f32),
        ],
        compiler_params=pltpu.CompilerParams(vmem_limit_bytes=VMEM_LIMIT),
        name="attend",
    )(row_clip, lengths, joined, joined, joined)


def attend_back(joined, et, inverse, grad_context, context):
    length, width = joined.shape[0], 2 * HEAD_DIM
    pairs = joined.shape[1] // (3 * width)
    block = lambda part: pl.BlockSpec((length, width), lambda p: (0, part * pairs + p))
    one = jax.ShapeDtypeStruct((length, pairs * width), bf16)
    return pl.pallas_call(
        attend_back_kernel,
        grid=(pairs,),
        in_specs=[
            block(0),
            block(1),
            block(2),
            pl.BlockSpec((2, length, length), lambda p: (p, 0, 0)),
            pl.BlockSpec((2, 1, length), lambda p: (p, 0, 0)),
            block(0),
            block(0),
        ],
        out_specs=[block(0), block(0), block(0), pl.BlockSpec((8, width), lambda p: (0, p))],
        out_shape=[one, one, one, jax.ShapeDtypeStruct((8, pairs * width), f32)],
        scratch_shapes=[pltpu.VMEM((length, length), bf16)],
        compiler_params=pltpu.CompilerParams(vmem_limit_bytes=VMEM_LIMIT),
        name="attend_back",
    )(joined, joined, joined, et, inverse, grad_context, context)


def mean_of(values):
    return jnp.mean(values, axis=-1, keepdims=True)


def mlp_body(v, live, spoken, wait, done, tick):
    length, width = v.stem.shape
    inner = v.w_up.shape[1]
    row_steps, wide_steps = length // BLOCK, inner // width
    ones = lambda values: jnp.sum(values, axis=0, keepdims=True)
    v.sums[...] = jnp.zeros_like(v.sums)
    v.b_up_line[...] = row_of(v.b_up)
    wait(0, 3, 1)

    @unrolled(row_steps)
    def _(i):
        rows = pl.ds(i * BLOCK, BLOCK)
        middle = v.stem[rows].astype(f32) + mm(v.ctx[rows], v.w_out[...]) + row_of(v.b_out)
        v.mid[rows] = middle
        centred = middle - mean_of(middle)
        scale = lax.rsqrt(mean_of(centred * centred) + epsilon)
        v.normed[rows] = (centred * scale * row_of(v.gain) + row_of(v.bias)).astype(bf16)

    wait(3, 1, 2)

    @unrolled(wide_steps)
    def _(j):
        cols = pl.ds(j * width, width)
        upward = mm(v.normed[...], v.w_up[:, cols]) + v.b_up_line[:, cols]
        hidden, slope = gelu_pair(upward)
        v.hidden[:, cols] = hidden.astype(bf16)
        v.slope[:, cols] = slope.astype(bf16)

    wait(4, 2, 0)

    @unrolled(row_steps)
    def _(i):
        rows = pl.ds(i * BLOCK, BLOCK)
        final = v.mid[rows] + mm(v.hidden[rows], v.w_down[...]) + row_of(v.b_down)
        v.out[rows] = final.astype(bf16)
        frame = i * BLOCK + lax.broadcasted_iota(jnp.int32, final.shape, 0)
        mismatch = jnp.where(frame < live, final - v.target[rows].astype(f32), 0.0)
        v.gmid[rows] = mismatch
        branch = mismatch.astype(bf16)
        v.branch[rows] = branch
        v.branch_t[:, rows] = turned(branch)
        v.normed_t[:, rows] = turned(v.normed[rows])
        v.sums[5:6] += ones(mismatch * mismatch)
        v.sums[1:2] += ones(branch.astype(f32))

    done("out")
    group = lax.broadcasted_iota(jnp.int32, (1, width), 1)
    loss = 0.5 * jnp.sum(v.sums[5:6], axis=1, keepdims=True)
    v.sums[0:1] = jnp.where(group == spoken, loss, 0.0)

    @unrolled(wide_steps)
    def _(j):
        cols = pl.ds(j * width, width)
        v.put_down(j, cols, mm(v.branch_t[...], v.hidden[:, cols]).astype(bf16))

    tick("down")

    @unrolled(wide_steps)
    def _(j):
        cols = pl.ds(j * width, width)
        grad = mm_nt(v.branch[...], v.w_down[cols]) * v.slope[:, cols].astype(f32)
        grad = grad.astype(bf16)
        v.gb_up[:, cols] = ones(grad.astype(f32))
        v.slope[:, cols] = grad
        v.put_up(j, cols, mm(v.normed_t[...], grad).astype(bf16))
        tick("tiles", j)

    tick("up")

    @unrolled(row_steps)
    def _(i):
        rows = pl.ds(i * BLOCK, BLOCK)
        grad = mm_nt(v.slope[rows], v.w_up[...])
        middle = v.mid[rows]
        centred = middle - mean_of(middle)
        scale = lax.rsqrt(mean_of(centred * centred) + epsilon)
        unit = centred * scale
        gained = grad * row_of(v.gain)
        back = scale * (gained - mean_of(gained) - unit * mean_of(gained * unit))
        grad_middle = v.gmid[rows] + back
        v.gmid[rows] = grad_middle
        attended = grad_middle.astype(bf16)
        v.branch[rows] = attended
        v.gctx[rows] = mm_nt(attended, v.w_out[...]).astype(bf16)
        v.normed_t[:, rows] = turned(v.ctx[rows])
        v.sums[2:3] += ones(grad * unit)
        v.sums[3:4] += ones(grad)
        v.sums[4:5] += ones(attended.astype(f32))
        done("gmid", i)
        done("gctx", i)
        tick("rows", i)

    v.gw_out[...] = mm(v.normed_t[...], v.branch[...]).astype(bf16)
    done("gw_out")
    tick("end")


def own_scalars(row_clip_ref, lengths_ref, language_ref):
    clip = own_clip(row_clip_ref)
    return lengths_ref[clip], language_ref[clip]


def mlp_kernel(row_clip, lengths, language, *refs):
    names = ("ctx", "stem", "w_out", "b_out", "gain", "bias", "w_up", "b_up", "w_down", "b_down", "target")
    names += ("out", "gctx", "gmid", "gw_up", "gw_down", "gw_out", "sums", "gb_up", "mid", "normed", "normed_t")
    names += ("hidden", "slope", "branch", "branch_t", "b_up_line")
    v = SimpleNamespace(**dict(zip(names, refs)))

    def put_down(j, cols, values):
        v.gw_down[:, cols] = values

    def put_up(j, cols, values):
        v.gw_up[:, cols] = values

    v.put_down, v.put_up = put_down, put_up
    nothing = lambda *_: None
    mlp_body(v, *own_scalars(row_clip, lengths, language), nothing, nothing, nothing)


def mlp_send_kernel(row_clip, lengths, language, *refs):
    far_in = ("ctx", "stem", "w_out", "w_up", "w_down", "target")
    far_out = ("out", "gctx", "gmid", "gw_out")
    near = ("b_out", "gain", "bias", "b_up", "b_down")
    names = far_in + near + far_out + ("half_down", "core_down", "core_up", "sums", "gb_up")
    given = SimpleNamespace(**dict(zip(names, refs)))
    held = far_in + far_out + ("mid", "normed", "normed_t", "hidden", "slope", "branch", "branch_t", "b_up_line")
    held += ("gw_up", "gw_blocks", "cin_d", "fin_d", "cin_u")
    rest = refs[len(names) :]
    v = SimpleNamespace(**dict(zip(held, rest)))
    for name in near + ("sums", "gb_up"):
        setattr(v, name, getattr(given, name))
    in_sems, out_sems = rest[len(held) : len(held) + 2]
    sems = SimpleNamespace(**dict(zip(SEMS, rest[len(held) + 2 :])))
    links = Links()
    links.greet([links.by_core, links.by_x, links.by_y])
    loads = [pltpu.make_async_copy(getattr(given, n), getattr(v, n), in_sems.at[i]) for i, n in enumerate(far_in)]
    for copy in loads[:3]:
        copy.start()
    width = v.stem.shape[1]
    part, third, block = given.half_down.shape[3], given.core_up.shape[3], given.core_up.shape[2]
    tasks = {}
    for k in range(3):
        source = lambda d, k=k: v.gw_blocks.at[d, :, pl.ds(k * part, part)]
        tasks[f"d{k}"] = Task(links, k != 0, sems, k, None, source, None, v.cin_d.at[k], v.fin_d.at[k], None, None, None)
    for k in range(3):
        source = rows_of(v.gw_up, block, k * third, third)
        tasks[f"u{k}"] = Task(links, k == 1, sems, 3 + k, None, source, None, v.cin_u.at[k], None, None, None, None)

    def put_down(j, cols, values):
        wide = v.gw_blocks.shape[2]
        for k in range(width // wide):
            v.gw_blocks[j * (width // wide) + k] = values[:, k * wide : (k + 1) * wide]

    def put_up(j, cols, values):
        for k in range(width // BLOCK):
            out = pl.ds((k * 4 + j) * BLOCK, BLOCK)
            v.gw_up[:, out] = values[:, k * BLOCK : (k + 1) * BLOCK]

    v.put_down, v.put_up = put_down, put_up
    leaving = []

    def leave(source, target):
        copy = pltpu.make_async_copy(source, target, out_sems.at[len(leaving)])
        copy.start()
        leaving.append(copy)

    steps = v.stem.shape[0] // BLOCK
    pieces = {"gmid": 8, "gctx": 8 + steps}

    def row_copy(name, i):
        rows = pl.ds(i * BLOCK, BLOCK)
        return pltpu.make_async_copy(getattr(v, name).at[rows], getattr(given, name).at[rows], out_sems.at[pieces[name] + i])

    def wait(first, count, ahead):
        for copy in loads[first : first + count]:
            copy.wait()
        for copy in loads[first + count : first + count + ahead]:
            copy.start()

    def done(name, i=None):
        if i is None:
            leave(getattr(v, name), getattr(given, name))
        else:
            row_copy(name, i).start()

    def tick(place, i=None):
        if place == "down":
            links.met([links.by_core, links.by_x, links.by_y])
            for k in range(3):
                tasks[f"d{k}"].begin()
        elif place == "tiles":
            pl.when(i == 1)(tasks["d0"].after_core)
            pl.when(i == 1)(tasks["d1"].after_core)
            pl.when(i == 3)(tasks["d2"].stop_at_core)
        elif place == "up":
            for k in range(3):
                tasks[f"u{k}"].begin()
            leave(v.cin_d.at[2], given.core_down)
        elif place == "rows":
            pl.when(i == 1)(tasks["u0"].stop_at_core)
            pl.when(i == 2)(tasks["u1"].stop_at_core)
        else:
            tasks["u2"].stop_at_core()
            leave(v.cin_u, given.core_up)
            for k in range(2):
                tasks[f"d{k}"].stop_at_first()
                leave(v.cin_d.at[k, pl.ds(0, 2)], given.half_down.at[k])

    mlp_body(v, *own_scalars(row_clip, lengths, language), wait, done, tick)
    for copy in leaving:
        copy.wait()
    for name in pieces:
        for i in range(steps):
            row_copy(name, i).wait()


def run_mlp_send(scalars, far, near):
    square, deep = far[0].shape, far[3].shape
    width, inner = deep
    block, part, third = width // 8, inner // 24, inner // 3
    in_smem = pl.BlockSpec(memory_space=pltpu.SMEM)
    in_vmem = pl.BlockSpec(memory_space=pltpu.VMEM)
    anywhere = pl.BlockSpec(memory_space=pl.ANY)
    whole = lambda x: pltpu.VMEM(x.shape, x.dtype)
    results = [
        (square, bf16),
        (square, bf16),
        (square, f32),
        ((width, width), bf16),
        ((2, 2, width, part), bf16),
        ((4, width, part), bf16),
        ((3, 4, block, third), bf16),
        ((8, width), f32),
        ((1, inner), f32),
    ]
    return pl.pallas_call(
        mlp_send_kernel,
        in_specs=[in_smem] * 3 + [anywhere] * len(far) + [in_vmem] * len(near),
        out_specs=[anywhere] * 7 + [in_vmem] * 2,
        out_shape=[jax.ShapeDtypeStruct(*r) for r in results],
        scratch_shapes=[whole(x) for x in far]
        + [pltpu.VMEM(*r) for r in results[:4]]
        + [
            pltpu.VMEM(square, f32),
            pltpu.VMEM(square, bf16),
            pltpu.VMEM(square, bf16),
            pltpu.VMEM((square[0], inner), bf16),
            pltpu.VMEM((square[0], inner), bf16),
            pltpu.VMEM(square, bf16),
            pltpu.VMEM(square, bf16),
            pltpu.VMEM((1, inner), f32),
            pltpu.VMEM(deep, bf16),
            pltpu.VMEM((8, width, inner // 8), bf16),
            *bufs_for(3, (width, part), 4, 2),
            *bufs_for(3, (block, third), 4),
            pltpu.SemaphoreType.DMA((len(far),)),
            pltpu.SemaphoreType.DMA((8 + 2 * (square[0] // BLOCK),)),
            *sems_for(6),
        ],
        compiler_params=pltpu.CompilerParams(
            vmem_limit_bytes=VMEM_LIMIT, collective_id=1, has_side_effects=True
        ),
        name="mlp",
    )(*scalars, *far, *near)


def shifted(values, step, axis):
    length = values.shape[axis]
    moved = pltpu.roll(values, step % length, axis)
    place = lax.broadcasted_iota(jnp.int32, values.shape, axis)
    return jnp.where(place == (0 if step > 0 else length - 1), 0.0, moved)


def pick_frames(slots, frames, offset):
    slot = lax.broadcasted_iota(jnp.int32, (slots, frames), 0)
    frame = lax.broadcasted_iota(jnp.int32, (slots, frames), 1)
    return jnp.where(frame == 2 * slot + offset, 1.0, 0.0).astype(bf16)


def flat_taps(ref):
    return ref[...].reshape(-1, ref.shape[-1])


def stem_kernel(*refs):
    near = ("mel", "w_one", "b_one", "b_two", "gain", "bias", "b_query", "b_value")
    far_in = ("w_two", "pos", "w_qkv")
    whole_out = ("taps", "act_even", "act_odd", "slope_even", "slope_odd")
    row_out = ("slope_two", "stem", "normed", "joined")
    far_out = whole_out + row_out
    names = near + far_in + far_out
    given = SimpleNamespace(**dict(zip(names, refs)))
    rest = refs[len(names) :]
    held = far_in + far_out + ("behind", "mel_out", "mel_in")
    v = SimpleNamespace(**dict(zip(held, rest)))
    in_sems, out_sems, send_g, recv_g = rest[len(held) :]
    loads = {}
    for i, name in enumerate(far_in):
        loads[name] = pltpu.make_async_copy(getattr(given, name), getattr(v, name), in_sems.at[i])
        loads[name].start()
    leaving = []

    def leave(source, target):
        copy = pltpu.make_async_copy(source, target, out_sems.at[len(leaving)])
        copy.start()
        leaving.append(copy)

    length, width = v.stem.shape
    steps = length // BLOCK
    links = Links()
    links.greet(links.by_z)
    bins_given = given.mel[...].astype(f32)
    share = bins_given.shape[0]
    for z in range(4):
        v.mel_out[z] = stacked(bins_given[:, z]).astype(bf16)
    links.met(links.by_z)
    copies = [
        remote(v.mel_out.at[(links.chan + r) % 4], v.mel_in.at[r - 1], send_g.at[r - 1], recv_g.at[r - 1], links.by_z[r - 1])
        for r in (1, 2, 3)
    ]
    for copy in copies:
        copy.start()
    picks = [pick_frames(BLOCK, 2 * BLOCK, offset) for offset in range(2)]
    for copy in copies:
        copy.wait()
    mel = jnp.concatenate(by_place(links, v.mel_out, v.mel_in, share), axis=0)
    taps = jnp.concatenate([shifted(mel, 1, 1), mel, shifted(mel, -1, 1)], axis=0).astype(bf16)
    v.taps[...] = taps
    leave(v.taps, given.taps)
    w_one = flat_taps(given.w_one)
    for pick, act_ref, slope_ref in (
        (picks[1], v.act_odd, v.slope_odd),
        (picks[0], v.act_even, v.slope_even),
    ):
        for i in range(steps):
            rows = slice(i * BLOCK, (i + 1) * BLOCK)
            frames = slice(2 * i * BLOCK, 2 * (i + 1) * BLOCK)
            picked = mm_nt(pick, taps[:, frames]).astype(bf16)
            act, slope = gelu_pair(mm(picked, w_one) + row_of(given.b_one))
            act_ref[rows] = act.astype(bf16)
            slope_ref[rows] = slope.astype(bf16)
    for name in whole_out[1:]:
        leave(getattr(v, name), getattr(given, name))
    for cols in chunks(width, BLOCK):
        v.behind[:, cols] = shifted(v.act_odd[:, cols].astype(f32), 1, 0).astype(bf16)
    for name in far_in:
        loads[name].wait()
    query, key, value = (slice(part * width, (part + 1) * width) for part in range(3))
    for i in range(steps):
        rows = slice(i * BLOCK, (i + 1) * BLOCK)
        two = (
            mm(v.behind[rows], v.w_two[0])
            + mm(v.act_even[rows], v.w_two[1])
            + mm(v.act_odd[rows], v.w_two[2])
            + row_of(given.b_two)
        )
        act, slope = gelu_pair(two)
        v.slope_two[rows] = slope.astype(bf16)
        stem = (act + v.pos[rows]).astype(bf16)
        v.stem[rows] = stem
        stem = stem.astype(f32)
        centred = stem - mean_of(stem)
        scale = lax.rsqrt(mean_of(centred * centred) + epsilon)
        normed = (centred * scale * row_of(given.gain) + row_of(given.bias)).astype(bf16)
        v.normed[rows] = normed
        v.joined[rows, query] = (mm(normed, v.w_qkv[:, query]) + row_of(given.b_query)).astype(bf16)
        v.joined[rows, key] = mm(normed, v.w_qkv[:, key]).astype(bf16)
        v.joined[rows, value] = (mm(normed, v.w_qkv[:, value]) + row_of(given.b_value)).astype(bf16)
        for name in row_out:
            leave(getattr(v, name).at[pl.ds(i * BLOCK, BLOCK)], getattr(given, name).at[pl.ds(i * BLOCK, BLOCK)])
    for copy in leaving:
        copy.wait()


def run_stem(near, far, length):
    width, frames = near[1].shape[2], near[0].shape[2]
    square = (length, width)
    results = [(3 * near[1].shape[1], frames)] + [square] * 7 + [(length, 3 * width)]
    in_vmem = pl.BlockSpec(memory_space=pltpu.VMEM)
    anywhere = pl.BlockSpec(memory_space=pl.ANY)
    return pl.pallas_call(
        stem_kernel,
        in_specs=[in_vmem] * len(near) + [anywhere] * len(far),
        out_specs=[anywhere] * len(results),
        out_shape=[jax.ShapeDtypeStruct(r, bf16) for r in results],
        scratch_shapes=[pltpu.VMEM(x.shape, x.dtype) for x in far]
        + [pltpu.VMEM(r, bf16) for r in results]
        + [
            pltpu.VMEM(square, bf16),
            pltpu.VMEM((4, near[0].shape[0] * frames // 128, 128), bf16),
            pltpu.VMEM((3, near[0].shape[0] * frames // 128, 128), bf16),
            pltpu.SemaphoreType.DMA((len(far),)),
            pltpu.SemaphoreType.DMA((5 + 4 * (length // BLOCK),)),
            pltpu.SemaphoreType.DMA((3,)),
            pltpu.SemaphoreType.DMA((3,)),
        ],
        compiler_params=pltpu.CompilerParams(
            vmem_limit_bytes=VMEM_LIMIT, collective_id=3, has_side_effects=True
        ),
        name="stem",
    )(*near, *far)


def stem_back_kernel(
    gq_ref,
    gk_ref,
    gv_ref,
    w_qkv_ref,
    gmid_ref,
    stem_ref,
    normed_ref,
    gain_ref,
    slope_two_ref,
    w_two_ref,
    act_even_ref,
    act_odd_ref,
    slope_even_ref,
    slope_odd_ref,
    w_one_ref,
    taps_ref,
    gw_qkv_ref,
    gw_two_ref,
    gw_one_ref,
    gmel_ref,
    sums_ref,
    normed_t_ref,
    two_ref,
    two_ahead_ref,
    two_t_ref,
    two_ahead_t_ref,
    even_ref,
    odd_ref,
):
    length, width = stem_ref.shape
    steps = length // BLOCK
    ones = lambda v: jnp.sum(v, axis=0, keepdims=True)
    sums_ref[...] = jnp.zeros_like(sums_ref)

    @pl.loop(0, steps)
    def _(i):
        rows = pl.ds(pl.multiple_of(i * BLOCK, BLOCK), BLOCK)
        normed_t_ref[:, rows] = turned(normed_ref[rows])
        grad = (
            mm_nt(gq_ref[rows], w_qkv_ref[:, 0:width])
            + mm_nt(gk_ref[rows], w_qkv_ref[:, width : 2 * width])
            + mm_nt(gv_ref[rows], w_qkv_ref[:, 2 * width : 3 * width])
        )
        stem = stem_ref[rows].astype(f32)
        centred = stem - mean_of(stem)
        scale = lax.rsqrt(mean_of(centred * centred) + epsilon)
        unit = centred * scale
        gained = grad * row_of(gain_ref)
        back = scale * (gained - mean_of(gained) - unit * mean_of(gained * unit))
        grad_stem = (gmid_ref[rows] + back).astype(bf16).astype(f32)
        two = (grad_stem * slope_two_ref[rows].astype(f32)).astype(bf16)
        two_ref[rows] = two
        two_t_ref[:, rows] = turned(two)
        sums_ref[0:1] += ones(grad * unit)
        sums_ref[1:2] += ones(grad)
        sums_ref[2:3] += ones(two.astype(f32))

    for cols in chunks(width, BLOCK):
        two_ahead_ref[:, cols] = shifted(two_ref[:, cols].astype(f32), -1, 0).astype(bf16)

    @pl.loop(0, steps)
    def _(i):
        rows = pl.ds(pl.multiple_of(i * BLOCK, BLOCK), BLOCK)
        two_ahead_t_ref[:, rows] = turned(two_ahead_ref[rows])
        even = mm_nt(two_ref[rows], w_two_ref[1]) * slope_even_ref[rows].astype(f32)
        odd = mm_nt(two_ref[rows], w_two_ref[2]) + mm_nt(two_ahead_ref[rows], w_two_ref[0])
        odd = odd * slope_odd_ref[rows].astype(f32)
        even_ref[rows] = even.astype(bf16)
        odd_ref[rows] = odd.astype(bf16)
        sums_ref[3:4] += ones(even.astype(bf16).astype(f32)) + ones(odd.astype(bf16).astype(f32))

    @pl.loop(0, width // BLOCK)
    def _(j):
        cols = pl.ds(pl.multiple_of(j * BLOCK, BLOCK), BLOCK)
        for part, grad_ref in enumerate((gq_ref, gk_ref, gv_ref)):
            out = pl.ds(pl.multiple_of(part * width + j * BLOCK, BLOCK), BLOCK)
            gw_qkv_ref[:, out] = mm(normed_t_ref[...], grad_ref[:, cols]).astype(bf16)
        gw_two_ref[0, :, cols] = mm(two_ahead_t_ref[...], act_odd_ref[:, cols]).astype(bf16)
        gw_two_ref[1, :, cols] = mm(two_t_ref[...], act_even_ref[:, cols]).astype(bf16)
        gw_two_ref[2, :, cols] = mm(two_t_ref[...], act_odd_ref[:, cols]).astype(bf16)

    bins = w_one_ref.shape[1]
    gw_one = jnp.zeros((3 * bins, width), f32)
    for offset, grad_ref in ((0, even_ref), (1, odd_ref)):
        picked = [
            mm_nt(taps_ref[:, 2 * i * BLOCK : 2 * (i + 1) * BLOCK], pick_frames(BLOCK, 2 * BLOCK, offset))
            for i in range(steps)
        ]
        gw_one += mm(jnp.concatenate(picked, axis=1).astype(bf16), grad_ref[...])
    gw_one_ref[...] = jnp.zeros_like(gw_one_ref)
    gw_one_ref[:, 0 : 3 * bins] = gw_one.T.astype(bf16)
    even, odd = even_ref[...], odd_ref[...]
    mel_even = (
        mm_nt(odd, w_one_ref[0])
        + mm_nt(even, w_one_ref[1])
        + shifted(mm_nt(odd, w_one_ref[2]), 1, 0)
    )
    mel_odd = (
        shifted(mm_nt(even, w_one_ref[0]), -1, 0)
        + mm_nt(odd, w_one_ref[1])
        + mm_nt(even, w_one_ref[2])
    )
    mel_even, mel_odd = turned(mel_even), turned(mel_odd)
    for i in range(steps):
        cols = slice(i * BLOCK, (i + 1) * BLOCK)
        frames = slice(2 * i * BLOCK, 2 * (i + 1) * BLOCK)
        gmel_ref[:, frames] = (
            mm(mel_even[:, cols], pick_frames(BLOCK, 2 * BLOCK, 0))
            + mm(mel_odd[:, cols], pick_frames(BLOCK, 2 * BLOCK, 1))
        ).astype(bf16)


MESH = pl.DeviceIdType.MESH


def remote(source, target, send, recv, to):
    return pltpu.make_async_remote_copy(source, target, send, recv, device_id=to, device_id_type=MESH)


class Links:
    def __init__(self):
        dp, chan = lax.axis_index(DP), lax.axis_index(CHAN)
        self.chan = chan
        self.core, self.x, self.y = dp % 2, (dp // 2) % 2, dp // 4
        self.by_core = (self.dest(0, 0, 1), chan)
        self.by_x = (self.dest(0, 1, 0), chan)
        self.by_y = (self.dest(1, 0, 0), chan)
        self.by_z = [(dp, (chan + r) % 4) for r in (1, 2, 3)]
        self.by_next = (dp, chan + 1 - 2 * (chan % 2))
        self.by_far = (dp, (chan + 2) % 4)
        self.partners = [self.by_core, self.by_x, self.by_y] + self.by_z

    def dest(self, dy, dx, dc):
        flip = lambda bit, turn: 1 - bit if turn else bit
        return 4 * flip(self.y, dy) + 2 * flip(self.x, dx) + flip(self.core, dc)

    def greet(self, partners):
        for partner in partners:
            pl.semaphore_signal(pltpu.get_barrier_semaphore(), inc=1, device_id=partner, device_id_type=MESH)

    def met(self, partners):
        pl.semaphore_wait(pltpu.get_barrier_semaphore(), len(partners))


def stacked(bins):
    return jnp.concatenate([bins[:, at : at + 128] for at in range(0, bins.shape[1], 128)], axis=0)


def by_place(links, out_ref, in_ref, share):
    parts = [out_ref[links.chan], in_ref[0], in_ref[1], in_ref[2]]
    parts = [part.astype(f32) for part in parts]
    parts = [jnp.concatenate([p[at : at + share] for at in range(0, p.shape[0], share)], axis=1) for p in parts]
    placed = []
    for z in range(4):
        value = parts[0]
        for r in (1, 2, 3):
            value = jnp.where((links.chan + 4 - r) % 4 == z, parts[r], value)
        placed.append(value)
    return placed


class Task:
    def __init__(self, links, x_first, sems, n, cut, source, own, cin, fin, sin, z_out, z_in, stage=0):
        self.links, self.x_first, self.sems, self.n, self.cut = links, x_first, sems, n, cut
        self.source, self.own, self.cin, self.fin, self.sin = source, own, cin, fin, sin
        self.z_out, self.z_in, self.stage = z_out, z_in, stage
        self.ways = (links.by_x, links.by_y) if x_first else (links.by_y, links.by_x)

    def dest(self, slot, dc):
        dx, dy = (slot // 2, slot % 2) if self.x_first else (slot % 2, slot // 2)
        return self.links.dest(dy, dx, dc)

    def begin(self):
        if self.stage == 0:
            for slot in (3, 2, 1, 0):
                source = self.source(self.dest(slot, 1))
                remote(source, self.cin.at[slot], self.sems.send_c.at[self.n], self.sems.recv_c.at[self.n], self.links.by_core).start()
                if self.own is not None:
                    source = self.source(self.dest(slot, 0))
                    pltpu.make_async_copy(source, self.own.at[slot], self.sems.load.at[self.n]).start()
            return
        if self.stage == 1:
            for slot in (3, 2):
                self.to_first(self.source.at[slot], slot)
        else:
            self.to_second(self.source.at[1])
        held = self.own.shape[0]
        pltpu.make_async_copy(self.source.at[pl.ds(0, held)], self.own, self.sems.load.at[self.n]).start()

    def to_first(self, ref, slot):
        remote(ref, self.fin.at[slot - 2], self.sems.send_f.at[self.n], self.sems.recv_f.at[self.n], self.ways[0]).start()

    def to_second(self, ref):
        remote(ref, self.sin, self.sems.send_s.at[self.n], self.sems.recv_s.at[self.n], self.ways[1]).start()

    def loaded(self, stage):
        if self.own is not None and self.stage == stage:
            pltpu.make_async_copy(self.own, self.own, self.sems.load.at[self.n]).wait()

    def wait(self, ref, send, recv, to):
        remote(ref, ref, send.at[self.n], recv.at[self.n], to).wait()

    def held(self, slot):
        if self.stage:
            return self.own[slot].astype(f32)
        own = self.own[slot] if self.own is not None else self.source(self.dest(slot, 0))[...]
        return own.astype(f32) + self.cin[slot].astype(f32)

    def core_done(self):
        self.loaded(0)
        self.wait(self.cin, self.sems.send_c, self.sems.recv_c, self.links.by_core)

    def after_core(self):
        self.core_done()
        for slot in (3, 2):
            self.cin[slot] = self.held(slot).astype(bf16)
            self.to_first(self.cin.at[slot], slot)

    def stop_at_core(self):
        self.core_done()
        for slot in (3, 2, 1, 0):
            self.cin[slot] = self.held(slot).astype(bf16)

    def stop_at_first(self):
        self.wait(self.fin, self.sems.send_f, self.sems.recv_f, self.ways[0])
        for slot in (1, 0):
            self.cin[slot] = (self.held(slot) + self.fin[slot].astype(f32)).astype(bf16)

    def after_first(self):
        self.loaded(1)
        self.wait(self.fin, self.sems.send_f, self.sems.recv_f, self.ways[0])
        leaving = self.own if self.stage else self.cin
        leaving[1] = (self.held(1) + self.fin[1].astype(f32)).astype(bf16)
        self.to_second(leaving.at[1])

    def z_copies(self):
        theirs = 1 - self.links.chan % 2
        sems = self.sems.send_z.at[self.n], self.sems.recv_z.at[self.n]
        return [remote(self.z_out.at[2 * a + theirs], self.z_in.at[a], *sems, self.links.by_next) for a in range(2)]

    def after_second(self):
        self.loaded(2)
        self.wait(self.sin, self.sems.send_s, self.sems.recv_s, self.ways[1])
        total = self.held(0) + self.sin[...].astype(f32)
        if self.stage < 2:
            total = total + self.fin[0].astype(f32)
        for z in range(4):
            self.z_out[z] = self.cut(total, z).astype(bf16)
        for copy in self.z_copies():
            copy.start()

    def after_third(self):
        chan = self.links.chan
        self.wait(self.z_in.at[pl.ds(0, 2)], self.sems.send_z, self.sems.recv_z, self.links.by_next)
        far = (chan + 2) % 4
        self.z_out[far] = (self.z_out[far].astype(f32) + self.z_in[far // 2].astype(f32)).astype(bf16)
        remote(self.z_out.at[far], self.z_in.at[2], self.sems.send_w.at[self.n], self.sems.recv_w.at[self.n], self.links.by_far).start()

    def finish(self):
        chan = self.links.chan
        self.wait(self.z_in.at[2], self.sems.send_w, self.sems.recv_w, self.links.by_far)
        return self.z_out[chan].astype(f32) + self.z_in[chan // 2].astype(f32) + self.z_in[2].astype(f32)


def cut_rows(block, z):
    share = block.shape[0] // 4
    return block[z * share : (z + 1) * share]


def cut_columns(block, z):
    share = block.shape[1] // 4
    first = z * share // 128 * 128
    taken = block[:, first : first + (share + 127) // 128 * 128]
    skip = z * share - first
    return pltpu.roll(taken, taken.shape[1] - skip, 1) if skip else taken


def cut_half_tiles(block, z):
    taken = block[:, z // 2 * 128 : (z // 2 + 1) * 128]
    return pltpu.roll(taken, 64, 1) if z % 2 else taken


SEMS = ("send_c", "recv_c", "load", "send_f", "recv_f", "send_s", "recv_s", "send_z", "recv_z", "send_w", "recv_w")


def sems_for(count):
    return [pltpu.SemaphoreType.DMA((count,)) for _ in SEMS]


def bufs_for(count, shape, *slots):
    return [pltpu.VMEM((count,) + ((slot,) if slot else ()) + shape, bf16) for slot in slots]


def rows_of(ref, block, start, count):
    return lambda d: ref.at[pl.ds(pl.multiple_of(d * block, block), block), pl.ds(start, count)]


def pair_back(p, q_ref, k_ref, v_ref, et_of, inverse_ref, gctx_ref, ctx_ref, dq_ref, dk_ref, dv_ref, sums_ref, ds_ref, between):
    length, width = q_ref.shape[0], 2 * HEAD_DIM
    cols = pl.ds(pl.multiple_of(p * width, width), width)
    lane = lax.broadcasted_iota(jnp.int32, (length, width), 1)
    row = lax.broadcasted_iota(jnp.int32, (width, length), 0)
    scale = HEAD_DIM ** (-0.5)
    grad_t = gctx_ref[:, cols].astype(f32).T
    grad_t = grad_t * jnp.where(row < HEAD_DIM, inverse_ref[2 * p], inverse_ref[2 * p + 1])
    grad_t = grad_t.astype(bf16).astype(f32)
    grad = grad_t.T
    inner_all = grad_t * ctx_ref[:, cols].astype(f32).T
    k_t = turned(k_ref[:, cols])
    q = q_ref[:, cols].astype(f32) * scale
    v = v_ref[:, cols].astype(f32)
    dq_t = []
    dk = jnp.zeros((length, width), f32)
    dv = jnp.zeros((length, width), f32)
    for h in range(2):
        at = HEAD_DIM * (1 - h)
        mine = lane // HEAD_DIM == h
        inner = jnp.sum(inner_all[h * HEAD_DIM : (h + 1) * HEAD_DIM], axis=0, keepdims=True)
        high = inner.astype(bf16).astype(f32)
        own_grad_t = jnp.where(row // HEAD_DIM == h, grad_t, 0.0)
        own_grad_t = jnp.where(row == at, -high, jnp.where(row == at + 1, high - inner, own_grad_t))
        own_grad_t = own_grad_t.astype(bf16)
        own_v = jnp.where(mine, v, jnp.where((lane == at) | (lane == at + 1), 1.0, 0.0)).astype(bf16)
        own_q = jnp.where(mine, q, 0.0).astype(bf16)
        own_grad = jnp.where(mine, grad, 0.0).astype(bf16)
        et_ref = et_of(h)
        ds_ref[...] = (et_ref[...].astype(f32) * mm(own_v, own_grad_t)).astype(bf16)
        dk += mm(ds_ref[...], own_q)
        dv += mm(et_ref[...], own_grad)
        dq_t.append(mm(k_t[h * HEAD_DIM : (h + 1) * HEAD_DIM], ds_ref[...]))
        if h == 0:
            between()
    dq = (jnp.concatenate(dq_t, axis=0).T * scale).astype(bf16)
    dv = dv.astype(bf16)
    dq_ref[:, cols] = dq
    dk_ref[:, cols] = dk.astype(bf16)
    dv_ref[:, cols] = dv
    sums_ref[0:1, cols] = jnp.sum(dq.astype(f32), axis=0, keepdims=True)
    sums_ref[1:2, cols] = jnp.sum(dv.astype(f32), axis=0, keepdims=True)


STEPS = ("begin", "after_core", "after_first", "after_second", "after_third", "finish")
TASKS = ("d0", "d1", "d2", "u0", "u1", "u2", "o", "q0", "q1", "q2", "t0", "t1", "t2", "t3", "t4", "t5", "n", "m")
SCHEDULE = {
    "pairs": (
        (0, 1, 6),
        (3, 4, 1),
        (5, 5, 1),
    ),
    "middle": (
        (1, 3, 0),
        (1, 3, 1),
        (3, 4, 0),
        (3, 2, 2),
        (3, 2, 3),
        (5, 5, 0),
        (5, 2, 4),
        (5, 2, 5),
    ),
    "qkv": (
        (1, 3, 2),
        (2, 2, 6),
    ),
    "rows": (
        (1, 3, 4),
        (1, 3, 3),
        (2, 4, 2),
        (2, 1, 7),
    ),
    "ahead": (
        (0, 1, 8),
        (0, 3, 5),
        (0, 1, 9),
        (0, 3, 6),
    ),
    "convs": (
        (1, 4, 4),
    ),
    "one": (
        (0, 4, 3),
        (0, 5, 2),
    ),
    "mel": (
        (0, 4, 5),
        (0, 2, 7),
        (0, 1, 17),
    ),
    "two": (
        (0, 4, 6),
        (0, 2, 8),
        (0, 1, 16),
        (0, 5, 4),
        (2, 5, 3),
    ),
    "tail": (
        (0, 2, 9),
        (0, 1, 10),
        (0, 1, 11),
        (0, 3, 7),
        (0, 1, 12),
        (0, 1, 13),
        (0, 2, 17),
        (0, 1, 14),
        (0, 3, 8),
        (0, 1, 15),
        (0, 5, 5),
        (0, 2, 16),
        (0, 5, 6),
        (0, 4, 7),
        (0, 3, 9),
        (0, 4, 8),
        (0, 2, 11),
        (0, 2, 10),
        (0, 4, 9),
        (0, 2, 13),
        (0, 3, 17),
        (0, 2, 12),
        (0, 5, 7),
        (0, 5, 8),
        (0, 2, 15),
        (0, 2, 14),
        (0, 4, 17),
        (0, 3, 16),
        (0, 3, 10),
        (0, 3, 11),
        (0, 5, 9),
        (0, 3, 12),
        (0, 3, 13),
        (0, 3, 14),
        (0, 4, 16),
        (0, 3, 15),
        (0, 4, 10),
        (0, 4, 11),
        (0, 4, 12),
        (0, 5, 17),
        (0, 4, 13),
        (0, 4, 14),
        (0, 5, 16),
        (0, 4, 15),
        (0, 5, 10),
        (0, 5, 11),
        (0, 5, 12),
        (0, 5, 13),
        (0, 5, 14),
        (0, 5, 15),
    ),
}


def back_kernel(*refs):
    joined, et, inverse, gctx, ctx, w_qkv, gmid, stem, normed, gain_ref, slope_two = refs[:11]
    w_two, act_even, act_odd, slope_even, slope_odd, w_one_ref, taps_ref = refs[11:18]
    half_down, core_down, core_up, gw_out, sums_b_ref, gb_up_ref = refs[18:24]
    up_z, down_z, out_z, qkv_z, two_z, one_z, small_z, gmel_z = refs[24:32]
    pool, d_ref, w_qkv_v, gmid_v, stem_v, normed_v, slope_two_v, w_two_v, gw_qkv = refs[32:41]
    gw_one, sums_a_ref, sums_ref = refs[41:44]
    rest = list(refs[44:])
    take = lambda count: [rest.pop(0) for _ in range(count)]
    own_h, sin_h, zo_h, zi_h = take(4)
    own_c, fin_c, sin_c, zo_c, zi_c = take(5)
    own_u, fin_u, sin_u, zo_u, zi_u = take(5)
    own_o, cin_o, fin_o, sin_o, zo_o, zi_o = take(6)
    bufs_q, bufs_t, bufs_n = take(5), take(5), take(5)
    small_buf, small_in, gmel_out, gmel_in = take(4)
    sems = SimpleNamespace(**dict(zip(SEMS, take(len(SEMS)))))
    loads, et_loads, send_m, recv_m, send_g, recv_g = rest
    length, width = ctx.shape
    steps, pairs, block = length // BLOCK, width // (2 * HEAD_DIM), width // 8
    bins = w_one_ref.shape[1]
    links = Links()
    links.greet(links.partners)

    q_v, k_v, v_v = (pool.at[i] for i in range(3))
    ctx_v, gctx_v, ds_v = pool.at[7], pool.at[8], pool.at[9]
    started = []

    def later(source, target):
        copy = pltpu.make_async_copy(source, target, loads.at[len(started)])
        started.append(copy)
        return copy

    def load(source, target):
        copy = later(source, target)
        copy.start()
        return copy

    def et_load(head, slot):
        return pltpu.make_async_copy(et.at[head], pool.at[3 + slot], et_loads.at[slot])

    first = [load(joined.at[:, pl.ds(i * width, width)], pool.at[i]) for i in range(3)]
    first += [load(gctx, gctx_v), load(ctx, ctx_v)]
    for head in range(2):
        et_load(head, head).start()

    tasks = {}

    def add(name, x_first, cut, source, own, cin, fin, sin, z_out, z_in, stage=0):
        tasks[name] = Task(
            links, x_first, sems, len(tasks), cut, source, own, cin, fin, sin, z_out, z_in, stage
        )

    at = lambda k, *bufs: [ref.at[k] for ref in bufs]
    part, third, rest_rows, half = core_down.shape[2], core_up.shape[3], block // 3, block // 2
    for k in range(2):
        own, sin, z_out, z_in = at(k, own_h, sin_h, zo_h, zi_h)
        add(f"d{k}", k != 0, cut_rows, half_down.at[k], own, None, None, sin, z_out, z_in, 2)
    own, *bufs = at(0, own_c, fin_c, sin_c, zo_c, zi_c)
    add("d2", True, cut_rows, core_down, own, None, *bufs, 1)
    for k in range(3):
        own, *bufs = at(k, own_u, fin_u, sin_u, zo_u, zi_u)
        add(f"u{k}", k == 1, cut_columns, core_up.at[k], own, None, *bufs, 1)
    own, *bufs = at(0, own_o, cin_o, fin_o, sin_o, zo_o, zi_o)
    add("o", True, cut_columns, rows_of(gw_out, block, 0, width), own, *bufs)
    for k in range(3):
        source = lambda d, k=k: gw_qkv.at[pl.ds(pl.multiple_of(d * block + k * rest_rows, rest_rows), rest_rows)]
        add(f"q{k}", k == 1, cut_columns, source, None, *at(k, *bufs_q))
    for k in range(6):
        source = lambda d, k=k: pool.at[7 + k // 2, pl.ds(pl.multiple_of(d * block + k % 2 * half, half), half)]
        add(f"t{k}", k % 2 == 0, cut_columns, source, None, *at(k, *bufs_t))
    add("n", False, cut_half_tiles, rows_of(gw_one, block, 0, gw_one.shape[1]), None, *at(0, *bufs_n))
    quarter = width // 4

    def store(name):
        total = tasks[name].finish()
        k = int(name[1:] or 0)
        if name[0] == "d":
            down_z[:, k * part : (k + 1) * part] = total
        elif name[0] == "u":
            up_z[:, k * third // 4 : (k + 1) * third // 4] = total
        elif name == "o":
            out_z[...] = total[:, 0:quarter]
        elif name[0] == "q":
            qkv_z[k * rest_rows : (k + 1) * rest_rows] = total[:, 0 : 3 * quarter]
        elif name[0] == "t":
            two_z[k // 2, k % 2 * half : (k % 2 + 1) * half] = total[:, 0:quarter]
        else:
            one_z[...] = total

    small_ways = [links.by_core, links.by_x, links.by_y, links.by_next, links.by_far]

    def small_step(step):
        i = STEPS.index(step)
        if i == 0:
            small_buf[0, 0:1] = sums_b_ref[0:1]
            small_buf[0, 1:2] = sums_ref[3:4]
            small_buf[0, 2:3] = sums_ref[2:3]
            small_buf[0, 3:5] = sums_ref[0:2]
            small_buf[0, 5:7] = sums_a_ref[0:2]
            small_buf[0, 7:8] = sums_b_ref[4:5]
            small_buf[0, 8:10] = sums_b_ref[2:4]
            small_buf[0, 10:11] = sums_b_ref[1:2]
            for k in range(4):
                small_buf[0, 11 + k : 12 + k] = gb_up_ref[:, k * width : (k + 1) * width]
            small_buf[0, 15:16] = jnp.zeros((1, width), f32)
        else:
            got = small_in.at[i - 1]
            remote(got, got, send_m.at[i - 1], recv_m.at[i - 1], small_ways[i - 1]).wait()
            total = small_buf[i - 1] + small_in[i - 1]
            if i == 5:
                small_z[...] = total
                return
            small_buf[i] = total
        remote(small_buf.at[i], small_in.at[i], send_m.at[i], recv_m.at[i], small_ways[i]).start()

    def run(step, *names):
        for name in names:
            if name == "m":
                small_step(step)
            elif step == STEPS[5]:
                store(name)
            else:
                getattr(tasks[name], step)()

    def ticks(place, at=None):
        for index, step, task in SCHEDULE.get(place, ()):
            work = lambda step=step, task=task: run(STEPS[step], TASKS[task])
            if at is None or isinstance(at, int):
                if at in (None, index):
                    work()
            else:
                pl.when(at == index)(work)

    links.met(links.partners)
    run(STEPS[0], "d0", "d1", "d2", "u0", "u1", "u2", "o")
    late = [
        later(normed, normed_v),
        later(w_qkv, w_qkv_v),
        later(gmid, gmid_v),
        later(stem, stem_v),
        later(slope_two, slope_two_v),
        later(w_two, w_two_v),
    ]
    for copy in first:
        copy.wait()
    for head in range(2, 4):
        et_load(head, head).start()

    @pl.loop(0, pairs)
    def _(p):
        for h in range(2):
            et_load(2 * p + h, (2 * p + h) % 4).wait()
        pair_back(
            p,
            q_v,
            k_v,
            v_v,
            lambda h: pool.at[3 + (2 * p + h) % 4],
            inverse,
            gctx_v,
            ctx_v,
            d_ref.at[0],
            d_ref.at[1],
            d_ref.at[2],
            sums_a_ref,
            ds_v,
            lambda: ticks("middle", p),
        )

        @pl.when(p == 0)
        def _():
            for copy in late:
                copy.start()

        @pl.when(p + 2 < pairs)
        def _():
            for h in range(2):
                et_load(2 * p + 4 + h, (2 * p + h) % 4).start()

        ticks("pairs", p)

    acts = [load(act_even, pool.at[5]), load(act_odd, pool.at[6])]
    for copy in late:
        copy.wait()
    ones = lambda v: jnp.sum(v, axis=0, keepdims=True)
    normed_t, two_v, two_ahead, two_t, two_ahead_t = (pool.at[i] for i in range(5))
    act_v = [pool.at[5], pool.at[6]]
    even_v, odd_v = pool.at[0], d_ref.at[2]
    gw_two = [pool.at[7 + k] for k in range(3)]
    sums_ref[...] = jnp.zeros_like(sums_ref)

    @unrolled(steps)
    def _(i):
        rows = pl.ds(i * BLOCK, BLOCK)
        normed_t[:, rows] = turned(normed_v[rows])

    ticks("turn")

    @unrolled(3)
    def _(j):
        cols = pl.ds(j * width, width)
        gw_qkv[:, cols] = mm(normed_t[...], d_ref[j]).astype(bf16)
        ticks("qkv", j)

    run(STEPS[0], "q0", "q1", "q2")

    @unrolled(steps)
    def _(i):
        rows = pl.ds(i * BLOCK, BLOCK)
        grad = (
            mm_nt(d_ref[0, rows], w_qkv_v[:, 0:width])
            + mm_nt(d_ref[1, rows], w_qkv_v[:, width : 2 * width])
            + mm_nt(d_ref[2, rows], w_qkv_v[:, 2 * width : 3 * width])
        )
        stem = stem_v[rows].astype(f32)
        centred = stem - mean_of(stem)
        scale = lax.rsqrt(mean_of(centred * centred) + epsilon)
        unit = centred * scale
        gained = grad * row_of(gain_ref)
        back = scale * (gained - mean_of(gained) - unit * mean_of(gained * unit))
        grad_stem = (gmid_v[rows] + back).astype(bf16).astype(f32)
        two = (grad_stem * slope_two_v[rows].astype(f32)).astype(bf16)
        two_v[rows] = two
        two_t[:, rows] = turned(two)
        sums_ref[0:1] += ones(grad * unit)
        sums_ref[1:2] += ones(grad)
        sums_ref[2:3] += ones(two.astype(f32))
        ticks("rows", i)

    slope_v = d_ref
    for copy in acts:
        copy.wait()
    slopes = [load(slope_even, slope_v.at[0]), load(slope_odd, slope_v.at[1])]
    for cols in chunks(width, BLOCK):
        two_ahead[:, cols] = shifted(two_v[:, cols].astype(f32), -1, 0).astype(bf16)

    @unrolled(steps)
    def _(i):
        rows = pl.ds(i * BLOCK, BLOCK)
        two_ahead_t[:, rows] = turned(two_ahead[rows])

    ticks("ahead")

    for copy in slopes:
        copy.wait()

    @unrolled(steps)
    def _(i):
        rows = pl.ds(i * BLOCK, BLOCK)
        even = mm_nt(two_v[rows], w_two_v[1]) * slope_v[0, rows].astype(f32)
        odd = mm_nt(two_v[rows], w_two_v[2]) + mm_nt(two_ahead[rows], w_two_v[0])
        odd = odd * slope_v[1, rows].astype(f32)
        even, odd = even.astype(bf16), odd.astype(bf16)
        even_v[rows] = even
        odd_v[rows] = odd
        sums_ref[3:4] += ones(even.astype(f32)) + ones(odd.astype(f32))
        ticks("convs", i)

    run(STEPS[0], "m")

    total_one = jnp.zeros((3 * bins, width), f32)
    for offset, grad_ref in ((0, even_v), (1, odd_v)):
        picked = [
            mm_nt(taps_ref[:, 2 * i * BLOCK : 2 * (i + 1) * BLOCK], pick_frames(BLOCK, 2 * BLOCK, offset))
            for i in range(steps)
        ]
        total_one += mm(jnp.concatenate(picked, axis=1).astype(bf16), grad_ref[...])
    share = bins // 4
    spread = []
    for z in range(4):
        spread += [total_one[(4 * j + z) * share : (4 * j + z + 1) * share] for j in range(3)]
        spread.append(jnp.zeros((64 - 3 * share, width), f32))
    gw_one[...] = jnp.concatenate(spread, axis=0).T.astype(bf16)
    run(STEPS[0], "n")
    ticks("one")

    even, odd = even_v[...], odd_v[...]
    mel_even = (
        mm_nt(odd, w_one_ref[0])
        + mm_nt(even, w_one_ref[1])
        + shifted(mm_nt(odd, w_one_ref[2]), 1, 0)
    )
    mel_odd = (
        shifted(mm_nt(even, w_one_ref[0]), -1, 0)
        + mm_nt(odd, w_one_ref[1])
        + mm_nt(even, w_one_ref[2])
    )
    mel_even, mel_odd = turned(mel_even), turned(mel_odd)
    share = bins // 4
    given = [[] for _ in range(4)]
    for i in range(steps):
        cols = slice(i * BLOCK, (i + 1) * BLOCK)
        frames = slice(2 * i * BLOCK, 2 * (i + 1) * BLOCK)
        gmel = mm(mel_even[:, cols], pick_frames(BLOCK, 2 * BLOCK, 0))
        gmel += mm(mel_odd[:, cols], pick_frames(BLOCK, 2 * BLOCK, 1))
        for z in range(4):
            given[z].append(gmel[z * share : (z + 1) * share])
    for z in range(4):
        gmel_out[z] = stacked(jnp.concatenate(given[z], axis=1)).astype(bf16)
    gmel_copies = [
        remote(gmel_out.at[(links.chan + r) % 4], gmel_in.at[r - 1], send_g.at[r - 1], recv_g.at[r - 1], links.by_z[r - 1])
        for r in (1, 2, 3)
    ]
    for copy in gmel_copies:
        copy.start()
    ticks("mel")
    for k, (left, right) in enumerate(((two_ahead_t, 1), (two_t, 0), (two_t, 1))):
        gw_two[k][...] = mm(left[...], act_v[right][...]).astype(bf16)
        run(STEPS[0], f"t{2 * k}", f"t{2 * k + 1}")
        ticks("two", k)
    ticks("tail")

    for copy in gmel_copies:
        copy.wait()
    placed = by_place(links, gmel_out, gmel_in, share)
    gmel_z[...] = jnp.concatenate([part[:, None] for part in placed], axis=1).astype(bf16)
    ticks("end")


def run_back(operands):
    joined, et, w_one, taps = operands[0], operands[1], operands[16], operands[17]
    length, width = operands[4].shape
    block, quarter = width // 8, width // 4
    bins, frames = w_one.shape[1], taps.shape[1]
    held = pl.BlockSpec(memory_space=pltpu.VMEM)
    far = pl.BlockSpec(memory_space=pl.ANY)
    near = (2, 9, 16, 17, 22, 23)
    part, third = operands[19].shape[2], operands[20].shape[3]
    square = (length, width)
    vmem = lambda *shape: pltpu.VMEM(shape, bf16)
    scratch = [
        vmem(10, *square),
        vmem(3, *square),
        vmem(width, 3 * width),
        pltpu.VMEM(square, f32),
        vmem(*square),
        vmem(*square),
        vmem(*square),
        vmem(3, width, width),
        vmem(width, 3 * width),
        vmem(width, 256),
        pltpu.VMEM((8, width), f32),
        pltpu.VMEM((8, width), f32),
        *bufs_for(2, (width, part), 1, 0),
        *bufs_for(2, (quarter, part), 4, 3),
        *bufs_for(1, (width, part), 2, 2, 0),
        *bufs_for(1, (quarter, part), 4, 3),
        *bufs_for(3, (block, third), 2, 2, 0),
        *bufs_for(3, (block, third // 4), 4, 3),
        *bufs_for(1, (block, width), 4, 4, 2, 0),
        *bufs_for(1, (block, 256), 4, 3),
        *bufs_for(3, (block // 3, 3 * width), 4, 2, 0),
        *bufs_for(3, (block // 3, 640), 4, 3),
        *bufs_for(6, (block // 2, width), 4, 2, 0),
        *bufs_for(6, (block // 2, 256), 4, 3),
        *bufs_for(1, (block, 256), 4, 2, 0),
        *bufs_for(1, (block, 128), 4, 3),
        pltpu.VMEM((5, 16, width), f32),
        pltpu.VMEM((5, 16, width), f32),
        vmem(4, bins // 4 * frames // 128, 128),
        vmem(3, bins // 4 * frames // 128, 128),
        *sems_for(17),
        pltpu.SemaphoreType.DMA((15,)),
        pltpu.SemaphoreType.DMA((4,)),
        pltpu.SemaphoreType.DMA((6,)),
        pltpu.SemaphoreType.DMA((6,)),
        pltpu.SemaphoreType.DMA((3,)),
        pltpu.SemaphoreType.DMA((3,)),
    ]
    shapes = (
        (block, width),
        (quarter, 3 * part),
        (block, quarter),
        (block, 3 * quarter),
        (3, block, quarter),
        (block, 128),
        (16, width),
    )
    return pl.pallas_call(
        back_kernel,
        in_specs=[held if i in near else far for i in range(len(operands))],
        out_specs=[held] * 8,
        out_shape=[jax.ShapeDtypeStruct(s, f32) for s in shapes]
        + [jax.ShapeDtypeStruct((bins // 4, 4, frames), bf16)],
        scratch_shapes=scratch,
        compiler_params=pltpu.CompilerParams(
            vmem_limit_bytes=VMEM_LIMIT, collective_id=2, has_side_effects=True
        ),
        name="back",
    )(*operands)


def last_kernel(*refs):
    lengths_ref, language_ref, down, up, out, qkv, two, one, small, gmel = refs[:10]
    outs = refs[10:]
    group_z, gmel_z, one_z, b_one_z, two_z, b_two_z, gain_a_z, bias_a_z, qkv_z, b_query_z = outs[:10]
    b_value_z, out_z, b_out_z, gain_b_z, bias_b_z, up_z, b_up_z, down_z, b_down_z = outs[10:]
    group = lax.broadcasted_iota(jnp.int32, (1, 128), 1)

    def count(c, total):
        return total + jnp.where(group == language_ref[c], lengths_ref[c], 0)

    frames = lax.fori_loop(0, lengths_ref.shape[0], count, jnp.zeros((1, 128), jnp.int32))
    width = small.shape[1]
    loss = small[0:1, 0:128] / (width * jnp.maximum(frames, 1).astype(f32))
    group_z[...] = loss.reshape(-1)[: group_z.shape[0]]
    gmel_z[...] = gmel[...]
    vectors = (b_one_z, b_two_z, gain_a_z, bias_a_z, b_query_z, b_value_z, b_out_z, gain_b_z, bias_b_z, b_down_z)
    for i, ref in enumerate(vectors):
        ref[...] = small[1 + i]
    for k in range(b_up_z.shape[0] // width):
        b_up_z[pl.ds(k * width, width)] = small[11 + k]
    up_z[...] = up[...]
    out_z[...] = out[...]
    qkv_z[...] = qkv[...]
    down_z[...] = down[...]
    for j in range(3):
        two_z[j] = two[j].T
    bins = one_z.shape[1]
    turned_one = one[...].T
    for j in range(3):
        one_z[j] = turned_one[j * bins : (j + 1) * bins]


def run_whole(kernel, name, operands, results, scratch):
    held = pl.BlockSpec(memory_space=pltpu.VMEM)
    scalar = pl.BlockSpec(memory_space=pltpu.SMEM)
    return pl.pallas_call(
        kernel,
        in_specs=[scalar if o.dtype == jnp.int32 else held for o in operands],
        out_specs=[held] * len(results),
        out_shape=[jax.ShapeDtypeStruct(*r) for r in results],
        scratch_shapes=[pltpu.VMEM(*s) for s in scratch],
        compiler_params=pltpu.CompilerParams(vmem_limit_bytes=VMEM_LIMIT),
        name=name,
    )(*operands)


def on_device(
    mel_input,
    w_conv1,
    b_conv1,
    w_conv2,
    b_conv2,
    gain_attn,
    bias_attn,
    w_qkv,
    b_query,
    b_value,
    w_out,
    b_out,
    gain_mlp,
    bias_mlp,
    w_up,
    b_up,
    w_down,
    b_down,
    target,
    lengths,
    row_clip,
    language,
):
    clip_count, frame_count, model_width = target.shape
    mel_count = mel_input.shape[2]
    bins = w_conv1.shape[1]
    fast = lax.axis_size(DP) == 8 and lax.axis_size(CHAN) == 4
    square = (frame_count, model_width)
    (
        taps,
        act_even,
        act_odd,
        slope_even,
        slope_odd,
        slope_two,
        stem,
        normed_a,
        joined,
    ) = run_stem(
        (mel_input, w_conv1, b_conv1, b_conv2, gain_attn, bias_attn, b_query, b_value),
        (w_conv2, jnp.asarray(sinusoids(frame_count, model_width)), w_qkv),
        frame_count,
    )
    context, weights_t, inverse = attend(joined, row_clip, lengths)
    inner = w_up.shape[1]
    deep = (model_width, inner)
    vectors = (b_out, gain_mlp, bias_mlp, b_up, b_down)
    if fast:
        (
            block_rows,
            grad_context,
            grad_middle,
            grad_w_out,
            half_down,
            core_down,
            core_up,
            sums_b,
            grad_b_up,
        ) = run_mlp_send((row_clip, lengths, language), (context, stem, w_out, w_up, w_down, target[0]), vectors)
    else:
        (
            block_rows,
            grad_context,
            grad_middle,
            grad_w_up,
            grad_w_down_t,
            grad_w_out,
            sums_b,
            grad_b_up,
        ) = run_whole(
            mlp_kernel,
            "mlp",
            (
                row_clip,
                lengths,
                language,
                context,
                stem,
                w_out,
                b_out,
                gain_mlp,
                bias_mlp,
                w_up,
                b_up,
                w_down,
                b_down,
                target[0],
            ),
            [
                (square, bf16),
                (square, bf16),
                (square, f32),
                (deep, bf16),
                (deep, bf16),
                ((model_width, model_width), bf16),
                ((8, model_width), f32),
                ((1, inner), f32),
            ],
            [
                (square, f32),
                (square, bf16),
                (square, bf16),
                ((frame_count, inner), bf16),
                ((frame_count, inner), bf16),
                (square, bf16),
                (square, bf16),
                ((1, inner), f32),
            ],
        )
    if fast:
        final_up, down_z, final_out, final_qkv, two_z, one_z, small, grad_mel = run_back(
            (
                joined,
                weights_t,
                inverse,
                grad_context,
                context,
                w_qkv,
                grad_middle,
                stem,
                normed_a,
                gain_attn,
                slope_two,
                w_conv2,
                act_even,
                act_odd,
                slope_even,
                slope_odd,
                w_conv1,
                taps,
                half_down,
                core_down,
                core_up,
                grad_w_out,
                sums_b,
                grad_b_up,
            )
        )
        part = bins // lax.axis_size(CHAN)
        vector = ((model_width,), f32)
        share = model_width // 4
        block = model_width // 8
        finals = run_whole(
            last_kernel,
            "last",
            (
                lengths,
                language,
                down_z,
                final_up,
                final_out,
                final_qkv,
                two_z,
                one_z,
                small,
                grad_mel,
            ),
            [
                ((GROUPS,), f32),
                (mel_input.shape, bf16),
                ((3, part, block), f32),
                vector,
                ((3, share, block), f32),
                vector,
                vector,
                vector,
                ((block, 3 * share), f32),
                vector,
                vector,
                ((block, share), f32),
                vector,
                vector,
                vector,
                ((block, inner // 4), f32),
                ((inner,), f32),
                ((share, inner // 8), f32),
                vector,
            ],
            [],
        )
        return (block_rows.reshape(target.shape), *finals[:17], finals[17].T, finals[18])
    else:
        *grads, sums_a = attend_back(joined, weights_t, inverse, grad_context, context)
        weight = (model_width, model_width)
        grad_w_qkv, grad_w_two_t, grad_w_one_t, back_mel, sums_c = run_whole(
            stem_back_kernel,
            "stem_back",
            (
                *grads,
                w_qkv,
                grad_middle,
                stem,
                normed_a,
                gain_attn,
                slope_two,
                w_conv2,
                act_even,
                act_odd,
                slope_even,
                slope_odd,
                w_conv1,
                taps,
            ),
            [
                ((model_width, 3 * model_width), bf16),
                ((3,) + weight, bf16),
                ((model_width, 256), bf16),
                ((bins, mel_count), bf16),
                ((8, model_width), f32),
            ],
            [
                ((model_width, frame_count), bf16),
                (square, bf16),
                (square, bf16),
                ((model_width, frame_count), bf16),
                ((model_width, frame_count), bf16),
                (square, bf16),
                (square, bf16),
            ],
        )
        grad_mel = lax.all_to_all(back_mel[:, None], CHAN, split_axis=0, concat_axis=1, tiled=True)

        small = jnp.concatenate(
            [
                sums_b[0:1],
                sums_c[3:4],
                sums_c[2:3],
                sums_c[0:2],
                sums_a[0:2],
                sums_b[4:5],
                sums_b[2:4],
                sums_b[1:2],
                grad_b_up.reshape(-1, model_width),
                jnp.zeros((1, model_width), f32),
            ]
        )

        def scatter(values, dp_at, chan_at):
            part = lax.psum_scatter(values, DP, scatter_dimension=dp_at, tiled=True)
            return lax.psum_scatter(part, CHAN, scatter_dimension=chan_at, tiled=True).astype(f32)

        final_down = scatter(grad_w_down_t, 1, 0).T
        final_up = scatter(grad_w_up, 0, 1)
        final_out = scatter(grad_w_out, 0, 1)
        final_qkv = scatter(grad_w_qkv, 0, 1)
        part_two = scatter(grad_w_two_t, 1, 2).transpose(0, 2, 1)
        one_rows = grad_w_one_t[:, : 3 * bins].reshape(-1, 3, bins).transpose(1, 2, 0)
        part_one = scatter(one_rows, 2, 1)
        small = lax.psum(small, (DP, CHAN))
    totals_all = [small[0, :GROUPS]] + [small[i] for i in range(1, 11)]
    totals_all.insert(10, small[11:15].reshape(-1))
    group_ids = jnp.arange(GROUPS, dtype=jnp.int32)
    member_all = language[:, None] == group_ids[None, :]
    frames_group = jnp.sum(jnp.where(member_all, lengths[:, None], 0), axis=0)
    group_loss = totals_all[0] / (model_width * jnp.maximum(frames_group, 1).astype(f32))
    return (
        block_rows.reshape(target.shape),
        group_loss,
        grad_mel,
        part_one,
        totals_all[1],
        part_two,
        totals_all[2],
        totals_all[3],
        totals_all[4],
        final_qkv,
        totals_all[5],
        totals_all[6],
        final_out,
        totals_all[7],
        totals_all[8],
        totals_all[9],
        final_up,
        totals_all[10],
        final_down,
        totals_all[11],
    )


def solution(mesh):
    whole = P()
    by_row = P((DP, CHAN), None, None)
    return jax.shard_map(
        on_device,
        mesh=mesh,
        in_specs=(P(CHAN, DP, None),) + (whole,) * 17 + (by_row,) + (whole,) * 3,
        out_specs=(
            by_row,
            whole,
            P(CHAN, DP, None),
            P(None, CHAN, DP),
            whole,
            P(None, CHAN, DP),
            whole,
            whole,
            whole,
            P(DP, CHAN),
            whole,
            whole,
            P(DP, CHAN),
            whole,
            whole,
            whole,
            P(DP, CHAN),
            whole,
            P(DP, CHAN),
            whole,
        ),
        check_vma=False,
    )
```
